32 devices in a mesh: gx: 4 (over z), gy: 4 (over x, core), gz: 2 (over y).
Axes of the slice: x: 2, y: 2, z: 4, core: 2. Of those that a mesh axis runs over, the one named last changes fastest.
Arguments:
- coarse_fields: float32 [4, 64, 64, 256], P(None, 'gx', 'gy', 'gz'), may hold values from -6 to 6
- coarse_wind: float32 [3, 64, 64, 256], P(None, 'gx', 'gy', 'gz'), may hold values from -0.4 to 0.4
- fine_fields: float32 [4, 128, 64, 256], P(None, 'gx', 'gy', 'gz'), may hold values from -6 to 6
- fine_wind: float32 [3, 128, 64, 256], P(None, 'gx', 'gy', 'gz'), may hold values from -0.4 to 0.4
- fine_owner: int32 [4, 4, 2], P('gx', 'gy', 'gz'), may hold values from 0 to 3, as said below
Outputs:
- coarse_next: float32 [4, 64, 64, 256], P(None, 'gx', 'gy', 'gz')
- fine_next: float32 [4, 128, 64, 256], P(None, 'gx', 'gy', 'gz')
The draws below stay inside these ranges and needn't reach their ends.
Inputs may be any that keep to these rules, and one draw needn't show every extreme that they name: `fine_owner`: in each row of fine boxes along the first direction (fixed second and third index), fine box i refines coarse box (i + r) mod 4 for an offset r of that row, so every row names every coarse box once.
All inputs are finite; a program needn't handle non-finite values.
Results may differ from the reference program's by a relative error of at most 0.0003.
Values sent between devices are 32-bit elements; how exact they have to be, the bound alone decides.
No kernel may reach another device: no remote copies, remote signals or barrier semaphores. Data moves between devices by JAX's collectives and lax.ppermute only.
A program may use at most 128 MiB of HBM per device.

```python
import jax
import jax.numpy as jnp
from jax import lax

FIELDS = 4
RATIO = 2
BOX_X = 16
BOX_Y = 16
BOX_Z = 128
BOXES_X = 4
BOXES_Y = 4
BOXES_Z = 2
NX = 64
NY = 64
NZ = 256
FINE_X = 128
FINE_Y = 64
FINE_Z = 256


def draw_fine_owner(key, part):
    row_count = BOXES_Y * BOXES_Z
    key_extra = jax.random.fold_in(key, 11)
    key_order = jax.random.fold_in(key, 23)
    extra = jax.random.randint(key_extra, (row_count,), 0, BOXES_X)
    places = jnp.arange(row_count)
    planted = jnp.where(places == 0, BOXES_X - 1, jnp.where(places == 1, BOXES_X // 2, jnp.where(places == 2, 1 % BOXES_X, extra)))
    order = jax.random.permutation(key_order, row_count)
    row_offset = planted[order].reshape(BOXES_Y, BOXES_Z)
    box_index = jnp.arange(BOXES_X)[:, None, None]
    return ((box_index + row_offset[None]) % BOXES_X).astype(jnp.int32)


def block_levels(stream_key, shape, pieces, least, high):
    loudness = 1.0
    for axis_at, shards_of in pieces:
        heights = jax.random.uniform(jax.random.fold_in(jax.random.fold_in(stream_key, 6), axis_at), (shards_of,), jnp.float32, least / len(pieces), high / len(pieces))
        loudness = loudness * jnp.repeat(jnp.exp(heights), shape[axis_at] // shards_of).reshape((-1,) + (1,) * (len(shape) - 1 - axis_at))
    return loudness


def normal_values(key, shape, deviation, bound, shards=(), held_as=jnp.bfloat16):
    entries = deviation * jax.random.normal(key, shape, jnp.float32)
    if shards:
        entries = entries * block_levels(key, shape, shards, -0.22, 0.18)
    return jnp.clip(entries, -bound, bound).astype(held_as)


def setup_inputs(seed: int = 0) -> dict:
    seeds = jax.random.split(jax.random.key(seed), 6)
    return {
        "coarse_fields": normal_values(seeds[0], (FIELDS, NX, NY, NZ), 1.0, 6.0, ((1, 4), (2, 4), (3, 2)), jnp.float32),
        "coarse_wind": jnp.clip(jax.random.uniform(seeds[1], (3, NX, NY, NZ), jnp.float32, -0.4, 0.4) * block_levels(seeds[1], (3, NX, NY, NZ), ((1, 4), (2, 4), (3, 2)), -0.4, 0.0), -0.4, 0.4),
        "fine_fields": normal_values(seeds[2], (FIELDS, FINE_X, FINE_Y, FINE_Z), 1.0, 6.0, ((1, 4), (2, 4), (3, 2)), jnp.float32),
        "fine_wind": jnp.clip(jax.random.uniform(seeds[3], (3, FINE_X, FINE_Y, FINE_Z), jnp.float32, -0.4, 0.4) * block_levels(seeds[3], (3, FINE_X, FINE_Y, FINE_Z), ((1, 4), (2, 4), (3, 2)), -0.4, 0.0), -0.4, 0.4),
        "fine_owner": draw_fine_owner(jax.random.fold_in(seeds[5], 71), 0),
    }


diffusion = 0.05
section_weights = (1.0 / 3.0, 0.5, 1.0)


def tendency(padded, velocity):
    center = padded[:, 1:-1, 1:-1, 1:-1]
    along_first = padded[:, 2:, 1:-1, 1:-1] - padded[:, :-2, 1:-1, 1:-1]
    along_second = padded[:, 1:-1, 2:, 1:-1] - padded[:, 1:-1, :-2, 1:-1]
    along_third = padded[:, 1:-1, 1:-1, 2:] - padded[:, 1:-1, 1:-1, :-2]
    beside_all = (padded[:, 2:, 1:-1, 1:-1] + padded[:, :-2, 1:-1, 1:-1]) + (padded[:, 1:-1, 2:, 1:-1] + padded[:, 1:-1, :-2, 1:-1]) + (padded[:, 1:-1, 1:-1, 2:] + padded[:, 1:-1, 1:-1, :-2])
    advect = velocity[0] * along_first + velocity[1] * along_second + velocity[2] * along_third
    return -0.5 * advect + diffusion * (beside_all - 6.0 * center)


def refine(coarse, direction):
    length = coarse.shape[direction]
    low_part = lax.slice_in_dim(coarse, 0, length - 1, axis=direction)
    high_part = lax.slice_in_dim(coarse, 1, length, axis=direction)
    odd_cells = 0.75 * low_part + 0.25 * high_part
    even_cells = 0.25 * low_part + 0.75 * high_part
    paired = jnp.stack((odd_cells, even_cells), axis=direction + 1)
    target = list(coarse.shape)
    target[direction] = 2 * (length - 1)
    return paired.reshape(target)


def coarse_slabs(padded, lead_y, span_y, lead_z, span_z):
    rows_y = jnp.concatenate((padded[:, :, lead_y:lead_y + 2], padded[:, :, lead_y + span_y:lead_y + span_y + 2]), axis=2)
    slab_y = rows_y[:, :, :, lead_z:lead_z + span_z + 2]
    rows_z = jnp.concatenate((padded[:, :, :, lead_z:lead_z + 2], padded[:, :, :, lead_z + span_z:lead_z + span_z + 2]), axis=3)
    slab_z = rows_z[:, :, lead_y:lead_y + span_y + 2, :]
    return slab_y, slab_z


def slab_faces(slab_y, slab_z):
    wide_y = refine(slab_y, 1)[:, 1:-1]
    low_y = 0.75 * wide_y[:, :, 0] + 0.25 * wide_y[:, :, 1]
    high_y = 0.25 * wide_y[:, :, 2] + 0.75 * wide_y[:, :, 3]
    faces_y = refine(jnp.stack((low_y, high_y), axis=2), 3)[:, :, :, 1:-1]
    wide_z = refine(refine(slab_z, 1)[:, 1:-1], 2)[:, :, 1:-1]
    low_z = 0.75 * wide_z[:, :, :, 0] + 0.25 * wide_z[:, :, :, 1]
    high_z = 0.25 * wide_z[:, :, :, 2] + 0.75 * wide_z[:, :, :, 3]
    faces_z = jnp.stack((low_z, high_z), axis=3)
    return faces_y, faces_z


def fine_padded(widened, faces_y, faces_z):
    padded = jnp.pad(widened, ((0, 0), (0, 0), (1, 1), (1, 1)))
    padded = padded.at[:, 1:-1, 0, 1:-1].set(faces_y[:, :, 0])
    padded = padded.at[:, 1:-1, -1, 1:-1].set(faces_y[:, :, 1])
    padded = padded.at[:, 1:-1, 1:-1, 0].set(faces_z[:, :, :, 0])
    padded = padded.at[:, 1:-1, 1:-1, -1].set(faces_z[:, :, :, 1])
    return padded


def coarsen(fine):
    blocks = fine.reshape(fine.shape[0], fine.shape[1] // 2, 2, fine.shape[2] // 2, 2, fine.shape[3] // 2, 2)
    return 0.125 * jnp.sum(blocks, axis=(2, 4, 6))


def split_boxes(whole, size_x, size_y, size_z):
    shaped = whole.reshape(whole.shape[0], whole.shape[1] // size_x, size_x, whole.shape[2] // size_y, size_y, whole.shape[3] // size_z, size_z)
    return shaped.transpose(1, 3, 5, 0, 2, 4, 6)


def join_boxes(boxes):
    shaped = boxes.transpose(3, 0, 4, 1, 5, 2, 6)
    return shaped.reshape(boxes.shape[3], boxes.shape[0] * boxes.shape[4], boxes.shape[1] * boxes.shape[5], boxes.shape[2] * boxes.shape[6])


def reference(coarse_fields, coarse_wind, fine_fields, fine_wind, fine_owner):
    lead_y = BOX_Y // 4
    span_y = BOX_Y // 2
    lead_z = BOX_Z // 4
    span_z = BOX_Z // 2
    total_boxes = BOXES_X * BOXES_Y * BOXES_Z
    rows_y = jnp.arange(BOXES_Y)[None, :, None]
    rows_z = jnp.arange(BOXES_Z)[None, None, :]
    fine_x = RATIO * BOX_X
    wind_boxes = split_boxes(fine_wind, fine_x, BOX_Y, BOX_Z).reshape((total_boxes, 3, fine_x, BOX_Y, BOX_Z))
    coarse_state = coarse_fields
    fine_state = fine_fields
    for fraction in section_weights:
        wrapped = jnp.pad(coarse_state, ((0, 0), (1, 1), (1, 1), (0, 0)), mode="wrap")
        padded = jnp.pad(wrapped, ((0, 0), (0, 0), (0, 0), (1, 1)))
        coarse_rate = tendency(padded, coarse_wind)

        def box_faces(number):
            index_x = (number // (BOXES_Y * BOXES_Z)).astype(jnp.int32)
            index_y = ((number // BOXES_Z) % BOXES_Y).astype(jnp.int32)
            index_z = (number % BOXES_Z).astype(jnp.int32)
            starts = (jnp.zeros((), jnp.int32), (index_x * BOX_X).astype(jnp.int32), (index_y * BOX_Y).astype(jnp.int32), (index_z * BOX_Z).astype(jnp.int32))
            window = lax.dynamic_slice(padded, starts, (FIELDS, BOX_X + 2, BOX_Y + 2, BOX_Z + 2))
            slab_y, slab_z = coarse_slabs(window, lead_y, span_y, lead_z, span_z)
            return slab_faces(slab_y, slab_z)

        faces_y, faces_z = lax.map(box_faces, jnp.arange(total_boxes, dtype=jnp.int32))
        faces_y = faces_y.reshape((BOXES_X, BOXES_Y, BOXES_Z) + faces_y.shape[1:])[fine_owner, rows_y, rows_z]
        faces_z = faces_z.reshape((BOXES_X, BOXES_Y, BOXES_Z) + faces_z.shape[1:])[fine_owner, rows_y, rows_z]
        fine_boxes = split_boxes(fine_state, fine_x, BOX_Y, BOX_Z)
        left_cells = jnp.roll(fine_boxes, 1, axis=0)[:, :, :, :, -1:]
        right_cells = jnp.roll(fine_boxes, -1, axis=0)[:, :, :, :, :1]
        widened = jnp.concatenate((left_cells, fine_boxes, right_cells), axis=4)
        widened = widened.reshape((total_boxes,) + widened.shape[3:])
        faces_y = faces_y.reshape((total_boxes,) + faces_y.shape[3:])
        faces_z = faces_z.reshape((total_boxes,) + faces_z.shape[3:])

        def fine_rate_of(inputs):
            return tendency(fine_padded(inputs[0], inputs[1], inputs[2]), inputs[3])

        rates = lax.map(fine_rate_of, (widened, faces_y, faces_z, wind_boxes))
        rates = join_boxes(rates.reshape((BOXES_X, BOXES_Y, BOXES_Z) + rates.shape[1:]))
        coarse_state = coarse_fields + fraction * coarse_rate
        fine_state = fine_fields + fraction * rates
    fine_boxes = split_boxes(fine_state, fine_x, BOX_Y, BOX_Z)
    averaged = jax.vmap(jax.vmap(jax.vmap(coarsen)))(fine_boxes)
    placed = jnp.zeros_like(averaged).at[fine_owner, rows_y, rows_z].set(averaged)
    coarse_boxes = split_boxes(coarse_state, BOX_X, BOX_Y, BOX_Z)
    coarse_boxes = coarse_boxes.at[:, :, :, :, :, lead_y:lead_y + span_y, lead_z:lead_z + span_z].set(placed)
    return join_boxes(coarse_boxes), fine_state
```

```python
import functools

import jax
import jax.numpy as jnp
import ml_dtypes
import numpy as np
from jax import lax
from jax.experimental import pallas as pl
from jax.experimental.pallas import tpu as pltpu
from jax.sharding import PartitionSpec as P

diffusion = 0.05
section_weights = (1.0 / 3.0, 0.5, 1.0)
F32 = jnp.float32
BF16 = jnp.bfloat16
PAD = 32
TOP = 8


class Sizes:
    def __init__(self, coarse_shape, fine_shape):
        self.q, self.x, self.y, self.z = coarse_shape
        self.fx = fine_shape[1]
        self.ly, self.sy = self.y // 4, self.y // 2
        self.lz, self.sz = self.z // 4, self.z // 2
        self.ex = self.x + 4
        self.ep = -(-self.ex // 8) * 8
        self.cols = self.sy + 4
        self.slab_rows = self.q * self.ex
        self.fe = self.fx + 4


def fine_weights(cells):
    out = np.zeros((2 * cells, cells + 2), np.float32)
    for m in range(cells):
        out[2 * m, m], out[2 * m, m + 1] = 0.25, 0.75
        out[2 * m + 1, m + 1], out[2 * m + 1, m + 2] = 0.75, 0.25
    return out


def constants(s):
    column = np.zeros((s.q, 16, s.z), np.float32)
    halo = np.zeros((s.q, 8, s.z), np.float32)
    for f in range(s.q):
        column[f, 2 * f, s.lz - 1], column[f, 2 * f, s.lz] = 0.75, 0.25
        column[f, 2 * f + 1, s.lz + s.sz - 1], column[f, 2 * f + 1, s.lz + s.sz] = 0.25, 0.75
        column[f, 8 + 2 * f, s.lz - 1] = 1.0
        column[f, 8 + 2 * f + 1, s.lz + s.sz] = 1.0
        halo[f, 2 * f, 0] = 1.0
        halo[f, 2 * f + 1, s.z - 1] = 1.0
    lanes = 256
    assert s.ex * s.cols <= lanes and s.q == 4 and s.y == 16 and s.z == 128
    keep = np.zeros((s.ep * s.y, lanes), np.float32)
    corner = np.zeros((s.ep * s.y, lanes), np.float32)
    for x in range(s.ex):
        for j in range(s.sy + 2):
            keep[x * s.y + s.ly - 1 + j, x * s.cols + 1 + j] = 1.0
        corner[x * s.y + s.ly - 1, x * s.cols] = 0.75
        corner[x * s.y + s.ly, x * s.cols] = 0.25
        corner[x * s.y + s.ly + s.sy - 1, x * s.cols + s.cols - 1] = 0.25
        corner[x * s.y + s.ly + s.sy, x * s.cols + s.cols - 1] = 0.75
    wide = -(-(s.fe * s.y + 2 * s.ep) // 128) * 128
    spread = np.zeros((lanes, wide), np.float32)
    along_x = fine_weights(s.x + 2)
    along_y = fine_weights(s.sy)
    assert along_x.shape == (s.fe, s.ex)
    for b in range(s.fe):
        for a in np.flatnonzero(along_x[b]):
            for h in range(s.y):
                for j in np.flatnonzero(along_y[h]):
                    spread[a * s.cols + 1 + j, b * s.y + h] = along_x[b, a] * along_y[h, j]
    for a in range(s.ex):
        spread[a * s.cols, s.fe * s.y + a] = 0.25
        spread[a * s.cols + s.cols - 1, s.fe * s.y + s.ep + a] = 0.25
    along_z = fine_weights(s.sz)
    to_fine = np.zeros((s.z, 2 * s.z), np.float32)
    to_fine[: s.sz, : s.z] = along_z[:, 1:-1].T
    to_fine[s.sz :, s.z :] = along_z[:, 1:-1].T
    place = np.zeros((3, s.q, 24, s.z), np.float32)
    for k in range(3):
        for f in range(s.q):
            place[k, f, 8 * k + 2 * f, 0] = 1.0
            place[k, f, 8 * k + 2 * f + 1, s.z - 1] = 1.0
    pair = np.zeros((2, s.z, s.z), np.float32)
    for h in range(s.z):
        pair[0, h, h // 2] = 0.125
        pair[1, h, s.sz + h // 2] = 0.125
    made = dict(column=column, halo=halo, keep=keep, corner=corner, spread=spread, to_fine=to_fine, place=place, pair=pair)
    return {name: jnp.asarray(value.astype(ml_dtypes.bfloat16)) for name, value in made.items()}


def halves(value):
    high = value.astype(BF16)
    return high, (value - high.astype(F32)).astype(BF16)


def times(value, matrix):
    high, low = halves(value)
    return jnp.dot(high, matrix, preferred_element_type=F32) + jnp.dot(low, matrix, preferred_element_type=F32)


def columns_of(matrix, value):
    high, low = halves(value)
    over = (((1,), (1,)), ((), ()))
    return lax.dot_general(matrix, high, over, preferred_element_type=F32) + lax.dot_general(
        matrix, low, over, preferred_element_type=F32
    )


def stencil(center, x_low, x_high, y_low, y_high, z_low, z_high, wind):
    advect = wind[0] * (x_high - x_low) + wind[1] * (y_high - y_low) + wind[2] * (z_high - z_low)
    beside = (x_high + x_low) + (y_high + y_low) + (z_high + z_low)
    return -0.5 * advect + diffusion * (beside - 6.0 * center)


def copies(pairs, sems):
    return [pltpu.make_async_copy(src, dst, sems.at[i]) for i, (src, dst) in enumerate(pairs)]


def pack_kernel(s, c0, f0, fw, halo, xup, xdn, yup, ydn, zs, fup, fdn, sems):
    x, fx, q = s.x, s.fx, s.q
    pairs = []
    for f in range(q):
        pairs.append((f0.at[f, fx - 3 : fx], fup.at[3 * f : 3 * f + 3]))
        pairs.append((f0.at[f, 0:3], fdn.at[3 * f : 3 * f + 3]))
    for w in range(3):
        at = 3 * q + 2 * w
        pairs.append((fw.at[w, fx - 2 : fx], fup.at[at : at + 2]))
        pairs.append((fw.at[w, 0:2], fdn.at[at : at + 2]))
    moves = copies(pairs, sems)
    for move in moves:
        move.start()
    xup[...] = c0[:, x - 2 : x]
    xdn[...] = c0[:, 0:2]
    pack_rows(s, c0, halo, yup, ydn, zs)
    for move in moves:
        move.wait()


def pack_rows(s, state, halo, yup, ydn, zs):
    flat = state.reshape(s.q * s.x * s.y, s.z)
    zs_sum = None
    for f in range(s.q):
        yup[f] = flat[pl.ds(f * s.x * s.y + s.y - 1, s.x, stride=s.y), :]
        ydn[f] = flat[pl.ds(f * s.x * s.y, s.x, stride=s.y), :]
        part = columns_of(halo[f], flat[f * s.x * s.y : (f + 1) * s.x * s.y, :])
        zs_sum = part if zs_sum is None else zs_sum + part
    zs[...] = zs_sum


def coarse_kernel(s, step, width, *refs):
    last = step == 2
    (place_in, c0, wind, ck, xlo, xhi, ylo, yhi, zc, column, keep, corner, place, halo), refs = refs[:14], refs[14:]
    if last:
        (out, slab), refs = refs[:2], refs[2:]
    else:
        (out, slab, xup, xdn, yup, ydn, zs), refs = refs[:7], refs[7:]
    pad, ghost, sems = refs
    q, x, y, z = s.q, s.x, s.y, s.z
    layers = s.ep
    moves = copies(
        [
            (ck, pad.at[:, 2 : 2 + x, TOP : TOP + y]),
            (xlo, pad.at[:, 2 - width : 2, TOP : TOP + y]),
            (xhi, pad.at[:, 2 + x : 2 + x + width, TOP : TOP + y]),
        ],
        sems,
    )
    for move in moves:
        move.start()
    if width < 2:
        for f in range(q):
            pad[f, 0, TOP : TOP + y, :] = jnp.zeros((y, z), F32)
            pad[f, x + 3, TOP : TOP + y, :] = jnp.zeros((y, z), F32)
    for f in range(q):
        for extra in range(s.ex, layers):
            pad[f, extra, TOP : TOP + y, :] = jnp.zeros((y, z), F32)
    flat = pad.reshape(q * layers * PAD, z)
    for f in range(q):
        base = (f * layers + 2) * PAD
        flat[pl.ds(base + TOP - 1, x, stride=PAD), :] = ylo[f]
        flat[pl.ds(base + TOP + y, x, stride=PAD), :] = yhi[f]
    turned = jnp.transpose(zc[...])
    lane = lax.broadcasted_iota(jnp.int32, (x * y, z), 1)
    has_low = place_in[0, 0].astype(F32)
    has_high = place_in[0, 1].astype(F32)
    for f in range(q):
        ghost[f] = jnp.where(
            lane == 0, turned[:, 2 * f + 1 : 2 * f + 2] * has_low, turned[:, 2 * f : 2 * f + 1] * has_high
        ).reshape(x, y, z)
    for move in moves:
        move.wait()
    total = None
    for f in range(q):
        start = f * layers * PAD + TOP
        rows = [flat[pl.ds(start + at, layers, stride=PAD), :] for at in (s.ly - 1, s.ly, s.ly + s.sy - 1, s.ly + s.sy)]
        low = 0.75 * rows[0] + 0.25 * rows[1]
        high = 0.25 * rows[2] + 0.75 * rows[3]
        lanes = lax.broadcasted_iota(jnp.int32, low.shape, 1)
        packed = jnp.where(lanes < s.sz, pltpu.roll(low, z - s.lz, 1), pltpu.roll(high, s.lz, 1))
        slab[f * s.ex : (f + 1) * s.ex, :] = packed[: s.ex]
        body = pad[f, :, TOP : TOP + y, :].reshape(layers * y, z)
        part = columns_of(column[f], body)
        total = part if total is None else total + part
    zl = times(total[:8], keep[...]) + times(total[8:], corner[...])
    slab[s.slab_rows : s.slab_rows + 8, :] = zl[:, :z]
    slab[s.slab_rows + 8 : s.slab_rows + 16, :] = zl[:, z:]
    fraction = section_weights[step]
    lane_tile = lax.broadcasted_iota(jnp.int32, (y, z), 1)

    def layer(at, carry):
        w = [wind[d, at] for d in range(3)]
        for f in range(q):
            center = pad[f, at + 2, TOP : TOP + y, :]
            edge = ghost[f, at]
            rate = stencil(
                center,
                pad[f, at + 1, TOP : TOP + y, :],
                pad[f, at + 3, TOP : TOP + y, :],
                pad[f, at + 2, TOP - 1 : TOP + y - 1, :],
                pad[f, at + 2, TOP + 1 : TOP + y + 1, :],
                jnp.where(lane_tile == 0, edge, pltpu.roll(center, 1, 1)),
                jnp.where(lane_tile == z - 1, edge, pltpu.roll(center, z - 1, 1)),
                w,
            )
            out[f, at] = c0[f, at] + fraction * rate
        return carry

    lax.fori_loop(0, x, layer, 0)
    if not last:
        xup[...] = out[:, x - 1 : x]
        xdn[...] = out[:, 0:1]
        pack_rows(s, out, halo, yup, ydn, zs)


def fine_kernel(s, f0, fw, flo, fhi, slab, spread, to_fine, place, pair, out, avg, *scratch):
    s0, s1, s2, wide_wind, ghost0, ghost1, ghost2, faces, sems = scratch
    states = (s0, s1, s2)
    ghosts = (ghost0, ghost1, ghost2)
    q, y, z, fx, fe = s.q, s.y, s.z, s.fx, s.fe
    layers = fx + 6
    rows = slice(TOP, TOP + y)
    pairs = [(f0, s0.at[:, 3 : 3 + fx, rows]), (fw, wide_wind.at[:, 2 : 2 + fx])]
    for f in range(q):
        pairs.append((flo.at[3 * f : 3 * f + 3], s0.at[f, 0:3, rows]))
        pairs.append((fhi.at[3 * f : 3 * f + 3], s0.at[f, 3 + fx : 6 + fx, rows]))
    for d in range(3):
        at = 3 * q + 2 * d
        pairs.append((flo.at[at : at + 2], wide_wind.at[d, 0:2]))
        pairs.append((fhi.at[at : at + 2], wide_wind.at[d, 2 + fx : 4 + fx]))
    moves = copies(pairs, sems)
    for move in moves:
        move.start()
    at = s.slab_rows
    zl = jnp.concatenate(
        [jnp.concatenate([slab[k, at : at + 8, :], slab[k, at + 8 : at + 16, :]], axis=1) for k in range(3)], axis=0
    )
    turned = jnp.transpose(times(zl, spread[...]))
    th, tl = halves(turned)
    t_rows = jnp.concatenate([slab[k, :at, :] for k in range(3)], axis=0)
    wide = times(t_rows, to_fine[...])
    half = fe // 2
    for k in range(3):
        flat = states[k].reshape(q * layers * PAD, z)
        for f in range(q):
            placed = jnp.dot(th, place[k, f], preferred_element_type=F32) + jnp.dot(
                tl, place[k, f], preferred_element_type=F32
            )
            ghosts[k][f] = placed[: fe * y].reshape(fe, y, z)
            for side in range(2):
                corner = placed[fe * y + side * s.ep : fe * y + side * s.ep + s.ex]
                first = (k * q + f) * s.ex
                faces[: s.ex, :] = wide[first : first + s.ex, side * z : side * z + z] + corner
                a = faces[0:half, :]
                b = faces[1 : half + 1, :]
                c = faces[2 : half + 2, :]
                even = 0.25 * a + 0.75 * b
                odd = 0.75 * b + 0.25 * c
                row = TOP - 1 if side == 0 else TOP + y
                base = (f * layers + 1) * PAD + row
                flat[pl.ds(base, half, stride=2 * PAD), :] = even
                flat[pl.ds(base + PAD, half, stride=2 * PAD), :] = odd
    for move in moves:
        move.wait()
    lane_tile = lax.broadcasted_iota(jnp.int32, (y, z), 1)
    for k in range(3):
        src, edge_of, fraction = states[k], ghosts[k], section_weights[k]

        def layer(b, carry, k=k, src=src, edge_of=edge_of, fraction=fraction):
            w = [wide_wind[d, b] for d in range(3)]
            for f in range(q):
                center = src[f, b + 1, rows, :]
                edge = edge_of[f, b]
                rate = stencil(
                    center,
                    src[f, b, rows, :],
                    src[f, b + 2, rows, :],
                    src[f, b + 1, TOP - 1 : TOP + y - 1, :],
                    src[f, b + 1, TOP + 1 : TOP + y + 1, :],
                    jnp.where(lane_tile == 0, edge, pltpu.roll(center, 1, 1)),
                    jnp.where(lane_tile == z - 1, edge, pltpu.roll(center, z - 1, 1)),
                    w,
                )
                value = s0[f, b + 1, rows, :] + fraction * rate
                if k < 2:
                    states[k + 1][f, b + 1, rows, :] = value
                else:
                    out[f, b - 2] = value
            return carry

        lax.fori_loop(k, fe - k, layer, 0)
    flat = out.reshape(q * fx * y, z)
    for f in range(q):
        sums = []
        for odd in range(2):
            parts = []
            for p in range(s.x // 2):
                base = (f * fx + 4 * p + 2 * odd) * y
                part = None
                for more in (0, 1, y, y + 1):
                    piece = flat[pl.ds(base + more, y // 2, stride=2), :]
                    part = piece if part is None else part + piece
                parts.append(part)
            sums.append(times(jnp.concatenate(parts, axis=0), pair[odd]))
        avg[f] = (sums[0] + sums[1]).reshape(s.x // 2, y // 2, z)


def merge_kernel(s, c3, avg, out):
    lanes = lax.broadcasted_iota(jnp.int32, (s.sy, s.z), 1)
    inside = (lanes >= s.lz) & (lanes < s.lz + s.sz)
    for f in range(s.q):
        for p in range(s.x // 2):
            both = avg[f, p]
            for odd in range(2):
                at = 2 * p + odd
                moved = pltpu.roll(both, s.lz if odd == 0 else s.z - s.lz, 1)
                out[f, at] = c3[f, at]
                out[f, at, s.ly : s.ly + s.sy, :] = jnp.where(
                    inside, moved, c3[f, at, s.ly : s.ly + s.sy, :]
                )


VMEM = pl.BlockSpec(memory_space=pltpu.VMEM)
ANY = pl.BlockSpec(memory_space=pl.ANY)
SMEM = pl.BlockSpec(memory_space=pltpu.SMEM)


def params(megabytes):
    return pltpu.CompilerParams(vmem_limit_bytes=megabytes << 20)


def shape(*dims):
    return jax.ShapeDtypeStruct(dims, F32)


def ring(array, axis, by):
    size = lax.axis_size(axis)
    return lax.ppermute(array, axis, [(i, (i + by) % size) for i in range(size)])


def move_by(array, amount):
    size = lax.axis_size("gx")
    if size <= 8:
        return lax.switch(amount, [lambda a, k=k: a if k == 0 else ring(a, "gx", k) for k in range(size)], array)
    for bit in range((size - 1).bit_length()):
        array = jnp.where((amount >> bit) % 2 == 1, ring(array, "gx", 1 << bit), array)
    return array


def z_columns(zs):
    size = lax.axis_size("gz")
    if size == 1:
        return jnp.zeros_like(zs)
    if size == 2:
        return lax.ppermute(zs, "gz", [(0, 1), (1, 0)])
    from_below = ring(zs, "gz", 1)
    from_above = ring(zs, "gz", -1)
    odd = lax.broadcasted_iota(jnp.int32, zs.shape, 0) % 2 == 1
    return jnp.where(odd, from_below, from_above)


def shards(coarse_fields, coarse_wind, fine_fields, fine_wind, fine_owner):
    s = Sizes(coarse_fields.shape, fine_fields.shape)
    k = constants(s)
    q, x, y, z, fx = s.q, s.x, s.y, s.z, s.fx
    size = lax.axis_size("gx")
    offset = (fine_owner[0, 0, 0] - lax.axis_index("gx")) % size
    level = lax.axis_index("gz")
    neighbours = jnp.stack([level > 0, level < lax.axis_size("gz") - 1]).astype(jnp.int32).reshape(1, 2)
    edges = 3 * q + 6
    xup, xdn, yup, ydn, zs, fup, fdn = pl.pallas_call(
        functools.partial(pack_kernel, s),
        out_shape=(
            shape(q, 2, y, z),
            shape(q, 2, y, z),
            shape(q, x, z),
            shape(q, x, z),
            shape(8, x * y),
            shape(edges, y, z),
            shape(edges, y, z),
        ),
        in_specs=[VMEM, ANY, ANY, VMEM],
        out_specs=(VMEM, VMEM, VMEM, VMEM, VMEM, ANY, ANY),
        scratch_shapes=[pltpu.SemaphoreType.DMA((2 * (q + 3),))],
        compiler_params=params(16),
        name="pack",
    )(coarse_fields, fine_fields, fine_wind, k["halo"])
    state = coarse_fields
    slabs = []
    for step in range(3):
        width = 2 if step == 0 else 1
        xlo, xhi = ring(xup, "gx", 1), ring(xdn, "gx", -1)
        ylo, yhi = ring(yup, "gy", 1), ring(ydn, "gy", -1)
        zc = z_columns(zs)
        if step == 0:
            flo, fhi = ring(fup, "gx", 1), ring(fdn, "gx", -1)
        outs = [shape(q, x, y, z), shape(s.slab_rows + 16, z)]
        if step < 2:
            outs += [shape(q, 1, y, z), shape(q, 1, y, z), shape(q, x, z), shape(q, x, z), shape(8, x * y)]
        made = pl.pallas_call(
            functools.partial(coarse_kernel, s, step, width),
            out_shape=tuple(outs),
            in_specs=[SMEM, VMEM, VMEM, ANY, ANY, ANY] + [VMEM] * 8,
            out_specs=tuple([VMEM] * len(outs)),
            scratch_shapes=[
                pltpu.VMEM((q, s.ep, PAD, z), F32),
                pltpu.VMEM((q, x, y, z), F32),
                pltpu.SemaphoreType.DMA((3,)),
            ],
            compiler_params=params(24),
            name="coarse",
        )(
            neighbours, coarse_fields, coarse_wind, state, xlo, xhi, ylo, yhi, zc,
            k["column"], k["keep"], k["corner"], k["place"], k["halo"],
        )
        state = made[0]
        slabs.append(made[1])
        if step < 2:
            xup, xdn, yup, ydn, zs = made[2:]
    slab = move_by(jnp.stack(slabs), (size - offset) % size)
    layers = fx + 6
    fine_next, averaged = pl.pallas_call(
        functools.partial(fine_kernel, s),
        out_shape=(shape(q, fx, y, z), shape(q, x // 2, y // 2, z)),
        in_specs=[ANY, ANY, ANY, ANY] + [VMEM] * 5,
        out_specs=(VMEM, VMEM),
        scratch_shapes=[
            pltpu.VMEM((q, layers, PAD, z), F32),
            pltpu.VMEM((q, layers, PAD, z), F32),
            pltpu.VMEM((q, layers, PAD, z), F32),
            pltpu.VMEM((3, s.fe, y, z), F32),
            pltpu.VMEM((q, s.fe, y, z), F32),
            pltpu.VMEM((q, s.fe, y, z), F32),
            pltpu.VMEM((q, s.fe, y, z), F32),
            pltpu.VMEM((s.ep, z), F32),
            pltpu.SemaphoreType.DMA((2 + 2 * (q + 3),)),
        ],
        compiler_params=params(40),
        name="fine",
    )(fine_fields, fine_wind, flo, fhi, slab, k["spread"], k["to_fine"], k["place"], k["pair"])
    averaged = move_by(averaged, offset)
    coarse_next = pl.pallas_call(
        functools.partial(merge_kernel, s),
        out_shape=shape(q, x, y, z),
        in_specs=[VMEM, VMEM],
        out_specs=VMEM,
        compiler_params=params(16),
        name="merge",
    )(state, averaged)
    return coarse_next, fine_next


def solution(mesh):
    spec = P(None, "gx", "gy", "gz")
    return jax.shard_map(
        shards,
        mesh=mesh,
        in_specs=(spec, spec, spec, spec, P("gx", "gy", "gz")),
        out_specs=(spec, spec),
        check_vma=False,
    )
```

```python
import functools

import jax
import jax.numpy as jnp
from jax import lax
from jax.experimental import pallas as pl
from jax.experimental.pallas import tpu as pltpu
from jax.sharding import PartitionSpec as P

diffusion = 0.05
section_weights = (1.0 / 3.0, 0.5, 1.0)
F32 = jnp.float32
BF16 = jnp.bfloat16
PAD = 32
TOP = 8


class Sizes:
    def __init__(self, coarse_shape, fine_shape):
        self.q, self.x, self.y, self.z = coarse_shape
        self.fx = fine_shape[1]
        self.ly, self.sy = self.y // 4, self.y // 2
        self.lz, self.sz = self.z // 4, self.z // 2
        self.ex = self.x + 4
        self.ep = -(-self.ex // 8) * 8
        self.fe = self.fx + 4
        self.halo = 3 * self.q + 6
        self.rows_y = 3 * self.q * self.ex
        self.rows_e = self.rows_y + self.ep
        self.rows_z = self.sy + 2
        self.slab = self.rows_e + self.q * self.rows_z
        assert self.q == 4 and self.y == 16 and self.z == 128 and self.ex <= 20 and self.fx == 2 * self.x


def lanes_of(shape):
    return lax.broadcasted_iota(jnp.int32, shape, len(shape) - 1)


def halves(value):
    high = value.astype(BF16)
    return high, (value - high.astype(F32)).astype(BF16)


def times(value, matrix):
    high, low = halves(value)
    return jnp.dot(high, matrix, preferred_element_type=F32) + jnp.dot(low, matrix, preferred_element_type=F32)


def coefficients(wind):
    out = []
    for w in wind:
        out += [diffusion - 0.5 * w, diffusion + 0.5 * w]
    return out


def rate_of(co, center, x_low, x_high, y_low, y_high, z_low, z_high):
    along = (co[0] * x_high + co[1] * x_low) + (co[2] * y_high + co[3] * y_low) + (co[4] * z_high + co[5] * z_low)
    return along - (6.0 * diffusion) * center


def layer_of(s, own, low, high, member, at, width, first):
    size = own.shape[1]
    if at < 0:
        return low[first + width * member + at + width]
    if at >= size:
        return high[first + width * member + at - size]
    return own[member, at]


def pack_kernel(s, fields, wind, up, down, sems):
    size = fields.shape[1]
    moves = []
    for f in range(s.q):
        moves.append((fields.at[f, size - 3 : size], up.at[3 * f : 3 * f + 3]))
        moves.append((fields.at[f, 0:3], down.at[3 * f : 3 * f + 3]))
    for d in range(3):
        at = 3 * s.q + 2 * d
        moves.append((wind.at[d, size - 2 : size], up.at[at : at + 2]))
        moves.append((wind.at[d, 0:2], down.at[at : at + 2]))
    moves = [pltpu.make_async_copy(src, dst, sems.at[i]) for i, (src, dst) in enumerate(moves)]
    for move in moves:
        move.start()
    for move in moves:
        move.wait()


def column_pack(s, tiles):
    total = None
    for j, tile in enumerate(tiles):
        lane = lanes_of(tile.shape)
        part = pltpu.roll(jnp.where((lane == 0) | (lane == s.z - 1), tile, 0.0), 2 * j, 1)
        total = part if total is None else total + part
    return total


def slab_kernel(s, c0, cw, lo, hi, slab, yup, ydn, zcol, pad0, pad1, pad2):
    q, x, y, z = s.q, s.x, s.y, s.z
    own = slice(TOP, TOP + y)
    zeros = jnp.zeros((s.ep, z), F32)
    pads = (pad0, pad1, pad2)
    flats = [pad.reshape(q * s.ep * PAD, z) for pad in pads]
    for f in range(q):
        for pad in (flats[0], flats[1]):
            pad[pl.ds(f * s.ep * PAD + TOP - 1, s.ep, stride=PAD), :] = zeros
            pad[pl.ds(f * s.ep * PAD + TOP + y, s.ep, stride=PAD), :] = zeros
        for at in range(-3, x + 3):
            pad0[f, at + 3, own, :] = layer_of(s, c0, lo, hi, f, at, 3, 0)
        pad2[f, 1, own, :] = zeros[:y]
        pad2[f, s.ex, own, :] = zeros[:y]
    for step in range(2):
        src, dst = pads[step], pads[step + 1]
        for at in range(step - 2, x + 2 - step):
            j = at + 3
            co = coefficients([layer_of(s, cw, lo, hi, d, at, 2, 3 * q) for d in range(3)])
            for f in range(q):
                center = src[f, j, own, :]
                rate = rate_of(
                    co,
                    center,
                    src[f, j - 1, own, :],
                    src[f, j + 1, own, :],
                    src[f, j, TOP - 1 : TOP + y - 1, :],
                    src[f, j, TOP + 1 : TOP + y + 1, :],
                    pltpu.roll(center, 1, 1),
                    pltpu.roll(center, z - 1, 1),
                )
                base = center if step == 0 else pad0[f, j, own, :]
                dst[f, j, own, :] = base + section_weights[step] * rate
    lane_x = lanes_of((s.ex, z))
    lane_y = lanes_of((y, z))
    ends = None
    columns = (lane_y == s.lz - 1) | (lane_y == s.lz) | (lane_y == s.lz + s.sz - 1) | (lane_y == s.lz + s.sz)
    low_at = (lane_y % 2 == 0) & (lane_y < z // 2)
    high_at = (lane_y % 2 == 0) & (lane_y >= z // 2)
    for f in range(q):
        zfaces = None
        for k in range(3):
            start = (f * s.ep + 1) * PAD + TOP
            rows = [
                flats[k][pl.ds(start + at, s.ex, stride=PAD), :] for at in (s.ly - 1, s.ly, s.ly + s.sy - 1, s.ly + s.sy)
            ]
            sides = (0.75 * rows[0] + 0.25 * rows[1], 0.25 * rows[2] + 0.75 * rows[3])
            first = (k * q + f) * s.ex
            slab[first : first + s.ex, :] = jnp.where(
                lane_x < s.sz, pltpu.roll(sides[0], z - s.lz, 1), pltpu.roll(sides[1], s.lz, 1)
            )
            for side in range(2):
                e = 4 * (q * k + f) + 2 * side + 1
                before = jnp.where(lane_x == s.lz - 1, sides[side], 0.0)
                after = jnp.where(lane_x == s.lz + s.sz, sides[side], 0.0)
                part = pltpu.roll(before, (e - s.lz + 1) % z, 1) + pltpu.roll(after, (e - 1 - s.lz - s.sz) % z, 1)
                ends = part if ends is None else ends + part
            raw = None
            for a in range(0 if k == 0 else 1, s.ex if k == 0 else s.ex - 1):
                part = jnp.where(columns, pads[k][f, a + 1, own, :], 0.0)
                part = pltpu.roll(part, (2 * a - s.lz + 1) % z, 1)
                raw = part if raw is None else raw + part
            beside = pltpu.roll(raw, z - 1, 1)
            low = jnp.where(low_at, 0.75 * raw + 0.25 * beside, 0.0)
            high = jnp.where(high_at, 0.25 * raw + 0.75 * beside, 0.0)
            part = pltpu.roll(low, (2 * s.ex * k - 1) % z, 1) + pltpu.roll(high, (2 * s.ex * k - z // 2) % z, 1)
            zfaces = part if zfaces is None else zfaces + part
        at = s.rows_e + f * s.rows_z
        slab[at : at + s.rows_z, :] = zfaces[s.ly - 1 : s.ly + s.sy + 1]
    slab[s.rows_y : s.rows_y + s.ex, :] = ends
    slab[s.rows_y + s.ex : s.rows_e, :] = zeros[: s.ep - s.ex]
    for f in range(q):
        start = (f * s.ep + 1) * PAD + TOP
        yup[f] = flats[0][pl.ds(start + y - 1, s.ex, stride=PAD), :]
        ydn[f] = flats[0][pl.ds(start, s.ex, stride=PAD), :]
        zcol[f] = column_pack(s, [pad0[f, a + 1, own, :] for a in range(s.ex)])


def coarse_kernel(s, step, *refs):
    q, x, y, z = s.q, s.x, s.y, s.z
    (sides, c0, cw, lo, hi), refs = refs[:5], refs[5:]
    if step:
        state, refs = refs[0], refs[1:]
    (ylo, yhi, zin, out), refs = refs[:4], refs[4:]
    if step < 2:
        (yup, ydn, zcol), refs = refs[:3], refs[3:]
    (pad,) = refs
    own = slice(TOP, TOP + y)
    count = s.ex - 2 * step
    flat = pad.reshape(q * s.ep * PAD, z)

    def before(f, at):
        if step == 0:
            return layer_of(s, c0, lo, hi, f, at, 3, 0)
        return state[f, at + 3 - step]

    lane = lanes_of((y, z))
    keep = jnp.where(lane % 2 == 1, sides[0, 0], sides[0, 1]).astype(F32)
    for f in range(q):
        flat[pl.ds(f * s.ep * PAD + TOP - 1, count, stride=PAD), :] = ylo[f]
        flat[pl.ds(f * s.ep * PAD + TOP + y, count, stride=PAD), :] = yhi[f]
        for j in range(count):
            pad[f, j, own, :] = before(f, j + step - 2)
    ghosts = [zin[f] * keep for f in range(q)]
    for j in range(count):
        at = j + step - 2
        co = coefficients([layer_of(s, cw, lo, hi, d, at, 2, 3 * q) for d in range(3)])
        for f in range(q):
            center = before(f, at)
            ghost = pltpu.roll(ghosts[f], (-2 * j) % z, 1)
            rate = rate_of(
                co,
                center,
                before(f, at - 1),
                before(f, at + 1),
                pad[f, j, TOP - 1 : TOP + y - 1, :],
                pad[f, j, TOP + 1 : TOP + y + 1, :],
                pltpu.roll(jnp.where(lane == z - 1, ghost, center), 1, 1),
                pltpu.roll(jnp.where(lane == 0, ghost, center), z - 1, 1),
            )
            base = center if step == 0 else layer_of(s, c0, lo, hi, f, at, 3, 0)
            out[f, j] = base + section_weights[step] * rate
    if step < 2:
        made = out.reshape(q * count * y, z)
        for f in range(q):
            start = (f * count + 1) * y
            yup[f] = made[pl.ds(start + y - 1, count - 2, stride=y), :]
            ydn[f] = made[pl.ds(start, count - 2, stride=y), :]
            zcol[f] = column_pack(s, [out[f, j + 1] for j in range(count - 2)])


def fine_kernel(s, f0, fw, flo, fhi, slab, out, avg, *scratch):
    s0, s1, s2, wide_wind, faces, zface, sems = scratch
    states = (s0, s1, s2)
    q, y, z, fx, fe = s.q, s.y, s.z, s.fx, s.fe
    layers = fx + 6
    rows = slice(TOP, TOP + y)
    pairs = [(f0, s0.at[:, 3 : 3 + fx, rows]), (fw, wide_wind.at[:, 2 : 2 + fx])]
    for f in range(q):
        pairs.append((flo.at[3 * f : 3 * f + 3], s0.at[f, 0:3, rows]))
        pairs.append((fhi.at[3 * f : 3 * f + 3], s0.at[f, 3 + fx : 6 + fx, rows]))
    for d in range(3):
        at = 3 * q + 2 * d
        pairs.append((flo.at[at : at + 2], wide_wind.at[d, 0:2]))
        pairs.append((fhi.at[at : at + 2], wide_wind.at[d, 2 + fx : 4 + fx]))
    moves = [pltpu.make_async_copy(src, dst, sems.at[i]) for i, (src, dst) in enumerate(pairs)]
    for move in moves:
        move.start()
    r = lax.broadcasted_iota(jnp.int32, (z, 2 * z), 0)
    c = lax.broadcasted_iota(jnp.int32, (z, 2 * z), 1)
    near = c // 2
    far = near + 2 * (c % 2) - 1
    same = (far // s.sz == near // s.sz) & (far >= 0)
    to_fine = jnp.where(r == near, 0.75, jnp.where((r == far) & same, 0.25, 0.0)).astype(BF16)
    wide = times(slab[: s.rows_y, :], to_fine)
    ends = slab[s.rows_y : s.rows_y + s.ex, :]
    lane_x = lanes_of((s.ex, z))
    edge = (lane_x == 0) | (lane_x == z - 1)
    half = fe // 2
    for k in range(3):
        flat = states[k].reshape(q * layers * PAD, z)
        for f in range(q):
            for side in range(2):
                e = 4 * (q * k + f) + 2 * side + 1
                corner = jnp.where(edge, 0.25 * pltpu.roll(ends, z - e, 1), 0.0)
                first = (k * q + f) * s.ex
                faces[: s.ex, :] = wide[first : first + s.ex, side * z : side * z + z] + corner
                a = faces[0:half, :]
                b = faces[1 : half + 1, :]
                d = faces[2 : half + 2, :]
                row = TOP - 1 if side == 0 else TOP + y
                base = (f * layers + 1) * PAD + row
                flat[pl.ds(base, half, stride=2 * PAD), :] = 0.25 * a + 0.75 * b
                flat[pl.ds(base + PAD, half, stride=2 * PAD), :] = 0.75 * b + 0.25 * d
    evens, odds = [], []
    for f in range(q):
        at = s.rows_e + f * s.rows_z
        a = slab[at : at + s.sy, :]
        b = slab[at + 1 : at + 1 + s.sy, :]
        d = slab[at + 2 : at + 2 + s.sy, :]
        zface[pl.ds(0, s.sy, stride=2), :] = 0.25 * a + 0.75 * b
        zface[pl.ds(1, s.sy, stride=2), :] = 0.75 * b + 0.25 * d
        a = zface[...]
        b = pltpu.roll(a, z - 2, 1)
        d = pltpu.roll(a, z - 4, 1)
        evens.append(0.25 * a + 0.75 * b)
        odds.append(0.75 * b + 0.25 * d)
    for move in moves:
        move.wait()
    lane = lanes_of((y, z))
    is_first, is_last = lane == 0, lane == z - 1
    for k in range(3):
        src, fraction = states[k], section_weights[k]
        begin, end = (0, half) if k < 2 else (1, half - 1)
        shift = -(2 * s.ex * k + 2 * begin) % z
        carried = tuple(pltpu.roll(g, shift, 1) if shift else g for g in evens + odds)

        def pair_of_layers(t, ghosts, k=k, src=src, fraction=fraction):
            for odd in range(2):
                b = 2 * t + odd
                co = coefficients([wide_wind[d, b] for d in range(3)])
                for f in range(q):
                    center = src[f, b + 1, rows, :]
                    ghost = ghosts[odd * q + f]
                    rate = rate_of(
                        co,
                        center,
                        src[f, b, rows, :],
                        src[f, b + 2, rows, :],
                        src[f, b + 1, TOP - 1 : TOP + y - 1, :],
                        src[f, b + 1, TOP + 1 : TOP + y + 1, :],
                        pltpu.roll(jnp.where(is_last, ghost, center), 1, 1),
                        pltpu.roll(jnp.where(is_first, ghost, center), z - 1, 1),
                    )
                    value = (center if k == 0 else s0[f, b + 1, rows, :]) + fraction * rate
                    if k < 2:
                        states[k + 1][f, b + 1, rows, :] = value
                    else:
                        out[f, b - 2] = value
            return tuple(pltpu.roll(g, z - 2, 1) for g in ghosts)

        lax.fori_loop(begin, end, pair_of_layers, carried)
    rz = lax.broadcasted_iota(jnp.int32, (z, z), 0)
    cz = lax.broadcasted_iota(jnp.int32, (z, z), 1)
    flat = out.reshape(q * fx * y, z)
    pairs_z = [jnp.where(cz == rz // 2 + odd * s.sz, 0.125, 0.0).astype(BF16) for odd in range(2)]
    for f in range(q):
        sums = []
        for odd in range(2):
            parts = []
            for p in range(s.x // 2):
                base = (f * fx + 4 * p + 2 * odd) * y
                part = None
                for more in (0, 1, y, y + 1):
                    piece = flat[pl.ds(base + more, y // 2, stride=2), :]
                    part = piece if part is None else part + piece
                parts.append(part)
            sums.append(times(jnp.concatenate(parts, axis=0), pairs_z[odd]))
        avg[f] = (sums[0] + sums[1]).reshape(s.x // 2, y // 2, z)


def merge_kernel(s, c3, avg, out):
    lane = lanes_of((s.sy, s.z))
    inside = (lane >= s.lz) & (lane < s.lz + s.sz)
    for f in range(s.q):
        for p in range(s.x // 2):
            both = avg[f, p]
            for odd in range(2):
                at = 2 * p + odd
                moved = pltpu.roll(both, s.lz if odd == 0 else s.z - s.lz, 1)
                out[f, at] = c3[f, at]
                out[f, at, s.ly : s.ly + s.sy, :] = jnp.where(inside, moved, c3[f, at, s.ly : s.ly + s.sy, :])


VMEM = pl.BlockSpec(memory_space=pltpu.VMEM)
SMEM = pl.BlockSpec(memory_space=pltpu.SMEM)
HBM = pl.BlockSpec(memory_space=pltpu.HBM)
ANY = pl.BlockSpec(memory_space=pl.ANY)


def params(megabytes):
    return pltpu.CompilerParams(vmem_limit_bytes=megabytes << 20)


def shape(*dims):
    return jax.ShapeDtypeStruct(dims, F32)


def ring(array, axis, by):
    size = lax.axis_size(axis)
    return lax.ppermute(array, axis, [(i, (i + by) % size) for i in range(size)])


def move_by(array, amount):
    size = lax.axis_size("gx")
    if size <= 8:
        return lax.switch(amount, [lambda a, k=k: a if k == 0 else ring(a, "gx", k) for k in range(size)], array)
    for bit in range((size - 1).bit_length()):
        array = jnp.where((amount >> bit) % 2 == 1, ring(array, "gx", 1 << bit), array)
    return array


def z_columns(zcol):
    size = lax.axis_size("gz")
    if size == 1:
        return jnp.zeros_like(zcol)
    if size == 2:
        return lax.ppermute(zcol, "gz", [(0, 1), (1, 0)])
    odd = lax.broadcasted_iota(jnp.int32, zcol.shape, 2) % 2 == 1
    return jnp.where(odd, ring(zcol, "gz", 1), ring(zcol, "gz", -1))


def pack(s, fields, wind, name):
    return pl.pallas_call(
        functools.partial(pack_kernel, s),
        out_shape=(shape(s.halo, s.y, s.z),) * 2,
        in_specs=[HBM, HBM],
        out_specs=(ANY, ANY),
        scratch_shapes=[pltpu.SemaphoreType.DMA((2 * (s.q + 3),))],
        name=name,
    )(fields, wind)


def shards(coarse_fields, coarse_wind, fine_fields, fine_wind, fine_owner):
    s = Sizes(coarse_fields.shape, fine_fields.shape)
    q, x, y, z, fx = s.q, s.x, s.y, s.z, s.fx
    size = lax.axis_size("gx")
    offset = (fine_owner[0, 0, 0] - lax.axis_index("gx")) % size
    level = lax.axis_index("gz")
    neighbours = jnp.stack([level > 0, level < lax.axis_size("gz") - 1]).astype(jnp.int32).reshape(1, 2)
    up, down = pack(s, coarse_fields, coarse_wind, "pack_coarse")
    lo, hi = ring(up, "gx", 1), ring(down, "gx", -1)
    up, down = pack(s, fine_fields, fine_wind, "pack_fine")
    flo, fhi = ring(up, "gx", 1), ring(down, "gx", -1)
    padded = pltpu.VMEM((q, s.ep, PAD, z), F32)
    slab, yup, ydn, zcol = pl.pallas_call(
        functools.partial(slab_kernel, s),
        out_shape=(shape(s.slab, z), shape(q, s.ex, z), shape(q, s.ex, z), shape(q, y, z)),
        in_specs=[VMEM] * 4,
        out_specs=(VMEM,) * 4,
        scratch_shapes=[padded] * 3,
        compiler_params=params(24),
        name="slab",
    )(coarse_fields, coarse_wind, lo, hi)
    state = None
    for step in range(3):
        count = s.ex - 2 * step
        ylo, yhi = ring(yup, "gy", 1), ring(ydn, "gy", -1)
        zin = z_columns(zcol)
        outs = [shape(q, count, y, z)]
        if step < 2:
            outs += [shape(q, count - 2, z), shape(q, count - 2, z), shape(q, y, z)]
        ins = [neighbours, coarse_fields, coarse_wind, lo, hi] + ([state] if step else []) + [ylo, yhi, zin]
        made = pl.pallas_call(
            functools.partial(coarse_kernel, s, step),
            out_shape=tuple(outs),
            in_specs=[SMEM] + [VMEM] * (len(ins) - 1),
            out_specs=(VMEM,) * len(outs),
            scratch_shapes=[padded],
            compiler_params=params(16),
            name="coarse",
        )(*ins)
        state = made[0]
        if step < 2:
            yup, ydn, zcol = made[1:]
    slab = move_by(slab, (size - offset) % size)
    layers = fx + 6
    fine_next, averaged = pl.pallas_call(
        functools.partial(fine_kernel, s),
        out_shape=(shape(q, fx, y, z), shape(q, x // 2, y // 2, z)),
        in_specs=[ANY, ANY, ANY, ANY, VMEM],
        out_specs=(VMEM, VMEM),
        scratch_shapes=[
            pltpu.VMEM((q, layers, PAD, z), F32),
            pltpu.VMEM((q, layers, PAD, z), F32),
            pltpu.VMEM((q, layers, PAD, z), F32),
            pltpu.VMEM((3, s.fe, y, z), F32),
            pltpu.VMEM((s.ep, z), F32),
            pltpu.VMEM((y, z), F32),
            pltpu.SemaphoreType.DMA((2 + 2 * (q + 3),)),
        ],
        compiler_params=params(32),
        name="fine",
    )(fine_fields, fine_wind, flo, fhi, slab)
    averaged = move_by(averaged, offset)
    coarse_next = pl.pallas_call(
        functools.partial(merge_kernel, s),
        out_shape=shape(q, x, y, z),
        in_specs=[VMEM, VMEM],
        out_specs=VMEM,
        compiler_params=params(16),
        name="merge",
    )(state, averaged)
    return coarse_next, fine_next


def solution(mesh):
    spec = P(None, "gx", "gy", "gz")
    return jax.shard_map(
        shards,
        mesh=mesh,
        in_specs=(spec, spec, spec, spec, P("gx", "gy", "gz")),
        out_specs=(spec, spec),
        check_vma=False,
    )
```

```python
import functools

import jax
import jax.numpy as jnp
from jax import lax
from jax.experimental import pallas as pl
from jax.experimental.pallas import tpu as pltpu
from jax.sharding import PartitionSpec as P

diffusion = 0.05
section_weights = (1.0 / 3.0, 0.5, 1.0)
F32 = jnp.float32
BF16 = jnp.bfloat16
PAD = 32
TOP = 8


class Sizes:
    def __init__(self, coarse_shape, fine_shape):
        self.q, self.x, self.y, self.z = coarse_shape
        self.fx = fine_shape[1]
        self.ly, self.sy = self.y // 4, self.y // 2
        self.lz, self.sz = self.z // 4, self.z // 2
        self.ex = self.x + 4
        self.ep = -(-self.ex // 8) * 8
        self.fe = self.fx + 4
        self.halo = 3 * self.q + 6
        self.rows_y = 3 * self.q * self.ex
        self.rows_e = self.rows_y + self.ep
        self.rows_z = self.sy + 2
        self.slab = self.rows_e + self.q * self.rows_z
        assert self.q == 4 and self.y == 16 and self.z == 128 and self.ex <= 20 and self.fx == 2 * self.x


def lanes_of(shape):
    return lax.broadcasted_iota(jnp.int32, shape, len(shape) - 1)


def halves(value):
    high = value.astype(BF16)
    return high, (value - high.astype(F32)).astype(BF16)


def times(value, matrix):
    high, low = halves(value)
    return jnp.dot(high, matrix, preferred_element_type=F32) + jnp.dot(low, matrix, preferred_element_type=F32)


def coefficients(wind):
    out = []
    for w in wind:
        out += [diffusion - 0.5 * w, diffusion + 0.5 * w]
    return out


def rate_of(co, center, x_low, x_high, y_low, y_high, z_low, z_high):
    along = (co[0] * x_high + co[1] * x_low) + (co[2] * y_high + co[3] * y_low) + (co[4] * z_high + co[5] * z_low)
    return along - (6.0 * diffusion) * center


def layer_of(s, own, low, high, member, at, width, first):
    size = own.shape[1]
    if at < 0:
        return low[first + width * member + at + width]
    if at >= size:
        return high[first + width * member + at - size]
    return own[member, at]


def pack_kernel(s, fields, wind, up, down, sems):
    size = fields.shape[1]
    moves = []
    for f in range(s.q):
        moves.append((fields.at[f, size - 3 : size], up.at[3 * f : 3 * f + 3]))
        moves.append((fields.at[f, 0:3], down.at[3 * f : 3 * f + 3]))
    for d in range(3):
        at = 3 * s.q + 2 * d
        moves.append((wind.at[d, size - 2 : size], up.at[at : at + 2]))
        moves.append((wind.at[d, 0:2], down.at[at : at + 2]))
    moves = [pltpu.make_async_copy(src, dst, sems.at[i]) for i, (src, dst) in enumerate(moves)]
    for move in moves:
        move.start()
    for move in moves:
        move.wait()


def slab_kernel(s, c0, cw, lo, hi, slab, yup, ydn, pad0, pad1, pad2):
    q, x, y, z = s.q, s.x, s.y, s.z
    own = slice(TOP, TOP + y)
    zeros = jnp.zeros((s.ep, z), F32)
    pads = (pad0, pad1, pad2)
    flats = [pad.reshape(q * s.ep * PAD, z) for pad in pads]
    for f in range(q):
        for pad in (flats[0], flats[1]):
            pad[pl.ds(f * s.ep * PAD + TOP - 1, s.ep, stride=PAD), :] = zeros
            pad[pl.ds(f * s.ep * PAD + TOP + y, s.ep, stride=PAD), :] = zeros
        for at in range(-3, x + 3):
            pad0[f, at + 3, own, :] = layer_of(s, c0, lo, hi, f, at, 3, 0)
        pad2[f, 1, own, :] = zeros[:y]
        pad2[f, s.ex, own, :] = zeros[:y]
    for step in range(2):
        src, dst = pads[step], pads[step + 1]
        for at in range(step - 2, x + 2 - step):
            j = at + 3
            co = coefficients([layer_of(s, cw, lo, hi, d, at, 2, 3 * q) for d in range(3)])
            for f in range(q):
                center = src[f, j, own, :]
                rate = rate_of(
                    co,
                    center,
                    src[f, j - 1, own, :],
                    src[f, j + 1, own, :],
                    src[f, j, TOP - 1 : TOP + y - 1, :],
                    src[f, j, TOP + 1 : TOP + y + 1, :],
                    pltpu.roll(center, 1, 1),
                    pltpu.roll(center, z - 1, 1),
                )
                base = center if step == 0 else pad0[f, j, own, :]
                dst[f, j, own, :] = base + section_weights[step] * rate
    lane_x = lanes_of((s.ex, z))
    lane_y = lanes_of((y, z))
    ends = None
    columns = (lane_y == s.lz - 1) | (lane_y == s.lz) | (lane_y == s.lz + s.sz - 1) | (lane_y == s.lz + s.sz)
    low_at = (lane_y % 2 == 0) & (lane_y < z // 2)
    high_at = (lane_y % 2 == 0) & (lane_y >= z // 2)
    for f in range(q):
        zfaces = None
        for k in range(3):
            start = (f * s.ep + 1) * PAD + TOP
            rows = [
                flats[k][pl.ds(start + at, s.ex, stride=PAD), :] for at in (s.ly - 1, s.ly, s.ly + s.sy - 1, s.ly + s.sy)
            ]
            sides = (0.75 * rows[0] + 0.25 * rows[1], 0.25 * rows[2] + 0.75 * rows[3])
            first = (k * q + f) * s.ex
            slab[first : first + s.ex, :] = jnp.where(
                lane_x < s.sz, pltpu.roll(sides[0], z - s.lz, 1), pltpu.roll(sides[1], s.lz, 1)
            )
            for side in range(2):
                e = 4 * (q * k + f) + 2 * side + 1
                before = jnp.where(lane_x == s.lz - 1, sides[side], 0.0)
                after = jnp.where(lane_x == s.lz + s.sz, sides[side], 0.0)
                part = pltpu.roll(before, (e - s.lz + 1) % z, 1) + pltpu.roll(after, (e - 1 - s.lz - s.sz) % z, 1)
                ends = part if ends is None else ends + part
            raw = None
            for a in range(0 if k == 0 else 1, s.ex if k == 0 else s.ex - 1):
                part = jnp.where(columns, pads[k][f, a + 1, own, :], 0.0)
                part = pltpu.roll(part, (2 * a - s.lz + 1) % z, 1)
                raw = part if raw is None else raw + part
            beside = pltpu.roll(raw, z - 1, 1)
            low = jnp.where(low_at, 0.75 * raw + 0.25 * beside, 0.0)
            high = jnp.where(high_at, 0.25 * raw + 0.75 * beside, 0.0)
            part = pltpu.roll(low, (2 * s.ex * k - 1) % z, 1) + pltpu.roll(high, (2 * s.ex * k - z // 2) % z, 1)
            zfaces = part if zfaces is None else zfaces + part
        at = s.rows_e + f * s.rows_z
        slab[at : at + s.rows_z, :] = zfaces[s.ly - 1 : s.ly + s.sy + 1]
    slab[s.rows_y : s.rows_y + s.ex, :] = ends
    slab[s.rows_y + s.ex : s.rows_e, :] = zeros[: s.ep - s.ex]
    for f in range(q):
        start = (f * s.ep + 1) * PAD + TOP
        for r in range(3):
            yup[3 * f + r] = flats[0][pl.ds(start + y - 3 + r, s.ex, stride=PAD), :]
            ydn[3 * f + r] = flats[0][pl.ds(start + r, s.ex, stride=PAD), :]
    flat_cw = cw.reshape(3 * x * y, z)
    flat_lo = lo.reshape(s.halo * y, z)
    flat_hi = hi.reshape(s.halo * y, z)
    for d in range(3):
        at = (3 * q + 2 * d) * y
        for r in range(2):
            for dst, row in ((yup, y - 2 + r), (ydn, r)):
                here = dst.at[3 * q + 2 * d + r]
                here[0:2, :] = flat_lo[pl.ds(at + row, 2, stride=y), :]
                here[2 : 2 + x, :] = flat_cw[pl.ds(d * x * y + row, x, stride=y), :]
                here[2 + x : 4 + x, :] = flat_hi[pl.ds(at + row, 2, stride=y), :]


WTOP, WPAD = 12, 40
BLOCK = slice(8, 32)


def assemble(s, c0, cw, lo, hi, ylo, yhi, pad, wind):
    q, x, y, z = s.q, s.x, s.y, s.z
    flat = pad.reshape(q * s.ep * WPAD, z)
    flat_wind = wind.reshape(3 * s.ex * 24, z)
    for f in range(q):
        for at in range(-3, x + 3):
            pad[f, at + 3, WTOP : WTOP + y, :] = layer_of(s, c0, lo, hi, f, at, 3, 0)
        base = (f * s.ep + 1) * WPAD + WTOP
        for r in range(3):
            flat[pl.ds(base - 3 + r, s.ex, stride=WPAD), :] = ylo[3 * f + r]
            flat[pl.ds(base + y + r, s.ex, stride=WPAD), :] = yhi[3 * f + r]
    for d in range(3):
        for at in range(-2, x + 2):
            wind[d, at + 2, 4 : 4 + y, :] = layer_of(s, cw, lo, hi, d, at, 2, 3 * q)
        base = d * s.ex * 24 + 4
        for r in range(2):
            flat_wind[pl.ds(base - 2 + r, s.ex, stride=24), :] = ylo[3 * q + 2 * d + r]
            flat_wind[pl.ds(base + y + r, s.ex, stride=24), :] = yhi[3 * q + 2 * d + r]


def edge_lanes(s, lane, width):
    return (lane < width) | (lane >= s.z - width)


def zpack_kernel(s, c0, cw, lo, hi, ylo, yhi, out, pad, wind):
    assemble(s, c0, cw, lo, hi, ylo, yhi, pad, wind)
    lane = lanes_of((24, s.z))
    keep = edge_lanes(s, lane, 3)
    for m in range(s.q + 3):
        total = None
        for a in range(s.ex):
            tile = pad[m, a + 1, BLOCK, :] if m < s.q else wind[m - s.q, a]
            part = pltpu.roll(jnp.where(keep, tile, 0.0), (6 * a + 3) % s.z, 1)
            total = part if total is None else total + part
        out[m] = total


def coarse_kernel(s, sides, c0, cw, lo, hi, ylo, yhi, zown, zin, out, pad0, pad1, pad2, wind, kept):
    q, x, y, z = s.q, s.x, s.y, s.z
    assemble(s, c0, cw, lo, hi, ylo, yhi, pad0, wind)
    pads = (pad0, pad1, pad2)
    lane = lanes_of((24, z))
    is_first, is_last = lane == 0, lane == z - 1
    ends = edge_lanes(s, lane, 1)
    group = lane % 6
    from_low = group == 2
    from_high = group == 3
    exists = jnp.where(group < 3, sides[0, 0], sides[0, 1]).astype(F32)
    co_z = coefficients([zin[q + d] for d in range(3)])
    beyond = [zin[f] * exists for f in range(q)]
    nearest = [zown[f] for f in range(q)]
    for step in range(3):
        src = pads[step]
        fraction = section_weights[step]
        packed = [None] * q
        for at in range(step - 2, x + 2 - step):
            a = at + 2
            co = coefficients([wind[d, a] for d in range(3)])
            for f in range(q):
                center = src[f, a + 1, BLOCK, :]
                ghost = pltpu.roll(beyond[f], (-6 * a - 3) % z, 1)
                rate = rate_of(
                    co,
                    center,
                    src[f, a, BLOCK, :],
                    src[f, a + 2, BLOCK, :],
                    src[f, a + 1, 7:31, :],
                    src[f, a + 1, 9:33, :],
                    pltpu.roll(jnp.where(is_last, ghost, center), 1, 1),
                    pltpu.roll(jnp.where(is_first, ghost, center), z - 1, 1),
                )
                base = center if step == 0 else pad0[f, a + 1, BLOCK, :]
                value = base + fraction * rate
                if step == 2:
                    kept[f, at, :, :] = value
                    continue
                pads[step + 1][f, a + 1, BLOCK, :] = value
                if step == 0 and 0 < a < s.ex - 1:
                    part = pltpu.roll(jnp.where(ends, value, 0.0), (6 * a + 3) % z, 1)
                    packed[f] = part if packed[f] is None else packed[f] + part
        if step == 2:
            break
        later = []
        for f in range(q):
            here, near = beyond[f], nearest[f]
            rate = rate_of(
                co_z,
                here,
                pltpu.roll(here, 6, 1),
                pltpu.roll(here, z - 6, 1),
                pltpu.roll(here, 1, 0),
                pltpu.roll(here, 23, 0),
                pltpu.roll(jnp.where(from_low, near, here), 1, 1),
                pltpu.roll(jnp.where(from_high, near, here), z - 1, 1),
            )
            base = here if step == 0 else zin[f] * exists
            later.append((base + fraction * rate) * exists)
        beyond = later
        nearest = packed
    for f in range(q):
        for at in range(x):
            out[f, at] = kept[f, at, 4 : 4 + y, :]


def fine_kernel(s, f0, fw, flo, fhi, slab, out, avg, *scratch):
    s0, s1, s2, wide_wind, faces, zface, sems = scratch
    states = (s0, s1, s2)
    q, y, z, fx, fe = s.q, s.y, s.z, s.fx, s.fe
    layers = fx + 6
    rows = slice(TOP, TOP + y)
    pairs = [(f0, s0.at[:, 3 : 3 + fx, rows]), (fw, wide_wind.at[:, 2 : 2 + fx])]
    for f in range(q):
        pairs.append((flo.at[3 * f : 3 * f + 3], s0.at[f, 0:3, rows]))
        pairs.append((fhi.at[3 * f : 3 * f + 3], s0.at[f, 3 + fx : 6 + fx, rows]))
    for d in range(3):
        at = 3 * q + 2 * d
        pairs.append((flo.at[at : at + 2], wide_wind.at[d, 0:2]))
        pairs.append((fhi.at[at : at + 2], wide_wind.at[d, 2 + fx : 4 + fx]))
    moves = [pltpu.make_async_copy(src, dst, sems.at[i]) for i, (src, dst) in enumerate(pairs)]
    for move in moves:
        move.start()
    r = lax.broadcasted_iota(jnp.int32, (z, 2 * z), 0)
    c = lax.broadcasted_iota(jnp.int32, (z, 2 * z), 1)
    near = c // 2
    far = near + 2 * (c % 2) - 1
    same = (far // s.sz == near // s.sz) & (far >= 0)
    to_fine = jnp.where(r == near, 0.75, jnp.where((r == far) & same, 0.25, 0.0)).astype(BF16)
    wide = times(slab[: s.rows_y, :], to_fine)
    ends = slab[s.rows_y : s.rows_y + s.ex, :]
    lane_x = lanes_of((s.ex, z))
    edge = (lane_x == 0) | (lane_x == z - 1)
    half = fe // 2
    for k in range(3):
        flat = states[k].reshape(q * layers * PAD, z)
        for f in range(q):
            for side in range(2):
                e = 4 * (q * k + f) + 2 * side + 1
                corner = jnp.where(edge, 0.25 * pltpu.roll(ends, z - e, 1), 0.0)
                first = (k * q + f) * s.ex
                faces[: s.ex, :] = wide[first : first + s.ex, side * z : side * z + z] + corner
                a = faces[0:half, :]
                b = faces[1 : half + 1, :]
                d = faces[2 : half + 2, :]
                row = TOP - 1 if side == 0 else TOP + y
                base = (f * layers + 1) * PAD + row
                flat[pl.ds(base, half, stride=2 * PAD), :] = 0.25 * a + 0.75 * b
                flat[pl.ds(base + PAD, half, stride=2 * PAD), :] = 0.75 * b + 0.25 * d
    evens, odds = [], []
    for f in range(q):
        at = s.rows_e + f * s.rows_z
        a = slab[at : at + s.sy, :]
        b = slab[at + 1 : at + 1 + s.sy, :]
        d = slab[at + 2 : at + 2 + s.sy, :]
        zface[pl.ds(0, s.sy, stride=2), :] = 0.25 * a + 0.75 * b
        zface[pl.ds(1, s.sy, stride=2), :] = 0.75 * b + 0.25 * d
        a = zface[...]
        b = pltpu.roll(a, z - 2, 1)
        d = pltpu.roll(a, z - 4, 1)
        evens.append(0.25 * a + 0.75 * b)
        odds.append(0.75 * b + 0.25 * d)
    for move in moves:
        move.wait()
    lane = lanes_of((y, z))
    is_first, is_last = lane == 0, lane == z - 1
    for k in range(3):
        src, fraction = states[k], section_weights[k]
        begin, end = (0, half) if k < 2 else (1, half - 1)
        shift = -(2 * s.ex * k + 2 * begin) % z
        carried = tuple(pltpu.roll(g, shift, 1) if shift else g for g in evens + odds)

        def pair_of_layers(t, ghosts, k=k, src=src, fraction=fraction):
            for odd in range(2):
                b = 2 * t + odd
                co = coefficients([wide_wind[d, b] for d in range(3)])
                for f in range(q):
                    center = src[f, b + 1, rows, :]
                    ghost = ghosts[odd * q + f]
                    rate = rate_of(
                        co,
                        center,
                        src[f, b, rows, :],
                        src[f, b + 2, rows, :],
                        src[f, b + 1, TOP - 1 : TOP + y - 1, :],
                        src[f, b + 1, TOP + 1 : TOP + y + 1, :],
                        pltpu.roll(jnp.where(is_last, ghost, center), 1, 1),
                        pltpu.roll(jnp.where(is_first, ghost, center), z - 1, 1),
                    )
                    value = (center if k == 0 else s0[f, b + 1, rows, :]) + fraction * rate
                    if k < 2:
                        states[k + 1][f, b + 1, rows, :] = value
                    else:
                        out[f, b - 2] = value
            return tuple(pltpu.roll(g, z - 2, 1) for g in ghosts)

        lax.fori_loop(begin, end, pair_of_layers, carried)
    rz = lax.broadcasted_iota(jnp.int32, (z, z), 0)
    cz = lax.broadcasted_iota(jnp.int32, (z, z), 1)
    flat = out.reshape(q * fx * y, z)
    pairs_z = [jnp.where(cz == rz // 2 + odd * s.sz, 0.125, 0.0).astype(BF16) for odd in range(2)]
    for f in range(q):
        sums = []
        for odd in range(2):
            parts = []
            for p in range(s.x // 2):
                base = (f * fx + 4 * p + 2 * odd) * y
                part = None
                for more in (0, 1, y, y + 1):
                    piece = flat[pl.ds(base + more, y // 2, stride=2), :]
                    part = piece if part is None else part + piece
                parts.append(part)
            sums.append(times(jnp.concatenate(parts, axis=0), pairs_z[odd]))
        avg[f] = (sums[0] + sums[1]).reshape(s.x // 2, y // 2, z)


def merge_kernel(s, c3, avg, out):
    lane = lanes_of((s.sy, s.z))
    inside = (lane >= s.lz) & (lane < s.lz + s.sz)
    for f in range(s.q):
        for p in range(s.x // 2):
            both = avg[f, p]
            for odd in range(2):
                at = 2 * p + odd
                moved = pltpu.roll(both, s.lz if odd == 0 else s.z - s.lz, 1)
                out[f, at] = c3[f, at]
                out[f, at, s.ly : s.ly + s.sy, :] = jnp.where(inside, moved, c3[f, at, s.ly : s.ly + s.sy, :])


VMEM = pl.BlockSpec(memory_space=pltpu.VMEM)
SMEM = pl.BlockSpec(memory_space=pltpu.SMEM)
HBM = pl.BlockSpec(memory_space=pltpu.HBM)
ANY = pl.BlockSpec(memory_space=pl.ANY)


def params(megabytes):
    return pltpu.CompilerParams(vmem_limit_bytes=megabytes << 20)


def shape(*dims):
    return jax.ShapeDtypeStruct(dims, F32)


def ring(array, axis, by):
    size = lax.axis_size(axis)
    return lax.ppermute(array, axis, [(i, (i + by) % size) for i in range(size)])


def move_by(array, amount, beside=None):
    size = lax.axis_size("gx")
    work, operands = beside or (lambda: (), ())
    if size <= 8:

        def branch(by, array, *operands):
            return array if by == 0 else ring(array, "gx", by), work(*operands)

        return lax.switch(amount, [functools.partial(branch, by) for by in range(size)], array, *operands)
    for bit in range((size - 1).bit_length()):
        array = jnp.where((amount >> bit) % 2 == 1, ring(array, "gx", 1 << bit), array)
    return array, work(*operands)


def z_columns(zown):
    size = lax.axis_size("gz")
    if size == 1:
        return zown
    if size == 2:
        return lax.ppermute(zown, "gz", [(0, 1), (1, 0)])
    below = lax.broadcasted_iota(jnp.int32, zown.shape, 2) % 6 < 3
    return jnp.where(below, ring(zown, "gz", 1), ring(zown, "gz", -1))


def pack(s, fields, wind, name):
    return pl.pallas_call(
        functools.partial(pack_kernel, s),
        out_shape=(shape(s.halo, s.y, s.z),) * 2,
        in_specs=[HBM, HBM],
        out_specs=(VMEM, VMEM),
        scratch_shapes=[pltpu.SemaphoreType.DMA((2 * (s.q + 3),))],
        name=name,
    )(fields, wind)


def shards(coarse_fields, coarse_wind, fine_fields, fine_wind, fine_owner):
    s = Sizes(coarse_fields.shape, fine_fields.shape)
    q, x, y, z, fx = s.q, s.x, s.y, s.z, s.fx
    size = lax.axis_size("gx")
    offset = (fine_owner[0, 0, 0] - lax.axis_index("gx")) % size
    level = lax.axis_index("gz")
    neighbours = jnp.stack([level > 0, level < lax.axis_size("gz") - 1]).astype(jnp.int32).reshape(1, 2)
    up, down = pack(s, coarse_fields, coarse_wind, "pack_coarse")
    lo, hi = ring(up, "gx", 1), ring(down, "gx", -1)
    up, down = pack(s, fine_fields, fine_wind, "pack_fine")
    flo, fhi = ring(up, "gx", 1), ring(down, "gx", -1)
    edges = s.halo
    slab, yup, ydn = pl.pallas_call(
        functools.partial(slab_kernel, s),
        out_shape=(shape(s.slab, z), shape(edges, s.ex, z), shape(edges, s.ex, z)),
        in_specs=[VMEM] * 4,
        out_specs=(VMEM,) * 3,
        scratch_shapes=[pltpu.VMEM((q, s.ep, PAD, z), F32)] * 3,
        compiler_params=params(24),
        name="slab",
    )(coarse_fields, coarse_wind, lo, hi)
    ylo, yhi = ring(yup, "gy", 1), ring(ydn, "gy", -1)
    slab, _ = move_by(slab, (size - offset) % size)
    padded = pltpu.VMEM((q, s.ep, WPAD, z), F32)
    wind_rows = pltpu.VMEM((3, s.ex, 24, z), F32)
    zown = pl.pallas_call(
        functools.partial(zpack_kernel, s),
        out_shape=shape(q + 3, 24, z),
        in_specs=[VMEM] * 6,
        out_specs=VMEM,
        scratch_shapes=[padded, wind_rows],
        compiler_params=params(24),
        name="zpack",
    )(coarse_fields, coarse_wind, lo, hi, ylo, yhi)
    zin = z_columns(zown)

    def coarse(*operands):
        return pl.pallas_call(
            functools.partial(coarse_kernel, s),
            out_shape=shape(q, x, y, z),
            in_specs=[SMEM] + [VMEM] * 8,
            out_specs=VMEM,
            scratch_shapes=[padded] * 3 + [wind_rows, pltpu.VMEM((q, x, 24, z), F32)],
            compiler_params=params(24),
            cost_estimate=pl.CostEstimate(flops=40_000_000, bytes_accessed=4_000_000, transcendentals=0),
            name="coarse",
        )(*operands)

    layers = fx + 6
    fine_next, averaged = pl.pallas_call(
        functools.partial(fine_kernel, s),
        out_shape=(shape(q, fx, y, z), shape(q, x // 2, y // 2, z)),
        in_specs=[ANY, ANY, ANY, ANY, VMEM],
        out_specs=(VMEM, VMEM),
        scratch_shapes=[
            pltpu.VMEM((q, layers, PAD, z), F32),
            pltpu.VMEM((q, layers, PAD, z), F32),
            pltpu.VMEM((q, layers, PAD, z), F32),
            pltpu.VMEM((3, s.fe, y, z), F32),
            pltpu.VMEM((s.ep, z), F32),
            pltpu.VMEM((y, z), F32),
            pltpu.SemaphoreType.DMA((2 + 2 * (q + 3),)),
        ],
        compiler_params=params(32),
        name="fine",
    )(fine_fields, fine_wind, flo, fhi, slab)
    averaged, state = move_by(
        averaged,
        offset,
        (coarse, (neighbours, coarse_fields, coarse_wind, lo, hi, ylo, yhi, zown, zin)),
    )
    coarse_next = pl.pallas_call(
        functools.partial(merge_kernel, s),
        out_shape=shape(q, x, y, z),
        in_specs=[VMEM, VMEM],
        out_specs=VMEM,
        compiler_params=params(16),
        name="merge",
    )(state, averaged)
    return coarse_next, fine_next


def solution(mesh):
    spec = P(None, "gx", "gy", "gz")
    return jax.shard_map(
        shards,
        mesh=mesh,
        in_specs=(spec, spec, spec, spec, P("gx", "gy", "gz")),
        out_specs=(spec, spec),
        check_vma=False,
    )
```

```python
import functools

import jax
import jax.numpy as jnp
from jax import lax
from jax.experimental import pallas as pl
from jax.experimental.pallas import tpu as pltpu
from jax.sharding import PartitionSpec as P

diffusion = 0.05
section_weights = (1.0 / 3.0, 0.5, 1.0)
F32 = jnp.float32
BF16 = jnp.bfloat16
PAD = 32
TOP = 8


class Sizes:
    def __init__(self, coarse_shape, fine_shape):
        self.q, self.x, self.y, self.z = coarse_shape
        self.fx = fine_shape[1]
        self.ly, self.sy = self.y // 4, self.y // 2
        self.lz, self.sz = self.z // 4, self.z // 2
        self.ex = self.x + 4
        self.ep = -(-self.ex // 8) * 8
        self.fe = self.fx + 4
        self.halo = 3 * self.q + 6
        self.rows_f, self.rows_w = self.q * (3 * self.x + 6), 3 * (2 * self.x + 2)
        self.rows_y = 3 * self.q * self.ex
        self.rows_e = self.rows_y + self.ep
        self.rows_z = self.sy + 2
        self.slab = self.rows_e + self.q * self.rows_z
        assert self.q == 4 and self.y == 16 and self.z == 128 and self.ex <= 20 and self.fx == 2 * self.x


def lanes_of(shape):
    return lax.broadcasted_iota(jnp.int32, shape, len(shape) - 1)


def halves(value):
    high = value.astype(BF16)
    return high, (value - high.astype(F32)).astype(BF16)


def times(value, matrix):
    high, low = halves(value)
    return jnp.dot(high, matrix, preferred_element_type=F32) + jnp.dot(low, matrix, preferred_element_type=F32)


def coefficients(wind):
    out = []
    for w in wind:
        out += [diffusion - 0.5 * w, diffusion + 0.5 * w]
    return out


def rate_of(co, center, x_low, x_high, y_low, y_high, z_low, z_high):
    along = (co[0] * x_high + co[1] * x_low) + (co[2] * y_high + co[3] * y_low) + (co[4] * z_high + co[5] * z_low)
    return along - (6.0 * diffusion) * center


def layer_of(s, own, low, high, member, at, width, first):
    size = own.shape[1]
    if at < 0:
        return low[first + width * member + at + width]
    if at >= size:
        return high[first + width * member + at - size]
    return own[member, at]


def pack_kernel(s, c0, cw, f0, fw, cup, cdown, fup, fdown, sems):
    moves = []
    for fields, wind, up, down in ((c0, cw, cup, cdown), (f0, fw, fup, fdown)):
        size = fields.shape[1]
        for f in range(s.q):
            moves.append((fields.at[f, size - 3 : size], up.at[3 * f : 3 * f + 3]))
            moves.append((fields.at[f, 0:3], down.at[3 * f : 3 * f + 3]))
        for d in range(3):
            at = 3 * s.q + 2 * d
            moves.append((wind.at[d, size - 2 : size], up.at[at : at + 2]))
            moves.append((wind.at[d, 0:2], down.at[at : at + 2]))
    moves = [pltpu.make_async_copy(src, dst, sems.at[i]) for i, (src, dst) in enumerate(moves)]
    for move in moves:
        move.start()
    for move in moves:
        move.wait()


def y_rows(s, members, width):
    below, above = [], []
    for out, extra in ((below, lambda r: r), (above, lambda r: width - 1 - r)):
        at = 0
        for m in range(members):
            for r in range(width):
                out.append((m, r, extra(r), at))
                at += s.x + 2 * extra(r)
    return below, above


def ypack_kernel(s, c0, cw, lo, hi, up, dn):
    x, y, z = s.x, s.y, s.z
    flat_lo = lo.reshape(s.halo * y, z)
    flat_hi = hi.reshape(s.halo * y, z)
    for own, members, width, first, place in ((c0, s.q, 3, 0, 0), (cw, 3, 2, 3 * s.q, s.rows_f)):
        flat = own.reshape(members * x * y, z)
        for dst, rows, start in zip((up, dn), y_rows(s, members, width), (y - width, 0)):
            for m, r, e, at in rows:
                row, at = start + r, at + place
                if e:
                    dst[at : at + e, :] = flat_lo[pl.ds((first + width * (m + 1) - e) * y + row, e, stride=y), :]
                    dst[at + e + x : at + x + 2 * e, :] = flat_hi[pl.ds((first + width * m) * y + row, e, stride=y), :]
                dst[at + e : at + e + x, :] = flat[pl.ds(m * x * y + row, x, stride=y), :]


def slab_kernel(s, c0, cw, lo, hi, slab, pad0, pad1, pad2, wind):
    q, x, y, z = s.q, s.x, s.y, s.z
    own = slice(TOP, TOP + y)
    zeros = jnp.zeros((s.ep, z), F32)
    pads = (pad0, pad1, pad2)
    flats = [pad.reshape(q * s.ep * PAD, z) for pad in pads]
    for f in range(q):
        for pad in (flats[0], flats[1]):
            pad[pl.ds(f * s.ep * PAD + TOP - 1, s.ep, stride=PAD), :] = zeros
            pad[pl.ds(f * s.ep * PAD + TOP + y, s.ep, stride=PAD), :] = zeros
        for at in range(-3, x + 3):
            pad0[f, at + 3, own, :] = layer_of(s, c0, lo, hi, f, at, 3, 0)
        pad2[f, 1, own, :] = zeros[:y]
        pad2[f, s.ex, own, :] = zeros[:y]
    for d in range(3):
        for at in range(-2, x + 2):
            wind[d, at + 2] = layer_of(s, cw, lo, hi, d, at, 2, 3 * q)
    for step in range(2):
        src, flat, dst = pads[step], flats[step], pads[step + 1]

        def two_layers(t, carry, step=step, src=src, flat=flat, dst=dst):
            for odd in range(2):
                j = 2 * t + odd + step + 1
                co = coefficients([wind[d, j - 1] for d in range(3)])
                for f in range(q):
                    center = src[f, j, own, :]
                    row = (f * s.ep + j) * PAD + TOP
                    rate = rate_of(
                        co,
                        center,
                        src[f, j - 1, own, :],
                        src[f, j + 1, own, :],
                        flat[pl.ds(row - 1, y), :],
                        flat[pl.ds(row + 1, y), :],
                        pltpu.roll(center, 1, 1),
                        pltpu.roll(center, z - 1, 1),
                    )
                    base = center if step == 0 else pad0[f, j, own, :]
                    dst[f, j, own, :] = base + section_weights[step] * rate
            return carry

        lax.fori_loop(0, s.ex // 2 - step, two_layers, 0)
    lane_x = lanes_of((s.ex, z))
    lane_y = lanes_of((y, z))
    ends = None
    columns = (lane_y == s.lz - 1) | (lane_y == s.lz) | (lane_y == s.lz + s.sz - 1) | (lane_y == s.lz + s.sz)
    low_at = (lane_y % 2 == 0) & (lane_y < z // 2)
    high_at = (lane_y % 2 == 0) & (lane_y >= z // 2)
    for f in range(q):
        zfaces = None
        for k in range(3):
            start = (f * s.ep + 1) * PAD + TOP
            rows = [
                flats[k][pl.ds(start + at, s.ex, stride=PAD), :] for at in (s.ly - 1, s.ly, s.ly + s.sy - 1, s.ly + s.sy)
            ]
            sides = (0.75 * rows[0] + 0.25 * rows[1], 0.25 * rows[2] + 0.75 * rows[3])
            first = (k * q + f) * s.ex
            slab[first : first + s.ex, :] = jnp.where(
                lane_x < s.sz, pltpu.roll(sides[0], z - s.lz, 1), pltpu.roll(sides[1], s.lz, 1)
            )
            for side in range(2):
                e = 4 * (q * k + f) + 2 * side + 1
                before = jnp.where(lane_x == s.lz - 1, sides[side], 0.0)
                after = jnp.where(lane_x == s.lz + s.sz, sides[side], 0.0)
                part = pltpu.roll(before, (e - s.lz + 1) % z, 1) + pltpu.roll(after, (e - 1 - s.lz - s.sz) % z, 1)
                ends = part if ends is None else ends + part
            raw = None
            for a in range(0 if k == 0 else 1, s.ex if k == 0 else s.ex - 1):
                part = jnp.where(columns, pads[k][f, a + 1, own, :], 0.0)
                part = pltpu.roll(part, (2 * a - s.lz + 1) % z, 1)
                raw = part if raw is None else raw + part
            beside = pltpu.roll(raw, z - 1, 1)
            low = jnp.where(low_at, 0.75 * raw + 0.25 * beside, 0.0)
            high = jnp.where(high_at, 0.25 * raw + 0.75 * beside, 0.0)
            part = pltpu.roll(low, (2 * s.ex * k - 1) % z, 1) + pltpu.roll(high, (2 * s.ex * k - z // 2) % z, 1)
            zfaces = part if zfaces is None else zfaces + part
        at = s.rows_e + f * s.rows_z
        slab[at : at + s.rows_z, :] = zfaces[s.ly - 1 : s.ly + s.sy + 1]
    slab[s.rows_y : s.rows_y + s.ex, :] = ends
    slab[s.rows_y + s.ex : s.rows_e, :] = zeros[: s.ep - s.ex]


WTOP, WPAD = 12, 40
BLOCK = slice(8, 32)


def assemble(s, c0, cw, lo, hi, below, above, pad, wind):
    q, x, y, z = s.q, s.x, s.y, s.z
    flat = pad.reshape(q * s.ep * WPAD, z)
    flat_wind = wind.reshape(3 * s.ex * 24, z)
    for f in range(q):
        for at in range(-3, x + 3):
            pad[f, at + 3, WTOP : WTOP + y, :] = layer_of(s, c0, lo, hi, f, at, 3, 0)
    for d in range(3):
        for at in range(-2, x + 2):
            wind[d, at + 2, 4 : 4 + y, :] = layer_of(s, cw, lo, hi, d, at, 2, 3 * q)
    for src, rows, start in zip((below, above), y_rows(s, q, 3), (WTOP - 3, WTOP + y)):
        for m, r, e, at in rows:
            count = x + 2 * e
            flat[pl.ds((m * s.ep + 3 - e) * WPAD + start + r, count, stride=WPAD), :] = src[at : at + count, :]
    for src, rows, start in zip((below, above), y_rows(s, 3, 2), (2, 4 + y)):
        for m, r, e, at in rows:
            count, at = x + 2 * e, at + s.rows_f
            flat_wind[pl.ds((m * s.ex + 2 - e) * 24 + start + r, count, stride=24), :] = src[at : at + count, :]


def edge_lanes(s, lane, width):
    return (lane < width) | (lane >= s.z - width)


def zpack_kernel(s, c0, cw, lo, hi, below, above, out, pad, wind):
    assemble(s, c0, cw, lo, hi, below, above, pad, wind)
    lane = lanes_of((24, s.z))
    keep = edge_lanes(s, lane, 3)
    for m in range(s.q + 3):
        total = None
        for a in range(s.ex):
            tile = pad[m, a + 1, BLOCK, :] if m < s.q else wind[m - s.q, a]
            part = pltpu.roll(jnp.where(keep, tile, 0.0), (6 * a + 3) % s.z, 1)
            total = part if total is None else total + part
        out[m] = total


def coarse_kernel(
    s, sides, c0, cw, lo, hi, below, above, zown, zin, out, pad0, pad1, pad2, wind, beyond, nearest
):
    q, x, y, z = s.q, s.x, s.y, s.z
    assemble(s, c0, cw, lo, hi, below, above, pad0, wind)
    pads = (pad0, pad1, pad2)
    lane = lanes_of((24, z))
    group = lane % 6
    from_low = group == 2
    from_high = group == 3
    exists = jnp.where(group < 3, sides[0, 0], sides[0, 1]).astype(F32)
    co_z = coefficients([zin[q + d] for d in range(3)])
    for f in range(q):
        beyond[0, f] = zin[f] * exists
        nearest[0, f] = zown[f]
    for step in range(3):
        src, fraction = pads[step], section_weights[step]
        flat = src.reshape(q * s.ep * WPAD, z)
        flat0 = pad0.reshape(q * s.ep * WPAD, z)
        flat_wind = wind.reshape(3 * s.ex * 24, z)
        flat_beyond = beyond.reshape(3 * q * 24, z)
        skip, height = (0, 24) if step < 2 else (4, y)
        here = lanes_of((height, z))
        is_first, is_last = here == 0, here == z - 1

        def layer(a, packed, step=step, flat=flat, fraction=fraction, skip=skip, height=height):
            made = []
            co = coefficients([flat_wind[pl.ds((d * s.ex + a) * 24 + skip, height), :] for d in range(3)])
            for f in range(q):
                row = (f * s.ep + a + 1) * WPAD + 8 + skip
                center = flat[pl.ds(row, height), :]
                ghost = pltpu.roll(flat_beyond[pl.ds((step * q + f) * 24 + skip, height), :], 2 * z - 6 * a - 3, 1)
                rate = rate_of(
                    co,
                    center,
                    flat[pl.ds(row - WPAD, height), :],
                    flat[pl.ds(row + WPAD, height), :],
                    flat[pl.ds(row - 1, height), :],
                    flat[pl.ds(row + 1, height), :],
                    pltpu.roll(jnp.where(is_last, ghost, center), 1, 1),
                    pltpu.roll(jnp.where(is_first, ghost, center), z - 1, 1),
                )
                base = center if step == 0 else flat0[pl.ds(row, height), :]
                value = base + fraction * rate
                if step == 2:
                    out[f, a - 2] = value
                else:
                    pads[step + 1][f, a + 1, BLOCK, :] = value
                if step == 0:
                    made.append(packed[f] + pltpu.roll(jnp.where(is_first | is_last, value, 0.0), 6 * a + 3, 1))
            return tuple(made)

        begin, end = step, s.ex - step
        start = tuple(jnp.zeros((24, z), F32) for _ in range(q)) if step == 0 else ()
        packed = lax.fori_loop(begin, end, layer, start)
        if step == 2:
            break
        for f in range(q):
            if step == 0:
                nearest[1, f] = packed[f]
            ghost, near = beyond[step, f], nearest[step, f]
            rate = rate_of(
                co_z,
                ghost,
                pltpu.roll(ghost, 6, 1),
                pltpu.roll(ghost, z - 6, 1),
                pltpu.roll(ghost, 1, 0),
                pltpu.roll(ghost, 23, 0),
                pltpu.roll(jnp.where(from_low, near, ghost), 1, 1),
                pltpu.roll(jnp.where(from_high, near, ghost), z - 1, 1),
            )
            beyond[step + 1, f] = (beyond[0, f] + fraction * rate) * exists


def fine_kernel(s, f0, fw, flo, fhi, slab, out, avg, *scratch):
    s0, s1, s2, wide_wind, faces, zface, sems = scratch
    states = (s0, s1, s2)
    q, y, z, fx, fe = s.q, s.y, s.z, s.fx, s.fe
    layers = fx + 6
    rows = slice(TOP, TOP + y)
    pairs = [(f0, s0.at[:, 3 : 3 + fx, rows]), (fw, wide_wind.at[:, 2 : 2 + fx])]
    for f in range(q):
        pairs.append((flo.at[3 * f : 3 * f + 3], s0.at[f, 0:3, rows]))
        pairs.append((fhi.at[3 * f : 3 * f + 3], s0.at[f, 3 + fx : 6 + fx, rows]))
    for d in range(3):
        at = 3 * q + 2 * d
        pairs.append((flo.at[at : at + 2], wide_wind.at[d, 0:2]))
        pairs.append((fhi.at[at : at + 2], wide_wind.at[d, 2 + fx : 4 + fx]))
    moves = [pltpu.make_async_copy(src, dst, sems.at[i]) for i, (src, dst) in enumerate(pairs)]
    for move in moves:
        move.start()
    r = lax.broadcasted_iota(jnp.int32, (z, 2 * z), 0)
    c = lax.broadcasted_iota(jnp.int32, (z, 2 * z), 1)
    near = c // 2
    far = near + 2 * (c % 2) - 1
    same = (far // s.sz == near // s.sz) & (far >= 0)
    to_fine = jnp.where(r == near, 0.75, jnp.where((r == far) & same, 0.25, 0.0)).astype(BF16)
    wide = times(slab[: s.rows_y, :], to_fine)
    ends = slab[s.rows_y : s.rows_y + s.ex, :]
    lane_x = lanes_of((s.ex, z))
    edge = (lane_x == 0) | (lane_x == z - 1)
    half = fe // 2
    for k in range(3):
        flat = states[k].reshape(q * layers * PAD, z)
        for f in range(q):
            for side in range(2):
                e = 4 * (q * k + f) + 2 * side + 1
                corner = jnp.where(edge, 0.25 * pltpu.roll(ends, z - e, 1), 0.0)
                first = (k * q + f) * s.ex
                here = faces.at[(k * q + f) * 2 + side]
                here[: s.ex, :] = wide[first : first + s.ex, side * z : side * z + z] + corner
                a = here[0:half, :]
                b = here[1 : half + 1, :]
                d = here[2 : half + 2, :]
                row = TOP - 1 if side == 0 else TOP + y
                base = (f * layers + 1) * PAD + row
                flat[pl.ds(base, half, stride=2 * PAD), :] = 0.25 * a + 0.75 * b
                flat[pl.ds(base + PAD, half, stride=2 * PAD), :] = 0.75 * b + 0.25 * d
    evens, odds = [], []
    for f in range(q):
        at = s.rows_e + f * s.rows_z
        a = slab[at : at + s.sy, :]
        b = slab[at + 1 : at + 1 + s.sy, :]
        d = slab[at + 2 : at + 2 + s.sy, :]
        zface[pl.ds(f * y, s.sy, stride=2), :] = 0.25 * a + 0.75 * b
        zface[pl.ds(f * y + 1, s.sy, stride=2), :] = 0.75 * b + 0.25 * d
        a = zface[f * y : f * y + y, :]
        b = pltpu.roll(a, z - 2, 1)
        d = pltpu.roll(a, z - 4, 1)
        evens.append(0.25 * a + 0.75 * b)
        odds.append(0.75 * b + 0.25 * d)
    for move in moves:
        move.wait()
    lane = lanes_of((y, z))
    is_first, is_last = lane == 0, lane == z - 1
    for k in range(3):
        src, fraction = states[k], section_weights[k]
        flat = src.reshape(q * layers * PAD, z)
        begin, end = (0, half) if k < 2 else (1, half - 1)
        shift = -(2 * s.ex * k + 2 * begin) % z
        carried = tuple(pltpu.roll(g, shift, 1) if shift else g for g in evens + odds)

        def pair_of_layers(t, ghosts, k=k, src=src, flat=flat, fraction=fraction):
            for odd in range(2):
                b = 2 * t + odd
                co = coefficients([wide_wind[d, b] for d in range(3)])
                for f in range(q):
                    center = src[f, b + 1, rows, :]
                    ghost = ghosts[odd * q + f]
                    row = (f * layers + b + 1) * PAD + TOP
                    rate = rate_of(
                        co,
                        center,
                        src[f, b, rows, :],
                        src[f, b + 2, rows, :],
                        flat[pl.ds(row - 1, y), :],
                        flat[pl.ds(row + 1, y), :],
                        pltpu.roll(jnp.where(is_last, ghost, center), 1, 1),
                        pltpu.roll(jnp.where(is_first, ghost, center), z - 1, 1),
                    )
                    value = (center if k == 0 else s0[f, b + 1, rows, :]) + fraction * rate
                    if k < 2:
                        states[k + 1][f, b + 1, rows, :] = value
                    else:
                        out[f, b - 2] = value
            return tuple(pltpu.roll(g, z - 2, 1) for g in ghosts)

        lax.fori_loop(begin, end, pair_of_layers, carried)
    rz = lax.broadcasted_iota(jnp.int32, (z, z), 0)
    cz = lax.broadcasted_iota(jnp.int32, (z, z), 1)
    flat = out.reshape(q * fx * y, z)
    pairs_z = [jnp.where(cz == rz // 2 + odd * s.sz, 0.125, 0.0).astype(BF16) for odd in range(2)]
    for f in range(q):
        sums = []
        for odd in range(2):
            parts = []
            for p in range(s.x // 2):
                base = (f * fx + 4 * p + 2 * odd) * y
                part = None
                for more in (0, 1, y, y + 1):
                    piece = flat[pl.ds(base + more, y // 2, stride=2), :]
                    part = piece if part is None else part + piece
                parts.append(part)
            sums.append(times(jnp.concatenate(parts, axis=0), pairs_z[odd]))
        avg[f] = (sums[0] + sums[1]).reshape(s.x // 2, y // 2, z)


def merge_kernel(s, c3, avg, out):
    lane = lanes_of((s.sy, s.z))
    inside = (lane >= s.lz) & (lane < s.lz + s.sz)
    for f in range(s.q):
        for p in range(s.x // 2):
            both = avg[f, p]
            for odd in range(2):
                at = 2 * p + odd
                moved = pltpu.roll(both, s.lz if odd == 0 else s.z - s.lz, 1)
                out[f, at] = c3[f, at]
                out[f, at, s.ly : s.ly + s.sy, :] = jnp.where(inside, moved, c3[f, at, s.ly : s.ly + s.sy, :])


VMEM = pl.BlockSpec(memory_space=pltpu.VMEM)
SMEM = pl.BlockSpec(memory_space=pltpu.SMEM)
HBM = pl.BlockSpec(memory_space=pltpu.HBM)
ANY = pl.BlockSpec(memory_space=pl.ANY)


SHORT = pl.CostEstimate(flops=1, bytes_accessed=1, transcendentals=0)


def params(megabytes):
    return pltpu.CompilerParams(vmem_limit_bytes=megabytes << 20)


def shape(*dims):
    return jax.ShapeDtypeStruct(dims, F32)


def ring(array, axis, by):
    size = lax.axis_size(axis)
    return lax.ppermute(array, axis, [(i, (i + by) % size) for i in range(size)])


def move_by(array, amount, beside=None):
    size = lax.axis_size("gx")
    work, operands = beside or (lambda: (), ())
    if size <= 8:

        def branch(by, array, *operands):
            return array if by == 0 else ring(array, "gx", by), work(*operands)

        return lax.switch(amount, [functools.partial(branch, by) for by in range(size)], array, *operands)
    for bit in range((size - 1).bit_length()):
        array = jnp.where((amount >> bit) % 2 == 1, ring(array, "gx", 1 << bit), array)
    return array, work(*operands)


def z_columns(zown):
    size = lax.axis_size("gz")
    if size == 1:
        return zown
    if size == 2:
        return lax.ppermute(zown, "gz", [(0, 1), (1, 0)])
    below = lax.broadcasted_iota(jnp.int32, zown.shape, 2) % 6 < 3
    return jnp.where(below, ring(zown, "gz", 1), ring(zown, "gz", -1))


def shards(coarse_fields, coarse_wind, fine_fields, fine_wind, fine_owner):
    s = Sizes(coarse_fields.shape, fine_fields.shape)
    q, x, y, z, fx = s.q, s.x, s.y, s.z, s.fx
    size = lax.axis_size("gx")
    offset = (fine_owner[0, 0, 0] - lax.axis_index("gx")) % size
    level = lax.axis_index("gz")
    neighbours = jnp.stack([level > 0, level < lax.axis_size("gz") - 1]).astype(jnp.int32).reshape(1, 2)
    cup, cdown, fup, fdown = pl.pallas_call(
        functools.partial(pack_kernel, s),
        out_shape=(shape(s.halo, y, z),) * 4,
        in_specs=[HBM] * 4,
        out_specs=(VMEM,) * 4,
        scratch_shapes=[pltpu.SemaphoreType.DMA((4 * (q + 3),))],
        cost_estimate=SHORT,
        name="pack",
    )(coarse_fields, coarse_wind, fine_fields, fine_wind)
    lo, hi = ring(cup, "gx", 1), ring(cdown, "gx", -1)
    flo, fhi = ring(fup, "gx", 1), ring(fdown, "gx", -1)
    yup, ydn = pl.pallas_call(
        functools.partial(ypack_kernel, s),
        out_shape=(shape(s.rows_f + s.rows_w, z),) * 2,
        in_specs=[VMEM] * 4,
        out_specs=(VMEM,) * 2,
        cost_estimate=SHORT,
        name="ypack",
    )(coarse_fields, coarse_wind, lo, hi)
    yrows = [ring(yup, "gy", 1), ring(ydn, "gy", -1)]
    slab = pl.pallas_call(
        functools.partial(slab_kernel, s),
        out_shape=shape(s.slab, z),
        in_specs=[VMEM] * 4,
        out_specs=VMEM,
        scratch_shapes=[pltpu.VMEM((q, s.ep, PAD, z), F32)] * 3 + [pltpu.VMEM((3, s.ex, y, z), F32)],
        compiler_params=params(24),
        cost_estimate=SHORT,
        name="slab",
    )(coarse_fields, coarse_wind, lo, hi)
    yrows, slab = lax.optimization_barrier((yrows, slab))
    padded = pltpu.VMEM((q, s.ep, WPAD, z), F32)
    wind_rows = pltpu.VMEM((3, s.ex, 24, z), F32)
    zown = pl.pallas_call(
        functools.partial(zpack_kernel, s),
        out_shape=shape(q + 3, 24, z),
        in_specs=[VMEM] * 6,
        out_specs=VMEM,
        scratch_shapes=[padded, wind_rows],
        compiler_params=params(24),
        cost_estimate=SHORT,
        name="zpack",
    )(coarse_fields, coarse_wind, lo, hi, *yrows)
    zin = z_columns(zown)
    slab, flo, fhi = lax.optimization_barrier((slab, flo, fhi))
    slab, _ = move_by(slab, (size - offset) % size)
    def coarse(*operands):
        return pl.pallas_call(
            functools.partial(coarse_kernel, s),
            out_shape=shape(q, x, y, z),
            in_specs=[SMEM] + [VMEM] * 8,
            out_specs=VMEM,
            scratch_shapes=[padded] * 3 + [wind_rows, pltpu.VMEM((3, q, 24, z), F32), pltpu.VMEM((2, q, 24, z), F32)],
            compiler_params=params(24),
            cost_estimate=pl.CostEstimate(flops=40_000_000, bytes_accessed=4_000_000, transcendentals=0),
            name="coarse",
        )(*operands)

    layers = fx + 6
    fine_next, averaged = pl.pallas_call(
        functools.partial(fine_kernel, s),
        out_shape=(shape(q, fx, y, z), shape(q, x // 2, y // 2, z)),
        in_specs=[ANY, ANY, ANY, ANY, VMEM],
        out_specs=(VMEM, VMEM),
        scratch_shapes=[
            pltpu.VMEM((q, layers, PAD, z), F32),
            pltpu.VMEM((q, layers, PAD, z), F32),
            pltpu.VMEM((q, layers, PAD, z), F32),
            pltpu.VMEM((3, s.fe, y, z), F32),
            pltpu.VMEM((6 * q, s.ep, z), F32),
            pltpu.VMEM((q * y, z), F32),
            pltpu.SemaphoreType.DMA((2 + 2 * (q + 3),)),
        ],
        compiler_params=params(32),
        name="fine",
    )(fine_fields, fine_wind, flo, fhi, slab)
    averaged, state = move_by(
        averaged,
        offset,
        (coarse, (neighbours, coarse_fields, coarse_wind, lo, hi, *yrows, zown, zin)),
    )
    coarse_next = pl.pallas_call(
        functools.partial(merge_kernel, s),
        out_shape=shape(q, x, y, z),
        in_specs=[VMEM, VMEM],
        out_specs=VMEM,
        compiler_params=params(16),
        name="merge",
    )(state, averaged)
    return coarse_next, fine_next


def solution(mesh):
    spec = P(None, "gx", "gy", "gz")
    return jax.shard_map(
        shards,
        mesh=mesh,
        in_specs=(spec, spec, spec, spec, P("gx", "gy", "gz")),
        out_specs=(spec, spec),
        check_vma=False,
    )
```

```python
import functools

import jax
import jax.numpy as jnp
from jax import lax
from jax.experimental import pallas as pl
from jax.experimental.pallas import tpu as pltpu
from jax.sharding import PartitionSpec as P

diffusion = 0.05
section_weights = (1.0 / 3.0, 0.5, 1.0)
F32 = jnp.float32
BF16 = jnp.bfloat16
PAD = 32
TOP = 8


class Sizes:
    def __init__(self, coarse_shape, fine_shape):
        self.q, self.x, self.y, self.z = coarse_shape
        self.fx = fine_shape[1]
        self.ly, self.sy = self.y // 4, self.y // 2
        self.lz, self.sz = self.z // 4, self.z // 2
        self.ex = self.x + 4
        self.ep = -(-self.ex // 8) * 8
        self.fe = self.fx + 4
        self.halo = 3 * self.q + 6
        self.rows_f, self.rows_w = self.q * (3 * self.x + 6), 3 * (2 * self.x + 2)
        self.rows_y = 3 * self.q * self.ex
        self.rows_e = self.rows_y + self.ep
        self.rows_z = self.sy + 2
        self.slab = self.rows_e + self.q * self.rows_z
        assert self.q == 4 and self.y == 16 and self.z == 128 and self.ex <= 20 and self.fx == 2 * self.x


def lanes_of(shape):
    return lax.broadcasted_iota(jnp.int32, shape, len(shape) - 1)


def halves(value):
    high = value.astype(BF16)
    return high, (value - high.astype(F32)).astype(BF16)


def times(value, matrix):
    high, low = halves(value)
    return jnp.dot(high, matrix, preferred_element_type=F32) + jnp.dot(low, matrix, preferred_element_type=F32)


def coefficients(wind):
    out = []
    for w in wind:
        out += [diffusion - 0.5 * w, diffusion + 0.5 * w]
    return out


def rate_of(co, center, x_low, x_high, y_low, y_high, z_low, z_high):
    along = (co[0] * x_high + co[1] * x_low) + (co[2] * y_high + co[3] * y_low) + (co[4] * z_high + co[5] * z_low)
    return along - (6.0 * diffusion) * center


def layer_of(s, own, low, high, member, at, width, first):
    size = own.shape[1]
    if at < 0:
        return low[first + width * member + at + width]
    if at >= size:
        return high[first + width * member + at - size]
    return own[member, at]


def unrolled(begin, end, at_once, body, carry=()):
    while (end - begin) % at_once:
        at_once -= 1

    def several(i, carry):
        for more in range(at_once):
            carry = body(begin + i * at_once + more, carry)
        return carry

    return lax.fori_loop(0, (end - begin) // at_once, several, carry)


def pack_kernel(s, c0, cw, f0, fw, cup, cdown, fup, fdown, sems):
    moves = []
    for fields, wind, up, down in ((c0, cw, cup, cdown), (f0, fw, fup, fdown)):
        size = fields.shape[1]
        for f in range(s.q):
            moves.append((fields.at[f, size - 3 : size], up.at[3 * f : 3 * f + 3]))
            moves.append((fields.at[f, 0:3], down.at[3 * f : 3 * f + 3]))
        for d in range(3):
            at = 3 * s.q + 2 * d
            moves.append((wind.at[d, size - 2 : size], up.at[at : at + 2]))
            moves.append((wind.at[d, 0:2], down.at[at : at + 2]))
    moves = [pltpu.make_async_copy(src, dst, sems.at[i]) for i, (src, dst) in enumerate(moves)]
    for move in moves:
        move.start()
    for move in moves:
        move.wait()


def y_rows(s, members, width):
    below, above = [], []
    for out, extra in ((below, lambda r: r), (above, lambda r: width - 1 - r)):
        at = 0
        for m in range(members):
            for r in range(width):
                out.append((m, r, extra(r), at))
                at += s.x + 2 * extra(r)
    return below, above


def ypack_kernel(s, c0, cw, lo, hi, up, dn):
    x, y, z = s.x, s.y, s.z
    flat_lo = lo.reshape(s.halo * y, z)
    flat_hi = hi.reshape(s.halo * y, z)
    for own, members, width, first, place in ((c0, s.q, 3, 0, 0), (cw, 3, 2, 3 * s.q, s.rows_f)):
        flat = own.reshape(members * x * y, z)
        for dst, rows, start in zip((up, dn), y_rows(s, members, width), (y - width, 0)):
            for m, r, e, at in rows:
                row, at = start + r, at + place
                if e:
                    dst[at : at + e, :] = flat_lo[pl.ds((first + width * (m + 1) - e) * y + row, e, stride=y), :]
                    dst[at + e + x : at + x + 2 * e, :] = flat_hi[pl.ds((first + width * m) * y + row, e, stride=y), :]
                dst[at + e : at + e + x, :] = flat[pl.ds(m * x * y + row, x, stride=y), :]


def slab_kernel(s, c0, cw, lo, hi, slab, pad0, pad1, pad2, wind):
    q, x, y, z = s.q, s.x, s.y, s.z
    own = slice(TOP, TOP + y)
    zeros = jnp.zeros((s.ep, z), F32)
    pads = (pad0, pad1, pad2)
    flats = [pad.reshape(q * s.ep * PAD, z) for pad in pads]
    for f in range(q):
        for pad in (flats[0], flats[1]):
            pad[pl.ds(f * s.ep * PAD + TOP - 1, s.ep, stride=PAD), :] = zeros
            pad[pl.ds(f * s.ep * PAD + TOP + y, s.ep, stride=PAD), :] = zeros
        for at in range(-3, x + 3):
            pad0[f, at + 3, own, :] = layer_of(s, c0, lo, hi, f, at, 3, 0)
        pad2[f, 1, own, :] = zeros[:y]
        pad2[f, s.ex, own, :] = zeros[:y]
    for d in range(3):
        for at in range(-2, x + 2):
            wind[d, at + 2] = layer_of(s, cw, lo, hi, d, at, 2, 3 * q)
    for step in range(2):
        src, flat, dst = pads[step], flats[step], pads[step + 1]

        def layer(j, carry, step=step, src=src, flat=flat, dst=dst):
            co = coefficients([wind[d, j - 1] for d in range(3)])
            for f in range(q):
                center = src[f, j, own, :]
                row = (f * s.ep + j) * PAD + TOP
                rate = rate_of(
                    co,
                    center,
                    src[f, j - 1, own, :],
                    src[f, j + 1, own, :],
                    flat[pl.ds(row - 1, y), :],
                    flat[pl.ds(row + 1, y), :],
                    pltpu.roll(center, 1, 1),
                    pltpu.roll(center, z - 1, 1),
                )
                base = center if step == 0 else pad0[f, j, own, :]
                dst[f, j, own, :] = base + section_weights[step] * rate
            return carry

        unrolled(step + 1, s.ex + 1 - step, 5 if step == 0 else 6, layer)
    lane_x = lanes_of((s.ex, z))
    lane_y = lanes_of((y, z))
    ends = None
    columns = (lane_y == s.lz - 1) | (lane_y == s.lz) | (lane_y == s.lz + s.sz - 1) | (lane_y == s.lz + s.sz)
    low_at = (lane_y % 2 == 0) & (lane_y < z // 2)
    high_at = (lane_y % 2 == 0) & (lane_y >= z // 2)
    for f in range(q):
        zfaces = None
        for k in range(3):
            start = (f * s.ep + 1) * PAD + TOP
            rows = [
                flats[k][pl.ds(start + at, s.ex, stride=PAD), :] for at in (s.ly - 1, s.ly, s.ly + s.sy - 1, s.ly + s.sy)
            ]
            sides = (0.75 * rows[0] + 0.25 * rows[1], 0.25 * rows[2] + 0.75 * rows[3])
            first = (k * q + f) * s.ex
            slab[first : first + s.ex, :] = jnp.where(
                lane_x < s.sz, pltpu.roll(sides[0], z - s.lz, 1), pltpu.roll(sides[1], s.lz, 1)
            )
            for side in range(2):
                e = 4 * (q * k + f) + 2 * side + 1
                before = jnp.where(lane_x == s.lz - 1, sides[side], 0.0)
                after = jnp.where(lane_x == s.lz + s.sz, sides[side], 0.0)
                part = pltpu.roll(before, (e - s.lz + 1) % z, 1) + pltpu.roll(after, (e - 1 - s.lz - s.sz) % z, 1)
                ends = part if ends is None else ends + part
            raw = None
            for a in range(0 if k == 0 else 1, s.ex if k == 0 else s.ex - 1):
                part = jnp.where(columns, pads[k][f, a + 1, own, :], 0.0)
                part = pltpu.roll(part, (2 * a - s.lz + 1) % z, 1)
                raw = part if raw is None else raw + part
            beside = pltpu.roll(raw, z - 1, 1)
            low = jnp.where(low_at, 0.75 * raw + 0.25 * beside, 0.0)
            high = jnp.where(high_at, 0.25 * raw + 0.75 * beside, 0.0)
            part = pltpu.roll(low, (2 * s.ex * k - 1) % z, 1) + pltpu.roll(high, (2 * s.ex * k - z // 2) % z, 1)
            zfaces = part if zfaces is None else zfaces + part
        at = s.rows_e + f * s.rows_z
        slab[at : at + s.rows_z, :] = zfaces[s.ly - 1 : s.ly + s.sy + 1]
    slab[s.rows_y : s.rows_y + s.ex, :] = ends
    slab[s.rows_y + s.ex : s.rows_e, :] = zeros[: s.ep - s.ex]


WTOP, WPAD = 12, 40
BLOCK = slice(8, 32)


def assemble(s, c0, cw, lo, hi, below, above, pad, wind):
    q, x, y, z = s.q, s.x, s.y, s.z
    flat = pad.reshape(q * s.ep * WPAD, z)
    flat_wind = wind.reshape(3 * s.ex * 24, z)
    for f in range(q):
        for at in range(-3, x + 3):
            pad[f, at + 3, WTOP : WTOP + y, :] = layer_of(s, c0, lo, hi, f, at, 3, 0)
    for d in range(3):
        for at in range(-2, x + 2):
            wind[d, at + 2, 4 : 4 + y, :] = layer_of(s, cw, lo, hi, d, at, 2, 3 * q)
    for src, rows, start in zip((below, above), y_rows(s, q, 3), (WTOP - 3, WTOP + y)):
        for m, r, e, at in rows:
            count = x + 2 * e
            flat[pl.ds((m * s.ep + 3 - e) * WPAD + start + r, count, stride=WPAD), :] = src[at : at + count, :]
    for src, rows, start in zip((below, above), y_rows(s, 3, 2), (2, 4 + y)):
        for m, r, e, at in rows:
            count, at = x + 2 * e, at + s.rows_f
            flat_wind[pl.ds((m * s.ex + 2 - e) * 24 + start + r, count, stride=24), :] = src[at : at + count, :]


def edge_lanes(s, lane, width):
    return (lane < width) | (lane >= s.z - width)


def zpack_kernel(s, c0, cw, lo, hi, below, above, out, pad, wind):
    assemble(s, c0, cw, lo, hi, below, above, pad, wind)
    lane = lanes_of((24, s.z))
    keep = edge_lanes(s, lane, 3)
    for m in range(s.q + 3):
        total = None
        for a in range(s.ex):
            tile = pad[m, a + 1, BLOCK, :] if m < s.q else wind[m - s.q, a]
            part = pltpu.roll(jnp.where(keep, tile, 0.0), (6 * a + 3) % s.z, 1)
            total = part if total is None else total + part
        out[m] = total


def coarse_kernel(
    s, sides, c0, cw, lo, hi, below, above, zown, zin, out, pad0, pad1, pad2, wind, beyond, nearest
):
    q, x, y, z = s.q, s.x, s.y, s.z
    assemble(s, c0, cw, lo, hi, below, above, pad0, wind)
    pads = (pad0, pad1, pad2)
    lane = lanes_of((24, z))
    group = lane % 6
    from_low = group == 2
    from_high = group == 3
    exists = jnp.where(group < 3, sides[0, 0], sides[0, 1]).astype(F32)
    co_z = coefficients([zin[q + d] for d in range(3)])
    for f in range(q):
        beyond[0, f] = zin[f] * exists
        nearest[0, f] = zown[f]
    for step in range(3):
        src, fraction = pads[step], section_weights[step]
        flat = src.reshape(q * s.ep * WPAD, z)
        flat0 = pad0.reshape(q * s.ep * WPAD, z)
        flat_wind = wind.reshape(3 * s.ex * 24, z)
        flat_beyond = beyond.reshape(3 * q * 24, z)
        skip, height = (0, 24) if step < 2 else (4, y)
        here = lanes_of((height, z))
        is_first, is_last = here == 0, here == z - 1

        def layer(a, packed, step=step, flat=flat, fraction=fraction, skip=skip, height=height):
            made = []
            co = coefficients([flat_wind[pl.ds((d * s.ex + a) * 24 + skip, height), :] for d in range(3)])
            for f in range(q):
                row = (f * s.ep + a + 1) * WPAD + 8 + skip
                center = flat[pl.ds(row, height), :]
                ghost = pltpu.roll(flat_beyond[pl.ds((step * q + f) * 24 + skip, height), :], 2 * z - 6 * a - 3, 1)
                rate = rate_of(
                    co,
                    center,
                    flat[pl.ds(row - WPAD, height), :],
                    flat[pl.ds(row + WPAD, height), :],
                    flat[pl.ds(row - 1, height), :],
                    flat[pl.ds(row + 1, height), :],
                    pltpu.roll(jnp.where(is_last, ghost, center), 1, 1),
                    pltpu.roll(jnp.where(is_first, ghost, center), z - 1, 1),
                )
                base = center if step == 0 else flat0[pl.ds(row, height), :]
                value = base + fraction * rate
                if step == 2:
                    out[f, a - 2] = value
                else:
                    pads[step + 1][f, a + 1, BLOCK, :] = value
                if step == 0:
                    made.append(packed[f] + pltpu.roll(jnp.where(is_first | is_last, value, 0.0), 6 * a + 3, 1))
            return tuple(made)

        begin, end = step, s.ex - step
        start = tuple(jnp.zeros((24, z), F32) for _ in range(q)) if step == 0 else ()
        packed = unrolled(begin, end, 4 + 2 * (step == 1), layer, start)
        if step == 2:
            break
        for f in range(q):
            if step == 0:
                nearest[1, f] = packed[f]
            ghost, near = beyond[step, f], nearest[step, f]
            rate = rate_of(
                co_z,
                ghost,
                pltpu.roll(ghost, 6, 1),
                pltpu.roll(ghost, z - 6, 1),
                pltpu.roll(ghost, 1, 0),
                pltpu.roll(ghost, 23, 0),
                pltpu.roll(jnp.where(from_low, near, ghost), 1, 1),
                pltpu.roll(jnp.where(from_high, near, ghost), z - 1, 1),
            )
            beyond[step + 1, f] = (beyond[0, f] + fraction * rate) * exists


def fine_kernel(s, f0, fw, flo, fhi, slab, out, avg, *scratch):
    s0, s1, s2, wide_wind, faces, zface, sems = scratch
    states = (s0, s1, s2)
    q, y, z, fx, fe = s.q, s.y, s.z, s.fx, s.fe
    layers = fx + 6
    rows = slice(TOP, TOP + y)
    pairs = [(f0, s0.at[:, 3 : 3 + fx, rows]), (fw, wide_wind.at[:, 2 : 2 + fx])]
    for f in range(q):
        pairs.append((flo.at[3 * f : 3 * f + 3], s0.at[f, 0:3, rows]))
        pairs.append((fhi.at[3 * f : 3 * f + 3], s0.at[f, 3 + fx : 6 + fx, rows]))
    for d in range(3):
        at = 3 * q + 2 * d
        pairs.append((flo.at[at : at + 2], wide_wind.at[d, 0:2]))
        pairs.append((fhi.at[at : at + 2], wide_wind.at[d, 2 + fx : 4 + fx]))
    moves = [pltpu.make_async_copy(src, dst, sems.at[i]) for i, (src, dst) in enumerate(pairs)]
    for move in moves:
        move.start()
    r = lax.broadcasted_iota(jnp.int32, (z, 2 * z), 0)
    c = lax.broadcasted_iota(jnp.int32, (z, 2 * z), 1)
    near = c // 2
    far = near + 2 * (c % 2) - 1
    same = (far // s.sz == near // s.sz) & (far >= 0)
    to_fine = jnp.where(r == near, 0.75, jnp.where((r == far) & same, 0.25, 0.0)).astype(BF16)
    wide = times(slab[: s.rows_y, :], to_fine)
    ends = slab[s.rows_y : s.rows_y + s.ex, :]
    lane_x = lanes_of((s.ex, z))
    edge = (lane_x == 0) | (lane_x == z - 1)
    half = fe // 2
    for k in range(3):
        flat = states[k].reshape(q * layers * PAD, z)
        for f in range(q):
            for side in range(2):
                e = 4 * (q * k + f) + 2 * side + 1
                corner = jnp.where(edge, 0.25 * pltpu.roll(ends, z - e, 1), 0.0)
                first = (k * q + f) * s.ex
                here = faces.at[(k * q + f) * 2 + side]
                here[: s.ex, :] = wide[first : first + s.ex, side * z : side * z + z] + corner
                a = here[0:half, :]
                b = here[1 : half + 1, :]
                d = here[2 : half + 2, :]
                row = TOP - 1 if side == 0 else TOP + y
                base = (f * layers + 1) * PAD + row
                flat[pl.ds(base, half, stride=2 * PAD), :] = 0.25 * a + 0.75 * b
                flat[pl.ds(base + PAD, half, stride=2 * PAD), :] = 0.75 * b + 0.25 * d
    evens, odds = [], []
    for f in range(q):
        at = s.rows_e + f * s.rows_z
        a = slab[at : at + s.sy, :]
        b = slab[at + 1 : at + 1 + s.sy, :]
        d = slab[at + 2 : at + 2 + s.sy, :]
        zface[pl.ds(f * y, s.sy, stride=2), :] = 0.25 * a + 0.75 * b
        zface[pl.ds(f * y + 1, s.sy, stride=2), :] = 0.75 * b + 0.25 * d
        a = zface[f * y : f * y + y, :]
        b = pltpu.roll(a, z - 2, 1)
        d = pltpu.roll(a, z - 4, 1)
        evens.append(0.25 * a + 0.75 * b)
        odds.append(0.75 * b + 0.25 * d)
    for move in moves:
        move.wait()
    lane = lanes_of((y, z))
    is_first, is_last = lane == 0, lane == z - 1
    for k in range(3):
        src, fraction = states[k], section_weights[k]
        flat = src.reshape(q * layers * PAD, z)
        begin, end = (0, half) if k < 2 else (1, half - 1)
        shift = -(2 * s.ex * k + 2 * begin) % z
        carried = tuple(pltpu.roll(g, shift, 1) if shift else g for g in evens + odds)

        def pair_of_layers(t, ghosts, k=k, src=src, flat=flat, fraction=fraction):
            for odd in range(2):
                b = 2 * t + odd
                co = coefficients([wide_wind[d, b] for d in range(3)])
                for f in range(q):
                    center = src[f, b + 1, rows, :]
                    ghost = ghosts[odd * q + f]
                    row = (f * layers + b + 1) * PAD + TOP
                    rate = rate_of(
                        co,
                        center,
                        src[f, b, rows, :],
                        src[f, b + 2, rows, :],
                        flat[pl.ds(row - 1, y), :],
                        flat[pl.ds(row + 1, y), :],
                        pltpu.roll(jnp.where(is_last, ghost, center), 1, 1),
                        pltpu.roll(jnp.where(is_first, ghost, center), z - 1, 1),
                    )
                    value = (center if k == 0 else s0[f, b + 1, rows, :]) + fraction * rate
                    if k < 2:
                        states[k + 1][f, b + 1, rows, :] = value
                    else:
                        out[f, b - 2] = value
            return tuple(pltpu.roll(g, z - 2, 1) for g in ghosts)

        unrolled(begin, end, 2, pair_of_layers, carried)
    rz = lax.broadcasted_iota(jnp.int32, (z, z), 0)
    cz = lax.broadcasted_iota(jnp.int32, (z, z), 1)
    flat = out.reshape(q * fx * y, z)
    pairs_z = [jnp.where(cz == rz // 2 + odd * s.sz, 0.125, 0.0).astype(BF16) for odd in range(2)]
    for f in range(q):
        sums = []
        for odd in range(2):
            parts = []
            for p in range(s.x // 2):
                base = (f * fx + 4 * p + 2 * odd) * y
                part = None
                for more in (0, 1, y, y + 1):
                    piece = flat[pl.ds(base + more, y // 2, stride=2), :]
                    part = piece if part is None else part + piece
                parts.append(part)
            sums.append(times(jnp.concatenate(parts, axis=0), pairs_z[odd]))
        avg[f] = (sums[0] + sums[1]).reshape(s.x // 2, y // 2, z)


def merge_kernel(s, c3, avg, out):
    lane = lanes_of((s.sy, s.z))
    inside = (lane >= s.lz) & (lane < s.lz + s.sz)
    for f in range(s.q):
        for p in range(s.x // 2):
            both = avg[f, p]
            for odd in range(2):
                at = 2 * p + odd
                moved = pltpu.roll(both, s.lz if odd == 0 else s.z - s.lz, 1)
                out[f, at] = c3[f, at]
                out[f, at, s.ly : s.ly + s.sy, :] = jnp.where(inside, moved, c3[f, at, s.ly : s.ly + s.sy, :])


VMEM = pl.BlockSpec(memory_space=pltpu.VMEM)
SMEM = pl.BlockSpec(memory_space=pltpu.SMEM)
HBM = pl.BlockSpec(memory_space=pltpu.HBM)
ANY = pl.BlockSpec(memory_space=pl.ANY)


SHORT = pl.CostEstimate(flops=1, bytes_accessed=1, transcendentals=0)


def params(megabytes):
    return pltpu.CompilerParams(vmem_limit_bytes=megabytes << 20)


def shape(*dims):
    return jax.ShapeDtypeStruct(dims, F32)


def ring(array, axis, by):
    size = lax.axis_size(axis)
    return lax.ppermute(array, axis, [(i, (i + by) % size) for i in range(size)])


def move_by(array, amount, beside=None):
    size = lax.axis_size("gx")
    work, operands = beside or (lambda: (), ())
    if size <= 8:

        def branch(by, array, *operands):
            return array if by == 0 else ring(array, "gx", by), work(*operands)

        return lax.switch(amount, [functools.partial(branch, by) for by in range(size)], array, *operands)
    for bit in range((size - 1).bit_length()):
        array = jnp.where((amount >> bit) % 2 == 1, ring(array, "gx", 1 << bit), array)
    return array, work(*operands)


def z_columns(zown):
    size = lax.axis_size("gz")
    if size == 1:
        return zown
    if size == 2:
        return lax.ppermute(zown, "gz", [(0, 1), (1, 0)])
    below = lax.broadcasted_iota(jnp.int32, zown.shape, 2) % 6 < 3
    return jnp.where(below, ring(zown, "gz", 1), ring(zown, "gz", -1))


def shards(coarse_fields, coarse_wind, fine_fields, fine_wind, fine_owner):
    s = Sizes(coarse_fields.shape, fine_fields.shape)
    q, x, y, z, fx = s.q, s.x, s.y, s.z, s.fx
    size = lax.axis_size("gx")
    offset = (fine_owner[0, 0, 0] - lax.axis_index("gx")) % size
    level = lax.axis_index("gz")
    neighbours = jnp.stack([level > 0, level < lax.axis_size("gz") - 1]).astype(jnp.int32).reshape(1, 2)
    cup, cdown, fup, fdown = pl.pallas_call(
        functools.partial(pack_kernel, s),
        out_shape=(shape(s.halo, y, z),) * 2 + (shape(s.halo + 2, y, z),) * 2,
        in_specs=[HBM] * 4,
        out_specs=(VMEM,) * 4,
        scratch_shapes=[pltpu.SemaphoreType.DMA((4 * (q + 3),))],
        cost_estimate=SHORT,
        name="pack",
    )(coarse_fields, coarse_wind, fine_fields, fine_wind)
    lo, hi = ring(cup, "gx", 1), ring(cdown, "gx", -1)
    flo, fhi = ring(fup, "gx", 1), ring(fdown, "gx", -1)
    yup, ydn = pl.pallas_call(
        functools.partial(ypack_kernel, s),
        out_shape=(shape(s.rows_f + s.rows_w, z),) * 2,
        in_specs=[VMEM] * 4,
        out_specs=(VMEM,) * 2,
        cost_estimate=SHORT,
        name="ypack",
    )(coarse_fields, coarse_wind, lo, hi)
    yrows = [ring(yup, "gy", 1), ring(ydn, "gy", -1)]
    slab = pl.pallas_call(
        functools.partial(slab_kernel, s),
        out_shape=shape(s.slab, z),
        in_specs=[VMEM] * 4,
        out_specs=VMEM,
        scratch_shapes=[pltpu.VMEM((q, s.ep, PAD, z), F32)] * 3 + [pltpu.VMEM((3, s.ex, y, z), F32)],
        compiler_params=params(24),
        cost_estimate=SHORT,
        name="slab",
    )(coarse_fields, coarse_wind, lo, hi)
    yrows, slab, flo, fhi = lax.optimization_barrier((yrows, slab, flo, fhi))
    padded = pltpu.VMEM((q, s.ep, WPAD, z), F32)
    wind_rows = pltpu.VMEM((3, s.ex, 24, z), F32)
    zown = pl.pallas_call(
        functools.partial(zpack_kernel, s),
        out_shape=shape(q + 3, 24, z),
        in_specs=[VMEM] * 6,
        out_specs=VMEM,
        scratch_shapes=[padded, wind_rows],
        compiler_params=params(24),
        cost_estimate=SHORT,
        name="zpack",
    )(coarse_fields, coarse_wind, lo, hi, *yrows)
    zin = z_columns(zown)
    slab, _ = move_by(slab, (size - offset) % size)
    def coarse(*operands):
        return pl.pallas_call(
            functools.partial(coarse_kernel, s),
            out_shape=shape(q, x, y, z),
            in_specs=[SMEM] + [VMEM] * 8,
            out_specs=VMEM,
            scratch_shapes=[padded] * 3 + [wind_rows, pltpu.VMEM((3, q, 24, z), F32), pltpu.VMEM((2, q, 24, z), F32)],
            compiler_params=params(24),
            cost_estimate=pl.CostEstimate(flops=40_000_000, bytes_accessed=4_000_000, transcendentals=0),
            name="coarse",
        )(*operands)

    layers = fx + 6
    fine_next, averaged = pl.pallas_call(
        functools.partial(fine_kernel, s),
        out_shape=(shape(q, fx, y, z), shape(q, x // 2, y // 2, z)),
        in_specs=[ANY, ANY, ANY, ANY, VMEM],
        out_specs=(VMEM, VMEM),
        scratch_shapes=[
            pltpu.VMEM((q, layers, PAD, z), F32),
            pltpu.VMEM((q, layers, PAD, z), F32),
            pltpu.VMEM((q, layers, PAD, z), F32),
            pltpu.VMEM((3, s.fe, y, z), F32),
            pltpu.VMEM((6 * q, s.ep, z), F32),
            pltpu.VMEM((q * y, z), F32),
            pltpu.SemaphoreType.DMA((2 + 2 * (q + 3),)),
        ],
        compiler_params=params(32),
        name="fine",
    )(fine_fields, fine_wind, flo, fhi, slab)
    averaged, state = move_by(
        averaged,
        offset,
        (coarse, (neighbours, coarse_fields, coarse_wind, lo, hi, *yrows, zown, zin)),
    )
    coarse_next = pl.pallas_call(
        functools.partial(merge_kernel, s),
        out_shape=shape(q, x, y, z),
        in_specs=[VMEM, VMEM],
        out_specs=VMEM,
        compiler_params=params(16),
        name="merge",
    )(state, averaged)
    return coarse_next, fine_next


def solution(mesh):
    spec = P(None, "gx", "gy", "gz")
    return jax.shard_map(
        shards,
        mesh=mesh,
        in_specs=(spec, spec, spec, spec, P("gx", "gy", "gz")),
        out_specs=(spec, spec),
        check_vma=False,
    )
```

```python
import functools

import jax
import jax.numpy as jnp
from jax import lax
from jax.experimental import pallas as pl
from jax.experimental.pallas import tpu as pltpu
from jax.sharding import PartitionSpec as P

diffusion = 0.05
section_weights = (1.0 / 3.0, 0.5, 1.0)
F32 = jnp.float32
BF16 = jnp.bfloat16
PAD = 32
TOP = 8


class Sizes:
    def __init__(self, coarse_shape, fine_shape):
        self.q, self.x, self.y, self.z = coarse_shape
        self.fx = fine_shape[1]
        self.ly, self.sy = self.y // 4, self.y // 2
        self.lz, self.sz = self.z // 4, self.z // 2
        self.ex = self.x + 4
        self.ep = -(-self.ex // 8) * 8
        self.fe = self.fx + 4
        self.halo = 3 * self.q + 6
        self.rows_f, self.rows_w = self.q * (3 * self.x + 6), 3 * (2 * self.x + 2)
        self.rows_y = 3 * self.q * self.ex
        self.rows_e = self.rows_y + self.ep
        self.rows_z = self.sy + 2
        self.slab = self.rows_e + self.q * self.rows_z
        assert self.q == 4 and self.y == 16 and self.z == 128 and self.ex <= 20 and self.fx == 2 * self.x


def lanes_of(shape):
    return lax.broadcasted_iota(jnp.int32, shape, len(shape) - 1)


def halves(value):
    high = value.astype(BF16)
    return high, (value - high.astype(F32)).astype(BF16)


def times(value, matrix):
    high, low = halves(value)
    return jnp.dot(high, matrix, preferred_element_type=F32) + jnp.dot(low, matrix, preferred_element_type=F32)


def coefficients(wind):
    out = []
    for w in wind:
        out += [diffusion - 0.5 * w, diffusion + 0.5 * w]
    return out


def rate_of(co, center, x_low, x_high, y_low, y_high, z_low, z_high):
    along = (co[0] * x_high + co[1] * x_low) + (co[2] * y_high + co[3] * y_low) + (co[4] * z_high + co[5] * z_low)
    return along - (6.0 * diffusion) * center


def layer_of(s, own, low, high, member, at, width, first):
    size = own.shape[1]
    if at < 0:
        return low[first + width * member + at + width]
    if at >= size:
        return high[first + width * member + at - size]
    return own[member, at]


def unrolled(begin, end, at_once, body, carry=()):
    while (end - begin) % at_once:
        at_once -= 1

    def several(i, carry):
        for more in range(at_once):
            carry = body(begin + i * at_once + more, carry)
        return carry

    return lax.fori_loop(0, (end - begin) // at_once, several, carry)


def pack_kernel(s, c0, cw, f0, fw, cup, cdown, fup, fdown, sems):
    moves = []
    for fields, wind, up, down in ((c0, cw, cup, cdown), (f0, fw, fup, fdown)):
        size = fields.shape[1]
        for own, members, width, first in ((fields, s.q, 3, 0), (wind, 3, 2, 3 * s.q)):
            for dst, at in ((up, size - width), (down, 0)):
                place = dst.at[first : first + members * width].reshape(members, width, s.y, s.z)
                moves.append((own.at[:, at : at + width], place))
    moves = [pltpu.make_async_copy(src, dst, sems.at[i]) for i, (src, dst) in enumerate(moves)]
    for move in moves:
        move.start()
    for move in moves:
        move.wait()


def y_rows(s, members, width):
    below, above = [], []
    for out, extra in ((below, lambda r: r), (above, lambda r: width - 1 - r)):
        at = 0
        for m in range(members):
            for r in range(width):
                out.append((m, r, extra(r), at))
                at += s.x + 2 * extra(r)
    return below, above


def ypack_kernel(s, c0, cw, lo, hi, up, dn):
    x, y, z = s.x, s.y, s.z
    flat_lo = lo.reshape(s.halo * y, z)
    flat_hi = hi.reshape(s.halo * y, z)
    for own, members, width, first, place in ((c0, s.q, 3, 0, 0), (cw, 3, 2, 3 * s.q, s.rows_f)):
        flat = own.reshape(members * x * y, z)
        for dst, rows, start in zip((up, dn), y_rows(s, members, width), (y - width, 0)):
            for m, r, e, at in rows:
                row, at = start + r, at + place
                if e:
                    dst[at : at + e, :] = flat_lo[pl.ds((first + width * (m + 1) - e) * y + row, e, stride=y), :]
                    dst[at + e + x : at + x + 2 * e, :] = flat_hi[pl.ds((first + width * m) * y + row, e, stride=y), :]
                dst[at + e : at + e + x, :] = flat[pl.ds(m * x * y + row, x, stride=y), :]


def slab_kernel(s, c0, cw, lo, hi, slab, pad0, pad1, pad2, wind):
    q, x, y, z = s.q, s.x, s.y, s.z
    own = slice(TOP, TOP + y)
    zeros = jnp.zeros((s.ep, z), F32)
    pads = (pad0, pad1, pad2)
    flats = [pad.reshape(q * s.ep * PAD, z) for pad in pads]
    for f in range(q):
        for pad in (flats[0], flats[1]):
            pad[pl.ds(f * s.ep * PAD + TOP - 1, s.ep, stride=PAD), :] = zeros
            pad[pl.ds(f * s.ep * PAD + TOP + y, s.ep, stride=PAD), :] = zeros
        for at in range(-3, x + 3):
            pad0[f, at + 3, own, :] = layer_of(s, c0, lo, hi, f, at, 3, 0)
        pad2[f, 1, own, :] = zeros[:y]
        pad2[f, s.ex, own, :] = zeros[:y]
    for d in range(3):
        for at in range(-2, x + 2):
            wind[d, at + 2] = layer_of(s, cw, lo, hi, d, at, 2, 3 * q)
    for step in range(2):
        src, flat, dst = pads[step], flats[step], pads[step + 1]

        def layer(j, carry, step=step, src=src, flat=flat, dst=dst):
            co = coefficients([wind[d, j - 1] for d in range(3)])
            for f in range(q):
                center = src[f, j, own, :]
                row = (f * s.ep + j) * PAD + TOP
                rate = rate_of(
                    co,
                    center,
                    src[f, j - 1, own, :],
                    src[f, j + 1, own, :],
                    flat[pl.ds(row - 1, y), :],
                    flat[pl.ds(row + 1, y), :],
                    pltpu.roll(center, 1, 1),
                    pltpu.roll(center, z - 1, 1),
                )
                base = center if step == 0 else pad0[f, j, own, :]
                dst[f, j, own, :] = base + section_weights[step] * rate
            return carry

        unrolled(step + 1, s.ex + 1 - step, 5 if step == 0 else 6, layer)
    lane_x = lanes_of((s.ex, z))
    lane_y = lanes_of((y, z))
    ends = None
    columns = (lane_y == s.lz - 1) | (lane_y == s.lz) | (lane_y == s.lz + s.sz - 1) | (lane_y == s.lz + s.sz)
    low_at = (lane_y % 2 == 0) & (lane_y < z // 2)
    high_at = (lane_y % 2 == 0) & (lane_y >= z // 2)
    for f in range(q):
        zfaces = None
        for k in range(3):
            start = (f * s.ep + 1) * PAD + TOP
            rows = [
                flats[k][pl.ds(start + at, s.ex, stride=PAD), :] for at in (s.ly - 1, s.ly, s.ly + s.sy - 1, s.ly + s.sy)
            ]
            sides = (0.75 * rows[0] + 0.25 * rows[1], 0.25 * rows[2] + 0.75 * rows[3])
            first = (k * q + f) * s.ex
            slab[first : first + s.ex, :] = jnp.where(
                lane_x < s.sz, pltpu.roll(sides[0], z - s.lz, 1), pltpu.roll(sides[1], s.lz, 1)
            )
            for side in range(2):
                e = 4 * (q * k + f) + 2 * side + 1
                before = jnp.where(lane_x == s.lz - 1, sides[side], 0.0)
                after = jnp.where(lane_x == s.lz + s.sz, sides[side], 0.0)
                part = pltpu.roll(before, (e - s.lz + 1) % z, 1) + pltpu.roll(after, (e - 1 - s.lz - s.sz) % z, 1)
                ends = part if ends is None else ends + part
            raw = None
            for a in range(0 if k == 0 else 1, s.ex if k == 0 else s.ex - 1):
                part = jnp.where(columns, pads[k][f, a + 1, own, :], 0.0)
                part = pltpu.roll(part, (2 * a - s.lz + 1) % z, 1)
                raw = part if raw is None else raw + part
            beside = pltpu.roll(raw, z - 1, 1)
            low = jnp.where(low_at, 0.75 * raw + 0.25 * beside, 0.0)
            high = jnp.where(high_at, 0.25 * raw + 0.75 * beside, 0.0)
            part = pltpu.roll(low, (2 * s.ex * k - 1) % z, 1) + pltpu.roll(high, (2 * s.ex * k - z // 2) % z, 1)
            zfaces = part if zfaces is None else zfaces + part
        at = s.rows_e + f * s.rows_z
        slab[at : at + s.rows_z, :] = zfaces[s.ly - 1 : s.ly + s.sy + 1]
    slab[s.rows_y : s.rows_y + s.ex, :] = ends
    slab[s.rows_y + s.ex : s.rows_e, :] = zeros[: s.ep - s.ex]


WTOP, WPAD = 12, 40
BLOCK = slice(8, 32)


def assemble(s, c0, cw, lo, hi, below, above, pad, wind):
    q, x, y, z = s.q, s.x, s.y, s.z
    flat = pad.reshape(q * s.ep * WPAD, z)
    flat_wind = wind.reshape(3 * s.ex * 24, z)
    for f in range(q):
        for at in range(-3, x + 3):
            pad[f, at + 3, WTOP : WTOP + y, :] = layer_of(s, c0, lo, hi, f, at, 3, 0)
    for d in range(3):
        for at in range(-2, x + 2):
            wind[d, at + 2, 4 : 4 + y, :] = layer_of(s, cw, lo, hi, d, at, 2, 3 * q)
    for src, rows, start in zip((below, above), y_rows(s, q, 3), (WTOP - 3, WTOP + y)):
        for m, r, e, at in rows:
            count = x + 2 * e
            flat[pl.ds((m * s.ep + 3 - e) * WPAD + start + r, count, stride=WPAD), :] = src[at : at + count, :]
    for src, rows, start in zip((below, above), y_rows(s, 3, 2), (2, 4 + y)):
        for m, r, e, at in rows:
            count, at = x + 2 * e, at + s.rows_f
            flat_wind[pl.ds((m * s.ex + 2 - e) * 24 + start + r, count, stride=24), :] = src[at : at + count, :]


def edge_lanes(s, lane, width):
    return (lane < width) | (lane >= s.z - width)


def zpack_kernel(s, c0, cw, lo, hi, below, above, out, pad, wind):
    assemble(s, c0, cw, lo, hi, below, above, pad, wind)
    lane = lanes_of((24, s.z))
    keep = edge_lanes(s, lane, 3)
    for m in range(s.q + 3):
        total = None
        for a in range(s.ex):
            tile = pad[m, a + 1, BLOCK, :] if m < s.q else wind[m - s.q, a]
            part = pltpu.roll(jnp.where(keep, tile, 0.0), (6 * a + 3) % s.z, 1)
            total = part if total is None else total + part
        out[m] = total


def coarse_kernel(
    s, sides, c0, cw, lo, hi, below, above, zown, zin, out, pad0, pad1, pad2, wind, beyond, nearest
):
    q, x, y, z = s.q, s.x, s.y, s.z
    assemble(s, c0, cw, lo, hi, below, above, pad0, wind)
    pads = (pad0, pad1, pad2)
    lane = lanes_of((24, z))
    group = lane % 6
    from_low = group == 2
    from_high = group == 3
    exists = jnp.where(group < 3, sides[0, 0], sides[0, 1]).astype(F32)
    co_z = coefficients([zin[q + d] for d in range(3)])
    for f in range(q):
        beyond[0, f] = zin[f] * exists
        nearest[0, f] = zown[f]
    for step in range(3):
        src, fraction = pads[step], section_weights[step]
        flat = src.reshape(q * s.ep * WPAD, z)
        flat0 = pad0.reshape(q * s.ep * WPAD, z)
        flat_wind = wind.reshape(3 * s.ex * 24, z)
        flat_beyond = beyond.reshape(3 * q * 24, z)
        skip, height = (0, 24) if step < 2 else (4, y)
        here = lanes_of((height, z))
        is_first, is_last = here == 0, here == z - 1

        def layer(a, packed, step=step, flat=flat, fraction=fraction, skip=skip, height=height):
            made = []
            co = coefficients([flat_wind[pl.ds((d * s.ex + a) * 24 + skip, height), :] for d in range(3)])
            for f in range(q):
                row = (f * s.ep + a + 1) * WPAD + 8 + skip
                center = flat[pl.ds(row, height), :]
                ghost = pltpu.roll(flat_beyond[pl.ds((step * q + f) * 24 + skip, height), :], 2 * z - 6 * a - 3, 1)
                rate = rate_of(
                    co,
                    center,
                    flat[pl.ds(row - WPAD, height), :],
                    flat[pl.ds(row + WPAD, height), :],
                    flat[pl.ds(row - 1, height), :],
                    flat[pl.ds(row + 1, height), :],
                    pltpu.roll(jnp.where(is_last, ghost, center), 1, 1),
                    pltpu.roll(jnp.where(is_first, ghost, center), z - 1, 1),
                )
                base = center if step == 0 else flat0[pl.ds(row, height), :]
                value = base + fraction * rate
                if step == 2:
                    out[f, a - 2] = value
                else:
                    pads[step + 1][f, a + 1, BLOCK, :] = value
                if step == 0:
                    made.append(packed[f] + pltpu.roll(jnp.where(is_first | is_last, value, 0.0), 6 * a + 3, 1))
            return tuple(made)

        begin, end = step, s.ex - step
        start = tuple(jnp.zeros((24, z), F32) for _ in range(q)) if step == 0 else ()
        packed = unrolled(begin, end, 4 + 2 * (step == 1), layer, start)
        if step == 2:
            break
        for f in range(q):
            if step == 0:
                nearest[1, f] = packed[f]
            ghost, near = beyond[step, f], nearest[step, f]
            rate = rate_of(
                co_z,
                ghost,
                pltpu.roll(ghost, 6, 1),
                pltpu.roll(ghost, z - 6, 1),
                pltpu.roll(ghost, 1, 0),
                pltpu.roll(ghost, 23, 0),
                pltpu.roll(jnp.where(from_low, near, ghost), 1, 1),
                pltpu.roll(jnp.where(from_high, near, ghost), z - 1, 1),
            )
            beyond[step + 1, f] = (beyond[0, f] + fraction * rate) * exists


def fine_kernel(s, f0, fw, flo, fhi, slab, out, avg, *scratch):
    s1, s2, faces, ghost_rows, zface, sems = scratch
    states = (None, s1, s2, s1)
    q, y, z, fx, fe = s.q, s.y, s.z, s.fx, s.fe
    layers = fx + 6
    rows = slice(TOP, TOP + y)
    r = lax.broadcasted_iota(jnp.int32, (z, 2 * z), 0)
    c = lax.broadcasted_iota(jnp.int32, (z, 2 * z), 1)
    near = c // 2
    far = near + 2 * (c % 2) - 1
    same = (far // s.sz == near // s.sz) & (far >= 0)
    to_fine = jnp.where(r == near, 0.75, jnp.where((r == far) & same, 0.25, 0.0)).astype(BF16)
    wide = times(slab[: s.rows_y, :], to_fine)
    ends = slab[s.rows_y : s.rows_y + s.ex, :]
    lane_x = lanes_of((s.ex, z))
    edge = (lane_x == 0) | (lane_x == z - 1)
    half = fe // 2
    for k in range(3):
        for f in range(q):
            for side in range(2):
                e = 4 * (q * k + f) + 2 * side + 1
                corner = jnp.where(edge, 0.25 * pltpu.roll(ends, z - e, 1), 0.0)
                first = (k * q + f) * s.ex
                here = faces.at[(k * q + f) * 2 + side]
                here[: s.ex, :] = wide[first : first + s.ex, side * z : side * z + z] + corner
                a = here[0:half, :]
                b = here[1 : half + 1, :]
                d = here[2 : half + 2, :]
                if k == 0:
                    flat, base, stride = ghost_rows, (2 * f + side) * fe, 1
                else:
                    flat, stride = states[k].reshape(q * layers * PAD, z), PAD
                    base = (f * layers + 1) * PAD + (TOP - 1 if side == 0 else TOP + y)
                flat[pl.ds(base, half, stride=2 * stride), :] = 0.25 * a + 0.75 * b
                flat[pl.ds(base + stride, half, stride=2 * stride), :] = 0.75 * b + 0.25 * d
    evens, odds = [], []
    for f in range(q):
        at = s.rows_e + f * s.rows_z
        a = slab[at : at + s.sy, :]
        b = slab[at + 1 : at + 1 + s.sy, :]
        d = slab[at + 2 : at + 2 + s.sy, :]
        zface[pl.ds(f * y, s.sy, stride=2), :] = 0.25 * a + 0.75 * b
        zface[pl.ds(f * y + 1, s.sy, stride=2), :] = 0.75 * b + 0.25 * d
        a = zface[f * y : f * y + y, :]
        b = pltpu.roll(a, z - 2, 1)
        d = pltpu.roll(a, z - 4, 1)
        evens.append(0.25 * a + 0.75 * b)
        odds.append(0.75 * b + 0.25 * d)
    lane = lanes_of((y, z))
    is_first, is_last = lane == 0, lane == z - 1
    row_in = lax.broadcasted_iota(jnp.int32, (y, z), 0)
    is_low, is_high = row_in == 0, row_in == y - 1
    flat_f0 = f0.reshape(q * fx * y, z)

    def ghosts_at(k, t):
        shift = -(2 * s.ex * k + 2 * t) % z
        return tuple(pltpu.roll(g, shift, 1) if shift else g for g in evens + odds)

    def pair_of_layers(k, t, ghosts, inner):
        src = states[k]
        for odd in range(2):
            b = 2 * t + odd
            at = b - 2

            def field(f, at):
                return f0[f, at] if inner else layer_of(s, f0, flo, fhi, f, at, 3, 0)

            if inner:
                winds = [fw[d, at] for d in range(3)]
            else:
                winds = [layer_of(s, fw, flo, fhi, d, at, 2, 3 * q) for d in range(3)]
            co = coefficients(winds)
            for f in range(q):
                if k == 0:
                    center, x_low, x_high = field(f, at), field(f, at - 1), field(f, at + 1)
                    if inner:
                        row = (f * fx + at) * y
                        y_low, y_high = flat_f0[pl.ds(row - 1, y), :], flat_f0[pl.ds(row + 1, y), :]
                    else:
                        y_low, y_high = pltpu.roll(center, 1, 0), pltpu.roll(center, y - 1, 0)
                    y_low = jnp.where(is_low, ghost_rows[pl.ds(2 * f * fe + b, 1), :], y_low)
                    y_high = jnp.where(is_high, ghost_rows[pl.ds((2 * f + 1) * fe + b, 1), :], y_high)
                    base = center
                else:
                    flat = src.reshape(q * layers * PAD, z)
                    row = (f * layers + b + 1) * PAD + TOP
                    center, x_low, x_high = src[f, b + 1, rows, :], src[f, b, rows, :], src[f, b + 2, rows, :]
                    y_low, y_high = flat[pl.ds(row - 1, y), :], flat[pl.ds(row + 1, y), :]
                    base = field(f, at)
                ghost = ghosts[odd * q + f]
                rate = rate_of(
                    co,
                    center,
                    x_low,
                    x_high,
                    y_low,
                    y_high,
                    pltpu.roll(jnp.where(is_last, ghost, center), 1, 1),
                    pltpu.roll(jnp.where(is_first, ghost, center), z - 1, 1),
                )
                states[k + 1][f, b + 1, rows, :] = base + section_weights[k] * rate
        return tuple(pltpu.roll(g, z - 2, 1) for g in ghosts)

    moves = []
    for k in range(3):
        if k < 2:
            outer = 2 - k
            for t in list(range(outer)) + list(range(half - outer, half)):
                pair_of_layers(k, t, ghosts_at(k, t), False)
            unrolled(outer, half - outer, 2, lambda t, g, k=k: pair_of_layers(k, t, g, True), ghosts_at(k, outer))
            continue
        carried = ghosts_at(k, 1)
        part = (half - 2) // 4
        for i in range(4):
            carried = unrolled(
                1 + i * part, 1 + (i + 1) * part, 2, lambda t, g, k=k: pair_of_layers(k, t, g, True), carried
            )
            begin, end = 2 * part * i, 2 * part * (i + 1)
            moves.append(pltpu.make_async_copy(s1.at[:, 3 + begin : 3 + end, rows], out.at[:, begin:end], sems.at[i]))
            moves[-1].start()
    rz = lax.broadcasted_iota(jnp.int32, (z, z), 0)
    cz = lax.broadcasted_iota(jnp.int32, (z, z), 1)
    flat = s1.reshape(q * layers * PAD, z)
    pairs_z = [jnp.where(cz == rz // 2 + odd * s.sz, 0.125, 0.0).astype(BF16) for odd in range(2)]
    for f in range(q):
        sums = []
        for odd in range(2):
            parts = []
            for p in range(s.x // 2):
                base = (f * layers + 3 + 4 * p + 2 * odd) * PAD + TOP
                part = None
                for more in (0, 1, PAD, PAD + 1):
                    piece = flat[pl.ds(base + more, y // 2, stride=2), :]
                    part = piece if part is None else part + piece
                parts.append(part)
            sums.append(times(jnp.concatenate(parts, axis=0), pairs_z[odd]))
        avg[f] = (sums[0] + sums[1]).reshape(s.x // 2, y // 2, z)
    for move in moves:
        move.wait()


def merge_kernel(s, c3, avg, out):
    lane = lanes_of((s.sy, s.z))
    inside = (lane >= s.lz) & (lane < s.lz + s.sz)
    for f in range(s.q):
        for p in range(s.x // 2):
            both = avg[f, p]
            for odd in range(2):
                at = 2 * p + odd
                moved = pltpu.roll(both, s.lz if odd == 0 else s.z - s.lz, 1)
                out[f, at] = c3[f, at]
                out[f, at, s.ly : s.ly + s.sy, :] = jnp.where(inside, moved, c3[f, at, s.ly : s.ly + s.sy, :])


VMEM = pl.BlockSpec(memory_space=pltpu.VMEM)
SMEM = pl.BlockSpec(memory_space=pltpu.SMEM)
HBM = pl.BlockSpec(memory_space=pltpu.HBM)
ANY = pl.BlockSpec(memory_space=pl.ANY)


SHORT = pl.CostEstimate(flops=1, bytes_accessed=1, transcendentals=0)


def params(megabytes):
    return pltpu.CompilerParams(vmem_limit_bytes=megabytes << 20)


def shape(*dims):
    return jax.ShapeDtypeStruct(dims, F32)


def ring(array, axis, by):
    size = lax.axis_size(axis)
    return lax.ppermute(array, axis, [(i, (i + by) % size) for i in range(size)])


def move_by(array, amount, beside=None):
    size = lax.axis_size("gx")
    work, operands = beside or (lambda: (), ())
    if size <= 8:

        def branch(by, array, *operands):
            return array if by == 0 else ring(array, "gx", by), work(*operands)

        return lax.switch(amount, [functools.partial(branch, by) for by in range(size)], array, *operands)
    for bit in range((size - 1).bit_length()):
        array = jnp.where((amount >> bit) % 2 == 1, ring(array, "gx", 1 << bit), array)
    return array, work(*operands)


def z_columns(zown):
    size = lax.axis_size("gz")
    if size == 1:
        return zown
    if size == 2:
        return lax.ppermute(zown, "gz", [(0, 1), (1, 0)])
    below = lax.broadcasted_iota(jnp.int32, zown.shape, 2) % 6 < 3
    return jnp.where(below, ring(zown, "gz", 1), ring(zown, "gz", -1))


def shards(coarse_fields, coarse_wind, fine_fields, fine_wind, fine_owner):
    s = Sizes(coarse_fields.shape, fine_fields.shape)
    q, x, y, z, fx = s.q, s.x, s.y, s.z, s.fx
    size = lax.axis_size("gx")
    offset = (fine_owner[0, 0, 0] - lax.axis_index("gx")) % size
    level = lax.axis_index("gz")
    neighbours = jnp.stack([level > 0, level < lax.axis_size("gz") - 1]).astype(jnp.int32).reshape(1, 2)
    cup, cdown, fup, fdown = pl.pallas_call(
        functools.partial(pack_kernel, s),
        out_shape=(shape(s.halo, y, z),) * 2 + (shape(s.halo + 2, y, z),) * 2,
        in_specs=[HBM] * 4,
        out_specs=(VMEM,) * 4,
        scratch_shapes=[pltpu.SemaphoreType.DMA((8,))],
        cost_estimate=SHORT,
        name="pack",
    )(coarse_fields, coarse_wind, fine_fields, fine_wind)
    lo, hi = ring(cup, "gx", 1), ring(cdown, "gx", -1)
    flo, fhi = ring(fup, "gx", 1), ring(fdown, "gx", -1)
    yup, ydn = pl.pallas_call(
        functools.partial(ypack_kernel, s),
        out_shape=(shape(s.rows_f + s.rows_w, z),) * 2,
        in_specs=[VMEM] * 4,
        out_specs=(VMEM,) * 2,
        cost_estimate=SHORT,
        name="ypack",
    )(coarse_fields, coarse_wind, lo, hi)
    yrows = [ring(yup, "gy", 1), ring(ydn, "gy", -1)]
    slab = pl.pallas_call(
        functools.partial(slab_kernel, s),
        out_shape=shape(s.slab, z),
        in_specs=[VMEM] * 4,
        out_specs=VMEM,
        scratch_shapes=[pltpu.VMEM((q, s.ep, PAD, z), F32)] * 3 + [pltpu.VMEM((3, s.ex, y, z), F32)],
        compiler_params=params(24),
        cost_estimate=SHORT,
        name="slab",
    )(coarse_fields, coarse_wind, lo, hi)
    yrows, slab, flo, fhi = lax.optimization_barrier((yrows, slab, flo, fhi))
    padded = pltpu.VMEM((q, s.ep, WPAD, z), F32)
    wind_rows = pltpu.VMEM((3, s.ex, 24, z), F32)
    def zpack(*operands):
        return pl.pallas_call(
            functools.partial(zpack_kernel, s),
            out_shape=shape(q + 3, 24, z),
            in_specs=[VMEM] * 6,
            out_specs=VMEM,
            scratch_shapes=[padded, wind_rows],
            compiler_params=params(24),
            cost_estimate=pl.CostEstimate(flops=4_000_000, bytes_accessed=2_000_000, transcendentals=0),
            name="zpack",
        )(*operands)

    slab, zown = move_by(slab, (size - offset) % size, (zpack, (coarse_fields, coarse_wind, lo, hi, *yrows)))
    zin = z_columns(zown)
    def coarse(*operands):
        return pl.pallas_call(
            functools.partial(coarse_kernel, s),
            out_shape=shape(q, x, y, z),
            in_specs=[SMEM] + [VMEM] * 8,
            out_specs=VMEM,
            scratch_shapes=[padded] * 3 + [wind_rows, pltpu.VMEM((3, q, 24, z), F32), pltpu.VMEM((2, q, 24, z), F32)],
            compiler_params=params(24),
            cost_estimate=pl.CostEstimate(flops=40_000_000, bytes_accessed=4_000_000, transcendentals=0),
            name="coarse",
        )(*operands)

    layers = fx + 6
    fine_next, averaged = pl.pallas_call(
        functools.partial(fine_kernel, s),
        out_shape=(shape(q, fx, y, z), shape(q, x // 2, y // 2, z)),
        in_specs=[VMEM] * 5,
        out_specs=(HBM, VMEM),
        scratch_shapes=[
            pltpu.VMEM((q, layers, PAD, z), F32),
            pltpu.VMEM((q, layers, PAD, z), F32),
            pltpu.VMEM((6 * q, s.ep, z), F32),
            pltpu.VMEM((2 * q * s.fe, z), F32),
            pltpu.VMEM((q * y, z), F32),
            pltpu.SemaphoreType.DMA((4,)),
        ],
        compiler_params=params(32),
        name="fine",
    )(fine_fields, fine_wind, flo, fhi, slab)
    averaged, state = move_by(
        averaged,
        offset,
        (coarse, (neighbours, coarse_fields, coarse_wind, lo, hi, *yrows, zown, zin)),
    )
    coarse_next = pl.pallas_call(
        functools.partial(merge_kernel, s),
        out_shape=shape(q, x, y, z),
        in_specs=[VMEM, VMEM],
        out_specs=VMEM,
        compiler_params=params(16),
        name="merge",
    )(state, averaged)
    return coarse_next, fine_next


def solution(mesh):
    spec = P(None, "gx", "gy", "gz")
    return jax.shard_map(
        shards,
        mesh=mesh,
        in_specs=(spec, spec, spec, spec, P("gx", "gy", "gz")),
        out_specs=(spec, spec),
        check_vma=False,
    )
```

```python
import functools

import jax
import jax.numpy as jnp
from jax import lax
from jax.experimental import pallas as pl
from jax.experimental.pallas import tpu as pltpu
from jax.sharding import PartitionSpec as P

diffusion = 0.05
section_weights = (1.0 / 3.0, 0.5, 1.0)
F32 = jnp.float32
BF16 = jnp.bfloat16
PAD = 32
TOP = 8


class Sizes:
    def __init__(self, coarse_shape, fine_shape):
        self.q, self.x, self.y, self.z = coarse_shape
        self.fx = fine_shape[1]
        self.ly, self.sy = self.y // 4, self.y // 2
        self.lz, self.sz = self.z // 4, self.z // 2
        self.ex = self.x + 4
        self.ep = -(-self.ex // 8) * 8
        self.fe = self.fx + 4
        self.halo = 3 * self.q + 6
        self.rows_f, self.rows_w = self.q * (3 * self.x + 6), 3 * (2 * self.x + 2)
        self.rows_y = 3 * self.q * self.ex
        self.rows_e = self.rows_y + self.ep
        self.rows_z = self.sy + 2
        self.slab = self.rows_e + self.q * self.rows_z
        assert self.q == 4 and self.y == 16 and self.z == 128 and self.ex <= 20 and self.fx == 2 * self.x


def lanes_of(shape):
    return lax.broadcasted_iota(jnp.int32, shape, len(shape) - 1)


def halves(value):
    high = value.astype(BF16)
    return high, (value - high.astype(F32)).astype(BF16)


def times(value, matrix):
    high, low = halves(value)
    return jnp.dot(high, matrix, preferred_element_type=F32) + jnp.dot(low, matrix, preferred_element_type=F32)


def coefficients(wind):
    out = []
    for w in wind:
        out += [diffusion - 0.5 * w, diffusion + 0.5 * w]
    return out


def rate_of(co, center, x_low, x_high, y_low, y_high, z_low, z_high):
    along = (co[0] * x_high + co[1] * x_low) + (co[2] * y_high + co[3] * y_low) + (co[4] * z_high + co[5] * z_low)
    return along - (6.0 * diffusion) * center


def layer_of(s, own, low, high, member, at, width, first):
    size = own.shape[1]
    if at < 0:
        return low[first + width * member + at + width]
    if at >= size:
        return high[first + width * member + at - size]
    return own[member, at]


def unrolled(begin, end, at_once, body, carry=None):
    while (end - begin) % at_once:
        at_once -= 1

    def several(i, carry):
        for more in range(at_once):
            carry = body(begin + i * at_once + more, carry)
        return carry

    return lax.fori_loop(0, (end - begin) // at_once, several, carry)


def pack_kernel(s, c0, cw, f0, fw, cup, cdown, fup, fdown, sems):
    moves = []
    for fields, wind, up, down in ((c0, cw, cup, cdown), (f0, fw, fup, fdown)):
        size = fields.shape[1]
        for own, members, width, first in ((fields, s.q, 3, 0), (wind, 3, 2, 3 * s.q)):
            for dst, at in ((up, size - width), (down, 0)):
                place = dst.at[first : first + members * width].reshape(members, width, s.y, s.z)
                moves.append((own.at[:, at : at + width], place))
    moves = [pltpu.make_async_copy(src, dst, sems.at[i]) for i, (src, dst) in enumerate(moves)]
    for move in moves:
        move.start()
    for move in moves:
        move.wait()


def y_rows(s, members, width):
    below, above = [], []
    for out, extra in ((below, lambda r: r), (above, lambda r: width - 1 - r)):
        at = 0
        for m in range(members):
            for r in range(width):
                out.append((m, r, extra(r), at))
                at += s.x + 2 * extra(r)
    return below, above


def ypack_kernel(s, c0, cw, lo, hi, up, dn):
    x, y, z = s.x, s.y, s.z
    flat_lo = lo.reshape(s.halo * y, z)
    flat_hi = hi.reshape(s.halo * y, z)
    for own, members, width, first, place in ((c0, s.q, 3, 0, 0), (cw, 3, 2, 3 * s.q, s.rows_f)):
        flat = own.reshape(members * x * y, z)
        for dst, rows, start in zip((up, dn), y_rows(s, members, width), (y - width, 0)):
            for m, r, e, at in rows:
                row, at = start + r, at + place
                if e:
                    dst[at : at + e, :] = flat_lo[pl.ds((first + width * (m + 1) - e) * y + row, e, stride=y), :]
                    dst[at + e + x : at + x + 2 * e, :] = flat_hi[pl.ds((first + width * m) * y + row, e, stride=y), :]
                dst[at + e : at + e + x, :] = flat[pl.ds(m * x * y + row, x, stride=y), :]


def slab_kernel(s, c0, cw, lo, hi, slab, pad0, pad1, pad2, wind):
    q, x, y, z = s.q, s.x, s.y, s.z
    own = slice(TOP, TOP + y)
    zeros = jnp.zeros((s.ep, z), F32)
    pads = (pad0, pad1, pad2)
    flats = [pad.reshape(q * s.ep * PAD, z) for pad in pads]
    for f in range(q):
        for pad in (flats[0], flats[1]):
            pad[pl.ds(f * s.ep * PAD + TOP - 1, s.ep, stride=PAD), :] = zeros
            pad[pl.ds(f * s.ep * PAD + TOP + y, s.ep, stride=PAD), :] = zeros
        for at in range(-3, x + 3):
            pad0[f, at + 3, own, :] = layer_of(s, c0, lo, hi, f, at, 3, 0)
        pad2[f, 1, own, :] = zeros[:y]
        pad2[f, s.ex, own, :] = zeros[:y]
    for d in range(3):
        for at in range(-2, x + 2):
            wind[d, at + 2] = layer_of(s, cw, lo, hi, d, at, 2, 3 * q)
    for step in range(2):
        src, dst = pads[step], pads[step + 1]

        def layer(j, carry, step=step, src=src, dst=dst):
            co = coefficients([wind[d, j - 1] for d in range(3)])
            for f in range(q):
                center = src[f, j, own, :]
                rate = rate_of(
                    co,
                    center,
                    src[f, j - 1, own, :],
                    src[f, j + 1, own, :],
                    pltpu.roll(center, 1, 0),
                    pltpu.roll(center, y - 1, 0),
                    pltpu.roll(center, 1, 1),
                    pltpu.roll(center, z - 1, 1),
                )
                base = center if step == 0 else pad0[f, j, own, :]
                dst[f, j, own, :] = base + section_weights[step] * rate
            return carry

        unrolled(step + 1, s.ex + 1 - step, 5 if step == 0 else 6, layer)
    lane_x = lanes_of((s.ex, z))
    lane_y = lanes_of((y, z))
    ends = None
    columns = (lane_y == s.lz - 1) | (lane_y == s.lz) | (lane_y == s.lz + s.sz - 1) | (lane_y == s.lz + s.sz)
    low_at = (lane_y % 2 == 0) & (lane_y < z // 2)
    high_at = (lane_y % 2 == 0) & (lane_y >= z // 2)
    for f in range(q):
        zfaces = None
        for k in range(3):
            start = (f * s.ep + 1) * PAD + TOP
            rows = [
                flats[k][pl.ds(start + at, s.ex, stride=PAD), :] for at in (s.ly - 1, s.ly, s.ly + s.sy - 1, s.ly + s.sy)
            ]
            sides = (0.75 * rows[0] + 0.25 * rows[1], 0.25 * rows[2] + 0.75 * rows[3])
            first = (k * q + f) * s.ex
            slab[first : first + s.ex, :] = jnp.where(
                lane_x < s.sz, pltpu.roll(sides[0], z - s.lz, 1), pltpu.roll(sides[1], s.lz, 1)
            )
            for side in range(2):
                e = 4 * (q * k + f) + 2 * side + 1
                before = jnp.where(lane_x == s.lz - 1, sides[side], 0.0)
                after = jnp.where(lane_x == s.lz + s.sz, sides[side], 0.0)
                part = pltpu.roll(before, (e - s.lz + 1) % z, 1) + pltpu.roll(after, (e - 1 - s.lz - s.sz) % z, 1)
                ends = part if ends is None else ends + part
            raw = None
            for a in range(0 if k == 0 else 1, s.ex if k == 0 else s.ex - 1):
                part = jnp.where(columns, pads[k][f, a + 1, own, :], 0.0)
                part = pltpu.roll(part, (2 * a - s.lz + 1) % z, 1)
                raw = part if raw is None else raw + part
            beside = pltpu.roll(raw, z - 1, 1)
            low = jnp.where(low_at, 0.75 * raw + 0.25 * beside, 0.0)
            high = jnp.where(high_at, 0.25 * raw + 0.75 * beside, 0.0)
            part = pltpu.roll(low, (2 * s.ex * k - 1) % z, 1) + pltpu.roll(high, (2 * s.ex * k - z // 2) % z, 1)
            zfaces = part if zfaces is None else zfaces + part
        at = s.rows_e + f * s.rows_z
        slab[at : at + s.rows_z, :] = zfaces[s.ly - 1 : s.ly + s.sy + 1]
    slab[s.rows_y : s.rows_y + s.ex, :] = ends
    slab[s.rows_y + s.ex : s.rows_e, :] = zeros[: s.ep - s.ex]


WTOP, WPAD = 12, 40
BLOCK = slice(8, 32)


def assemble(s, c0, cw, lo, hi, below, above, pad, wind):
    q, x, y, z = s.q, s.x, s.y, s.z
    flat = pad.reshape(q * s.ep * WPAD, z)
    flat_wind = wind.reshape(3 * s.ex * 24, z)
    for f in range(q):
        for at in range(-3, x + 3):
            pad[f, at + 3, WTOP : WTOP + y, :] = layer_of(s, c0, lo, hi, f, at, 3, 0)
    for d in range(3):
        for at in range(-2, x + 2):
            wind[d, at + 2, 4 : 4 + y, :] = layer_of(s, cw, lo, hi, d, at, 2, 3 * q)
    for src, rows, start in zip((below, above), y_rows(s, q, 3), (WTOP - 3, WTOP + y)):
        for m, r, e, at in rows:
            count = x + 2 * e
            flat[pl.ds((m * s.ep + 3 - e) * WPAD + start + r, count, stride=WPAD), :] = src[at : at + count, :]
    for src, rows, start in zip((below, above), y_rows(s, 3, 2), (2, 4 + y)):
        for m, r, e, at in rows:
            count, at = x + 2 * e, at + s.rows_f
            flat_wind[pl.ds((m * s.ex + 2 - e) * 24 + start + r, count, stride=24), :] = src[at : at + count, :]


def edge_lanes(s, lane, width):
    return (lane < width) | (lane >= s.z - width)


def zpack_kernel(s, c0, cw, lo, hi, below, above, out, pad, wind):
    assemble(s, c0, cw, lo, hi, below, above, pad, wind)
    lane = lanes_of((24, s.z))
    keep = edge_lanes(s, lane, 3)
    for m in range(s.q + 3):
        total = None
        for a in range(s.ex):
            tile = pad[m, a + 1, BLOCK, :] if m < s.q else wind[m - s.q, a]
            part = pltpu.roll(jnp.where(keep, tile, 0.0), (6 * a + 3) % s.z, 1)
            total = part if total is None else total + part
        out[m] = total


def coarse_kernel(
    s, sides, c0, cw, lo, hi, below, above, zown, zin, out, pad0, pad1, pad2, wind, beyond, nearest
):
    q, x, y, z = s.q, s.x, s.y, s.z
    assemble(s, c0, cw, lo, hi, below, above, pad0, wind)
    pads = (pad0, pad1, pad2)
    lane = lanes_of((24, z))
    group = lane % 6
    from_low = group == 2
    from_high = group == 3
    exists = jnp.where(group < 3, sides[0, 0], sides[0, 1]).astype(F32)
    co_z = coefficients([zin[q + d] for d in range(3)])
    for f in range(q):
        beyond[0, f] = zin[f] * exists
        nearest[0, f] = zown[f]
    for step in range(3):
        src, fraction = pads[step], section_weights[step]
        flat = src.reshape(q * s.ep * WPAD, z)
        flat_wind = wind.reshape(3 * s.ex * 24, z)
        flat_beyond = beyond.reshape(3 * q * 24, z)
        skip, height = (0, 24) if step < 2 else (4, y)
        here = lanes_of((height, z))
        is_first, is_last = here == 0, here == z - 1

        def layer(a, packed, step=step, src=src, flat=flat, fraction=fraction, skip=skip, height=height):
            made = []
            if step < 2:
                co = coefficients([wind[d, a] for d in range(3)])
            else:
                co = coefficients([flat_wind[pl.ds((d * s.ex + a) * 24 + skip, height), :] for d in range(3)])
            for f in range(q):
                row = (f * s.ep + a + 1) * WPAD + 8 + skip

                def at_layer(of, layer, row, f=f):
                    return of[f, layer, BLOCK, :] if step < 2 else of.reshape(flat.shape)[pl.ds(row, height), :]

                center = at_layer(src, a + 1, row)
                ghost = pltpu.roll(flat_beyond[pl.ds((step * q + f) * 24 + skip, height), :], 2 * z - 6 * a - 3, 1)
                rate = rate_of(
                    co,
                    center,
                    at_layer(src, a, row - WPAD),
                    at_layer(src, a + 2, row + WPAD),
                    flat[pl.ds(row - 1, height), :],
                    flat[pl.ds(row + 1, height), :],
                    pltpu.roll(jnp.where(is_last, ghost, center), 1, 1),
                    pltpu.roll(jnp.where(is_first, ghost, center), z - 1, 1),
                )
                base = center if step == 0 else at_layer(pad0, a + 1, row)
                value = base + fraction * rate
                if step == 2:
                    out[f, a - 2] = value
                else:
                    pads[step + 1][f, a + 1, BLOCK, :] = value
                if step == 0:
                    made.append(packed[f] + pltpu.roll(jnp.where(is_first | is_last, value, 0.0), 6 * a + 3, 1))
            return tuple(made)

        begin, end = step, s.ex - step
        start = tuple(jnp.zeros((24, z), F32) for _ in range(q)) if step == 0 else ()
        packed = unrolled(begin, end, 4 + 2 * (step == 1), layer, start)
        if step == 2:
            break
        for f in range(q):
            if step == 0:
                nearest[1, f] = packed[f]
            ghost, near = beyond[step, f], nearest[step, f]
            rate = rate_of(
                co_z,
                ghost,
                pltpu.roll(ghost, 6, 1),
                pltpu.roll(ghost, z - 6, 1),
                pltpu.roll(ghost, 1, 0),
                pltpu.roll(ghost, 23, 0),
                pltpu.roll(jnp.where(from_low, near, ghost), 1, 1),
                pltpu.roll(jnp.where(from_high, near, ghost), z - 1, 1),
            )
            beyond[step + 1, f] = (beyond[0, f] + fraction * rate) * exists


def fine_kernel(s, f0, fw, flo, fhi, slab, out, avg, *scratch):
    s1, s2, faces, ghost_rows, zface, sems = scratch
    states = (None, s1, s2, s1)
    q, y, z, fx, fe = s.q, s.y, s.z, s.fx, s.fe
    layers = fx + 6
    rows = slice(TOP, TOP + y)
    r = lax.broadcasted_iota(jnp.int32, (z, 2 * z), 0)
    c = lax.broadcasted_iota(jnp.int32, (z, 2 * z), 1)
    near = c // 2
    far = near + 2 * (c % 2) - 1
    same = (far // s.sz == near // s.sz) & (far >= 0)
    to_fine = jnp.where(r == near, 0.75, jnp.where((r == far) & same, 0.25, 0.0)).astype(BF16)
    wide = times(slab[: s.rows_y, :], to_fine)
    ends = slab[s.rows_y : s.rows_y + s.ex, :]
    lane_x = lanes_of((s.ex, z))
    edge = (lane_x == 0) | (lane_x == z - 1)
    half = fe // 2
    for k in range(3):
        for f in range(q):
            for side in range(2):
                e = 4 * (q * k + f) + 2 * side + 1
                corner = jnp.where(edge, 0.25 * pltpu.roll(ends, z - e, 1), 0.0)
                first = (k * q + f) * s.ex
                here = faces.at[(k * q + f) * 2 + side]
                here[: s.ex, :] = wide[first : first + s.ex, side * z : side * z + z] + corner
                a = here[0:half, :]
                b = here[1 : half + 1, :]
                d = here[2 : half + 2, :]
                if k == 0:
                    flat, base, stride = ghost_rows, (2 * f + side) * fe, 1
                else:
                    flat, stride = states[k].reshape(q * layers * PAD, z), PAD
                    base = (f * layers + 1) * PAD + (TOP - 1 if side == 0 else TOP + y)
                flat[pl.ds(base, half, stride=2 * stride), :] = 0.25 * a + 0.75 * b
                flat[pl.ds(base + stride, half, stride=2 * stride), :] = 0.75 * b + 0.25 * d
    for f in range(q):
        at = s.rows_e + f * s.rows_z
        a = slab[at : at + s.sy, :]
        b = slab[at + 1 : at + 1 + s.sy, :]
        d = slab[at + 2 : at + 2 + s.sy, :]
        zface[pl.ds(f * y, s.sy, stride=2), :] = 0.25 * a + 0.75 * b
        zface[pl.ds(f * y + 1, s.sy, stride=2), :] = 0.75 * b + 0.25 * d
        a = zface[f * y : f * y + y, :]
        b = pltpu.roll(a, z - 2, 1)
        d = pltpu.roll(a, z - 4, 1)
        zface[f * y : f * y + y, :] = 0.25 * a + 0.75 * b
        zface[(q + f) * y : (q + f + 1) * y, :] = 0.75 * b + 0.25 * d
    lane = lanes_of((y, z))
    is_first, is_last = lane == 0, lane == z - 1
    row_in = lax.broadcasted_iota(jnp.int32, (y, z), 0)
    is_low, is_high = row_in == 0, row_in == y - 1
    flat_f0 = f0.reshape(q * fx * y, z)

    def pair_of_layers(k, t, inner):
        src = states[k]
        for odd in range(2):
            b = 2 * t + odd
            at = b - 2

            def field(f, at):
                return f0[f, at] if inner else layer_of(s, f0, flo, fhi, f, at, 3, 0)

            if inner:
                winds = [fw[d, at] for d in range(3)]
            else:
                winds = [layer_of(s, fw, flo, fhi, d, at, 2, 3 * q) for d in range(3)]
            co = coefficients(winds)
            for f in range(q):
                if k == 0:
                    center, x_low, x_high = field(f, at), field(f, at - 1), field(f, at + 1)
                    if inner:
                        row = (f * fx + at) * y
                        y_low, y_high = flat_f0[pl.ds(row - 1, y), :], flat_f0[pl.ds(row + 1, y), :]
                    else:
                        y_low, y_high = pltpu.roll(center, 1, 0), pltpu.roll(center, y - 1, 0)
                    y_low = jnp.where(is_low, ghost_rows[pl.ds(2 * f * fe + b, 1), :], y_low)
                    y_high = jnp.where(is_high, ghost_rows[pl.ds((2 * f + 1) * fe + b, 1), :], y_high)
                    base = center
                else:
                    flat = src.reshape(q * layers * PAD, z)
                    row = (f * layers + b + 1) * PAD + TOP
                    center, x_low, x_high = src[f, b + 1, rows, :], src[f, b, rows, :], src[f, b + 2, rows, :]
                    y_low, y_high = flat[pl.ds(row - 1, y), :], flat[pl.ds(row + 1, y), :]
                    base = field(f, at)
                ghost = zface[(odd * q + f) * y : (odd * q + f + 1) * y, :]
                ghost = pltpu.roll(ghost, (2 * z - 2 * s.ex * k - 2 * t) if inner else -(2 * s.ex * k + 2 * t) % z, 1)
                rate = rate_of(
                    co,
                    center,
                    x_low,
                    x_high,
                    y_low,
                    y_high,
                    pltpu.roll(jnp.where(is_last, ghost, center), 1, 1),
                    pltpu.roll(jnp.where(is_first, ghost, center), z - 1, 1),
                )
                states[k + 1][f, b + 1, rows, :] = base + section_weights[k] * rate

    moves = []
    for k in range(3):
        if k < 2:
            outer = 2 - k
            for t in list(range(outer)) + list(range(half - outer, half)):
                pair_of_layers(k, t, False)
            unrolled(outer, half - outer, 2, lambda t, g, k=k: pair_of_layers(k, t, True))
            continue
        part = (half - 2) // 4
        for i in range(4):
            unrolled(1 + i * part, 1 + (i + 1) * part, 2, lambda t, g, k=k: pair_of_layers(k, t, True))
            begin, end = 2 * part * i, 2 * part * (i + 1)
            moves.append(pltpu.make_async_copy(s1.at[:, 3 + begin : 3 + end, rows], out.at[:, begin:end], sems.at[i]))
            moves[-1].start()
    rz = lax.broadcasted_iota(jnp.int32, (z, z), 0)
    cz = lax.broadcasted_iota(jnp.int32, (z, z), 1)
    flat = s1.reshape(q * layers * PAD, z)
    pairs_z = [jnp.where(cz == rz // 2 + odd * s.sz, 0.125, 0.0).astype(BF16) for odd in range(2)]
    for f in range(q):
        sums = []
        for odd in range(2):
            parts = []
            for p in range(s.x // 2):
                base = (f * layers + 3 + 4 * p + 2 * odd) * PAD + TOP
                part = None
                for more in (0, 1, PAD, PAD + 1):
                    piece = flat[pl.ds(base + more, y // 2, stride=2), :]
                    part = piece if part is None else part + piece
                parts.append(part)
            sums.append(times(jnp.concatenate(parts, axis=0), pairs_z[odd]))
        avg[f] = (sums[0] + sums[1]).reshape(s.x // 2, y // 2, z)
    for move in moves:
        move.wait()


def merge_kernel(s, c3, avg, out):
    lane = lanes_of((s.sy, s.z))
    inside = (lane >= s.lz) & (lane < s.lz + s.sz)
    for f in range(s.q):
        for p in range(s.x // 2):
            both = avg[f, p]
            for odd in range(2):
                at = 2 * p + odd
                moved = pltpu.roll(both, s.lz if odd == 0 else s.z - s.lz, 1)
                out[f, at] = c3[f, at]
                out[f, at, s.ly : s.ly + s.sy, :] = jnp.where(inside, moved, c3[f, at, s.ly : s.ly + s.sy, :])


VMEM = pl.BlockSpec(memory_space=pltpu.VMEM)
SMEM = pl.BlockSpec(memory_space=pltpu.SMEM)
HBM = pl.BlockSpec(memory_space=pltpu.HBM)
ANY = pl.BlockSpec(memory_space=pl.ANY)


SHORT = pl.CostEstimate(flops=1, bytes_accessed=1, transcendentals=0)


def params(megabytes):
    return pltpu.CompilerParams(vmem_limit_bytes=megabytes << 20)


def shape(*dims):
    return jax.ShapeDtypeStruct(dims, F32)


def ring(array, axis, by):
    size = lax.axis_size(axis)
    return lax.ppermute(array, axis, [(i, (i + by) % size) for i in range(size)])


def move_by(array, amount, beside=None):
    size = lax.axis_size("gx")
    work, operands = beside or (lambda: (), ())
    if size <= 8:

        def branch(by, array, *operands):
            return array if by == 0 else ring(array, "gx", by), work(*operands)

        return lax.switch(amount, [functools.partial(branch, by) for by in range(size)], array, *operands)
    for bit in range((size - 1).bit_length()):
        array = jnp.where((amount >> bit) % 2 == 1, ring(array, "gx", 1 << bit), array)
    return array, work(*operands)


def z_columns(zown):
    size = lax.axis_size("gz")
    if size == 1:
        return zown
    if size == 2:
        return lax.ppermute(zown, "gz", [(0, 1), (1, 0)])
    below = lax.broadcasted_iota(jnp.int32, zown.shape, 2) % 6 < 3
    return jnp.where(below, ring(zown, "gz", 1), ring(zown, "gz", -1))


def shards(coarse_fields, coarse_wind, fine_fields, fine_wind, fine_owner):
    s = Sizes(coarse_fields.shape, fine_fields.shape)
    q, x, y, z, fx = s.q, s.x, s.y, s.z, s.fx
    size = lax.axis_size("gx")
    offset = (fine_owner[0, 0, 0] - lax.axis_index("gx")) % size
    level = lax.axis_index("gz")
    neighbours = jnp.stack([level > 0, level < lax.axis_size("gz") - 1]).astype(jnp.int32).reshape(1, 2)
    cup, cdown, fup, fdown = pl.pallas_call(
        functools.partial(pack_kernel, s),
        out_shape=(shape(s.halo, y, z),) * 2 + (shape(s.halo + 2, y, z),) * 2,
        in_specs=[HBM] * 4,
        out_specs=(VMEM,) * 4,
        scratch_shapes=[pltpu.SemaphoreType.DMA((8,))],
        compiler_params=params(4),
        cost_estimate=SHORT,
        name="pack",
    )(coarse_fields, coarse_wind, fine_fields, fine_wind)
    lo, hi = ring(cup, "gx", 1), ring(cdown, "gx", -1)
    flo, fhi = ring(fup, "gx", 1), ring(fdown, "gx", -1)
    yup, ydn = pl.pallas_call(
        functools.partial(ypack_kernel, s),
        out_shape=(shape(s.rows_f + s.rows_w, z),) * 2,
        in_specs=[VMEM] * 4,
        out_specs=(VMEM,) * 2,
        compiler_params=params(4),
        cost_estimate=SHORT,
        name="ypack",
    )(coarse_fields, coarse_wind, lo, hi)
    yrows = [ring(yup, "gy", 1), ring(ydn, "gy", -1)]
    slab = pl.pallas_call(
        functools.partial(slab_kernel, s),
        out_shape=shape(s.slab, z),
        in_specs=[VMEM] * 4,
        out_specs=VMEM,
        scratch_shapes=[pltpu.VMEM((q, s.ep, PAD, z), F32)] * 3 + [pltpu.VMEM((3, s.ex, y, z), F32)],
        compiler_params=params(10),
        cost_estimate=SHORT,
        name="slab",
    )(coarse_fields, coarse_wind, lo, hi)
    yrows, slab, flo, fhi = lax.optimization_barrier((yrows, slab, flo, fhi))
    padded = pltpu.VMEM((q, s.ep, WPAD, z), F32)
    wind_rows = pltpu.VMEM((3, s.ex, 24, z), F32)
    def zpack(*operands):
        return pl.pallas_call(
            functools.partial(zpack_kernel, s),
            out_shape=shape(q + 3, 24, z),
            in_specs=[VMEM] * 6,
            out_specs=VMEM,
            scratch_shapes=[padded, wind_rows],
            compiler_params=params(6),
            cost_estimate=pl.CostEstimate(flops=4_000_000, bytes_accessed=2_000_000, transcendentals=0),
            name="zpack",
        )(*operands)

    slab, zown = move_by(slab, (size - offset) % size, (zpack, (coarse_fields, coarse_wind, lo, hi, *yrows)))
    zin = z_columns(zown)
    def coarse(*operands):
        return pl.pallas_call(
            functools.partial(coarse_kernel, s),
            out_shape=shape(q, x, y, z),
            in_specs=[SMEM] + [VMEM] * 8,
            out_specs=VMEM,
            scratch_shapes=[padded] * 3 + [wind_rows, pltpu.VMEM((3, q, 24, z), F32), pltpu.VMEM((2, q, 24, z), F32)],
            compiler_params=params(12),
            cost_estimate=pl.CostEstimate(flops=40_000_000, bytes_accessed=4_000_000, transcendentals=0),
            name="coarse",
        )(*operands)

    layers = fx + 6
    fine_next, averaged = pl.pallas_call(
        functools.partial(fine_kernel, s),
        out_shape=(shape(q, fx, y, z), shape(q, x // 2, y // 2, z)),
        in_specs=[VMEM] * 5,
        out_specs=(HBM, VMEM),
        scratch_shapes=[
            pltpu.VMEM((q, layers, PAD, z), F32),
            pltpu.VMEM((q, layers, PAD, z), F32),
            pltpu.VMEM((6 * q, s.ep, z), F32),
            pltpu.VMEM((2 * q * s.fe, z), F32),
            pltpu.VMEM((2 * q * y, z), F32),
            pltpu.SemaphoreType.DMA((4,)),
        ],
        compiler_params=params(10),
        name="fine",
    )(fine_fields, fine_wind, flo, fhi, slab)
    averaged, state = move_by(
        averaged,
        offset,
        (coarse, (neighbours, coarse_fields, coarse_wind, lo, hi, *yrows, zown, zin)),
    )
    coarse_next = pl.pallas_call(
        functools.partial(merge_kernel, s),
        out_shape=shape(q, x, y, z),
        in_specs=[VMEM, VMEM],
        out_specs=VMEM,
        compiler_params=params(4),
        name="merge",
    )(state, averaged)
    return coarse_next, fine_next


def solution(mesh):
    spec = P(None, "gx", "gy", "gz")
    return jax.shard_map(
        shards,
        mesh=mesh,
        in_specs=(spec, spec, spec, spec, P("gx", "gy", "gz")),
        out_specs=(spec, spec),
        check_vma=False,
    )
```

```python
import functools

import jax
import jax.numpy as jnp
from jax import lax
from jax.experimental import pallas as pl
from jax.experimental.pallas import tpu as pltpu
from jax.sharding import PartitionSpec as P

diffusion = 0.05
section_weights = (1.0 / 3.0, 0.5, 1.0)
F32 = jnp.float32
BF16 = jnp.bfloat16
PAD = 32
TOP = 8


class Sizes:
    def __init__(self, coarse_shape, fine_shape):
        self.q, self.x, self.y, self.z = coarse_shape
        self.fx = fine_shape[1]
        self.ly, self.sy = self.y // 4, self.y // 2
        self.lz, self.sz = self.z // 4, self.z // 2
        self.ex = self.x + 4
        self.ep = -(-self.ex // 8) * 8
        self.fe = self.fx + 4
        self.halo = 3 * self.q + 6
        self.rows_f, self.rows_w = self.q * (3 * self.x + 6), 3 * (2 * self.x + 2)
        self.rows_y = 3 * self.q * self.ex
        self.rows_e = self.rows_y + self.ep
        self.rows_z = self.sy + 2
        self.slab = self.rows_e + self.q * self.rows_z
        assert self.q == 4 and self.y == 16 and self.z == 128 and self.ex <= 20 and self.fx == 2 * self.x


def lanes_of(shape):
    return lax.broadcasted_iota(jnp.int32, shape, len(shape) - 1)


def halves(value):
    high = value.astype(BF16)
    return high, (value - high.astype(F32)).astype(BF16)


def times(value, matrix):
    high, low = halves(value)
    return jnp.dot(high, matrix, preferred_element_type=F32) + jnp.dot(low, matrix, preferred_element_type=F32)


def coefficients(wind):
    out = []
    for w in wind:
        out += [diffusion - 0.5 * w, diffusion + 0.5 * w]
    return out


def rate_of(co, center, x_low, x_high, y_low, y_high, z_low, z_high):
    along = (co[0] * x_high + co[1] * x_low) + (co[2] * y_high + co[3] * y_low) + (co[4] * z_high + co[5] * z_low)
    return along - (6.0 * diffusion) * center


def layer_of(s, own, low, high, member, at, width, first):
    size = own.shape[1]
    if at < 0:
        return low[first + width * member + at + width]
    if at >= size:
        return high[first + width * member + at - size]
    return own[member, at]


def unrolled(begin, end, at_once, body, carry=None):
    while (end - begin) % at_once:
        at_once -= 1

    def several(i, carry):
        for more in range(at_once):
            carry = body(begin + i * at_once + more, carry)
        return carry

    return lax.fori_loop(0, (end - begin) // at_once, several, carry)


def pack_kernel(s, fields, wind, up, down, sems):
    size = fields.shape[1]
    moves = []
    for own, members, width, first in ((fields, s.q, 3, 0), (wind, 3, 2, 3 * s.q)):
        for dst, at in ((up, size - width), (down, 0)):
            place = dst.at[first : first + members * width].reshape(members, width, s.y, s.z)
            moves.append((own.at[:, at : at + width], place))
    moves = [pltpu.make_async_copy(src, dst, sems.at[i]) for i, (src, dst) in enumerate(moves)]
    for move in moves:
        move.start()
    for move in moves:
        move.wait()


def y_rows(s, members, width):
    below, above = [], []
    for out, extra in ((below, lambda r: r), (above, lambda r: width - 1 - r)):
        at = 0
        for m in range(members):
            for r in range(width):
                out.append((m, r, extra(r), at))
                at += s.x + 2 * extra(r)
    return below, above


def ypack_kernel(s, c0, cw, lo, hi, up, dn):
    x, y, z = s.x, s.y, s.z
    flat_lo = lo.reshape(s.halo * y, z)
    flat_hi = hi.reshape(s.halo * y, z)
    for own, members, width, first, place in ((c0, s.q, 3, 0, 0), (cw, 3, 2, 3 * s.q, s.rows_f)):
        flat = own.reshape(members * x * y, z)
        for dst, rows, start in zip((up, dn), y_rows(s, members, width), (y - width, 0)):
            for m, r, e, at in rows:
                row, at = start + r, at + place
                if e:
                    dst[at : at + e, :] = flat_lo[pl.ds((first + width * (m + 1) - e) * y + row, e, stride=y), :]
                    dst[at + e + x : at + x + 2 * e, :] = flat_hi[pl.ds((first + width * m) * y + row, e, stride=y), :]
                dst[at + e : at + e + x, :] = flat[pl.ds(m * x * y + row, x, stride=y), :]


EDGE = 4


def turned_rate(co, center, x_low, x_high):
    y, z = center.shape
    return rate_of(
        co,
        center,
        x_low,
        x_high,
        pltpu.roll(center, 1, 0),
        pltpu.roll(center, y - 1, 0),
        pltpu.roll(center, 1, 1),
        pltpu.roll(center, z - 1, 1),
    )


def slab_parts(s, rows_of, tile_of, layers_of, put):
    q, y, z = s.q, s.y, s.z
    lane_y = lanes_of((y, z))
    columns = (lane_y == s.lz - 1) | (lane_y == s.lz) | (lane_y == s.lz + s.sz - 1) | (lane_y == s.lz + s.sz)
    low_at = (lane_y % 2 == 0) & (lane_y < z // 2)
    high_at = (lane_y % 2 == 0) & (lane_y >= z // 2)
    ends = None
    for f in range(q):
        zfaces = None
        for k in range(3):
            rows = [rows_of(k, f, row) for row in (s.ly - 1, s.ly, s.ly + s.sy - 1, s.ly + s.sy)]
            sides = (0.75 * rows[0] + 0.25 * rows[1], 0.25 * rows[2] + 0.75 * rows[3])
            lane_x = lanes_of(sides[0].shape)
            put(
                "y",
                (k * q + f) * s.ex,
                jnp.where(lane_x < s.sz, pltpu.roll(sides[0], z - s.lz, 1), pltpu.roll(sides[1], s.lz, 1)),
            )
            for side in range(2):
                e = 4 * (q * k + f) + 2 * side + 1
                before = jnp.where(lane_x == s.lz - 1, sides[side], 0.0)
                after = jnp.where(lane_x == s.lz + s.sz, sides[side], 0.0)
                part = pltpu.roll(before, (e - s.lz + 1) % z, 1) + pltpu.roll(after, (e - 1 - s.lz - s.sz) % z, 1)
                ends = part if ends is None else ends + part
            raw = None
            for a in layers_of(k):
                part = jnp.where(columns, tile_of(k, f, a), 0.0)
                part = pltpu.roll(part, (2 * a - s.lz + 1) % z, 1)
                raw = part if raw is None else raw + part
            beside = pltpu.roll(raw, z - 1, 1)
            low = jnp.where(low_at, 0.75 * raw + 0.25 * beside, 0.0)
            high = jnp.where(high_at, 0.25 * raw + 0.75 * beside, 0.0)
            part = pltpu.roll(low, (2 * s.ex * k - 1) % z, 1) + pltpu.roll(high, (2 * s.ex * k - z // 2) % z, 1)
            zfaces = part if zfaces is None else zfaces + part
        put("z", s.rows_e + f * s.rows_z, zfaces[s.ly - 1 : s.ly + s.sy + 1])
    put("e", s.rows_y, ends)


def inner_kernel(s, c0, cw, part, near, state1, state2):
    q, x, y, z = s.q, s.x, s.y, s.z
    states = (c0, state1, state2)
    for step in range(2):
        src, dst = states[step], states[step + 1]

        def layer(j, carry, step=step, src=src, dst=dst):
            co = coefficients([cw[d, j] for d in range(3)])
            for f in range(q):
                center = src[f, j]
                rate = turned_rate(co, center, src[f, j - 1], src[f, j + 1])
                dst[f, j] = (center if step == 0 else c0[f, j]) + section_weights[step] * rate
            return carry

        unrolled(step + 1, x - 1 - step, 7 if step == 0 else 6, layer)
    for f in range(q):
        near[f, 0] = state1[f, EDGE - 2]
        near[f, 1] = state1[f, x + 1 - EDGE]
    count = s.ex - 2 * EDGE
    part[...] = jnp.zeros_like(part)

    def rows_of(k, f, row):
        flat = states[k].reshape(q * x * y, z)
        return flat[pl.ds((f * x + EDGE - 2) * y + row, count, stride=y), :]

    def put(kind, at, rows):
        if kind == "z":
            part[at : at + s.rows_z, :] = rows
        else:
            part[at + EDGE : at + EDGE + count, :] = rows

    slab_parts(s, rows_of, lambda k, f, a: states[k][f, a - 2], lambda k: range(EDGE, s.ex - EDGE), put)


def slab_kernel(s, c0, cw, lo, hi, part, near, slab, ends0, ends1, ends2):
    q, x, y, z = s.q, s.x, s.y, s.z
    states = (ends0, ends1, ends2)
    places = list(range(-2, EDGE - 2)) + list(range(x + 2 - EDGE, x + 2))
    slab[...] = part[...]
    for j, at in enumerate(places):
        for f in range(q):
            ends0[f, j] = layer_of(s, c0, lo, hi, f, at, 3, 0)
    for step in range(2):
        for j, at in enumerate(places):
            if step == 1 and at in (-2, x + 1):
                for f in range(q):
                    ends2[f, j] = jnp.zeros((y, z), F32)
                continue
            co = coefficients([layer_of(s, cw, lo, hi, d, at, 2, 3 * q) for d in range(3)])
            for f in range(q):

                def beside(at, f=f):
                    if step == 0:
                        return layer_of(s, c0, lo, hi, f, at, 3, 0)
                    if at in places:
                        return ends1[f, places.index(at)]
                    return near[f, 0 if at < x // 2 else 1]

                rate = turned_rate(co, beside(at), beside(at - 1), beside(at + 1))
                states[step + 1][f, j] = ends0[f, j] + section_weights[step] * rate

    def rows_of(k, f, row):
        flat = states[k].reshape(q * 2 * EDGE * y, z)
        return flat[pl.ds(f * 2 * EDGE * y + row, 2 * EDGE, stride=y), :]

    def put(kind, at, rows):
        if kind == "z":
            slab[at : at + s.rows_z, :] = part[at : at + s.rows_z, :] + rows
        else:
            slab[at : at + EDGE, :] = rows[:EDGE]
            slab[at + s.ex - EDGE : at + s.ex, :] = rows[EDGE:]

    def layers_of(k):
        some = range(0 if k == 0 else 1, EDGE)
        return list(some) + [s.ex - 1 - a for a in some]

    def tile_of(k, f, a):
        return states[k][f, a if a < EDGE else a - s.ex + 2 * EDGE]

    slab_parts(s, rows_of, tile_of, layers_of, put)


WTOP, WPAD = 12, 40
BLOCK = slice(8, 32)


def assemble(s, c0, cw, lo, hi, below, above, pad, wind):
    q, x, y, z = s.q, s.x, s.y, s.z
    flat = pad.reshape(q * s.ep * WPAD, z)
    flat_wind = wind.reshape(3 * s.ex * 24, z)
    for f in range(q):
        for at in range(-3, x + 3):
            pad[f, at + 3, WTOP : WTOP + y, :] = layer_of(s, c0, lo, hi, f, at, 3, 0)
    for d in range(3):
        for at in range(-2, x + 2):
            wind[d, at + 2, 4 : 4 + y, :] = layer_of(s, cw, lo, hi, d, at, 2, 3 * q)
    for src, rows, start in zip((below, above), y_rows(s, q, 3), (WTOP - 3, WTOP + y)):
        for m, r, e, at in rows:
            count = x + 2 * e
            flat[pl.ds((m * s.ep + 3 - e) * WPAD + start + r, count, stride=WPAD), :] = src[at : at + count, :]
    for src, rows, start in zip((below, above), y_rows(s, 3, 2), (2, 4 + y)):
        for m, r, e, at in rows:
            count, at = x + 2 * e, at + s.rows_f
            flat_wind[pl.ds((m * s.ex + 2 - e) * 24 + start + r, count, stride=24), :] = src[at : at + count, :]


def edge_lanes(s, lane, width):
    return (lane < width) | (lane >= s.z - width)


def zpack_kernel(s, c0, cw, lo, hi, below, above, out, pad, wind):
    assemble(s, c0, cw, lo, hi, below, above, pad, wind)
    lane = lanes_of((24, s.z))
    keep = edge_lanes(s, lane, 3)
    for m in range(s.q + 3):
        total = None
        for a in range(s.ex):
            tile = pad[m, a + 1, BLOCK, :] if m < s.q else wind[m - s.q, a]
            part = pltpu.roll(jnp.where(keep, tile, 0.0), (6 * a + 3) % s.z, 1)
            total = part if total is None else total + part
        out[m] = total


def coarse_kernel(
    s, sides, c0, cw, lo, hi, below, above, zown, zin, out, pad0, pad1, pad2, wind, beyond, nearest
):
    q, x, y, z = s.q, s.x, s.y, s.z
    assemble(s, c0, cw, lo, hi, below, above, pad0, wind)
    pads = (pad0, pad1, pad2)
    lane = lanes_of((24, z))
    group = lane % 6
    from_low = group == 2
    from_high = group == 3
    exists = jnp.where(group < 3, sides[0, 0], sides[0, 1]).astype(F32)
    co_z = coefficients([zin[q + d] for d in range(3)])
    for f in range(q):
        beyond[0, f] = zin[f] * exists
        nearest[0, f] = zown[f]
    for step in range(3):
        src, fraction = pads[step], section_weights[step]
        flat = src.reshape(q * s.ep * WPAD, z)
        flat_wind = wind.reshape(3 * s.ex * 24, z)
        flat_beyond = beyond.reshape(3 * q * 24, z)
        skip, height = (0, 24) if step < 2 else (4, y)
        here = lanes_of((height, z))
        is_first, is_last = here == 0, here == z - 1

        def layer(a, packed, step=step, src=src, flat=flat, fraction=fraction, skip=skip, height=height):
            made = []
            if step < 2:
                co = coefficients([wind[d, a] for d in range(3)])
            else:
                co = coefficients([flat_wind[pl.ds((d * s.ex + a) * 24 + skip, height), :] for d in range(3)])
            for f in range(q):
                row = (f * s.ep + a + 1) * WPAD + 8 + skip

                def at_layer(of, layer, row, f=f):
                    return of[f, layer, BLOCK, :] if step < 2 else of.reshape(flat.shape)[pl.ds(row, height), :]

                center = at_layer(src, a + 1, row)
                ghost = pltpu.roll(flat_beyond[pl.ds((step * q + f) * 24 + skip, height), :], 2 * z - 6 * a - 3, 1)
                rate = rate_of(
                    co,
                    center,
                    at_layer(src, a, row - WPAD),
                    at_layer(src, a + 2, row + WPAD),
                    flat[pl.ds(row - 1, height), :],
                    flat[pl.ds(row + 1, height), :],
                    pltpu.roll(jnp.where(is_last, ghost, center), 1, 1),
                    pltpu.roll(jnp.where(is_first, ghost, center), z - 1, 1),
                )
                base = center if step == 0 else at_layer(pad0, a + 1, row)
                value = base + fraction * rate
                if step == 2:
                    out[f, a - 2] = value
                else:
                    pads[step + 1][f, a + 1, BLOCK, :] = value
                if step == 0:
                    made.append(packed[f] + pltpu.roll(jnp.where(is_first | is_last, value, 0.0), 6 * a + 3, 1))
            return tuple(made)

        begin, end = step, s.ex - step
        start = tuple(jnp.zeros((24, z), F32) for _ in range(q)) if step == 0 else ()
        packed = unrolled(begin, end, 4 + 2 * (step == 1), layer, start)
        if step == 2:
            break
        for f in range(q):
            if step == 0:
                nearest[1, f] = packed[f]
            ghost, near = beyond[step, f], nearest[step, f]
            rate = rate_of(
                co_z,
                ghost,
                pltpu.roll(ghost, 6, 1),
                pltpu.roll(ghost, z - 6, 1),
                pltpu.roll(ghost, 1, 0),
                pltpu.roll(ghost, 23, 0),
                pltpu.roll(jnp.where(from_low, near, ghost), 1, 1),
                pltpu.roll(jnp.where(from_high, near, ghost), z - 1, 1),
            )
            beyond[step + 1, f] = (beyond[0, f] + fraction * rate) * exists


def fine_kernel(s, f0, fw, flo, fhi, slab, out, avg, *scratch):
    s1, s2, faces, ghost_rows, zface, sems = scratch
    states = (None, s1, s2, s1)
    q, y, z, fx, fe = s.q, s.y, s.z, s.fx, s.fe
    layers = fx + 6
    rows = slice(TOP, TOP + y)
    r = lax.broadcasted_iota(jnp.int32, (z, 2 * z), 0)
    c = lax.broadcasted_iota(jnp.int32, (z, 2 * z), 1)
    near = c // 2
    far = near + 2 * (c % 2) - 1
    same = (far // s.sz == near // s.sz) & (far >= 0)
    to_fine = jnp.where(r == near, 0.75, jnp.where((r == far) & same, 0.25, 0.0)).astype(BF16)
    wide = times(slab[: s.rows_y, :], to_fine)
    ends = slab[s.rows_y : s.rows_y + s.ex, :]
    lane_x = lanes_of((s.ex, z))
    edge = (lane_x == 0) | (lane_x == z - 1)
    half = fe // 2
    for k in range(3):
        for f in range(q):
            for side in range(2):
                e = 4 * (q * k + f) + 2 * side + 1
                corner = jnp.where(edge, 0.25 * pltpu.roll(ends, z - e, 1), 0.0)
                first = (k * q + f) * s.ex
                here = faces.at[(k * q + f) * 2 + side]
                here[: s.ex, :] = wide[first : first + s.ex, side * z : side * z + z] + corner
                a = here[0:half, :]
                b = here[1 : half + 1, :]
                d = here[2 : half + 2, :]
                if k == 0:
                    flat, base, stride = ghost_rows, (2 * f + side) * fe, 1
                else:
                    flat, stride = states[k].reshape(q * layers * PAD, z), PAD
                    base = (f * layers + 1) * PAD + (TOP - 1 if side == 0 else TOP + y)
                flat[pl.ds(base, half, stride=2 * stride), :] = 0.25 * a + 0.75 * b
                flat[pl.ds(base + stride, half, stride=2 * stride), :] = 0.75 * b + 0.25 * d
    for f in range(q):
        at = s.rows_e + f * s.rows_z
        a = slab[at : at + s.sy, :]
        b = slab[at + 1 : at + 1 + s.sy, :]
        d = slab[at + 2 : at + 2 + s.sy, :]
        zface[pl.ds(f * y, s.sy, stride=2), :] = 0.25 * a + 0.75 * b
        zface[pl.ds(f * y + 1, s.sy, stride=2), :] = 0.75 * b + 0.25 * d
        a = zface[f * y : f * y + y, :]
        b = pltpu.roll(a, z - 2, 1)
        d = pltpu.roll(a, z - 4, 1)
        zface[f * y : f * y + y, :] = 0.25 * a + 0.75 * b
        zface[(q + f) * y : (q + f + 1) * y, :] = 0.75 * b + 0.25 * d
    lane = lanes_of((y, z))
    is_first, is_last = lane == 0, lane == z - 1
    row_in = lax.broadcasted_iota(jnp.int32, (y, z), 0)
    is_low, is_high = row_in == 0, row_in == y - 1
    flat_f0 = f0.reshape(q * fx * y, z)

    def pair_of_layers(k, t, inner):
        src = states[k]
        for odd in range(2):
            b = 2 * t + odd
            at = b - 2

            def field(f, at):
                return f0[f, at] if inner else layer_of(s, f0, flo, fhi, f, at, 3, 0)

            if inner:
                winds = [fw[d, at] for d in range(3)]
            else:
                winds = [layer_of(s, fw, flo, fhi, d, at, 2, 3 * q) for d in range(3)]
            co = coefficients(winds)
            for f in range(q):
                if k == 0:
                    center, x_low, x_high = field(f, at), field(f, at - 1), field(f, at + 1)
                    if inner:
                        row = (f * fx + at) * y
                        y_low, y_high = flat_f0[pl.ds(row - 1, y), :], flat_f0[pl.ds(row + 1, y), :]
                    else:
                        y_low, y_high = pltpu.roll(center, 1, 0), pltpu.roll(center, y - 1, 0)
                    y_low = jnp.where(is_low, ghost_rows[pl.ds(2 * f * fe + b, 1), :], y_low)
                    y_high = jnp.where(is_high, ghost_rows[pl.ds((2 * f + 1) * fe + b, 1), :], y_high)
                    base = center
                else:
                    flat = src.reshape(q * layers * PAD, z)
                    row = (f * layers + b + 1) * PAD + TOP
                    center, x_low, x_high = src[f, b + 1, rows, :], src[f, b, rows, :], src[f, b + 2, rows, :]
                    y_low, y_high = flat[pl.ds(row - 1, y), :], flat[pl.ds(row + 1, y), :]
                    base = field(f, at)
                ghost = zface[(odd * q + f) * y : (odd * q + f + 1) * y, :]
                ghost = pltpu.roll(ghost, (2 * z - 2 * s.ex * k - 2 * t) if inner else -(2 * s.ex * k + 2 * t) % z, 1)
                rate = rate_of(
                    co,
                    center,
                    x_low,
                    x_high,
                    y_low,
                    y_high,
                    pltpu.roll(jnp.where(is_last, ghost, center), 1, 1),
                    pltpu.roll(jnp.where(is_first, ghost, center), z - 1, 1),
                )
                states[k + 1][f, b + 1, rows, :] = base + section_weights[k] * rate

    moves = []
    for k in range(3):
        if k < 2:
            outer = 2 - k
            for t in list(range(outer)) + list(range(half - outer, half)):
                pair_of_layers(k, t, False)
            unrolled(outer, half - outer, 2, lambda t, g, k=k: pair_of_layers(k, t, True))
            continue
        part = (half - 2) // 4
        for i in range(4):
            unrolled(1 + i * part, 1 + (i + 1) * part, 2, lambda t, g, k=k: pair_of_layers(k, t, True))
            begin, end = 2 * part * i, 2 * part * (i + 1)
            moves.append(pltpu.make_async_copy(s1.at[:, 3 + begin : 3 + end, rows], out.at[:, begin:end], sems.at[i]))
            moves[-1].start()
    rz = lax.broadcasted_iota(jnp.int32, (z, z), 0)
    cz = lax.broadcasted_iota(jnp.int32, (z, z), 1)
    flat = s1.reshape(q * layers * PAD, z)
    pairs_z = [jnp.where(cz == rz // 2 + odd * s.sz, 0.125, 0.0).astype(BF16) for odd in range(2)]
    for f in range(q):
        sums = []
        for odd in range(2):
            parts = []
            for p in range(s.x // 2):
                base = (f * layers + 3 + 4 * p + 2 * odd) * PAD + TOP
                part = None
                for more in (0, 1, PAD, PAD + 1):
                    piece = flat[pl.ds(base + more, y // 2, stride=2), :]
                    part = piece if part is None else part + piece
                parts.append(part)
            sums.append(times(jnp.concatenate(parts, axis=0), pairs_z[odd]))
        avg[f] = (sums[0] + sums[1]).reshape(s.x // 2, y // 2, z)
    for move in moves:
        move.wait()


def merge_kernel(s, c3, avg, out):
    lane = lanes_of((s.sy, s.z))
    inside = (lane >= s.lz) & (lane < s.lz + s.sz)
    for f in range(s.q):
        for p in range(s.x // 2):
            both = avg[f, p]
            for odd in range(2):
                at = 2 * p + odd
                moved = pltpu.roll(both, s.lz if odd == 0 else s.z - s.lz, 1)
                out[f, at] = c3[f, at]
                out[f, at, s.ly : s.ly + s.sy, :] = jnp.where(inside, moved, c3[f, at, s.ly : s.ly + s.sy, :])


VMEM = pl.BlockSpec(memory_space=pltpu.VMEM)
SMEM = pl.BlockSpec(memory_space=pltpu.SMEM)
HBM = pl.BlockSpec(memory_space=pltpu.HBM)
ANY = pl.BlockSpec(memory_space=pl.ANY)


SHORT = pl.CostEstimate(flops=1, bytes_accessed=1, transcendentals=0)


def params(megabytes):
    return pltpu.CompilerParams(vmem_limit_bytes=megabytes << 20)


def shape(*dims):
    return jax.ShapeDtypeStruct(dims, F32)


def ring(array, axis, by):
    size = lax.axis_size(axis)
    return lax.ppermute(array, axis, [(i, (i + by) % size) for i in range(size)])


def move_by(array, amount, beside=None):
    size = lax.axis_size("gx")
    work, operands = beside or (lambda: (), ())
    if size <= 8:

        def branch(by, array, *operands):
            return array if by == 0 else ring(array, "gx", by), work(*operands)

        return lax.switch(amount, [functools.partial(branch, by) for by in range(size)], array, *operands)
    for bit in range((size - 1).bit_length()):
        array = jnp.where((amount >> bit) % 2 == 1, ring(array, "gx", 1 << bit), array)
    return array, work(*operands)


def z_columns(zown):
    size = lax.axis_size("gz")
    if size == 1:
        return zown
    if size == 2:
        return lax.ppermute(zown, "gz", [(0, 1), (1, 0)])
    below = lax.broadcasted_iota(jnp.int32, zown.shape, 2) % 6 < 3
    return jnp.where(below, ring(zown, "gz", 1), ring(zown, "gz", -1))


def pack(s, fields, wind, spare, name):
    return pl.pallas_call(
        functools.partial(pack_kernel, s),
        out_shape=(shape(s.halo + spare, s.y, s.z),) * 2,
        in_specs=[HBM] * 2,
        out_specs=(VMEM,) * 2,
        scratch_shapes=[pltpu.SemaphoreType.DMA((4,))],
        compiler_params=params(4),
        cost_estimate=SHORT,
        name=name,
    )(fields, wind)


def shards(coarse_fields, coarse_wind, fine_fields, fine_wind, fine_owner):
    s = Sizes(coarse_fields.shape, fine_fields.shape)
    q, x, y, z, fx = s.q, s.x, s.y, s.z, s.fx
    size = lax.axis_size("gx")
    offset = (fine_owner[0, 0, 0] - lax.axis_index("gx")) % size
    level = lax.axis_index("gz")
    neighbours = jnp.stack([level > 0, level < lax.axis_size("gz") - 1]).astype(jnp.int32).reshape(1, 2)
    cup, cdown = pack(s, coarse_fields, coarse_wind, 0, "pack_coarse")
    lo, hi = ring(cup, "gx", 1), ring(cdown, "gx", -1)
    ends = pltpu.VMEM((q, 2 * EDGE, y, z), F32)
    part, near = pl.pallas_call(
        functools.partial(inner_kernel, s),
        out_shape=(shape(s.slab, z), shape(q, 2, y, z)),
        in_specs=[VMEM] * 2,
        out_specs=(VMEM,) * 2,
        scratch_shapes=[pltpu.VMEM((q, x, y, z), F32)] * 2,
        compiler_params=params(6),
        cost_estimate=SHORT,
        name="inner",
    )(coarse_fields, coarse_wind)
    fup, fdown = pack(s, fine_fields, fine_wind, 2, "pack_fine")
    fup, fdown, part, near, offset = lax.optimization_barrier((fup, fdown, part, near, offset))
    flo, fhi = ring(fup, "gx", 1), ring(fdown, "gx", -1)
    yup, ydn = pl.pallas_call(
        functools.partial(ypack_kernel, s),
        out_shape=(shape(s.rows_f + s.rows_w, z),) * 2,
        in_specs=[VMEM] * 4,
        out_specs=(VMEM,) * 2,
        compiler_params=params(4),
        cost_estimate=SHORT,
        name="ypack",
    )(coarse_fields, coarse_wind, lo, hi)
    yrows = [ring(yup, "gy", 1), ring(ydn, "gy", -1)]
    slab = pl.pallas_call(
        functools.partial(slab_kernel, s),
        out_shape=shape(s.slab, z),
        in_specs=[VMEM] * 6,
        out_specs=VMEM,
        scratch_shapes=[ends] * 3,
        compiler_params=params(6),
        cost_estimate=SHORT,
        name="slab",
    )(coarse_fields, coarse_wind, lo, hi, part, near)
    yrows, slab, flo, fhi = lax.optimization_barrier((yrows, slab, flo, fhi))
    padded = pltpu.VMEM((q, s.ep, WPAD, z), F32)
    wind_rows = pltpu.VMEM((3, s.ex, 24, z), F32)
    def zpack(*operands):
        return pl.pallas_call(
            functools.partial(zpack_kernel, s),
            out_shape=shape(q + 3, 24, z),
            in_specs=[VMEM] * 6,
            out_specs=VMEM,
            scratch_shapes=[padded, wind_rows],
            compiler_params=params(6),
            cost_estimate=pl.CostEstimate(flops=4_000_000, bytes_accessed=2_000_000, transcendentals=0),
            name="zpack",
        )(*operands)

    slab, zown = move_by(slab, (size - offset) % size, (zpack, (coarse_fields, coarse_wind, lo, hi, *yrows)))
    zin = z_columns(zown)
    def coarse(*operands):
        return pl.pallas_call(
            functools.partial(coarse_kernel, s),
            out_shape=shape(q, x, y, z),
            in_specs=[SMEM] + [VMEM] * 8,
            out_specs=VMEM,
            scratch_shapes=[padded] * 3 + [wind_rows, pltpu.VMEM((3, q, 24, z), F32), pltpu.VMEM((2, q, 24, z), F32)],
            compiler_params=params(12),
            cost_estimate=pl.CostEstimate(flops=40_000_000, bytes_accessed=4_000_000, transcendentals=0),
            name="coarse",
        )(*operands)

    layers = fx + 6
    fine_next, averaged = pl.pallas_call(
        functools.partial(fine_kernel, s),
        out_shape=(shape(q, fx, y, z), shape(q, x // 2, y // 2, z)),
        in_specs=[VMEM] * 5,
        out_specs=(HBM, VMEM),
        scratch_shapes=[
            pltpu.VMEM((q, layers, PAD, z), F32),
            pltpu.VMEM((q, layers, PAD, z), F32),
            pltpu.VMEM((6 * q, s.ep, z), F32),
            pltpu.VMEM((2 * q * s.fe, z), F32),
            pltpu.VMEM((2 * q * y, z), F32),
            pltpu.SemaphoreType.DMA((4,)),
        ],
        compiler_params=params(10),
        name="fine",
    )(fine_fields, fine_wind, flo, fhi, slab)
    averaged, state = move_by(
        averaged,
        offset,
        (coarse, (neighbours, coarse_fields, coarse_wind, lo, hi, *yrows, zown, zin)),
    )
    coarse_next = pl.pallas_call(
        functools.partial(merge_kernel, s),
        out_shape=shape(q, x, y, z),
        in_specs=[VMEM, VMEM],
        out_specs=VMEM,
        compiler_params=params(4),
        name="merge",
    )(state, averaged)
    return coarse_next, fine_next


def solution(mesh):
    spec = P(None, "gx", "gy", "gz")
    return jax.shard_map(
        shards,
        mesh=mesh,
        in_specs=(spec, spec, spec, spec, P("gx", "gy", "gz")),
        out_specs=(spec, spec),
        check_vma=False,
    )
```

```python
import functools

import jax
import jax.numpy as jnp
from jax import lax
from jax.experimental import pallas as pl
from jax.experimental.pallas import tpu as pltpu
from jax.sharding import PartitionSpec as P

diffusion = 0.05
section_weights = (1.0 / 3.0, 0.5, 1.0)
F32 = jnp.float32
BF16 = jnp.bfloat16
PAD = 32
TOP = 8


class Sizes:
    def __init__(self, coarse_shape, fine_shape):
        self.q, self.x, self.y, self.z = coarse_shape
        self.fx = fine_shape[1]
        self.ly, self.sy = self.y // 4, self.y // 2
        self.lz, self.sz = self.z // 4, self.z // 2
        self.ex = self.x + 4
        self.ep = -(-self.ex // 8) * 8
        self.fe = self.fx + 4
        self.halo = 3 * self.q + 6
        self.rows_f, self.rows_w = self.q * (3 * self.x + 6), 3 * (2 * self.x + 2)
        self.rows_y = 3 * self.q * self.ex
        self.rows_e = self.rows_y + self.ep
        self.rows_z = self.sy + 2
        self.slab = self.rows_e + self.q * self.rows_z
        assert self.q == 4 and self.y == 16 and self.z == 128 and self.ex <= 20 and self.fx == 2 * self.x


def lanes_of(shape):
    return lax.broadcasted_iota(jnp.int32, shape, len(shape) - 1)


def halves(value):
    high = value.astype(BF16)
    return high, (value - high.astype(F32)).astype(BF16)


def times(value, matrix):
    high, low = halves(value)
    return jnp.dot(high, matrix, preferred_element_type=F32) + jnp.dot(low, matrix, preferred_element_type=F32)


def coefficients(wind):
    out = []
    for w in wind:
        out += [diffusion - 0.5 * w, diffusion + 0.5 * w]
    return out


def rate_of(co, center, x_low, x_high, y_low, y_high, z_low, z_high):
    along = (co[0] * x_high + co[1] * x_low) + (co[2] * y_high + co[3] * y_low) + (co[4] * z_high + co[5] * z_low)
    return along - (6.0 * diffusion) * center


def layer_of(s, own, low, high, member, at, width, first):
    size = own.shape[1]
    if at < 0:
        return low[first + width * member + at + width]
    if at >= size:
        return high[first + width * member + at - size]
    return own[member, at]


def unrolled(begin, end, at_once, body, carry=None):
    while (end - begin) % at_once:
        at_once -= 1

    def several(i, carry):
        for more in range(at_once):
            carry = body(begin + i * at_once + more, carry)
        return carry

    return lax.fori_loop(0, (end - begin) // at_once, several, carry)


def pack_kernel(s, fields, wind, up, down, sems):
    size = fields.shape[1]
    moves = []
    for own, members, width, first in ((fields, s.q, 3, 0), (wind, 3, 2, 3 * s.q)):
        for dst, at in ((up, size - width), (down, 0)):
            place = dst.at[first : first + members * width].reshape(members, width, s.y, s.z)
            moves.append((own.at[:, at : at + width], place))
    moves = [pltpu.make_async_copy(src, dst, sems.at[i]) for i, (src, dst) in enumerate(moves)]
    for move in moves:
        move.start()
    for move in moves:
        move.wait()


def y_rows(s, members, width):
    below, above = [], []
    for out, extra in ((below, lambda r: r), (above, lambda r: width - 1 - r)):
        at = 0
        for m in range(members):
            for r in range(width):
                out.append((m, r, extra(r), at))
                at += s.x + 2 * extra(r)
    return below, above


def ypack_kernel(s, c0, cw, lo, hi, up, dn):
    x, y, z = s.x, s.y, s.z
    flat_lo = lo.reshape(s.halo * y, z)
    flat_hi = hi.reshape(s.halo * y, z)
    for own, members, width, first, place in ((c0, s.q, 3, 0, 0), (cw, 3, 2, 3 * s.q, s.rows_f)):
        flat = own.reshape(members * x * y, z)
        for dst, rows, start in zip((up, dn), y_rows(s, members, width), (y - width, 0)):
            for m, r, e, at in rows:
                row, at = start + r, at + place
                if e:
                    dst[at : at + e, :] = flat_lo[pl.ds((first + width * (m + 1) - e) * y + row, e, stride=y), :]
                    dst[at + e + x : at + x + 2 * e, :] = flat_hi[pl.ds((first + width * m) * y + row, e, stride=y), :]
                dst[at + e : at + e + x, :] = flat[pl.ds(m * x * y + row, x, stride=y), :]


EDGE = 4


def turned_rate(co, center, x_low, x_high):
    y, z = center.shape
    return rate_of(
        co,
        center,
        x_low,
        x_high,
        pltpu.roll(center, 1, 0),
        pltpu.roll(center, y - 1, 0),
        pltpu.roll(center, 1, 1),
        pltpu.roll(center, z - 1, 1),
    )


def slab_parts(s, rows_of, tile_of, layers_of, put):
    q, y, z = s.q, s.y, s.z
    lane_y = lanes_of((y, z))
    columns = (lane_y == s.lz - 1) | (lane_y == s.lz) | (lane_y == s.lz + s.sz - 1) | (lane_y == s.lz + s.sz)
    low_at = (lane_y % 2 == 0) & (lane_y < z // 2)
    high_at = (lane_y % 2 == 0) & (lane_y >= z // 2)
    ends = None
    for f in range(q):
        zfaces = None
        for k in range(3):
            rows = [rows_of(k, f, row) for row in (s.ly - 1, s.ly, s.ly + s.sy - 1, s.ly + s.sy)]
            sides = (0.75 * rows[0] + 0.25 * rows[1], 0.25 * rows[2] + 0.75 * rows[3])
            lane_x = lanes_of(sides[0].shape)
            put(
                "y",
                (k * q + f) * s.ex,
                jnp.where(lane_x < s.sz, pltpu.roll(sides[0], z - s.lz, 1), pltpu.roll(sides[1], s.lz, 1)),
            )
            for side in range(2):
                e = 4 * (q * k + f) + 2 * side + 1
                before = jnp.where(lane_x == s.lz - 1, sides[side], 0.0)
                after = jnp.where(lane_x == s.lz + s.sz, sides[side], 0.0)
                part = pltpu.roll(before, (e - s.lz + 1) % z, 1) + pltpu.roll(after, (e - 1 - s.lz - s.sz) % z, 1)
                ends = part if ends is None else ends + part
            raw = None
            for a in layers_of(k):
                part = jnp.where(columns, tile_of(k, f, a), 0.0)
                part = pltpu.roll(part, (2 * a - s.lz + 1) % z, 1)
                raw = part if raw is None else raw + part
            beside = pltpu.roll(raw, z - 1, 1)
            low = jnp.where(low_at, 0.75 * raw + 0.25 * beside, 0.0)
            high = jnp.where(high_at, 0.25 * raw + 0.75 * beside, 0.0)
            part = pltpu.roll(low, (2 * s.ex * k - 1) % z, 1) + pltpu.roll(high, (2 * s.ex * k - z // 2) % z, 1)
            zfaces = part if zfaces is None else zfaces + part
        put("z", s.rows_e + f * s.rows_z, zfaces[s.ly - 1 : s.ly + s.sy + 1])
    put("e", s.rows_y, ends)


def inner_kernel(s, c0, cw, part, near, state1, state2):
    q, x, y, z = s.q, s.x, s.y, s.z
    states = (c0, state1, state2)
    for step in range(2):
        src, dst = states[step], states[step + 1]

        def layer(j, carry, step=step, src=src, dst=dst):
            co = coefficients([cw[d, j] for d in range(3)])
            for f in range(q):
                center = src[f, j]
                rate = turned_rate(co, center, src[f, j - 1], src[f, j + 1])
                dst[f, j] = (center if step == 0 else c0[f, j]) + section_weights[step] * rate
            return carry

        unrolled(step + 1, x - 1 - step, 7 if step == 0 else 6, layer)
    for f in range(q):
        near[f, 0] = state1[f, EDGE - 2]
        near[f, 1] = state1[f, x + 1 - EDGE]
    count = s.ex - 2 * EDGE
    part[...] = jnp.zeros_like(part)

    def rows_of(k, f, row):
        flat = states[k].reshape(q * x * y, z)
        return flat[pl.ds((f * x + EDGE - 2) * y + row, count, stride=y), :]

    def put(kind, at, rows):
        if kind == "z":
            part[at : at + s.rows_z, :] = rows
        else:
            part[at + EDGE : at + EDGE + count, :] = rows

    slab_parts(s, rows_of, lambda k, f, a: states[k][f, a - 2], lambda k: range(EDGE, s.ex - EDGE), put)


def slab_kernel(s, c0, cw, lo, hi, part, near, slab, ends0, ends1, ends2):
    q, x, y, z = s.q, s.x, s.y, s.z
    states = (ends0, ends1, ends2)
    places = list(range(-2, EDGE - 2)) + list(range(x + 2 - EDGE, x + 2))
    slab[...] = part[...]
    for j, at in enumerate(places):
        for f in range(q):
            ends0[f, j] = layer_of(s, c0, lo, hi, f, at, 3, 0)
    for step in range(2):
        for j, at in enumerate(places):
            if step == 1 and at in (-2, x + 1):
                for f in range(q):
                    ends2[f, j] = jnp.zeros((y, z), F32)
                continue
            co = coefficients([layer_of(s, cw, lo, hi, d, at, 2, 3 * q) for d in range(3)])
            for f in range(q):

                def beside(at, f=f):
                    if step == 0:
                        return layer_of(s, c0, lo, hi, f, at, 3, 0)
                    if at in places:
                        return ends1[f, places.index(at)]
                    return near[f, 0 if at < x // 2 else 1]

                rate = turned_rate(co, beside(at), beside(at - 1), beside(at + 1))
                states[step + 1][f, j] = ends0[f, j] + section_weights[step] * rate

    def rows_of(k, f, row):
        flat = states[k].reshape(q * 2 * EDGE * y, z)
        return flat[pl.ds(f * 2 * EDGE * y + row, 2 * EDGE, stride=y), :]

    def put(kind, at, rows):
        if kind == "z":
            slab[at : at + s.rows_z, :] = part[at : at + s.rows_z, :] + rows
        else:
            slab[at : at + EDGE, :] = rows[:EDGE]
            slab[at + s.ex - EDGE : at + s.ex, :] = rows[EDGE:]

    def layers_of(k):
        some = range(0 if k == 0 else 1, EDGE)
        return list(some) + [s.ex - 1 - a for a in some]

    def tile_of(k, f, a):
        return states[k][f, a if a < EDGE else a - s.ex + 2 * EDGE]

    slab_parts(s, rows_of, tile_of, layers_of, put)


WTOP, WPAD = 12, 40
BLOCK = slice(8, 32)


def assemble(s, c0, cw, lo, hi, below, above, pad, wind):
    q, x, y, z = s.q, s.x, s.y, s.z
    flat = pad.reshape(q * s.ep * WPAD, z)
    flat_wind = wind.reshape(3 * s.ex * 24, z)
    for f in range(q):
        for at in range(-3, x + 3):
            pad[f, at + 3, WTOP : WTOP + y, :] = layer_of(s, c0, lo, hi, f, at, 3, 0)
    for d in range(3):
        for at in range(-2, x + 2):
            wind[d, at + 2, 4 : 4 + y, :] = layer_of(s, cw, lo, hi, d, at, 2, 3 * q)
    for src, rows, start in zip((below, above), y_rows(s, q, 3), (WTOP - 3, WTOP + y)):
        for m, r, e, at in rows:
            count = x + 2 * e
            flat[pl.ds((m * s.ep + 3 - e) * WPAD + start + r, count, stride=WPAD), :] = src[at : at + count, :]
    for src, rows, start in zip((below, above), y_rows(s, 3, 2), (2, 4 + y)):
        for m, r, e, at in rows:
            count, at = x + 2 * e, at + s.rows_f
            flat_wind[pl.ds((m * s.ex + 2 - e) * 24 + start + r, count, stride=24), :] = src[at : at + count, :]


def edge_lanes(s, lane, width):
    return (lane < width) | (lane >= s.z - width)


def zpack_kernel(s, c0, cw, lo, hi, below, above, out, pad, wind):
    assemble(s, c0, cw, lo, hi, below, above, pad, wind)
    lane = lanes_of((24, s.z))
    keep = edge_lanes(s, lane, 3)
    for m in range(s.q + 3):
        total = None
        for a in range(s.ex):
            tile = pad[m, a + 1, BLOCK, :] if m < s.q else wind[m - s.q, a]
            part = pltpu.roll(jnp.where(keep, tile, 0.0), (6 * a + 3) % s.z, 1)
            total = part if total is None else total + part
        out[m] = total


def coarse_kernel(
    s, sides, c0, cw, lo, hi, below, above, zown, zin, out, pad0, pad1, pad2, wind, beyond, nearest
):
    q, x, y, z = s.q, s.x, s.y, s.z
    assemble(s, c0, cw, lo, hi, below, above, pad0, wind)
    pads = (pad0, pad1, pad2)
    lane = lanes_of((24, z))
    group = lane % 6
    from_low = group == 2
    from_high = group == 3
    exists = jnp.where(group < 3, sides[0, 0], sides[0, 1]).astype(F32)
    co_z = coefficients([zin[q + d] for d in range(3)])
    for f in range(q):
        beyond[0, f] = zin[f] * exists
        nearest[0, f] = zown[f]
    for step in range(3):
        src, fraction = pads[step], section_weights[step]
        flat = src.reshape(q * s.ep * WPAD, z)
        flat_wind = wind.reshape(3 * s.ex * 24, z)
        flat_beyond = beyond.reshape(3 * q * 24, z)
        skip, height = (0, 24) if step < 2 else (4, y)
        here = lanes_of((height, z))
        is_first, is_last = here == 0, here == z - 1

        def layer(a, packed, step=step, src=src, flat=flat, fraction=fraction, skip=skip, height=height):
            made = []
            if step < 2:
                co = coefficients([wind[d, a] for d in range(3)])
            else:
                co = coefficients([flat_wind[pl.ds((d * s.ex + a) * 24 + skip, height), :] for d in range(3)])
            for f in range(q):
                row = (f * s.ep + a + 1) * WPAD + 8 + skip

                def at_layer(of, layer, row, f=f):
                    return of[f, layer, BLOCK, :] if step < 2 else of.reshape(flat.shape)[pl.ds(row, height), :]

                center = at_layer(src, a + 1, row)
                ghost = pltpu.roll(flat_beyond[pl.ds((step * q + f) * 24 + skip, height), :], 2 * z - 6 * a - 3, 1)
                rate = rate_of(
                    co,
                    center,
                    at_layer(src, a, row - WPAD),
                    at_layer(src, a + 2, row + WPAD),
                    flat[pl.ds(row - 1, height), :],
                    flat[pl.ds(row + 1, height), :],
                    pltpu.roll(jnp.where(is_last, ghost, center), 1, 1),
                    pltpu.roll(jnp.where(is_first, ghost, center), z - 1, 1),
                )
                base = center if step == 0 else at_layer(pad0, a + 1, row)
                value = base + fraction * rate
                if step == 2:
                    out[f, a - 2] = value
                else:
                    pads[step + 1][f, a + 1, BLOCK, :] = value
                if step == 0:
                    made.append(packed[f] + pltpu.roll(jnp.where(is_first | is_last, value, 0.0), 6 * a + 3, 1))
            return tuple(made)

        begin, end = step, s.ex - step
        start = tuple(jnp.zeros((24, z), F32) for _ in range(q)) if step == 0 else ()
        packed = unrolled(begin, end, 4 + 2 * (step == 1), layer, start)
        if step == 2:
            break
        for f in range(q):
            if step == 0:
                nearest[1, f] = packed[f]
            ghost, near = beyond[step, f], nearest[step, f]
            rate = rate_of(
                co_z,
                ghost,
                pltpu.roll(ghost, 6, 1),
                pltpu.roll(ghost, z - 6, 1),
                pltpu.roll(ghost, 1, 0),
                pltpu.roll(ghost, 23, 0),
                pltpu.roll(jnp.where(from_low, near, ghost), 1, 1),
                pltpu.roll(jnp.where(from_high, near, ghost), z - 1, 1),
            )
            beyond[step + 1, f] = (beyond[0, f] + fraction * rate) * exists


def fine_kernel(s, f0, fw, flo, fhi, slab, out, avg, *scratch):
    s1, s2, faces, ghost_rows, zface, sems = scratch
    states = (None, s1, s2, s1)
    q, y, z, fx, fe = s.q, s.y, s.z, s.fx, s.fe
    layers = fx + 6
    rows = slice(TOP, TOP + y)
    r = lax.broadcasted_iota(jnp.int32, (z, 2 * z), 0)
    c = lax.broadcasted_iota(jnp.int32, (z, 2 * z), 1)
    near = c // 2
    far = near + 2 * (c % 2) - 1
    same = (far // s.sz == near // s.sz) & (far >= 0)
    to_fine = jnp.where(r == near, 0.75, jnp.where((r == far) & same, 0.25, 0.0)).astype(BF16)
    wide = times(slab[: s.rows_y, :], to_fine)
    ends = slab[s.rows_y : s.rows_y + s.ex, :]
    lane_x = lanes_of((s.ex, z))
    edge = (lane_x == 0) | (lane_x == z - 1)
    half = fe // 2
    for k in range(3):
        for f in range(q):
            for side in range(2):
                e = 4 * (q * k + f) + 2 * side + 1
                corner = jnp.where(edge, 0.25 * pltpu.roll(ends, z - e, 1), 0.0)
                first = (k * q + f) * s.ex
                here = faces.at[(k * q + f) * 2 + side]
                here[: s.ex, :] = wide[first : first + s.ex, side * z : side * z + z] + corner
                a = here[0:half, :]
                b = here[1 : half + 1, :]
                d = here[2 : half + 2, :]
                if k == 0:
                    flat, base, stride = ghost_rows, (2 * f + side) * fe, 1
                else:
                    flat, stride = states[k].reshape(q * layers * PAD, z), PAD
                    base = (f * layers + 1) * PAD + (TOP - 1 if side == 0 else TOP + y)
                flat[pl.ds(base, half, stride=2 * stride), :] = 0.25 * a + 0.75 * b
                flat[pl.ds(base + stride, half, stride=2 * stride), :] = 0.75 * b + 0.25 * d
    for f in range(q):
        at = s.rows_e + f * s.rows_z
        a = slab[at : at + s.sy, :]
        b = slab[at + 1 : at + 1 + s.sy, :]
        d = slab[at + 2 : at + 2 + s.sy, :]
        zface[pl.ds(f * y, s.sy, stride=2), :] = 0.25 * a + 0.75 * b
        zface[pl.ds(f * y + 1, s.sy, stride=2), :] = 0.75 * b + 0.25 * d
        a = zface[f * y : f * y + y, :]
        b = pltpu.roll(a, z - 2, 1)
        d = pltpu.roll(a, z - 4, 1)
        zface[f * y : f * y + y, :] = 0.25 * a + 0.75 * b
        zface[(q + f) * y : (q + f + 1) * y, :] = 0.75 * b + 0.25 * d
    lane = lanes_of((y, z))
    is_first, is_last = lane == 0, lane == z - 1
    row_in = lax.broadcasted_iota(jnp.int32, (y, z), 0)
    is_low, is_high = row_in == 0, row_in == y - 1
    flat_f0 = f0.reshape(q * fx * y, z)

    def pair_of_layers(k, t, inner):
        src = states[k]
        for odd in range(2):
            b = 2 * t + odd
            at = b - 2

            def field(f, at):
                return f0[f, at] if inner else layer_of(s, f0, flo, fhi, f, at, 3, 0)

            if inner:
                winds = [fw[d, at] for d in range(3)]
            else:
                winds = [layer_of(s, fw, flo, fhi, d, at, 2, 3 * q) for d in range(3)]
            co = coefficients(winds)
            for f in range(q):
                if k == 0:
                    center, x_low, x_high = field(f, at), field(f, at - 1), field(f, at + 1)
                    if inner:
                        row = (f * fx + at) * y
                        y_low, y_high = flat_f0[pl.ds(row - 1, y), :], flat_f0[pl.ds(row + 1, y), :]
                    else:
                        y_low, y_high = pltpu.roll(center, 1, 0), pltpu.roll(center, y - 1, 0)
                    y_low = jnp.where(is_low, ghost_rows[pl.ds(2 * f * fe + b, 1), :], y_low)
                    y_high = jnp.where(is_high, ghost_rows[pl.ds((2 * f + 1) * fe + b, 1), :], y_high)
                    base = center
                else:
                    flat = src.reshape(q * layers * PAD, z)
                    row = (f * layers + b + 1) * PAD + TOP
                    center, x_low, x_high = src[f, b + 1, rows, :], src[f, b, rows, :], src[f, b + 2, rows, :]
                    y_low, y_high = flat[pl.ds(row - 1, y), :], flat[pl.ds(row + 1, y), :]
                    base = field(f, at)
                ghost = zface[(odd * q + f) * y : (odd * q + f + 1) * y, :]
                ghost = pltpu.roll(ghost, (2 * z - 2 * s.ex * k - 2 * t) if inner else -(2 * s.ex * k + 2 * t) % z, 1)
                rate = rate_of(
                    co,
                    center,
                    x_low,
                    x_high,
                    y_low,
                    y_high,
                    pltpu.roll(jnp.where(is_last, ghost, center), 1, 1),
                    pltpu.roll(jnp.where(is_first, ghost, center), z - 1, 1),
                )
                states[k + 1][f, b + 1, rows, :] = base + section_weights[k] * rate

    moves = []
    for k in range(3):
        if k < 2:
            outer = 2 - k
            for t in list(range(outer)) + list(range(half - outer, half)):
                pair_of_layers(k, t, False)
            unrolled(outer, half - outer, 2, lambda t, g, k=k: pair_of_layers(k, t, True))
            continue
        part = (half - 2) // 4
        for i in range(4):
            unrolled(1 + i * part, 1 + (i + 1) * part, 2, lambda t, g, k=k: pair_of_layers(k, t, True))
            begin, end = 2 * part * i, 2 * part * (i + 1)
            moves.append(pltpu.make_async_copy(s1.at[:, 3 + begin : 3 + end, rows], out.at[:, begin:end], sems.at[i]))
            moves[-1].start()
    rz = lax.broadcasted_iota(jnp.int32, (z, z), 0)
    cz = lax.broadcasted_iota(jnp.int32, (z, z), 1)
    flat = s1.reshape(q * layers * PAD, z)
    pairs_z = [jnp.where(cz == rz // 2 + odd * s.sz, 0.125, 0.0).astype(BF16) for odd in range(2)]
    for f in range(q):
        sums = []
        for odd in range(2):
            parts = []
            for p in range(s.x // 2):
                base = (f * layers + 3 + 4 * p + 2 * odd) * PAD + TOP
                part = None
                for more in (0, 1, PAD, PAD + 1):
                    piece = flat[pl.ds(base + more, y // 2, stride=2), :]
                    part = piece if part is None else part + piece
                parts.append(part)
            sums.append(times(jnp.concatenate(parts, axis=0), pairs_z[odd]))
        avg[f] = (sums[0] + sums[1]).reshape(s.x // 2, y // 2, z)
    for move in moves:
        move.wait()


def merge_kernel(s, c3, avg, out, made, sems):
    lane = lanes_of((s.sy, s.z))
    inside = (lane >= s.lz) & (lane < s.lz + s.sz)
    moves = []
    for f in range(s.q):
        for p in range(s.x // 2):
            both = avg[f, p]
            for odd in range(2):
                at = 2 * p + odd
                moved = pltpu.roll(both, s.lz if odd == 0 else s.z - s.lz, 1)
                made[f, at] = c3[f, at]
                made[f, at, s.ly : s.ly + s.sy, :] = jnp.where(inside, moved, c3[f, at, s.ly : s.ly + s.sy, :])
        moves.append(pltpu.make_async_copy(made.at[f], out.at[f], sems.at[f]))
        moves[-1].start()
    for move in moves:
        move.wait()


SHORT = pl.CostEstimate(flops=1, bytes_accessed=1, transcendentals=0)


def run(kernel, name, ins, outs, scratch, megabytes, spaces=None, cost=SHORT):
    spaces = spaces or [pltpu.VMEM] * len(ins)
    outs = [out if isinstance(out[0], tuple) else (out, pltpu.VMEM) for out in outs]
    ins = [i if space is pltpu.SMEM else pltpu.with_memory_space_constraint(i, space) for i, space in zip(ins, spaces)]
    return pl.pallas_call(
        kernel,
        out_shape=tuple(space(dims, F32) for dims, space in outs),
        in_specs=[pl.BlockSpec(memory_space=space) for space in spaces],
        out_specs=tuple(pl.BlockSpec(memory_space=space) for _, space in outs),
        scratch_shapes=scratch,
        compiler_params=pltpu.CompilerParams(vmem_limit_bytes=megabytes << 20),
        cost_estimate=cost,
        name=name,
    )(*ins)


def ring(array, axis, by):
    size = lax.axis_size(axis)
    return lax.ppermute(array, axis, [(i, (i + by) % size) for i in range(size)])


def move_by(array, amount, beside=None):
    size = lax.axis_size("gx")
    work, operands = beside or (lambda: (), ())
    if size <= 8:

        def branch(by, array, *operands):
            return array if by == 0 else ring(array, "gx", by), work(*operands)

        return lax.switch(amount, [functools.partial(branch, by) for by in range(size)], array, *operands)
    for bit in range((size - 1).bit_length()):
        array = jnp.where((amount >> bit) % 2 == 1, ring(array, "gx", 1 << bit), array)
    return array, work(*operands)


def z_columns(zown):
    size = lax.axis_size("gz")
    if size == 1:
        return zown
    if size == 2:
        return lax.ppermute(zown, "gz", [(0, 1), (1, 0)])
    below = lax.broadcasted_iota(jnp.int32, zown.shape, 2) % 6 < 3
    return jnp.where(below, ring(zown, "gz", 1), ring(zown, "gz", -1))


def pack(s, fields, wind, spare, name):
    return run(
        functools.partial(pack_kernel, s),
        name,
        [fields, wind],
        [(s.halo + spare, s.y, s.z)] * 2,
        [pltpu.SemaphoreType.DMA((4,))],
        4,
        [pltpu.HBM] * 2,
    )


def shards(coarse_fields, coarse_wind, fine_fields, fine_wind, fine_owner):
    s = Sizes(coarse_fields.shape, fine_fields.shape)
    q, x, y, z, fx = s.q, s.x, s.y, s.z, s.fx
    size = lax.axis_size("gx")
    offset = (fine_owner[0, 0, 0] - lax.axis_index("gx")) % size
    level = lax.axis_index("gz")
    neighbours = jnp.stack([level > 0, level < lax.axis_size("gz") - 1]).astype(jnp.int32).reshape(1, 2)
    cup, cdown = pack(s, coarse_fields, coarse_wind, 0, "pack_coarse")
    lo, hi = ring(cup, "gx", 1), ring(cdown, "gx", -1)
    part, near = run(
        functools.partial(inner_kernel, s),
        "inner",
        [coarse_fields, coarse_wind],
        [(s.slab, z), (q, 2, y, z)],
        [pltpu.VMEM((q, x, y, z), F32)] * 2,
        6,
    )
    fup, fdown = pack(s, fine_fields, fine_wind, 2, "pack_fine")
    fup, fdown, part, near, offset = lax.optimization_barrier((fup, fdown, part, near, offset))
    flo, fhi = ring(fup, "gx", 1), ring(fdown, "gx", -1)
    coarse_level = [coarse_fields, coarse_wind, lo, hi]
    yup, ydn = run(functools.partial(ypack_kernel, s), "ypack", coarse_level, [(s.rows_f + s.rows_w, z)] * 2, [], 4)
    yrows = [ring(yup, "gy", 1), ring(ydn, "gy", -1)]
    ends = [pltpu.VMEM((q, 2 * EDGE, y, z), F32)] * 3
    (slab,) = run(functools.partial(slab_kernel, s), "slab", coarse_level + [part, near], [(s.slab, z)], ends, 6)
    yrows, slab, flo, fhi = lax.optimization_barrier((yrows, slab, flo, fhi))
    padded = [pltpu.VMEM((q, s.ep, WPAD, z), F32)]
    wind_rows = [pltpu.VMEM((3, s.ex, 24, z), F32)]

    def zpack(*ins):
        cost = pl.CostEstimate(flops=4_000_000, bytes_accessed=2_000_000, transcendentals=0)
        kernel = functools.partial(zpack_kernel, s)
        return run(kernel, "zpack", ins, [(q + 3, 24, z)], padded + wind_rows, 6, cost=cost)[0]

    slab, zown = move_by(slab, (size - offset) % size, (zpack, (*coarse_level, *yrows)))
    zin = z_columns(zown)
    layers = fx + 6
    fine_next, averaged = run(
        functools.partial(fine_kernel, s),
        "fine",
        [fine_fields, fine_wind, flo, fhi, slab],
        [((q, fx, y, z), pltpu.HBM), (q, x // 2, y // 2, z)],
        [
            pltpu.VMEM((q, layers, PAD, z), F32),
            pltpu.VMEM((q, layers, PAD, z), F32),
            pltpu.VMEM((6 * q, s.ep, z), F32),
            pltpu.VMEM((2 * q * s.fe, z), F32),
            pltpu.VMEM((2 * q * y, z), F32),
            pltpu.SemaphoreType.DMA((4,)),
        ],
        10,
    )

    def coarse(*ins):
        cost = pl.CostEstimate(flops=40_000_000, bytes_accessed=4_000_000, transcendentals=0)
        columns = [pltpu.VMEM((3, q, 24, z), F32), pltpu.VMEM((2, q, 24, z), F32)]
        spaces = [pltpu.SMEM] + [pltpu.VMEM] * (len(ins) - 1)
        kernel = functools.partial(coarse_kernel, s)
        return run(kernel, "coarse", ins, [(q, x, y, z)], padded * 3 + wind_rows + columns, 12, spaces, cost)[0]

    averaged, state = move_by(averaged, offset, (coarse, (neighbours, *coarse_level, *yrows, zown, zin)))
    (coarse_next,) = run(
        functools.partial(merge_kernel, s),
        "merge",
        [state, averaged],
        [((q, x, y, z), pltpu.HBM)],
        [pltpu.VMEM((q, x, y, z), F32), pltpu.SemaphoreType.DMA((q,))],
        4,
    )
    return coarse_next, fine_next


def solution(mesh):
    spec = P(None, "gx", "gy", "gz")
    return jax.shard_map(
        shards,
        mesh=mesh,
        in_specs=(spec, spec, spec, spec, P("gx", "gy", "gz")),
        out_specs=(spec, spec),
        check_vma=False,
    )
```

```python
import functools

import jax
import jax.numpy as jnp
from jax import lax
from jax.experimental import pallas as pl
from jax.experimental.pallas import tpu as pltpu
from jax.sharding import PartitionSpec as P

diffusion = 0.05
section_weights = (1.0 / 3.0, 0.5, 1.0)
F32 = jnp.float32
BF16 = jnp.bfloat16
PAD = 32
TOP = 8


class Sizes:
    def __init__(self, coarse_shape, fine_shape):
        self.q, self.x, self.y, self.z = coarse_shape
        self.fx = fine_shape[1]
        self.ly, self.sy = self.y // 4, self.y // 2
        self.lz, self.sz = self.z // 4, self.z // 2
        self.ex = self.x + 4
        self.ep = -(-self.ex // 8) * 8
        self.fe = self.fx + 4
        self.halo = 3 * self.q + 6
        self.rows_f, self.rows_w = self.q * (3 * self.x + 6), 3 * (2 * self.x + 2)
        self.rows_y = 3 * self.q * self.ex
        self.rows_e = self.rows_y + self.ep
        self.rows_z = self.sy + 2
        self.slab = self.rows_e + self.q * self.rows_z
        assert self.q == 4 and self.y == 16 and self.z == 128 and self.ex <= 20 and self.fx == 2 * self.x


def lanes_of(shape):
    return lax.broadcasted_iota(jnp.int32, shape, len(shape) - 1)


def halves(value):
    high = value.astype(BF16)
    return high, (value - high.astype(F32)).astype(BF16)


def times(value, matrix):
    high, low = halves(value)
    return jnp.dot(high, matrix, preferred_element_type=F32) + jnp.dot(low, matrix, preferred_element_type=F32)


def scaled(wind):
    return [w * (-0.5 / diffusion) for w in wind]


def advanced(base, fraction, wind, center, x_low, x_high, y_low, y_high, z_low, z_high):
    total = (x_high + x_low) + wind[0] * (x_high - x_low)
    total = total + ((y_high + y_low) + wind[1] * (y_high - y_low))
    total = total + ((z_high + z_low) + wind[2] * (z_high - z_low))
    if base is None:
        return center * (1.0 - 6.0 * diffusion * fraction) + total * (diffusion * fraction)
    return (base - center * (6.0 * diffusion * fraction)) + total * (diffusion * fraction)


def layer_of(s, own, low, high, member, at, width, first):
    size = own.shape[1]
    if at < 0:
        return low[first + width * member + at + width]
    if at >= size:
        return high[first + width * member + at - size]
    return own[member, at]


def unrolled(begin, end, at_once, body, carry=None):
    while (end - begin) % at_once:
        at_once -= 1

    def several(i, carry):
        for more in range(at_once):
            carry = body(begin + i * at_once + more, carry)
        return carry

    return lax.fori_loop(0, (end - begin) // at_once, several, carry)


def pack_kernel(s, fields, wind, up, down, sems):
    size = fields.shape[1]
    moves = []
    for own, members, width, first in ((fields, s.q, 3, 0), (wind, 3, 2, 3 * s.q)):
        for dst, at in ((up, size - width), (down, 0)):
            place = dst.at[first : first + members * width].reshape(members, width, s.y, s.z)
            moves.append((own.at[:, at : at + width], place))
    moves = [pltpu.make_async_copy(src, dst, sems.at[i]) for i, (src, dst) in enumerate(moves)]
    for move in moves:
        move.start()
    for move in moves:
        move.wait()


def y_rows(s, members, width):
    below, above = [], []
    for out, extra in ((below, lambda r: r), (above, lambda r: width - 1 - r)):
        at = 0
        for m in range(members):
            for r in range(width):
                out.append((m, r, extra(r), at))
                at += s.x + 2 * extra(r)
    return below, above


def ypack_kernel(s, c0, cw, lo, hi, up, dn):
    x, y, z = s.x, s.y, s.z
    flat_lo = lo.reshape(s.halo * y, z)
    flat_hi = hi.reshape(s.halo * y, z)
    for own, members, width, first, place in ((c0, s.q, 3, 0, 0), (cw, 3, 2, 3 * s.q, s.rows_f)):
        flat = own.reshape(members * x * y, z)
        for dst, rows, start in zip((up, dn), y_rows(s, members, width), (y - width, 0)):
            for m, r, e, at in rows:
                row, at = start + r, at + place
                if e:
                    dst[at : at + e, :] = flat_lo[pl.ds((first + width * (m + 1) - e) * y + row, e, stride=y), :]
                    dst[at + e + x : at + x + 2 * e, :] = flat_hi[pl.ds((first + width * m) * y + row, e, stride=y), :]
                dst[at + e : at + e + x, :] = flat[pl.ds(m * x * y + row, x, stride=y), :]


EDGE = 4


def turned(base, fraction, wind, center, x_low, x_high):
    y, z = center.shape
    return advanced(
        base,
        fraction,
        wind,
        center,
        x_low,
        x_high,
        pltpu.roll(center, 1, 0),
        pltpu.roll(center, y - 1, 0),
        pltpu.roll(center, 1, 1),
        pltpu.roll(center, z - 1, 1),
    )


def slab_parts(s, rows_of, tile_of, layers_of, put):
    q, y, z = s.q, s.y, s.z
    lane_y = lanes_of((y, z))
    columns = (lane_y == s.lz - 1) | (lane_y == s.lz) | (lane_y == s.lz + s.sz - 1) | (lane_y == s.lz + s.sz)
    low_at = (lane_y % 2 == 0) & (lane_y < z // 2)
    high_at = (lane_y % 2 == 0) & (lane_y >= z // 2)
    ends = None
    for f in range(q):
        zfaces = None
        for k in range(3):
            rows = [rows_of(k, f, row) for row in (s.ly - 1, s.ly, s.ly + s.sy - 1, s.ly + s.sy)]
            sides = (0.75 * rows[0] + 0.25 * rows[1], 0.25 * rows[2] + 0.75 * rows[3])
            lane_x = lanes_of(sides[0].shape)
            put(
                "y",
                (k * q + f) * s.ex,
                jnp.where(lane_x < s.sz, pltpu.roll(sides[0], z - s.lz, 1), pltpu.roll(sides[1], s.lz, 1)),
            )
            for side in range(2):
                e = 4 * (q * k + f) + 2 * side + 1
                before = jnp.where(lane_x == s.lz - 1, sides[side], 0.0)
                after = jnp.where(lane_x == s.lz + s.sz, sides[side], 0.0)
                part = pltpu.roll(before, (e - s.lz + 1) % z, 1) + pltpu.roll(after, (e - 1 - s.lz - s.sz) % z, 1)
                ends = part if ends is None else ends + part
            raw = None
            for a in layers_of(k):
                part = jnp.where(columns, tile_of(k, f, a), 0.0)
                part = pltpu.roll(part, (2 * a - s.lz + 1) % z, 1)
                raw = part if raw is None else raw + part
            beside = pltpu.roll(raw, z - 1, 1)
            low = jnp.where(low_at, 0.75 * raw + 0.25 * beside, 0.0)
            high = jnp.where(high_at, 0.25 * raw + 0.75 * beside, 0.0)
            part = pltpu.roll(low, (2 * s.ex * k - 1) % z, 1) + pltpu.roll(high, (2 * s.ex * k - z // 2) % z, 1)
            zfaces = part if zfaces is None else zfaces + part
        put("z", s.rows_e + f * s.rows_z, zfaces[s.ly - 1 : s.ly + s.sy + 1])
    put("e", s.rows_y, ends)


def inner_kernel(s, c0, cw, part, near, state1, state2):
    q, x, y, z = s.q, s.x, s.y, s.z
    states = (c0, state1, state2)
    for step in range(2):
        src, dst = states[step], states[step + 1]

        def layer(j, carry, step=step, src=src, dst=dst):
            w = scaled([cw[d, j] for d in range(3)])
            for f in range(q):
                base = None if step == 0 else c0[f, j]
                dst[f, j] = turned(base, section_weights[step], w, src[f, j], src[f, j - 1], src[f, j + 1])
            return carry

        unrolled(step + 1, x - 1 - step, 7 if step == 0 else 6, layer)
    for f in range(q):
        near[f, 0] = state1[f, EDGE - 2]
        near[f, 1] = state1[f, x + 1 - EDGE]
    count = s.ex - 2 * EDGE
    part[...] = jnp.zeros_like(part)

    def rows_of(k, f, row):
        flat = states[k].reshape(q * x * y, z)
        return flat[pl.ds((f * x + EDGE - 2) * y + row, count, stride=y), :]

    def put(kind, at, rows):
        if kind == "z":
            part[at : at + s.rows_z, :] = rows
        else:
            part[at + EDGE : at + EDGE + count, :] = rows

    slab_parts(s, rows_of, lambda k, f, a: states[k][f, a - 2], lambda k: range(EDGE, s.ex - EDGE), put)


def slab_kernel(s, c0, cw, lo, hi, part, near, slab, ends0, ends1, ends2):
    q, x, y, z = s.q, s.x, s.y, s.z
    states = (ends0, ends1, ends2)
    places = list(range(-2, EDGE - 2)) + list(range(x + 2 - EDGE, x + 2))
    slab[...] = part[...]
    for j, at in enumerate(places):
        for f in range(q):
            ends0[f, j] = layer_of(s, c0, lo, hi, f, at, 3, 0)
    for step in range(2):
        for j, at in enumerate(places):
            if step == 1 and at in (-2, x + 1):
                for f in range(q):
                    ends2[f, j] = jnp.zeros((y, z), F32)
                continue
            w = scaled([layer_of(s, cw, lo, hi, d, at, 2, 3 * q) for d in range(3)])
            for f in range(q):

                def beside(at, f=f):
                    if step == 0:
                        return layer_of(s, c0, lo, hi, f, at, 3, 0)
                    if at in places:
                        return ends1[f, places.index(at)]
                    return near[f, 0 if at < x // 2 else 1]

                base = None if step == 0 else ends0[f, j]
                states[step + 1][f, j] = turned(
                    base, section_weights[step], w, beside(at), beside(at - 1), beside(at + 1)
                )

    def rows_of(k, f, row):
        flat = states[k].reshape(q * 2 * EDGE * y, z)
        return flat[pl.ds(f * 2 * EDGE * y + row, 2 * EDGE, stride=y), :]

    def put(kind, at, rows):
        if kind == "z":
            slab[at : at + s.rows_z, :] = part[at : at + s.rows_z, :] + rows
        else:
            slab[at : at + EDGE, :] = rows[:EDGE]
            slab[at + s.ex - EDGE : at + s.ex, :] = rows[EDGE:]

    def layers_of(k):
        some = range(0 if k == 0 else 1, EDGE)
        return list(some) + [s.ex - 1 - a for a in some]

    def tile_of(k, f, a):
        return states[k][f, a if a < EDGE else a - s.ex + 2 * EDGE]

    slab_parts(s, rows_of, tile_of, layers_of, put)


WTOP, WPAD = 12, 40
BLOCK = slice(8, 32)


def assemble(s, c0, cw, lo, hi, below, above, pad, wind):
    q, x, y, z = s.q, s.x, s.y, s.z
    flat = pad.reshape(q * s.ep * WPAD, z)
    flat_wind = wind.reshape(3 * s.ex * 24, z)
    for f in range(q):
        for at in range(-3, x + 3):
            pad[f, at + 3, WTOP : WTOP + y, :] = layer_of(s, c0, lo, hi, f, at, 3, 0)
    for d in range(3):
        for at in range(-2, x + 2):
            wind[d, at + 2, 4 : 4 + y, :] = layer_of(s, cw, lo, hi, d, at, 2, 3 * q)
    for src, rows, start in zip((below, above), y_rows(s, q, 3), (WTOP - 3, WTOP + y)):
        for m, r, e, at in rows:
            count = x + 2 * e
            flat[pl.ds((m * s.ep + 3 - e) * WPAD + start + r, count, stride=WPAD), :] = src[at : at + count, :]
    for src, rows, start in zip((below, above), y_rows(s, 3, 2), (2, 4 + y)):
        for m, r, e, at in rows:
            count, at = x + 2 * e, at + s.rows_f
            flat_wind[pl.ds((m * s.ex + 2 - e) * 24 + start + r, count, stride=24), :] = src[at : at + count, :]


def edge_lanes(s, lane, width):
    return (lane < width) | (lane >= s.z - width)


def zpack_kernel(s, c0, cw, lo, hi, below, above, out, pad, wind):
    assemble(s, c0, cw, lo, hi, below, above, pad, wind)
    lane = lanes_of((24, s.z))
    keep = edge_lanes(s, lane, 3)
    for m in range(s.q + 3):
        total = None
        for a in range(s.ex):
            tile = pad[m, a + 1, BLOCK, :] if m < s.q else wind[m - s.q, a]
            part = pltpu.roll(jnp.where(keep, tile, 0.0), (6 * a + 3) % s.z, 1)
            total = part if total is None else total + part
        out[m] = total


def coarse_kernel(
    s, sides, c0, cw, lo, hi, below, above, zown, zin, out, pad0, pad1, pad2, wind, beyond, nearest
):
    q, x, y, z = s.q, s.x, s.y, s.z
    assemble(s, c0, cw, lo, hi, below, above, pad0, wind)
    pads = (pad0, pad1, pad2)
    lane = lanes_of((24, z))
    group = lane % 6
    from_low = group == 2
    from_high = group == 3
    exists = jnp.where(group < 3, sides[0, 0], sides[0, 1]).astype(F32)
    wind_z = scaled([zin[q + d] for d in range(3)])
    for f in range(q):
        beyond[0, f] = zin[f] * exists
        nearest[0, f] = zown[f]
    for step in range(3):
        src, fraction = pads[step], section_weights[step]
        flat = src.reshape(q * s.ep * WPAD, z)
        flat_wind = wind.reshape(3 * s.ex * 24, z)
        flat_beyond = beyond.reshape(3 * q * 24, z)
        skip, height = (0, 24) if step < 2 else (4, y)
        here = lanes_of((height, z))
        is_first, is_last = here == 0, here == z - 1

        def layer(a, packed, step=step, src=src, flat=flat, fraction=fraction, skip=skip, height=height):
            made = []
            if step < 2:
                w = scaled([wind[d, a] for d in range(3)])
            else:
                w = scaled([flat_wind[pl.ds((d * s.ex + a) * 24 + skip, height), :] for d in range(3)])
            for f in range(q):
                row = (f * s.ep + a + 1) * WPAD + 8 + skip

                def at_layer(of, layer, row, f=f):
                    return of[f, layer, BLOCK, :] if step < 2 else of.reshape(flat.shape)[pl.ds(row, height), :]

                center = at_layer(src, a + 1, row)
                ghost = pltpu.roll(flat_beyond[pl.ds((step * q + f) * 24 + skip, height), :], 2 * z - 6 * a - 3, 1)
                value = advanced(
                    None if step == 0 else at_layer(pad0, a + 1, row),
                    fraction,
                    w,
                    center,
                    at_layer(src, a, row - WPAD),
                    at_layer(src, a + 2, row + WPAD),
                    flat[pl.ds(row - 1, height), :],
                    flat[pl.ds(row + 1, height), :],
                    pltpu.roll(jnp.where(is_last, ghost, center), 1, 1),
                    pltpu.roll(jnp.where(is_first, ghost, center), z - 1, 1),
                )
                if step == 2:
                    out[f, a - 2] = value
                else:
                    pads[step + 1][f, a + 1, BLOCK, :] = value
                if step == 0:
                    made.append(packed[f] + pltpu.roll(jnp.where(is_first | is_last, value, 0.0), 6 * a + 3, 1))
            return tuple(made)

        begin, end = step, s.ex - step
        start = tuple(jnp.zeros((24, z), F32) for _ in range(q)) if step == 0 else ()
        packed = unrolled(begin, end, 4 + 2 * (step == 1), layer, start)
        if step == 2:
            break
        for f in range(q):
            if step == 0:
                nearest[1, f] = packed[f]
            ghost, near = beyond[step, f], nearest[step, f]
            value = advanced(
                None if step == 0 else beyond[0, f],
                fraction,
                wind_z,
                ghost,
                pltpu.roll(ghost, 6, 1),
                pltpu.roll(ghost, z - 6, 1),
                pltpu.roll(ghost, 1, 0),
                pltpu.roll(ghost, 23, 0),
                pltpu.roll(jnp.where(from_low, near, ghost), 1, 1),
                pltpu.roll(jnp.where(from_high, near, ghost), z - 1, 1),
            )
            beyond[step + 1, f] = value * exists


def fine_kernel(s, f0, fw, flo_there, fhi_there, slab, out, avg, *scratch):
    s1, s2, faces, ghost_rows, zface, flo, fhi, sems = scratch
    arrivals = [
        pltpu.make_async_copy(flo_there, flo, sems.at[4]),
        pltpu.make_async_copy(fhi_there, fhi, sems.at[5]),
    ]
    for move in arrivals:
        move.start()
    states = (None, s1, s2, s1)
    q, y, z, fx, fe = s.q, s.y, s.z, s.fx, s.fe
    layers = fx + 6
    rows = slice(TOP, TOP + y)
    r = lax.broadcasted_iota(jnp.int32, (z, 2 * z), 0)
    c = lax.broadcasted_iota(jnp.int32, (z, 2 * z), 1)
    near = c // 2
    far = near + 2 * (c % 2) - 1
    same = (far // s.sz == near // s.sz) & (far >= 0)
    to_fine = jnp.where(r == near, 0.75, jnp.where((r == far) & same, 0.25, 0.0)).astype(BF16)
    wide = times(slab[: s.rows_y, :], to_fine)
    ends = slab[s.rows_y : s.rows_y + s.ex, :]
    lane_x = lanes_of((s.ex, z))
    edge = (lane_x == 0) | (lane_x == z - 1)
    half = fe // 2
    for k in range(3):
        for f in range(q):
            for side in range(2):
                e = 4 * (q * k + f) + 2 * side + 1
                corner = jnp.where(edge, 0.25 * pltpu.roll(ends, z - e, 1), 0.0)
                first = (k * q + f) * s.ex
                here = faces.at[(k * q + f) * 2 + side]
                here[: s.ex, :] = wide[first : first + s.ex, side * z : side * z + z] + corner
                a = here[0:half, :]
                b = here[1 : half + 1, :]
                d = here[2 : half + 2, :]
                if k == 0:
                    flat, base, stride = ghost_rows, (2 * f + side) * fe, 1
                else:
                    flat, stride = states[k].reshape(q * layers * PAD, z), PAD
                    base = (f * layers + 1) * PAD + (TOP - 1 if side == 0 else TOP + y)
                flat[pl.ds(base, half, stride=2 * stride), :] = 0.25 * a + 0.75 * b
                flat[pl.ds(base + stride, half, stride=2 * stride), :] = 0.75 * b + 0.25 * d
    for f in range(q):
        at = s.rows_e + f * s.rows_z
        a = slab[at : at + s.sy, :]
        b = slab[at + 1 : at + 1 + s.sy, :]
        d = slab[at + 2 : at + 2 + s.sy, :]
        zface[pl.ds(f * y, s.sy, stride=2), :] = 0.25 * a + 0.75 * b
        zface[pl.ds(f * y + 1, s.sy, stride=2), :] = 0.75 * b + 0.25 * d
        a = zface[f * y : f * y + y, :]
        b = pltpu.roll(a, z - 2, 1)
        d = pltpu.roll(a, z - 4, 1)
        zface[f * y : f * y + y, :] = 0.25 * a + 0.75 * b
        zface[(q + f) * y : (q + f + 1) * y, :] = 0.75 * b + 0.25 * d
    lane = lanes_of((y, z))
    is_first, is_last = lane == 0, lane == z - 1
    row_in = lax.broadcasted_iota(jnp.int32, (y, z), 0)
    is_low, is_high = row_in == 0, row_in == y - 1
    flat_f0 = f0.reshape(q * fx * y, z)

    def pair_of_layers(k, t, inner):
        src = states[k]
        for odd in range(2):
            b = 2 * t + odd
            at = b - 2

            def field(f, at):
                return f0[f, at] if inner else layer_of(s, f0, flo, fhi, f, at, 3, 0)

            if inner:
                winds = [fw[d, at] for d in range(3)]
            else:
                winds = [layer_of(s, fw, flo, fhi, d, at, 2, 3 * q) for d in range(3)]
            w = scaled(winds)
            for f in range(q):
                if k == 0:
                    center, x_low, x_high = field(f, at), field(f, at - 1), field(f, at + 1)
                    if inner:
                        row = (f * fx + at) * y
                        y_low, y_high = flat_f0[pl.ds(row - 1, y), :], flat_f0[pl.ds(row + 1, y), :]
                    else:
                        y_low, y_high = pltpu.roll(center, 1, 0), pltpu.roll(center, y - 1, 0)
                    y_low = jnp.where(is_low, ghost_rows[pl.ds(2 * f * fe + b, 1), :], y_low)
                    y_high = jnp.where(is_high, ghost_rows[pl.ds((2 * f + 1) * fe + b, 1), :], y_high)
                    base = None
                else:
                    flat = src.reshape(q * layers * PAD, z)
                    row = (f * layers + b + 1) * PAD + TOP
                    center, x_low, x_high = src[f, b + 1, rows, :], src[f, b, rows, :], src[f, b + 2, rows, :]
                    y_low, y_high = flat[pl.ds(row - 1, y), :], flat[pl.ds(row + 1, y), :]
                    base = field(f, at)
                ghost = zface[(odd * q + f) * y : (odd * q + f + 1) * y, :]
                ghost = pltpu.roll(ghost, (2 * z - 2 * s.ex * k - 2 * t) if inner else -(2 * s.ex * k + 2 * t) % z, 1)
                value = advanced(
                    base,
                    section_weights[k],
                    w,
                    center,
                    x_low,
                    x_high,
                    y_low,
                    y_high,
                    pltpu.roll(jnp.where(is_last, ghost, center), 1, 1),
                    pltpu.roll(jnp.where(is_first, ghost, center), z - 1, 1),
                )
                states[k + 1][f, b + 1, rows, :] = value

    for move in arrivals:
        move.wait()
    moves = []
    for k in range(3):
        if k < 2:
            outer = 2 - k
            for t in list(range(outer)) + list(range(half - outer, half)):
                pair_of_layers(k, t, False)
            unrolled(outer, half - outer, 2, lambda t, g, k=k: pair_of_layers(k, t, True))
            continue
        part = (half - 2) // 4
        for i in range(4):
            unrolled(1 + i * part, 1 + (i + 1) * part, 2, lambda t, g, k=k: pair_of_layers(k, t, True))
            begin, end = 2 * part * i, 2 * part * (i + 1)
            moves.append(pltpu.make_async_copy(s1.at[:, 3 + begin : 3 + end, rows], out.at[:, begin:end], sems.at[i]))
            moves[-1].start()
    rz = lax.broadcasted_iota(jnp.int32, (z, z), 0)
    cz = lax.broadcasted_iota(jnp.int32, (z, z), 1)
    flat = s1.reshape(q * layers * PAD, z)
    pairs_z = [jnp.where(cz == rz // 2 + odd * s.sz, 0.125, 0.0).astype(BF16) for odd in range(2)]
    for f in range(q):
        sums = []
        for odd in range(2):
            parts = []
            for p in range(s.x // 2):
                base = (f * layers + 3 + 4 * p + 2 * odd) * PAD + TOP
                part = None
                for more in (0, 1, PAD, PAD + 1):
                    piece = flat[pl.ds(base + more, y // 2, stride=2), :]
                    part = piece if part is None else part + piece
                parts.append(part)
            sums.append(times(jnp.concatenate(parts, axis=0), pairs_z[odd]))
        avg[f] = (sums[0] + sums[1]).reshape(s.x // 2, y // 2, z)
    for move in moves:
        move.wait()


def merge_kernel(s, c3, avg, out, made, sems):
    lane = lanes_of((s.sy, s.z))
    inside = (lane >= s.lz) & (lane < s.lz + s.sz)
    moves = []
    for f in range(s.q):
        for p in range(s.x // 2):
            both = avg[f, p]
            for odd in range(2):
                at = 2 * p + odd
                moved = pltpu.roll(both, s.lz if odd == 0 else s.z - s.lz, 1)
                made[f, at] = c3[f, at]
                made[f, at, s.ly : s.ly + s.sy, :] = jnp.where(inside, moved, c3[f, at, s.ly : s.ly + s.sy, :])
        moves.append(pltpu.make_async_copy(made.at[f], out.at[f], sems.at[f]))
        moves[-1].start()
    for move in moves:
        move.wait()


SHORT = pl.CostEstimate(flops=1, bytes_accessed=1, transcendentals=0)


def run(kernel, name, ins, outs, scratch, megabytes, spaces=None, cost=SHORT):
    spaces = spaces or [pltpu.VMEM] * len(ins)
    outs = [out if isinstance(out[0], tuple) else (out, pltpu.VMEM) for out in outs]
    ins = [i if space is pltpu.SMEM else pltpu.with_memory_space_constraint(i, space) for i, space in zip(ins, spaces)]
    return pl.pallas_call(
        kernel,
        out_shape=tuple(space(dims, F32) for dims, space in outs),
        in_specs=[pl.BlockSpec(memory_space=space) for space in spaces],
        out_specs=tuple(pl.BlockSpec(memory_space=space) for _, space in outs),
        scratch_shapes=scratch,
        compiler_params=pltpu.CompilerParams(vmem_limit_bytes=megabytes << 20),
        cost_estimate=cost,
        name=name,
    )(*ins)


def ring(array, axis, by):
    size = lax.axis_size(axis)
    return lax.ppermute(array, axis, [(i, (i + by) % size) for i in range(size)])


def move_by(array, amount, beside=None):
    size = lax.axis_size("gx")
    work, operands = beside or (lambda: (), ())
    if size <= 8:

        def branch(by, array, *operands):
            return array if by == 0 else ring(array, "gx", by), work(*operands)

        return lax.switch(amount, [functools.partial(branch, by) for by in range(size)], array, *operands)
    for bit in range((size - 1).bit_length()):
        array = jnp.where((amount >> bit) % 2 == 1, ring(array, "gx", 1 << bit), array)
    return array, work(*operands)


def z_columns(zown):
    size = lax.axis_size("gz")
    if size == 1:
        return zown
    if size == 2:
        return lax.ppermute(zown, "gz", [(0, 1), (1, 0)])
    below = lax.broadcasted_iota(jnp.int32, zown.shape, 2) % 6 < 3
    return jnp.where(below, ring(zown, "gz", 1), ring(zown, "gz", -1))


def pack(s, fields, wind, spare, name):
    return run(
        functools.partial(pack_kernel, s),
        name,
        [fields, wind],
        [(s.halo + spare, s.y, s.z)] * 2,
        [pltpu.SemaphoreType.DMA((4,))],
        4,
        [pltpu.HBM] * 2,
    )


def shards(coarse_fields, coarse_wind, fine_fields, fine_wind, fine_owner):
    s = Sizes(coarse_fields.shape, fine_fields.shape)
    q, x, y, z, fx = s.q, s.x, s.y, s.z, s.fx
    size = lax.axis_size("gx")
    offset = (fine_owner[0, 0, 0] - lax.axis_index("gx")) % size
    level = lax.axis_index("gz")
    neighbours = jnp.stack([level > 0, level < lax.axis_size("gz") - 1]).astype(jnp.int32).reshape(1, 2)
    cup, cdown = pack(s, coarse_fields, coarse_wind, 0, "pack_coarse")
    lo, hi = ring(cup, "gx", 1), ring(cdown, "gx", -1)
    part, near = run(
        functools.partial(inner_kernel, s),
        "inner",
        [coarse_fields, coarse_wind],
        [(s.slab, z), (q, 2, y, z)],
        [pltpu.VMEM((q, x, y, z), F32)] * 2,
        6,
    )
    fup, fdown = pack(s, fine_fields, fine_wind, 2, "pack_fine")
    fup, fdown, part, near, offset = lax.optimization_barrier((fup, fdown, part, near, offset))
    flo, fhi = ring(fup, "gx", 1), ring(fdown, "gx", -1)
    coarse_level = [coarse_fields, coarse_wind, lo, hi]
    yup, ydn = run(functools.partial(ypack_kernel, s), "ypack", coarse_level, [(s.rows_f + s.rows_w, z)] * 2, [], 4)
    yrows = [ring(yup, "gy", 1), ring(ydn, "gy", -1)]
    ends = [pltpu.VMEM((q, 2 * EDGE, y, z), F32)] * 3
    (slab,) = run(functools.partial(slab_kernel, s), "slab", coarse_level + [part, near], [(s.slab, z)], ends, 6)
    yrows, slab, flo, fhi = lax.optimization_barrier((yrows, slab, flo, fhi))
    padded = [pltpu.VMEM((q, s.ep, WPAD, z), F32)]
    wind_rows = [pltpu.VMEM((3, s.ex, 24, z), F32)]

    def zpack(*ins):
        cost = pl.CostEstimate(flops=4_000_000, bytes_accessed=2_000_000, transcendentals=0)
        kernel = functools.partial(zpack_kernel, s)
        return run(kernel, "zpack", ins, [(q + 3, 24, z)], padded + wind_rows, 6, cost=cost)[0]

    slab, zown = move_by(slab, (size - offset) % size, (zpack, (*coarse_level, *yrows)))
    zin = z_columns(zown)
    layers = fx + 6
    fine_next, averaged = run(
        functools.partial(fine_kernel, s),
        "fine",
        [fine_fields, fine_wind, flo, fhi, slab],
        [((q, fx, y, z), pltpu.HBM), (q, x // 2, y // 2, z)],
        [
            pltpu.VMEM((q, layers, PAD, z), F32),
            pltpu.VMEM((q, layers, PAD, z), F32),
            pltpu.VMEM((6 * q, s.ep, z), F32),
            pltpu.VMEM((2 * q * s.fe, z), F32),
            pltpu.VMEM((2 * q * y, z), F32),
            pltpu.VMEM(flo.shape, F32),
            pltpu.VMEM(fhi.shape, F32),
            pltpu.SemaphoreType.DMA((6,)),
        ],
        10,
        [pltpu.VMEM, pltpu.VMEM, pltpu.HBM, pltpu.HBM, pltpu.VMEM],
    )

    def coarse(*ins):
        cost = pl.CostEstimate(flops=40_000_000, bytes_accessed=4_000_000, transcendentals=0)
        columns = [pltpu.VMEM((3, q, 24, z), F32), pltpu.VMEM((2, q, 24, z), F32)]
        spaces = [pltpu.SMEM] + [pltpu.VMEM] * (len(ins) - 1)
        kernel = functools.partial(coarse_kernel, s)
        return run(kernel, "coarse", ins, [(q, x, y, z)], padded * 3 + wind_rows + columns, 12, spaces, cost)[0]

    averaged, state = move_by(averaged, offset, (coarse, (neighbours, *coarse_level, *yrows, zown, zin)))
    (coarse_next,) = run(
        functools.partial(merge_kernel, s),
        "merge",
        [state, averaged],
        [((q, x, y, z), pltpu.HBM)],
        [pltpu.VMEM((q, x, y, z), F32), pltpu.SemaphoreType.DMA((q,))],
        4,
    )
    return coarse_next, fine_next


def solution(mesh):
    spec = P(None, "gx", "gy", "gz")
    return jax.shard_map(
        shards,
        mesh=mesh,
        in_specs=(spec, spec, spec, spec, P("gx", "gy", "gz")),
        out_specs=(spec, spec),
        check_vma=False,
    )
```

```python
import functools

import jax
import jax.numpy as jnp
from jax import lax
from jax.experimental import pallas as pl
from jax.experimental.pallas import tpu as pltpu
from jax.sharding import PartitionSpec as P

diffusion = 0.05
section_weights = (1.0 / 3.0, 0.5, 1.0)
F32 = jnp.float32
BF16 = jnp.bfloat16
PAD = 32
TOP = 8


class Sizes:
    def __init__(self, coarse_shape, fine_shape):
        self.q, self.x, self.y, self.z = coarse_shape
        self.fx = fine_shape[1]
        self.ly, self.sy = self.y // 4, self.y // 2
        self.lz, self.sz = self.z // 4, self.z // 2
        self.ex = self.x + 4
        self.ep = -(-self.ex // 8) * 8
        self.fe = self.fx + 4
        self.halo = 3 * self.q + 6
        self.rows_f, self.rows_w = self.q * (3 * self.x + 6), 3 * (2 * self.x + 2)
        self.rows_y = 3 * self.q * self.ex
        self.rows_e = self.rows_y + self.ep
        self.rows_z = self.sy + 2
        self.slab = self.rows_e + self.q * self.rows_z
        assert self.q == 4 and self.y == 16 and self.z == 128 and self.ex <= 20 and self.fx == 2 * self.x


def lanes_of(shape):
    return lax.broadcasted_iota(jnp.int32, shape, len(shape) - 1)


def halves(value):
    high = value.astype(BF16)
    return high, (value - high.astype(F32)).astype(BF16)


def times(value, matrix):
    high, low = halves(value)
    return jnp.dot(high, matrix, preferred_element_type=F32) + jnp.dot(low, matrix, preferred_element_type=F32)


def scaled(wind):
    return [w * (-0.5 / diffusion) for w in wind]


def advanced(base, fraction, wind, center, x_low, x_high, y_low, y_high, z_low, z_high):
    total = (x_high + x_low) + wind[0] * (x_high - x_low)
    total = total + ((y_high + y_low) + wind[1] * (y_high - y_low))
    total = total + ((z_high + z_low) + wind[2] * (z_high - z_low))
    if base is None:
        return center * (1.0 - 6.0 * diffusion * fraction) + total * (diffusion * fraction)
    return (base - center * (6.0 * diffusion * fraction)) + total * (diffusion * fraction)


def layer_of(s, own, low, high, member, at, width, first):
    size = own.shape[1]
    if at < 0:
        return low[first + width * member + at + width]
    if at >= size:
        return high[first + width * member + at - size]
    return own[member, at]


def unrolled(begin, end, at_once, body, carry=None):
    while (end - begin) % at_once:
        at_once -= 1

    def several(i, carry):
        for more in range(at_once):
            carry = body(begin + i * at_once + more, carry)
        return carry

    return lax.fori_loop(0, (end - begin) // at_once, several, carry)


def pack_kernel(s, fields, wind, up, down, sems):
    size = fields.shape[1]
    moves = []
    for own, members, width, first in ((fields, s.q, 3, 0), (wind, 3, 2, 3 * s.q)):
        for dst, at in ((up, size - width), (down, 0)):
            place = dst.at[first : first + members * width].reshape(members, width, s.y, s.z)
            moves.append((own.at[:, at : at + width], place))
    moves = [pltpu.make_async_copy(src, dst, sems.at[i]) for i, (src, dst) in enumerate(moves)]
    for move in moves:
        move.start()
    for move in moves:
        move.wait()


def y_rows(s, members, width):
    below, above = [], []
    for out, extra in ((below, lambda r: r), (above, lambda r: width - 1 - r)):
        at = 0
        for m in range(members):
            for r in range(width):
                out.append((m, r, extra(r), at))
                at += s.x + 2 * extra(r)
    return below, above


def ypack_kernel(s, c0, cw, lo, hi, up, dn):
    x, y, z = s.x, s.y, s.z
    flat_lo = lo.reshape(s.halo * y, z)
    flat_hi = hi.reshape(s.halo * y, z)
    for own, members, width, first, place in ((c0, s.q, 3, 0, 0), (cw, 3, 2, 3 * s.q, s.rows_f)):
        flat = own.reshape(members * x * y, z)
        for dst, rows, start in zip((up, dn), y_rows(s, members, width), (y - width, 0)):
            for m, r, e, at in rows:
                row, at = start + r, at + place
                if e:
                    dst[at : at + e, :] = flat_lo[pl.ds((first + width * (m + 1) - e) * y + row, e, stride=y), :]
                    dst[at + e + x : at + x + 2 * e, :] = flat_hi[pl.ds((first + width * m) * y + row, e, stride=y), :]
                dst[at + e : at + e + x, :] = flat[pl.ds(m * x * y + row, x, stride=y), :]


EDGE = 4


def turned(base, fraction, wind, center, x_low, x_high):
    y, z = center.shape
    return advanced(
        base,
        fraction,
        wind,
        center,
        x_low,
        x_high,
        pltpu.roll(center, 1, 0),
        pltpu.roll(center, y - 1, 0),
        pltpu.roll(center, 1, 1),
        pltpu.roll(center, z - 1, 1),
    )


def slab_parts(s, rows_of, tile_of, layers_of, put):
    q, y, z = s.q, s.y, s.z
    lane_y = lanes_of((y, z))
    columns = (lane_y == s.lz - 1) | (lane_y == s.lz) | (lane_y == s.lz + s.sz - 1) | (lane_y == s.lz + s.sz)
    low_at = (lane_y % 2 == 0) & (lane_y < z // 2)
    high_at = (lane_y % 2 == 0) & (lane_y >= z // 2)
    ends = None
    for f in range(q):
        zfaces = None
        for k in range(3):
            rows = [rows_of(k, f, row) for row in (s.ly - 1, s.ly, s.ly + s.sy - 1, s.ly + s.sy)]
            sides = (0.75 * rows[0] + 0.25 * rows[1], 0.25 * rows[2] + 0.75 * rows[3])
            lane_x = lanes_of(sides[0].shape)
            put(
                "y",
                (k * q + f) * s.ex,
                jnp.where(lane_x < s.sz, pltpu.roll(sides[0], z - s.lz, 1), pltpu.roll(sides[1], s.lz, 1)),
            )
            for side in range(2):
                e = 4 * (q * k + f) + 2 * side + 1
                before = jnp.where(lane_x == s.lz - 1, sides[side], 0.0)
                after = jnp.where(lane_x == s.lz + s.sz, sides[side], 0.0)
                part = pltpu.roll(before, (e - s.lz + 1) % z, 1) + pltpu.roll(after, (e - 1 - s.lz - s.sz) % z, 1)
                ends = part if ends is None else ends + part
            raw = None
            for a in layers_of(k):
                part = jnp.where(columns, tile_of(k, f, a), 0.0)
                part = pltpu.roll(part, (2 * a - s.lz + 1) % z, 1)
                raw = part if raw is None else raw + part
            beside = pltpu.roll(raw, z - 1, 1)
            low = jnp.where(low_at, 0.75 * raw + 0.25 * beside, 0.0)
            high = jnp.where(high_at, 0.25 * raw + 0.75 * beside, 0.0)
            part = pltpu.roll(low, (2 * s.ex * k - 1) % z, 1) + pltpu.roll(high, (2 * s.ex * k - z // 2) % z, 1)
            zfaces = part if zfaces is None else zfaces + part
        put("z", s.rows_e + f * s.rows_z, zfaces[s.ly - 1 : s.ly + s.sy + 1])
    put("e", s.rows_y, ends)


def inner_kernel(s, c0, cw, part, near, state1, state2):
    q, x, y, z = s.q, s.x, s.y, s.z
    states = (c0, state1, state2)
    for step in range(2):
        src, dst = states[step], states[step + 1]

        def layer(j, carry, step=step, src=src, dst=dst):
            w = scaled([cw[d, j] for d in range(3)])
            for f in range(q):
                base = None if step == 0 else c0[f, j]
                dst[f, j] = turned(base, section_weights[step], w, src[f, j], src[f, j - 1], src[f, j + 1])
            return carry

        unrolled(step + 1, x - 1 - step, 7 if step == 0 else 6, layer)
    for f in range(q):
        near[f, 0] = state1[f, EDGE - 2]
        near[f, 1] = state1[f, x + 1 - EDGE]
    count = s.ex - 2 * EDGE
    part[...] = jnp.zeros_like(part)

    def rows_of(k, f, row):
        flat = states[k].reshape(q * x * y, z)
        return flat[pl.ds((f * x + EDGE - 2) * y + row, count, stride=y), :]

    def put(kind, at, rows):
        if kind == "z":
            part[at : at + s.rows_z, :] = rows
        else:
            part[at + EDGE : at + EDGE + count, :] = rows

    slab_parts(s, rows_of, lambda k, f, a: states[k][f, a - 2], lambda k: range(EDGE, s.ex - EDGE), put)


def slab_kernel(s, c0, cw, lo, hi, part, near, slab, ends0, ends1, ends2):
    q, x, y, z = s.q, s.x, s.y, s.z
    states = (ends0, ends1, ends2)
    places = list(range(-2, EDGE - 2)) + list(range(x + 2 - EDGE, x + 2))
    slab[...] = part[...]
    for j, at in enumerate(places):
        for f in range(q):
            ends0[f, j] = layer_of(s, c0, lo, hi, f, at, 3, 0)
    for step in range(2):
        for j, at in enumerate(places):
            if step == 1 and at in (-2, x + 1):
                for f in range(q):
                    ends2[f, j] = jnp.zeros((y, z), F32)
                continue
            w = scaled([layer_of(s, cw, lo, hi, d, at, 2, 3 * q) for d in range(3)])
            for f in range(q):

                def beside(at, f=f):
                    if step == 0:
                        return layer_of(s, c0, lo, hi, f, at, 3, 0)
                    if at in places:
                        return ends1[f, places.index(at)]
                    return near[f, 0 if at < x // 2 else 1]

                base = None if step == 0 else ends0[f, j]
                states[step + 1][f, j] = turned(
                    base, section_weights[step], w, beside(at), beside(at - 1), beside(at + 1)
                )

    def rows_of(k, f, row):
        flat = states[k].reshape(q * 2 * EDGE * y, z)
        return flat[pl.ds(f * 2 * EDGE * y + row, 2 * EDGE, stride=y), :]

    def put(kind, at, rows):
        if kind == "z":
            slab[at : at + s.rows_z, :] = part[at : at + s.rows_z, :] + rows
        else:
            slab[at : at + EDGE, :] = rows[:EDGE]
            slab[at + s.ex - EDGE : at + s.ex, :] = rows[EDGE:]

    def layers_of(k):
        some = range(0 if k == 0 else 1, EDGE)
        return list(some) + [s.ex - 1 - a for a in some]

    def tile_of(k, f, a):
        return states[k][f, a if a < EDGE else a - s.ex + 2 * EDGE]

    slab_parts(s, rows_of, tile_of, layers_of, put)


WTOP, WPAD = 12, 40
BLOCK = slice(8, 32)


def assemble(s, c0, cw, lo, hi, below, above, pad, wind):
    q, x, y, z = s.q, s.x, s.y, s.z
    flat = pad.reshape(q * s.ep * WPAD, z)
    flat_wind = wind.reshape(3 * s.ex * 24, z)
    for f in range(q):
        for at in range(-3, x + 3):
            pad[f, at + 3, WTOP : WTOP + y, :] = layer_of(s, c0, lo, hi, f, at, 3, 0)
    for d in range(3):
        for at in range(-2, x + 2):
            wind[d, at + 2, 4 : 4 + y, :] = layer_of(s, cw, lo, hi, d, at, 2, 3 * q)
    for src, rows, start in zip((below, above), y_rows(s, q, 3), (WTOP - 3, WTOP + y)):
        for m, r, e, at in rows:
            count = x + 2 * e
            flat[pl.ds((m * s.ep + 3 - e) * WPAD + start + r, count, stride=WPAD), :] = src[at : at + count, :]
    for src, rows, start in zip((below, above), y_rows(s, 3, 2), (2, 4 + y)):
        for m, r, e, at in rows:
            count, at = x + 2 * e, at + s.rows_f
            flat_wind[pl.ds((m * s.ex + 2 - e) * 24 + start + r, count, stride=24), :] = src[at : at + count, :]


def edge_lanes(s, lane, width):
    return (lane < width) | (lane >= s.z - width)


def zpack_kernel(s, c0, cw, lo, hi, below, above, out, pad, wind):
    assemble(s, c0, cw, lo, hi, below, above, pad, wind)
    lane = lanes_of((24, s.z))
    keep = edge_lanes(s, lane, 3)
    for m in range(s.q + 3):
        total = None
        for a in range(s.ex):
            tile = pad[m, a + 1, BLOCK, :] if m < s.q else wind[m - s.q, a]
            part = pltpu.roll(jnp.where(keep, tile, 0.0), (6 * a + 3) % s.z, 1)
            total = part if total is None else total + part
        out[m] = total


def coarse_kernel(
    s, sides, c0, cw, lo, hi, below, above, zown, zin, out, pad0, pad1, pad2, wind, beyond, nearest
):
    q, x, y, z = s.q, s.x, s.y, s.z
    assemble(s, c0, cw, lo, hi, below, above, pad0, wind)
    pads = (pad0, pad1, pad2)
    lane = lanes_of((24, z))
    group = lane % 6
    from_low = group == 2
    from_high = group == 3
    exists = jnp.where(group < 3, sides[0, 0], sides[0, 1]).astype(F32)
    wind_z = scaled([zin[q + d] for d in range(3)])
    for f in range(q):
        beyond[0, f] = zin[f] * exists
        nearest[0, f] = zown[f]
    for step in range(3):
        src, fraction = pads[step], section_weights[step]
        flat = src.reshape(q * s.ep * WPAD, z)
        flat_wind = wind.reshape(3 * s.ex * 24, z)
        flat_beyond = beyond.reshape(3 * q * 24, z)
        skip, height = (0, 24) if step < 2 else (4, y)
        here = lanes_of((height, z))
        is_first, is_last = here == 0, here == z - 1

        def layer(a, packed, step=step, src=src, flat=flat, fraction=fraction, skip=skip, height=height):
            made = []
            if step < 2:
                w = scaled([wind[d, a] for d in range(3)])
            else:
                w = scaled([flat_wind[pl.ds((d * s.ex + a) * 24 + skip, height), :] for d in range(3)])
            for f in range(q):
                row = (f * s.ep + a + 1) * WPAD + 8 + skip

                def at_layer(of, layer, row, f=f):
                    return of[f, layer, BLOCK, :] if step < 2 else of.reshape(flat.shape)[pl.ds(row, height), :]

                center = at_layer(src, a + 1, row)
                ghost = pltpu.roll(flat_beyond[pl.ds((step * q + f) * 24 + skip, height), :], 2 * z - 6 * a - 3, 1)
                value = advanced(
                    None if step == 0 else at_layer(pad0, a + 1, row),
                    fraction,
                    w,
                    center,
                    at_layer(src, a, row - WPAD),
                    at_layer(src, a + 2, row + WPAD),
                    flat[pl.ds(row - 1, height), :],
                    flat[pl.ds(row + 1, height), :],
                    pltpu.roll(jnp.where(is_last, ghost, center), 1, 1),
                    pltpu.roll(jnp.where(is_first, ghost, center), z - 1, 1),
                )
                if step == 2:
                    out[f, a - 2] = value
                else:
                    pads[step + 1][f, a + 1, BLOCK, :] = value
                if step == 0:
                    made.append(packed[f] + pltpu.roll(jnp.where(is_first | is_last, value, 0.0), 6 * a + 3, 1))
            return tuple(made)

        begin, end = step, s.ex - step
        start = tuple(jnp.zeros((24, z), F32) for _ in range(q)) if step == 0 else ()
        packed = unrolled(begin, end, 4 + 2 * (step == 1), layer, start)
        if step == 2:
            break
        for f in range(q):
            if step == 0:
                nearest[1, f] = packed[f]
            ghost, near = beyond[step, f], nearest[step, f]
            value = advanced(
                None if step == 0 else beyond[0, f],
                fraction,
                wind_z,
                ghost,
                pltpu.roll(ghost, 6, 1),
                pltpu.roll(ghost, z - 6, 1),
                pltpu.roll(ghost, 1, 0),
                pltpu.roll(ghost, 23, 0),
                pltpu.roll(jnp.where(from_low, near, ghost), 1, 1),
                pltpu.roll(jnp.where(from_high, near, ghost), z - 1, 1),
            )
            beyond[step + 1, f] = value * exists


def fine_kernel(s, f0, fw, flo_there, fhi_there, slab, out, avg, *scratch):
    s1, s2, faces, ghost_rows, zface, flo, fhi, sems = scratch
    arrivals = [
        pltpu.make_async_copy(flo_there, flo, sems.at[4]),
        pltpu.make_async_copy(fhi_there, fhi, sems.at[5]),
    ]
    for move in arrivals:
        move.start()
    states = (None, s1, s2, s1)
    q, y, z, fx, fe = s.q, s.y, s.z, s.fx, s.fe
    layers = fx + 6
    rows = slice(TOP, TOP + y)
    r = lax.broadcasted_iota(jnp.int32, (z, 2 * z), 0)
    c = lax.broadcasted_iota(jnp.int32, (z, 2 * z), 1)
    near = c // 2
    far = near + 2 * (c % 2) - 1
    same = (far // s.sz == near // s.sz) & (far >= 0)
    to_fine = jnp.where(r == near, 0.75, jnp.where((r == far) & same, 0.25, 0.0)).astype(BF16)
    wide = times(slab[: s.rows_y, :], to_fine)
    ends = slab[s.rows_y : s.rows_y + s.ex, :]
    lane_x = lanes_of((s.ex, z))
    edge = (lane_x == 0) | (lane_x == z - 1)
    half = fe // 2
    for k in range(3):
        for f in range(q):
            for side in range(2):
                e = 4 * (q * k + f) + 2 * side + 1
                corner = jnp.where(edge, 0.25 * pltpu.roll(ends, z - e, 1), 0.0)
                first = (k * q + f) * s.ex
                here = faces.at[(k * q + f) * 2 + side]
                here[: s.ex, :] = wide[first : first + s.ex, side * z : side * z + z] + corner
                a = here[0:half, :]
                b = here[1 : half + 1, :]
                d = here[2 : half + 2, :]
                if k == 0:
                    flat, base, stride = ghost_rows, (2 * f + side) * fe, 1
                else:
                    flat, stride = states[k].reshape(q * layers * PAD, z), PAD
                    base = (f * layers + 1) * PAD + (TOP - 1 if side == 0 else TOP + y)
                flat[pl.ds(base, half, stride=2 * stride), :] = 0.25 * a + 0.75 * b
                flat[pl.ds(base + stride, half, stride=2 * stride), :] = 0.75 * b + 0.25 * d
    for f in range(q):
        at = s.rows_e + f * s.rows_z
        a = slab[at : at + s.sy, :]
        b = slab[at + 1 : at + 1 + s.sy, :]
        d = slab[at + 2 : at + 2 + s.sy, :]
        zface[pl.ds(f * y, s.sy, stride=2), :] = 0.25 * a + 0.75 * b
        zface[pl.ds(f * y + 1, s.sy, stride=2), :] = 0.75 * b + 0.25 * d
        a = zface[f * y : f * y + y, :]
        b = pltpu.roll(a, z - 2, 1)
        d = pltpu.roll(a, z - 4, 1)
        zface[f * y : f * y + y, :] = 0.25 * a + 0.75 * b
        zface[(q + f) * y : (q + f + 1) * y, :] = 0.75 * b + 0.25 * d
    lane = lanes_of((y, z))
    is_first, is_last = lane == 0, lane == z - 1
    row_in = lax.broadcasted_iota(jnp.int32, (y, z), 0)
    is_low, is_high = row_in == 0, row_in == y - 1
    flat_f0 = f0.reshape(q * fx * y, z)

    def pair_of_layers(k, t, inner):
        src = states[k]
        for odd in range(2):
            b = 2 * t + odd
            at = b - 2

            def field(f, at):
                return f0[f, at] if inner else layer_of(s, f0, flo, fhi, f, at, 3, 0)

            if inner:
                winds = [fw[d, at] for d in range(3)]
            else:
                winds = [layer_of(s, fw, flo, fhi, d, at, 2, 3 * q) for d in range(3)]
            w = scaled(winds)
            for f in range(q):
                if k == 0:
                    center, x_low, x_high = field(f, at), field(f, at - 1), field(f, at + 1)
                    if inner:
                        row = (f * fx + at) * y
                        y_low, y_high = flat_f0[pl.ds(row - 1, y), :], flat_f0[pl.ds(row + 1, y), :]
                    else:
                        y_low, y_high = pltpu.roll(center, 1, 0), pltpu.roll(center, y - 1, 0)
                    y_low = jnp.where(is_low, ghost_rows[pl.ds(2 * f * fe + b, 1), :], y_low)
                    y_high = jnp.where(is_high, ghost_rows[pl.ds((2 * f + 1) * fe + b, 1), :], y_high)
                    base = None
                else:
                    flat = src.reshape(q * layers * PAD, z)
                    row = (f * layers + b + 1) * PAD + TOP
                    center, x_low, x_high = src[f, b + 1, rows, :], src[f, b, rows, :], src[f, b + 2, rows, :]
                    y_low, y_high = flat[pl.ds(row - 1, y), :], flat[pl.ds(row + 1, y), :]
                    base = field(f, at)
                ghost = zface[(odd * q + f) * y : (odd * q + f + 1) * y, :]
                ghost = pltpu.roll(ghost, (2 * z - 2 * s.ex * k - 2 * t) if inner else -(2 * s.ex * k + 2 * t) % z, 1)
                value = advanced(
                    base,
                    section_weights[k],
                    w,
                    center,
                    x_low,
                    x_high,
                    y_low,
                    y_high,
                    pltpu.roll(jnp.where(is_last, ghost, center), 1, 1),
                    pltpu.roll(jnp.where(is_first, ghost, center), z - 1, 1),
                )
                states[k + 1][f, b + 1, rows, :] = value

    for move in arrivals:
        move.wait()
    moves = []
    for k in range(3):
        if k < 2:
            outer = 2 - k
            for t in list(range(outer)) + list(range(half - outer, half)):
                pair_of_layers(k, t, False)
            unrolled(outer, half - outer, 2, lambda t, g, k=k: pair_of_layers(k, t, True))
            continue
        part = (half - 2) // 4
        for i in range(4):
            unrolled(1 + i * part, 1 + (i + 1) * part, 2, lambda t, g, k=k: pair_of_layers(k, t, True))
            begin, end = 2 * part * i, 2 * part * (i + 1)
            moves.append(pltpu.make_async_copy(s1.at[:, 3 + begin : 3 + end, rows], out.at[:, begin:end], sems.at[i]))
            moves[-1].start()
    rz = lax.broadcasted_iota(jnp.int32, (z, z), 0)
    cz = lax.broadcasted_iota(jnp.int32, (z, z), 1)
    flat = s1.reshape(q * layers * PAD, z)
    pairs_z = [jnp.where(cz == rz // 2 + odd * s.sz, 0.125, 0.0).astype(BF16) for odd in range(2)]
    for f in range(q):
        sums = []
        for odd in range(2):
            parts = []
            for p in range(s.x // 2):
                base = (f * layers + 3 + 4 * p + 2 * odd) * PAD + TOP
                part = None
                for more in (0, 1, PAD, PAD + 1):
                    piece = flat[pl.ds(base + more, y // 2, stride=2), :]
                    part = piece if part is None else part + piece
                parts.append(part)
            sums.append(times(jnp.concatenate(parts, axis=0), pairs_z[odd]))
        avg[f] = (sums[0] + sums[1]).reshape(s.x // 2, y // 2, z)
    for move in moves:
        move.wait()


def merge_kernel(s, c3, avg, out, made, sems):
    lane = lanes_of((s.sy, s.z))
    inside = (lane >= s.lz) & (lane < s.lz + s.sz)
    moves = []
    for f in range(s.q):
        for p in range(s.x // 2):
            both = avg[f, p]
            for odd in range(2):
                at = 2 * p + odd
                moved = pltpu.roll(both, s.lz if odd == 0 else s.z - s.lz, 1)
                made[f, at] = c3[f, at]
                made[f, at, s.ly : s.ly + s.sy, :] = jnp.where(inside, moved, c3[f, at, s.ly : s.ly + s.sy, :])
        moves.append(pltpu.make_async_copy(made.at[f], out.at[f], sems.at[f]))
        moves[-1].start()
    for move in moves:
        move.wait()


SHORT = pl.CostEstimate(flops=1, bytes_accessed=1, transcendentals=0)


def run(kernel, name, ins, outs, scratch, megabytes, spaces=None, cost=SHORT):
    spaces = spaces or [pltpu.VMEM] * len(ins)
    outs = [out if isinstance(out[0], tuple) else (out, pltpu.VMEM) for out in outs]
    ins = [i if space is pltpu.SMEM else pltpu.with_memory_space_constraint(i, space) for i, space in zip(ins, spaces)]
    return pl.pallas_call(
        kernel,
        out_shape=tuple(space(dims, F32) for dims, space in outs),
        in_specs=[pl.BlockSpec(memory_space=space) for space in spaces],
        out_specs=tuple(pl.BlockSpec(memory_space=space) for _, space in outs),
        scratch_shapes=scratch,
        compiler_params=pltpu.CompilerParams(vmem_limit_bytes=megabytes << 20),
        cost_estimate=cost,
        name=name,
    )(*ins)


def ring(array, axis, by):
    size = lax.axis_size(axis)
    return lax.ppermute(array, axis, [(i, (i + by) % size) for i in range(size)])


def move_by(array, amount, beside=None):
    size = lax.axis_size("gx")
    work, operands = beside or (lambda: (), ())
    if size <= 8:

        def branch(by, array, *operands):
            return array if by == 0 else ring(array, "gx", by), work(*operands)

        return lax.switch(amount, [functools.partial(branch, by) for by in range(size)], array, *operands)
    for bit in range((size - 1).bit_length()):
        array = jnp.where((amount >> bit) % 2 == 1, ring(array, "gx", 1 << bit), array)
    return array, work(*operands)


def z_columns(zown):
    size = lax.axis_size("gz")
    if size == 1:
        return zown
    if size == 2:
        return lax.ppermute(zown, "gz", [(0, 1), (1, 0)])
    below = lax.broadcasted_iota(jnp.int32, zown.shape, 2) % 6 < 3
    return jnp.where(below, ring(zown, "gz", 1), ring(zown, "gz", -1))


def pack(s, fields, wind, name):
    return run(
        functools.partial(pack_kernel, s),
        name,
        [fields, wind],
        [(s.halo, s.y, s.z)] * 2,
        [pltpu.SemaphoreType.DMA((4,))],
        4,
        [pltpu.HBM] * 2,
    )


def shards(coarse_fields, coarse_wind, fine_fields, fine_wind, fine_owner):
    s = Sizes(coarse_fields.shape, fine_fields.shape)
    q, x, y, z, fx = s.q, s.x, s.y, s.z, s.fx
    size = lax.axis_size("gx")
    offset = (fine_owner[0, 0, 0] - lax.axis_index("gx")) % size
    level = lax.axis_index("gz")
    neighbours = jnp.stack([level > 0, level < lax.axis_size("gz") - 1]).astype(jnp.int32).reshape(1, 2)
    cup, cdown = pack(s, coarse_fields, coarse_wind, "pack_coarse")
    lo, hi = ring(cup, "gx", 1), ring(cdown, "gx", -1)
    part, near = run(
        functools.partial(inner_kernel, s),
        "inner",
        [coarse_fields, coarse_wind],
        [(s.slab, z), (q, 2, y, z)],
        [pltpu.VMEM((q, x, y, z), F32)] * 2,
        6,
    )
    fup, fdown = pack(s, fine_fields, fine_wind, "pack_fine")
    fup, fdown, part, near, offset = lax.optimization_barrier((fup, fdown, part, near, offset))
    flo, fhi = ring(fup, "gx", 1), ring(fdown, "gx", -1)
    padded = [pltpu.VMEM((q, s.ep, WPAD, z), F32)]
    wind_rows = [pltpu.VMEM((3, s.ex, 24, z), F32)]

    def exchange(coarse_level, part, near):
        yup, ydn = run(functools.partial(ypack_kernel, s), "ypack", coarse_level, [(s.rows_f + s.rows_w, z)] * 2, [], 4)
        yrows = [ring(yup, "gy", 1), ring(ydn, "gy", -1)]
        ends = [pltpu.VMEM((q, 2 * EDGE, y, z), F32)] * 3
        (slab,) = run(functools.partial(slab_kernel, s), "slab", coarse_level + [part, near], [(s.slab, z)], ends, 6)
        yrows, slab = lax.optimization_barrier((yrows, slab))
        kernel = functools.partial(zpack_kernel, s)
        (zown,) = run(kernel, "zpack", coarse_level + yrows, [(q + 3, 24, z)], padded + wind_rows, 6)
        return slab, yrows, zown, z_columns(zown)

    def nothing(coarse_level, part, near):
        rows = jnp.zeros((s.rows_f + s.rows_w, z), F32)
        columns = jnp.zeros((q + 3, 24, z), F32)
        return jnp.zeros((s.slab, z), F32), [rows, rows], columns, columns

    coarse_level = [coarse_fields, coarse_wind, lo, hi]
    slab, yrows, zown, zin = lax.cond(fine_owner[0, 0, 0] >= 0, exchange, nothing, coarse_level, part, near)

    def coarse(*ins):
        cost = pl.CostEstimate(flops=40_000_000, bytes_accessed=4_000_000, transcendentals=0)
        columns = [pltpu.VMEM((3, q, 24, z), F32), pltpu.VMEM((2, q, 24, z), F32)]
        spaces = [pltpu.SMEM] + [pltpu.VMEM] * (len(ins) - 1)
        kernel = functools.partial(coarse_kernel, s)
        return run(kernel, "coarse", ins, [(q, x, y, z)], padded * 3 + wind_rows + columns, 12, spaces, cost)[0]

    beside = (coarse, (neighbours, *coarse_level, *yrows, zown, zin))
    slab, state = move_by(slab, (size - offset) % size, beside)
    layers = fx + 6
    fine_next, averaged = run(
        functools.partial(fine_kernel, s),
        "fine",
        [fine_fields, fine_wind, flo, fhi, slab],
        [((q, fx, y, z), pltpu.HBM), (q, x // 2, y // 2, z)],
        [
            pltpu.VMEM((q, layers, PAD, z), F32),
            pltpu.VMEM((q, layers, PAD, z), F32),
            pltpu.VMEM((6 * q, s.ep, z), F32),
            pltpu.VMEM((2 * q * s.fe, z), F32),
            pltpu.VMEM((2 * q * y, z), F32),
            pltpu.VMEM(flo.shape, F32),
            pltpu.VMEM(fhi.shape, F32),
            pltpu.SemaphoreType.DMA((6,)),
        ],
        10,
        [pltpu.VMEM, pltpu.VMEM, pltpu.HBM, pltpu.HBM, pltpu.VMEM],
    )

    averaged, _ = move_by(averaged, offset)
    (coarse_next,) = run(
        functools.partial(merge_kernel, s),
        "merge",
        [state, averaged],
        [((q, x, y, z), pltpu.HBM)],
        [pltpu.VMEM((q, x, y, z), F32), pltpu.SemaphoreType.DMA((q,))],
        4,
    )
    return coarse_next, fine_next


def solution(mesh):
    spec = P(None, "gx", "gy", "gz")
    return jax.shard_map(
        shards,
        mesh=mesh,
        in_specs=(spec, spec, spec, spec, P("gx", "gy", "gz")),
        out_specs=(spec, spec),
        check_vma=False,
    )
```

```python
import functools

import jax
import jax.numpy as jnp
from jax import lax
from jax.experimental import pallas as pl
from jax.experimental.pallas import tpu as pltpu
from jax.sharding import PartitionSpec as P

diffusion = 0.05
section_weights = (1.0 / 3.0, 0.5, 1.0)
F32 = jnp.float32
BF16 = jnp.bfloat16
PAD = 32
TOP = 8


class Sizes:
    def __init__(self, coarse_shape, fine_shape):
        self.q, self.x, self.y, self.z = coarse_shape
        self.fx = fine_shape[1]
        self.ly, self.sy = self.y // 4, self.y // 2
        self.lz, self.sz = self.z // 4, self.z // 2
        self.ex = self.x + 4
        self.ep = -(-self.ex // 8) * 8
        self.fe = self.fx + 4
        self.halo = 3 * self.q + 6
        self.rows_f, self.rows_w = self.q * (3 * self.x + 6), 3 * (2 * self.x + 2)
        self.rows_y = 3 * self.q * self.ex
        self.rows_e = self.rows_y + self.ep
        self.rows_z = self.sy + 2
        self.slab = self.rows_e + self.q * self.rows_z
        assert self.q == 4 and self.y == 16 and self.z == 128 and self.ex <= 20 and self.fx == 2 * self.x


def lanes_of(shape):
    return lax.broadcasted_iota(jnp.int32, shape, len(shape) - 1)


def halves(value):
    high = value.astype(BF16)
    return high, (value - high.astype(F32)).astype(BF16)


def times(value, matrix):
    high, low = halves(value)
    return jnp.dot(high, matrix, preferred_element_type=F32) + jnp.dot(low, matrix, preferred_element_type=F32)


def scaled(wind):
    return [w * (-0.5 / diffusion) for w in wind]


def advanced(base, fraction, wind, center, x_low, x_high, y_low, y_high, z_low, z_high):
    total = (x_high + x_low) + wind[0] * (x_high - x_low)
    total = total + ((y_high + y_low) + wind[1] * (y_high - y_low))
    total = total + ((z_high + z_low) + wind[2] * (z_high - z_low))
    if base is None:
        return center * (1.0 - 6.0 * diffusion * fraction) + total * (diffusion * fraction)
    return (base - center * (6.0 * diffusion * fraction)) + total * (diffusion * fraction)


def layer_of(s, own, low, high, member, at, width, first):
    size = own.shape[1]
    if at < 0:
        return low[first + width * member + at + width]
    if at >= size:
        return high[first + width * member + at - size]
    return own[member, at]


def unrolled(begin, end, at_once, body, carry=None):
    while (end - begin) % at_once:
        at_once -= 1

    def several(i, carry):
        for more in range(at_once):
            carry = body(begin + i * at_once + more, carry)
        return carry

    return lax.fori_loop(0, (end - begin) // at_once, several, carry)


def pack_kernel(s, fields, wind, up, down, sems):
    size = fields.shape[1]
    moves = []
    for own, members, width, first in ((fields, s.q, 3, 0), (wind, 3, 2, 3 * s.q)):
        for dst, at in ((up, size - width), (down, 0)):
            place = dst.at[first : first + members * width].reshape(members, width, s.y, s.z)
            moves.append((own.at[:, at : at + width], place))
    moves = [pltpu.make_async_copy(src, dst, sems.at[i]) for i, (src, dst) in enumerate(moves)]
    for move in moves:
        move.start()
    for move in moves:
        move.wait()


def y_rows(s, members, width):
    below, above = [], []
    for out, extra in ((below, lambda r: r), (above, lambda r: width - 1 - r)):
        at = 0
        for m in range(members):
            for r in range(width):
                out.append((m, r, extra(r), at))
                at += s.x + 2 * extra(r)
    return below, above


def ypack_kernel(s, c0, cw, lo, hi, up, dn):
    x, y, z = s.x, s.y, s.z
    flat_lo = lo.reshape(s.halo * y, z)
    flat_hi = hi.reshape(s.halo * y, z)
    for own, members, width, first, place in ((c0, s.q, 3, 0, 0), (cw, 3, 2, 3 * s.q, s.rows_f)):
        flat = own.reshape(members * x * y, z)
        for dst, rows, start in zip((up, dn), y_rows(s, members, width), (y - width, 0)):
            for m, r, e, at in rows:
                row, at = start + r, at + place
                if e:
                    dst[at : at + e, :] = flat_lo[pl.ds((first + width * (m + 1) - e) * y + row, e, stride=y), :]
                    dst[at + e + x : at + x + 2 * e, :] = flat_hi[pl.ds((first + width * m) * y + row, e, stride=y), :]
                dst[at + e : at + e + x, :] = flat[pl.ds(m * x * y + row, x, stride=y), :]


EDGE = 4


def turned(base, fraction, wind, center, x_low, x_high):
    y, z = center.shape
    return advanced(
        base,
        fraction,
        wind,
        center,
        x_low,
        x_high,
        pltpu.roll(center, 1, 0),
        pltpu.roll(center, y - 1, 0),
        pltpu.roll(center, 1, 1),
        pltpu.roll(center, z - 1, 1),
    )


def slab_parts(s, rows_of, tile_of, layers_of, put):
    q, y, z = s.q, s.y, s.z
    lane_y = lanes_of((y, z))
    columns = (lane_y == s.lz - 1) | (lane_y == s.lz) | (lane_y == s.lz + s.sz - 1) | (lane_y == s.lz + s.sz)
    low_at = (lane_y % 2 == 0) & (lane_y < z // 2)
    high_at = (lane_y % 2 == 0) & (lane_y >= z // 2)
    ends = None
    for f in range(q):
        zfaces = None
        for k in range(3):
            rows = [rows_of(k, f, row) for row in (s.ly - 1, s.ly, s.ly + s.sy - 1, s.ly + s.sy)]
            sides = (0.75 * rows[0] + 0.25 * rows[1], 0.25 * rows[2] + 0.75 * rows[3])
            lane_x = lanes_of(sides[0].shape)
            put(
                "y",
                (k * q + f) * s.ex,
                jnp.where(lane_x < s.sz, pltpu.roll(sides[0], z - s.lz, 1), pltpu.roll(sides[1], s.lz, 1)),
            )
            for side in range(2):
                e = 4 * (q * k + f) + 2 * side + 1
                before = jnp.where(lane_x == s.lz - 1, sides[side], 0.0)
                after = jnp.where(lane_x == s.lz + s.sz, sides[side], 0.0)
                part = pltpu.roll(before, (e - s.lz + 1) % z, 1) + pltpu.roll(after, (e - 1 - s.lz - s.sz) % z, 1)
                ends = part if ends is None else ends + part
            raw = None
            for a in layers_of(k):
                part = jnp.where(columns, tile_of(k, f, a), 0.0)
                part = pltpu.roll(part, (2 * a - s.lz + 1) % z, 1)
                raw = part if raw is None else raw + part
            beside = pltpu.roll(raw, z - 1, 1)
            low = jnp.where(low_at, 0.75 * raw + 0.25 * beside, 0.0)
            high = jnp.where(high_at, 0.25 * raw + 0.75 * beside, 0.0)
            part = pltpu.roll(low, (2 * s.ex * k - 1) % z, 1) + pltpu.roll(high, (2 * s.ex * k - z // 2) % z, 1)
            zfaces = part if zfaces is None else zfaces + part
        put("z", s.rows_e + f * s.rows_z, zfaces[s.ly - 1 : s.ly + s.sy + 1])
    put("e", s.rows_y, ends)


def inner_kernel(s, c0, cw, part, near, state1, state2):
    q, x, y, z = s.q, s.x, s.y, s.z
    states = (c0, state1, state2)
    for step in range(2):
        src, dst = states[step], states[step + 1]

        def layer(j, carry, step=step, src=src, dst=dst):
            w = scaled([cw[d, j] for d in range(3)])
            for f in range(q):
                base = None if step == 0 else c0[f, j]
                dst[f, j] = turned(base, section_weights[step], w, src[f, j], src[f, j - 1], src[f, j + 1])
            return carry

        unrolled(step + 1, x - 1 - step, 7 if step == 0 else 6, layer)
    for f in range(q):
        near[f, 0] = state1[f, EDGE - 2]
        near[f, 1] = state1[f, x + 1 - EDGE]
    count = s.ex - 2 * EDGE
    part[...] = jnp.zeros_like(part)

    def rows_of(k, f, row):
        flat = states[k].reshape(q * x * y, z)
        return flat[pl.ds((f * x + EDGE - 2) * y + row, count, stride=y), :]

    def put(kind, at, rows):
        if kind == "z":
            part[at : at + s.rows_z, :] = rows
        else:
            part[at + EDGE : at + EDGE + count, :] = rows

    slab_parts(s, rows_of, lambda k, f, a: states[k][f, a - 2], lambda k: range(EDGE, s.ex - EDGE), put)


def slab_kernel(s, c0, cw, lo, hi, part, near, slab, ends0, ends1, ends2):
    q, x, y, z = s.q, s.x, s.y, s.z
    states = (ends0, ends1, ends2)
    places = list(range(-2, EDGE - 2)) + list(range(x + 2 - EDGE, x + 2))
    slab[...] = part[...]
    for j, at in enumerate(places):
        for f in range(q):
            ends0[f, j] = layer_of(s, c0, lo, hi, f, at, 3, 0)
    for step in range(2):
        for j, at in enumerate(places):
            if step == 1 and at in (-2, x + 1):
                for f in range(q):
                    ends2[f, j] = jnp.zeros((y, z), F32)
                continue
            w = scaled([layer_of(s, cw, lo, hi, d, at, 2, 3 * q) for d in range(3)])
            for f in range(q):

                def beside(at, f=f):
                    if step == 0:
                        return layer_of(s, c0, lo, hi, f, at, 3, 0)
                    if at in places:
                        return ends1[f, places.index(at)]
                    return near[f, 0 if at < x // 2 else 1]

                base = None if step == 0 else ends0[f, j]
                states[step + 1][f, j] = turned(
                    base, section_weights[step], w, beside(at), beside(at - 1), beside(at + 1)
                )

    def rows_of(k, f, row):
        flat = states[k].reshape(q * 2 * EDGE * y, z)
        return flat[pl.ds(f * 2 * EDGE * y + row, 2 * EDGE, stride=y), :]

    def put(kind, at, rows):
        if kind == "z":
            slab[at : at + s.rows_z, :] = part[at : at + s.rows_z, :] + rows
        else:
            slab[at : at + EDGE, :] = rows[:EDGE]
            slab[at + s.ex - EDGE : at + s.ex, :] = rows[EDGE:]

    def layers_of(k):
        some = range(0 if k == 0 else 1, EDGE)
        return list(some) + [s.ex - 1 - a for a in some]

    def tile_of(k, f, a):
        return states[k][f, a if a < EDGE else a - s.ex + 2 * EDGE]

    slab_parts(s, rows_of, tile_of, layers_of, put)


WTOP, WPAD = 12, 40
BLOCK = slice(8, 32)


def assemble(s, c0, cw, lo, hi, below, above, pad, wind):
    q, x, y, z = s.q, s.x, s.y, s.z
    flat = pad.reshape(q * s.ep * WPAD, z)
    flat_wind = wind.reshape(3 * s.ex * 24, z)
    for f in range(q):
        for at in range(-3, x + 3):
            pad[f, at + 3, WTOP : WTOP + y, :] = layer_of(s, c0, lo, hi, f, at, 3, 0)
    for d in range(3):
        for at in range(-2, x + 2):
            wind[d, at + 2, 4 : 4 + y, :] = layer_of(s, cw, lo, hi, d, at, 2, 3 * q)
    for src, rows, start in zip((below, above), y_rows(s, q, 3), (WTOP - 3, WTOP + y)):
        for m, r, e, at in rows:
            count = x + 2 * e
            flat[pl.ds((m * s.ep + 3 - e) * WPAD + start + r, count, stride=WPAD), :] = src[at : at + count, :]
    for src, rows, start in zip((below, above), y_rows(s, 3, 2), (2, 4 + y)):
        for m, r, e, at in rows:
            count, at = x + 2 * e, at + s.rows_f
            flat_wind[pl.ds((m * s.ex + 2 - e) * 24 + start + r, count, stride=24), :] = src[at : at + count, :]


def edge_lanes(s, lane, width):
    return (lane < width) | (lane >= s.z - width)


def zpack_kernel(s, c0, cw, lo, hi, below, above, out, pad, wind):
    assemble(s, c0, cw, lo, hi, below, above, pad, wind)
    lane = lanes_of((24, s.z))
    keep = edge_lanes(s, lane, 3)
    for m in range(s.q + 3):
        total = None
        for a in range(s.ex):
            tile = pad[m, a + 1, BLOCK, :] if m < s.q else wind[m - s.q, a]
            part = pltpu.roll(jnp.where(keep, tile, 0.0), (6 * a + 3) % s.z, 1)
            total = part if total is None else total + part
        out[m] = total


def coarse_kernel(
    s, sides, c0, cw, lo, hi, below, above, zown, zin, out, pad0, pad1, pad2, wind, beyond, nearest
):
    q, x, y, z = s.q, s.x, s.y, s.z
    assemble(s, c0, cw, lo, hi, below, above, pad0, wind)
    pads = (pad0, pad1, pad2)
    lane = lanes_of((24, z))
    group = lane % 6
    from_low = group == 2
    from_high = group == 3
    exists = jnp.where(group < 3, sides[0, 0], sides[0, 1]).astype(F32)
    wind_z = scaled([zin[q + d] for d in range(3)])
    for f in range(q):
        beyond[0, f] = zin[f] * exists
        nearest[0, f] = zown[f]
    for step in range(3):
        src, fraction = pads[step], section_weights[step]
        flat = src.reshape(q * s.ep * WPAD, z)
        flat_wind = wind.reshape(3 * s.ex * 24, z)
        flat_beyond = beyond.reshape(3 * q * 24, z)
        skip, height = (0, 24) if step < 2 else (4, y)
        here = lanes_of((height, z))
        is_first, is_last = here == 0, here == z - 1

        def layer(a, packed, step=step, src=src, flat=flat, fraction=fraction, skip=skip, height=height):
            made = []
            if step < 2:
                w = scaled([wind[d, a] for d in range(3)])
            else:
                w = scaled([flat_wind[pl.ds((d * s.ex + a) * 24 + skip, height), :] for d in range(3)])
            for f in range(q):
                row = (f * s.ep + a + 1) * WPAD + 8 + skip

                def at_layer(of, layer, row, f=f):
                    return of[f, layer, BLOCK, :] if step < 2 else of.reshape(flat.shape)[pl.ds(row, height), :]

                center = at_layer(src, a + 1, row)
                ghost = pltpu.roll(flat_beyond[pl.ds((step * q + f) * 24 + skip, height), :], 2 * z - 6 * a - 3, 1)
                value = advanced(
                    None if step == 0 else at_layer(pad0, a + 1, row),
                    fraction,
                    w,
                    center,
                    at_layer(src, a, row - WPAD),
                    at_layer(src, a + 2, row + WPAD),
                    flat[pl.ds(row - 1, height), :],
                    flat[pl.ds(row + 1, height), :],
                    pltpu.roll(jnp.where(is_last, ghost, center), 1, 1),
                    pltpu.roll(jnp.where(is_first, ghost, center), z - 1, 1),
                )
                if step == 2:
                    out[f, a - 2] = value
                else:
                    pads[step + 1][f, a + 1, BLOCK, :] = value
                if step == 0:
                    made.append(packed[f] + pltpu.roll(jnp.where(is_first | is_last, value, 0.0), 6 * a + 3, 1))
            return tuple(made)

        begin, end = step, s.ex - step
        start = tuple(jnp.zeros((24, z), F32) for _ in range(q)) if step == 0 else ()
        packed = unrolled(begin, end, 4 + 2 * (step == 1), layer, start)
        if step == 2:
            break
        for f in range(q):
            if step == 0:
                nearest[1, f] = packed[f]
            ghost, near = beyond[step, f], nearest[step, f]
            value = advanced(
                None if step == 0 else beyond[0, f],
                fraction,
                wind_z,
                ghost,
                pltpu.roll(ghost, 6, 1),
                pltpu.roll(ghost, z - 6, 1),
                pltpu.roll(ghost, 1, 0),
                pltpu.roll(ghost, 23, 0),
                pltpu.roll(jnp.where(from_low, near, ghost), 1, 1),
                pltpu.roll(jnp.where(from_high, near, ghost), z - 1, 1),
            )
            beyond[step + 1, f] = value * exists


def fine_kernel(s, f0, fw, flo_there, fhi_there, slab, out, avg, *scratch):
    s1, s2, faces, ghost_rows, zface, flo, fhi, sems = scratch
    arrivals = [
        pltpu.make_async_copy(flo_there, flo, sems.at[4]),
        pltpu.make_async_copy(fhi_there, fhi, sems.at[5]),
    ]
    for move in arrivals:
        move.start()
    states = (None, s1, s2, s1)
    q, y, z, fx, fe = s.q, s.y, s.z, s.fx, s.fe
    layers = fx + 6
    rows = slice(TOP, TOP + y)
    r = lax.broadcasted_iota(jnp.int32, (z, 2 * z), 0)
    c = lax.broadcasted_iota(jnp.int32, (z, 2 * z), 1)
    near = c // 2
    far = near + 2 * (c % 2) - 1
    same = (far // s.sz == near // s.sz) & (far >= 0)
    to_fine = jnp.where(r == near, 0.75, jnp.where((r == far) & same, 0.25, 0.0)).astype(BF16)
    wide = times(slab[: s.rows_y, :], to_fine)
    ends = slab[s.rows_y : s.rows_y + s.ex, :]
    lane_x = lanes_of((s.ex, z))
    edge = (lane_x == 0) | (lane_x == z - 1)
    half = fe // 2
    for k in range(3):
        for f in range(q):
            for side in range(2):
                e = 4 * (q * k + f) + 2 * side + 1
                corner = jnp.where(edge, 0.25 * pltpu.roll(ends, z - e, 1), 0.0)
                first = (k * q + f) * s.ex
                here = faces.at[(k * q + f) * 2 + side]
                here[: s.ex, :] = wide[first : first + s.ex, side * z : side * z + z] + corner
                a = here[0:half, :]
                b = here[1 : half + 1, :]
                d = here[2 : half + 2, :]
                if k == 0:
                    flat, base, stride = ghost_rows, (2 * f + side) * fe, 1
                else:
                    flat, stride = states[k].reshape(q * layers * PAD, z), PAD
                    base = (f * layers + 1) * PAD + (TOP - 1 if side == 0 else TOP + y)
                flat[pl.ds(base, half, stride=2 * stride), :] = 0.25 * a + 0.75 * b
                flat[pl.ds(base + stride, half, stride=2 * stride), :] = 0.75 * b + 0.25 * d
    for f in range(q):
        at = s.rows_e + f * s.rows_z
        a = slab[at : at + s.sy, :]
        b = slab[at + 1 : at + 1 + s.sy, :]
        d = slab[at + 2 : at + 2 + s.sy, :]
        zface[pl.ds(f * y, s.sy, stride=2), :] = 0.25 * a + 0.75 * b
        zface[pl.ds(f * y + 1, s.sy, stride=2), :] = 0.75 * b + 0.25 * d
        a = zface[f * y : f * y + y, :]
        b = pltpu.roll(a, z - 2, 1)
        d = pltpu.roll(a, z - 4, 1)
        zface[f * y : f * y + y, :] = 0.25 * a + 0.75 * b
        zface[(q + f) * y : (q + f + 1) * y, :] = 0.75 * b + 0.25 * d
    lane = lanes_of((y, z))
    is_first, is_last = lane == 0, lane == z - 1
    row_in = lax.broadcasted_iota(jnp.int32, (y, z), 0)
    is_low, is_high = row_in == 0, row_in == y - 1
    flat_f0 = f0.reshape(q * fx * y, z)

    def pair_of_layers(k, t, inner):
        src = states[k]
        for odd in range(2):
            b = 2 * t + odd
            at = b - 2

            def field(f, at):
                return f0[f, at] if inner else layer_of(s, f0, flo, fhi, f, at, 3, 0)

            if inner:
                winds = [fw[d, at] for d in range(3)]
            else:
                winds = [layer_of(s, fw, flo, fhi, d, at, 2, 3 * q) for d in range(3)]
            w = scaled(winds)
            for f in range(q):
                if k == 0:
                    center, x_low, x_high = field(f, at), field(f, at - 1), field(f, at + 1)
                    if inner:
                        row = (f * fx + at) * y
                        y_low, y_high = flat_f0[pl.ds(row - 1, y), :], flat_f0[pl.ds(row + 1, y), :]
                    else:
                        y_low, y_high = pltpu.roll(center, 1, 0), pltpu.roll(center, y - 1, 0)
                    y_low = jnp.where(is_low, ghost_rows[pl.ds(2 * f * fe + b, 1), :], y_low)
                    y_high = jnp.where(is_high, ghost_rows[pl.ds((2 * f + 1) * fe + b, 1), :], y_high)
                    base = None
                else:
                    flat = src.reshape(q * layers * PAD, z)
                    row = (f * layers + b + 1) * PAD + TOP
                    center, x_low, x_high = src[f, b + 1, rows, :], src[f, b, rows, :], src[f, b + 2, rows, :]
                    y_low, y_high = flat[pl.ds(row - 1, y), :], flat[pl.ds(row + 1, y), :]
                    base = field(f, at)
                ghost = zface[(odd * q + f) * y : (odd * q + f + 1) * y, :]
                ghost = pltpu.roll(ghost, (2 * z - 2 * s.ex * k - 2 * t) if inner else -(2 * s.ex * k + 2 * t) % z, 1)
                value = advanced(
                    base,
                    section_weights[k],
                    w,
                    center,
                    x_low,
                    x_high,
                    y_low,
                    y_high,
                    pltpu.roll(jnp.where(is_last, ghost, center), 1, 1),
                    pltpu.roll(jnp.where(is_first, ghost, center), z - 1, 1),
                )
                states[k + 1][f, b + 1, rows, :] = value

    for move in arrivals:
        move.wait()
    moves = []
    for k in range(3):
        if k < 2:
            outer = 2 - k
            for t in list(range(outer)) + list(range(half - outer, half)):
                pair_of_layers(k, t, False)
            unrolled(outer, half - outer, 2, lambda t, g, k=k: pair_of_layers(k, t, True))
            continue
        part = (half - 2) // 4
        for i in range(4):
            unrolled(1 + i * part, 1 + (i + 1) * part, 2, lambda t, g, k=k: pair_of_layers(k, t, True))
            begin, end = 2 * part * i, 2 * part * (i + 1)
            moves.append(pltpu.make_async_copy(s1.at[:, 3 + begin : 3 + end, rows], out.at[:, begin:end], sems.at[i]))
            moves[-1].start()
    rz = lax.broadcasted_iota(jnp.int32, (z, z), 0)
    cz = lax.broadcasted_iota(jnp.int32, (z, z), 1)
    flat = s1.reshape(q * layers * PAD, z)
    pairs_z = [jnp.where(cz == rz // 2 + odd * s.sz, 0.125, 0.0).astype(BF16) for odd in range(2)]
    for f in range(q):
        sums = []
        for odd in range(2):
            parts = []
            for p in range(s.x // 2):
                base = (f * layers + 3 + 4 * p + 2 * odd) * PAD + TOP
                part = None
                for more in (0, 1, PAD, PAD + 1):
                    piece = flat[pl.ds(base + more, y // 2, stride=2), :]
                    part = piece if part is None else part + piece
                parts.append(part)
            sums.append(times(jnp.concatenate(parts, axis=0), pairs_z[odd]))
        avg[f] = (sums[0] + sums[1]).reshape(s.x // 2, y // 2, z)
    for move in moves:
        move.wait()


def merge_kernel(s, c3, avg, out, made, sems):
    lane = lanes_of((s.sy, s.z))
    inside = (lane >= s.lz) & (lane < s.lz + s.sz)
    moves = []
    for f in range(s.q):
        for p in range(s.x // 2):
            both = avg[f, p]
            for odd in range(2):
                at = 2 * p + odd
                moved = pltpu.roll(both, s.lz if odd == 0 else s.z - s.lz, 1)
                made[f, at] = c3[f, at]
                made[f, at, s.ly : s.ly + s.sy, :] = jnp.where(inside, moved, c3[f, at, s.ly : s.ly + s.sy, :])
        moves.append(pltpu.make_async_copy(made.at[f], out.at[f], sems.at[f]))
        moves[-1].start()
    for move in moves:
        move.wait()


SHORT = pl.CostEstimate(flops=1, bytes_accessed=1, transcendentals=0)


def run(kernel, name, ins, outs, scratch, megabytes, spaces=None, cost=SHORT):
    spaces = spaces or [pltpu.VMEM] * len(ins)
    outs = [out if isinstance(out[0], tuple) else (out, pltpu.VMEM) for out in outs]
    ins = [i if space is pltpu.SMEM else pltpu.with_memory_space_constraint(i, space) for i, space in zip(ins, spaces)]
    return pl.pallas_call(
        kernel,
        out_shape=tuple(space(dims, F32) for dims, space in outs),
        in_specs=[pl.BlockSpec(memory_space=space) for space in spaces],
        out_specs=tuple(pl.BlockSpec(memory_space=space) for _, space in outs),
        scratch_shapes=scratch,
        compiler_params=pltpu.CompilerParams(vmem_limit_bytes=megabytes << 20),
        cost_estimate=cost,
        name=name,
    )(*ins)


def ring(array, axis, by):
    size = lax.axis_size(axis)
    return lax.ppermute(array, axis, [(i, (i + by) % size) for i in range(size)])


def move_by(array, amount, beside=None):
    size = lax.axis_size("gx")
    work, operands = beside or (lambda: (), ())
    if size <= 8:

        def branch(by, array, *operands):
            return array if by == 0 else ring(array, "gx", by), work(*operands)

        return lax.switch(amount, [functools.partial(branch, by) for by in range(size)], array, *operands)
    for bit in range((size - 1).bit_length()):
        array = jnp.where((amount >> bit) % 2 == 1, ring(array, "gx", 1 << bit), array)
    return array, work(*operands)


def z_columns(zown):
    size = lax.axis_size("gz")
    if size == 1:
        return zown
    if size == 2:
        return lax.ppermute(zown, "gz", [(0, 1), (1, 0)])
    below = lax.broadcasted_iota(jnp.int32, zown.shape, 2) % 6 < 3
    return jnp.where(below, ring(zown, "gz", 1), ring(zown, "gz", -1))


def pack(s, fields, wind, spare, name):
    return run(
        functools.partial(pack_kernel, s),
        name,
        [fields, wind],
        [(s.halo + spare, s.y, s.z)] * 2,
        [pltpu.SemaphoreType.DMA((4,))],
        4,
        [pltpu.HBM] * 2,
    )


def shards(coarse_fields, coarse_wind, fine_fields, fine_wind, fine_owner):
    s = Sizes(coarse_fields.shape, fine_fields.shape)
    q, x, y, z, fx = s.q, s.x, s.y, s.z, s.fx
    size = lax.axis_size("gx")
    offset = (fine_owner[0, 0, 0] - lax.axis_index("gx")) % size
    level = lax.axis_index("gz")
    neighbours = jnp.stack([level > 0, level < lax.axis_size("gz") - 1]).astype(jnp.int32).reshape(1, 2)
    cup, cdown = pack(s, coarse_fields, coarse_wind, 0, "pack_coarse")
    lo, hi = ring(cup, "gx", 1), ring(cdown, "gx", -1)
    part, near = run(
        functools.partial(inner_kernel, s),
        "inner",
        [coarse_fields, coarse_wind],
        [(s.slab, z), (q, 2, y, z)],
        [pltpu.VMEM((q, x, y, z), F32)] * 2,
        6,
    )
    fup, fdown = pack(s, fine_fields, fine_wind, 2, "pack_fine")
    fup, fdown, part, near, offset = lax.optimization_barrier((fup, fdown, part, near, offset))
    flo, fhi = ring(fup, "gx", 1), ring(fdown, "gx", -1)
    padded = [pltpu.VMEM((q, s.ep, WPAD, z), F32)]
    wind_rows = [pltpu.VMEM((3, s.ex, 24, z), F32)]

    coarse_level = [coarse_fields, coarse_wind, lo, hi]
    yup, ydn = run(functools.partial(ypack_kernel, s), "ypack", coarse_level, [(s.rows_f + s.rows_w, z)] * 2, [], 4)
    yrows = [ring(yup, "gy", 1), ring(ydn, "gy", -1)]
    ends = [pltpu.VMEM((q, 2 * EDGE, y, z), F32)] * 3
    (slab,) = run(functools.partial(slab_kernel, s), "slab", coarse_level + [part, near], [(s.slab, z)], ends, 6)
    slab, _ = move_by(slab, (size - offset) % size)
    yrows, slab, flo, fhi = lax.optimization_barrier((yrows, slab, flo, fhi))
    kernel = functools.partial(zpack_kernel, s)
    (zown,) = run(kernel, "zpack", coarse_level + yrows, [(q + 3, 24, z)], padded + wind_rows, 6)
    zin = z_columns(zown)
    layers = fx + 6
    fine_next, averaged = run(
        functools.partial(fine_kernel, s),
        "fine",
        [fine_fields, fine_wind, flo, fhi, slab],
        [((q, fx, y, z), pltpu.HBM), (q, x // 2, y // 2, z)],
        [
            pltpu.VMEM((q, layers, PAD, z), F32),
            pltpu.VMEM((q, layers, PAD, z), F32),
            pltpu.VMEM((6 * q, s.ep, z), F32),
            pltpu.VMEM((2 * q * s.fe, z), F32),
            pltpu.VMEM((2 * q * y, z), F32),
            pltpu.VMEM(flo.shape, F32),
            pltpu.VMEM(fhi.shape, F32),
            pltpu.SemaphoreType.DMA((6,)),
        ],
        10,
        [pltpu.VMEM, pltpu.VMEM, pltpu.HBM, pltpu.HBM, pltpu.VMEM],
    )

    def coarse(*ins):
        cost = pl.CostEstimate(flops=40_000_000, bytes_accessed=4_000_000, transcendentals=0)
        columns = [pltpu.VMEM((3, q, 24, z), F32), pltpu.VMEM((2, q, 24, z), F32)]
        spaces = [pltpu.SMEM] + [pltpu.VMEM] * (len(ins) - 1)
        kernel = functools.partial(coarse_kernel, s)
        return run(kernel, "coarse", ins, [(q, x, y, z)], padded * 3 + wind_rows + columns, 12, spaces, cost)[0]

    averaged, state = move_by(averaged, offset, (coarse, (neighbours, *coarse_level, *yrows, zown, zin)))
    (coarse_next,) = run(
        functools.partial(merge_kernel, s),
        "merge",
        [state, averaged],
        [((q, x, y, z), pltpu.HBM)],
        [pltpu.VMEM((q, x, y, z), F32), pltpu.SemaphoreType.DMA((q,))],
        4,
    )
    return coarse_next, fine_next


def solution(mesh):
    spec = P(None, "gx", "gy", "gz")
    return jax.shard_map(
        shards,
        mesh=mesh,
        in_specs=(spec, spec, spec, spec, P("gx", "gy", "gz")),
        out_specs=(spec, spec),
        check_vma=False,
    )
```

```python
import functools

import jax
import jax.numpy as jnp
from jax import lax
from jax.experimental import pallas as pl
from jax.experimental.pallas import tpu as pltpu
from jax.sharding import PartitionSpec as P

diffusion = 0.05
section_weights = (1.0 / 3.0, 0.5, 1.0)
F32 = jnp.float32
BF16 = jnp.bfloat16
PAD = 32
TOP = 8


class Sizes:
    def __init__(self, coarse_shape, fine_shape):
        self.q, self.x, self.y, self.z = coarse_shape
        self.fx = fine_shape[1]
        self.ly, self.sy = self.y // 4, self.y // 2
        self.lz, self.sz = self.z // 4, self.z // 2
        self.ex = self.x + 4
        self.ep = -(-self.ex // 8) * 8
        self.fe = self.fx + 4
        self.halo = 3 * self.q + 6
        self.rows_f, self.rows_w = self.q * (3 * self.x + 6), 3 * (2 * self.x + 2)
        self.rows_y = 3 * self.q * self.ex
        self.rows_e = self.rows_y + self.ep
        self.rows_z = self.sy + 2
        self.slab = self.rows_e + self.q * self.rows_z
        assert self.q == 4 and self.y == 16 and self.z == 128 and self.ex <= 20 and self.fx == 2 * self.x


def lanes_of(shape):
    return lax.broadcasted_iota(jnp.int32, shape, len(shape) - 1)


def halves(value):
    high = value.astype(BF16)
    return high, (value - high.astype(F32)).astype(BF16)


def times(value, matrix):
    high, low = halves(value)
    return jnp.dot(high, matrix, preferred_element_type=F32) + jnp.dot(low, matrix, preferred_element_type=F32)


def scaled(wind):
    return [w * (-0.5 / diffusion) for w in wind]


def advanced(base, fraction, wind, center, x_low, x_high, y_low, y_high, z_low, z_high):
    total = (x_high + x_low) + wind[0] * (x_high - x_low)
    total = total + ((y_high + y_low) + wind[1] * (y_high - y_low))
    total = total + ((z_high + z_low) + wind[2] * (z_high - z_low))
    if base is None:
        return center * (1.0 - 6.0 * diffusion * fraction) + total * (diffusion * fraction)
    return (base - center * (6.0 * diffusion * fraction)) + total * (diffusion * fraction)


def layer_of(s, own, low, high, member, at, width, first):
    size = own.shape[1]
    if at < 0:
        return low[first + width * member + at + width]
    if at >= size:
        return high[first + width * member + at - size]
    return own[member, at]


def unrolled(begin, end, at_once, body, carry=None):
    while (end - begin) % at_once:
        at_once -= 1

    def several(i, carry):
        for more in range(at_once):
            carry = body(begin + i * at_once + more, carry)
        return carry

    return lax.fori_loop(0, (end - begin) // at_once, several, carry)


def pack_kernel(s, fields, wind, up, down, sems):
    size = fields.shape[1]
    moves = []
    for own, members, width, first in ((fields, s.q, 3, 0), (wind, 3, 2, 3 * s.q)):
        for dst, at in ((up, size - width), (down, 0)):
            place = dst.at[first : first + members * width].reshape(members, width, s.y, s.z)
            moves.append((own.at[:, at : at + width], place))
    moves = [pltpu.make_async_copy(src, dst, sems.at[i]) for i, (src, dst) in enumerate(moves)]
    for move in moves:
        move.start()
    for move in moves:
        move.wait()


def y_rows(s, members, width):
    below, above = [], []
    for out, extra in ((below, lambda r: r), (above, lambda r: width - 1 - r)):
        at = 0
        for m in range(members):
            for r in range(width):
                out.append((m, r, extra(r), at))
                at += s.x + 2 * extra(r)
    return below, above


def ypack_kernel(s, c0, cw, lo, hi, up, dn):
    x, y, z = s.x, s.y, s.z
    flat_lo = lo.reshape(s.halo * y, z)
    flat_hi = hi.reshape(s.halo * y, z)
    for own, members, width, first, place in ((c0, s.q, 3, 0, 0), (cw, 3, 2, 3 * s.q, s.rows_f)):
        flat = own.reshape(members * x * y, z)
        for dst, rows, start in zip((up, dn), y_rows(s, members, width), (y - width, 0)):
            for m, r, e, at in rows:
                row, at = start + r, at + place
                if e:
                    dst[at : at + e, :] = flat_lo[pl.ds((first + width * (m + 1) - e) * y + row, e, stride=y), :]
                    dst[at + e + x : at + x + 2 * e, :] = flat_hi[pl.ds((first + width * m) * y + row, e, stride=y), :]
                dst[at + e : at + e + x, :] = flat[pl.ds(m * x * y + row, x, stride=y), :]


EDGE = 4


def turned(base, fraction, wind, center, x_low, x_high):
    y, z = center.shape
    return advanced(
        base,
        fraction,
        wind,
        center,
        x_low,
        x_high,
        pltpu.roll(center, 1, 0),
        pltpu.roll(center, y - 1, 0),
        pltpu.roll(center, 1, 1),
        pltpu.roll(center, z - 1, 1),
    )


def slab_parts(s, rows_of, tile_of, layers_of, put):
    q, y, z = s.q, s.y, s.z
    lane_y = lanes_of((y, z))
    columns = (lane_y == s.lz - 1) | (lane_y == s.lz) | (lane_y == s.lz + s.sz - 1) | (lane_y == s.lz + s.sz)
    low_at = (lane_y % 2 == 0) & (lane_y < z // 2)
    high_at = (lane_y % 2 == 0) & (lane_y >= z // 2)
    ends = None
    for f in range(q):
        zfaces = None
        for k in range(3):
            rows = [rows_of(k, f, row) for row in (s.ly - 1, s.ly, s.ly + s.sy - 1, s.ly + s.sy)]
            sides = (0.75 * rows[0] + 0.25 * rows[1], 0.25 * rows[2] + 0.75 * rows[3])
            lane_x = lanes_of(sides[0].shape)
            put(
                "y",
                (k * q + f) * s.ex,
                jnp.where(lane_x < s.sz, pltpu.roll(sides[0], z - s.lz, 1), pltpu.roll(sides[1], s.lz, 1)),
            )
            for side in range(2):
                e = 4 * (q * k + f) + 2 * side + 1
                before = jnp.where(lane_x == s.lz - 1, sides[side], 0.0)
                after = jnp.where(lane_x == s.lz + s.sz, sides[side], 0.0)
                part = pltpu.roll(before, (e - s.lz + 1) % z, 1) + pltpu.roll(after, (e - 1 - s.lz - s.sz) % z, 1)
                ends = part if ends is None else ends + part
            raw = None
            for a in layers_of(k):
                part = jnp.where(columns, tile_of(k, f, a), 0.0)
                part = pltpu.roll(part, (2 * a - s.lz + 1) % z, 1)
                raw = part if raw is None else raw + part
            beside = pltpu.roll(raw, z - 1, 1)
            low = jnp.where(low_at, 0.75 * raw + 0.25 * beside, 0.0)
            high = jnp.where(high_at, 0.25 * raw + 0.75 * beside, 0.0)
            part = pltpu.roll(low, (2 * s.ex * k - 1) % z, 1) + pltpu.roll(high, (2 * s.ex * k - z // 2) % z, 1)
            zfaces = part if zfaces is None else zfaces + part
        put("z", s.rows_e + f * s.rows_z, zfaces[s.ly - 1 : s.ly + s.sy + 1])
    put("e", s.rows_y, ends)


def inner_kernel(s, c0, cw, part, near, state1, state2):
    q, x, y, z = s.q, s.x, s.y, s.z
    states = (c0, state1, state2)
    for step in range(2):
        src, dst = states[step], states[step + 1]

        def layer(j, carry, step=step, src=src, dst=dst):
            w = scaled([cw[d, j] for d in range(3)])
            for f in range(q):
                base = None if step == 0 else c0[f, j]
                dst[f, j] = turned(base, section_weights[step], w, src[f, j], src[f, j - 1], src[f, j + 1])
            return carry

        unrolled(step + 1, x - 1 - step, 7 if step == 0 else 6, layer)
    for f in range(q):
        near[f, 0] = state1[f, EDGE - 2]
        near[f, 1] = state1[f, x + 1 - EDGE]
    count = s.ex - 2 * EDGE
    part[...] = jnp.zeros_like(part)

    def rows_of(k, f, row):
        flat = states[k].reshape(q * x * y, z)
        return flat[pl.ds((f * x + EDGE - 2) * y + row, count, stride=y), :]

    def put(kind, at, rows):
        if kind == "z":
            part[at : at + s.rows_z, :] = rows
        else:
            part[at + EDGE : at + EDGE + count, :] = rows

    slab_parts(s, rows_of, lambda k, f, a: states[k][f, a - 2], lambda k: range(EDGE, s.ex - EDGE), put)


def slab_kernel(s, c0, cw, lo, hi, part, near, slab, ends0, ends1, ends2):
    q, x, y, z = s.q, s.x, s.y, s.z
    states = (ends0, ends1, ends2)
    places = list(range(-2, EDGE - 2)) + list(range(x + 2 - EDGE, x + 2))
    slab[...] = part[...]
    for j, at in enumerate(places):
        for f in range(q):
            ends0[f, j] = layer_of(s, c0, lo, hi, f, at, 3, 0)
    for step in range(2):
        for j, at in enumerate(places):
            if step == 1 and at in (-2, x + 1):
                for f in range(q):
                    ends2[f, j] = jnp.zeros((y, z), F32)
                continue
            w = scaled([layer_of(s, cw, lo, hi, d, at, 2, 3 * q) for d in range(3)])
            for f in range(q):

                def beside(at, f=f):
                    if step == 0:
                        return layer_of(s, c0, lo, hi, f, at, 3, 0)
                    if at in places:
                        return ends1[f, places.index(at)]
                    return near[f, 0 if at < x // 2 else 1]

                base = None if step == 0 else ends0[f, j]
                states[step + 1][f, j] = turned(
                    base, section_weights[step], w, beside(at), beside(at - 1), beside(at + 1)
                )

    def rows_of(k, f, row):
        flat = states[k].reshape(q * 2 * EDGE * y, z)
        return flat[pl.ds(f * 2 * EDGE * y + row, 2 * EDGE, stride=y), :]

    def put(kind, at, rows):
        if kind == "z":
            slab[at : at + s.rows_z, :] = part[at : at + s.rows_z, :] + rows
        else:
            slab[at : at + EDGE, :] = rows[:EDGE]
            slab[at + s.ex - EDGE : at + s.ex, :] = rows[EDGE:]

    def layers_of(k):
        some = range(0 if k == 0 else 1, EDGE)
        return list(some) + [s.ex - 1 - a for a in some]

    def tile_of(k, f, a):
        return states[k][f, a if a < EDGE else a - s.ex + 2 * EDGE]

    slab_parts(s, rows_of, tile_of, layers_of, put)


WTOP, WPAD = 12, 40
BLOCK = slice(8, 32)


def assemble(s, c0, cw, lo, hi, below, above, pad, wind):
    q, x, y, z = s.q, s.x, s.y, s.z
    flat = pad.reshape(q * s.ep * WPAD, z)
    flat_wind = wind.reshape(3 * s.ex * 24, z)
    for f in range(q):
        for at in range(-3, x + 3):
            pad[f, at + 3, WTOP : WTOP + y, :] = layer_of(s, c0, lo, hi, f, at, 3, 0)
    for d in range(3):
        for at in range(-2, x + 2):
            wind[d, at + 2, 4 : 4 + y, :] = layer_of(s, cw, lo, hi, d, at, 2, 3 * q)
    for src, rows, start in zip((below, above), y_rows(s, q, 3), (WTOP - 3, WTOP + y)):
        for m, r, e, at in rows:
            count = x + 2 * e
            flat[pl.ds((m * s.ep + 3 - e) * WPAD + start + r, count, stride=WPAD), :] = src[at : at + count, :]
    for src, rows, start in zip((below, above), y_rows(s, 3, 2), (2, 4 + y)):
        for m, r, e, at in rows:
            count, at = x + 2 * e, at + s.rows_f
            flat_wind[pl.ds((m * s.ex + 2 - e) * 24 + start + r, count, stride=24), :] = src[at : at + count, :]


def edge_lanes(s, lane, width):
    return (lane < width) | (lane >= s.z - width)


def zpack_kernel(s, c0, cw, lo, hi, below, above, out, pad, wind):
    assemble(s, c0, cw, lo, hi, below, above, pad, wind)
    lane = lanes_of((24, s.z))
    keep = edge_lanes(s, lane, 3)
    for m in range(s.q + 3):
        total = None
        for a in range(s.ex):
            tile = pad[m, a + 1, BLOCK, :] if m < s.q else wind[m - s.q, a]
            part = pltpu.roll(jnp.where(keep, tile, 0.0), (6 * a + 3) % s.z, 1)
            total = part if total is None else total + part
        out[m] = total


def coarse_kernel(
    s, sides, c0, cw, lo, hi, below, above, zown, zin, out, pad0, pad1, pad2, wind, beyond, nearest
):
    q, x, y, z = s.q, s.x, s.y, s.z
    assemble(s, c0, cw, lo, hi, below, above, pad0, wind)
    pads = (pad0, pad1, pad2)
    lane = lanes_of((24, z))
    group = lane % 6
    from_low = group == 2
    from_high = group == 3
    exists = jnp.where(group < 3, sides[0, 0], sides[0, 1]).astype(F32)
    wind_z = scaled([zin[q + d] for d in range(3)])
    for f in range(q):
        beyond[0, f] = zin[f] * exists
        nearest[0, f] = zown[f]
    for step in range(3):
        src, fraction = pads[step], section_weights[step]
        flat = src.reshape(q * s.ep * WPAD, z)
        flat_wind = wind.reshape(3 * s.ex * 24, z)
        flat_beyond = beyond.reshape(3 * q * 24, z)
        skip, height = (0, 24) if step < 2 else (4, y)
        here = lanes_of((height, z))
        is_first, is_last = here == 0, here == z - 1

        def layer(a, packed, step=step, src=src, flat=flat, fraction=fraction, skip=skip, height=height):
            made = []
            if step < 2:
                w = scaled([wind[d, a] for d in range(3)])
            else:
                w = scaled([flat_wind[pl.ds((d * s.ex + a) * 24 + skip, height), :] for d in range(3)])
            for f in range(q):
                row = (f * s.ep + a + 1) * WPAD + 8 + skip

                def at_layer(of, layer, row, f=f):
                    return of[f, layer, BLOCK, :] if step < 2 else of.reshape(flat.shape)[pl.ds(row, height), :]

                center = at_layer(src, a + 1, row)
                ghost = pltpu.roll(flat_beyond[pl.ds((step * q + f) * 24 + skip, height), :], 2 * z - 6 * a - 3, 1)
                value = advanced(
                    None if step == 0 else at_layer(pad0, a + 1, row),
                    fraction,
                    w,
                    center,
                    at_layer(src, a, row - WPAD),
                    at_layer(src, a + 2, row + WPAD),
                    flat[pl.ds(row - 1, height), :],
                    flat[pl.ds(row + 1, height), :],
                    pltpu.roll(jnp.where(is_last, ghost, center), 1, 1),
                    pltpu.roll(jnp.where(is_first, ghost, center), z - 1, 1),
                )
                if step == 2:
                    out[f, a - 2] = value
                else:
                    pads[step + 1][f, a + 1, BLOCK, :] = value
                if step == 0:
                    made.append(packed[f] + pltpu.roll(jnp.where(is_first | is_last, value, 0.0), 6 * a + 3, 1))
            return tuple(made)

        begin, end = step, s.ex - step
        start = tuple(jnp.zeros((24, z), F32) for _ in range(q)) if step == 0 else ()
        packed = unrolled(begin, end, (end - begin) // 2, layer, start)
        if step == 2:
            break
        for f in range(q):
            if step == 0:
                nearest[1, f] = packed[f]
            ghost, near = beyond[step, f], nearest[step, f]
            value = advanced(
                None if step == 0 else beyond[0, f],
                fraction,
                wind_z,
                ghost,
                pltpu.roll(ghost, 6, 1),
                pltpu.roll(ghost, z - 6, 1),
                pltpu.roll(ghost, 1, 0),
                pltpu.roll(ghost, 23, 0),
                pltpu.roll(jnp.where(from_low, near, ghost), 1, 1),
                pltpu.roll(jnp.where(from_high, near, ghost), z - 1, 1),
            )
            beyond[step + 1, f] = value * exists


def fine_kernel(s, f0, fw, flo_there, fhi_there, slab, out, avg, *scratch):
    s1, s2, faces, ghost_rows, zface, flo, fhi, sems = scratch
    arrivals = [
        pltpu.make_async_copy(flo_there, flo, sems.at[4]),
        pltpu.make_async_copy(fhi_there, fhi, sems.at[5]),
    ]
    for move in arrivals:
        move.start()
    states = (None, s1, s2, s1)
    q, y, z, fx, fe = s.q, s.y, s.z, s.fx, s.fe
    layers = fx + 6
    rows = slice(TOP, TOP + y)
    r = lax.broadcasted_iota(jnp.int32, (z, 2 * z), 0)
    c = lax.broadcasted_iota(jnp.int32, (z, 2 * z), 1)
    near = c // 2
    far = near + 2 * (c % 2) - 1
    same = (far // s.sz == near // s.sz) & (far >= 0)
    to_fine = jnp.where(r == near, 0.75, jnp.where((r == far) & same, 0.25, 0.0)).astype(BF16)
    wide = times(slab[: s.rows_y, :], to_fine)
    ends = slab[s.rows_y : s.rows_y + s.ex, :]
    lane_x = lanes_of((s.ex, z))
    edge = (lane_x == 0) | (lane_x == z - 1)
    half = fe // 2
    for k in range(3):
        for f in range(q):
            for side in range(2):
                e = 4 * (q * k + f) + 2 * side + 1
                corner = jnp.where(edge, 0.25 * pltpu.roll(ends, z - e, 1), 0.0)
                first = (k * q + f) * s.ex
                here = faces.at[(k * q + f) * 2 + side]
                here[: s.ex, :] = wide[first : first + s.ex, side * z : side * z + z] + corner
                a = here[0:half, :]
                b = here[1 : half + 1, :]
                d = here[2 : half + 2, :]
                if k == 0:
                    flat, base, stride = ghost_rows, (2 * f + side) * fe, 1
                else:
                    flat, stride = states[k].reshape(q * layers * PAD, z), PAD
                    base = (f * layers + 1) * PAD + (TOP - 1 if side == 0 else TOP + y)
                flat[pl.ds(base, half, stride=2 * stride), :] = 0.25 * a + 0.75 * b
                flat[pl.ds(base + stride, half, stride=2 * stride), :] = 0.75 * b + 0.25 * d
    for f in range(q):
        at = s.rows_e + f * s.rows_z
        a = slab[at : at + s.sy, :]
        b = slab[at + 1 : at + 1 + s.sy, :]
        d = slab[at + 2 : at + 2 + s.sy, :]
        zface[pl.ds(f * y, s.sy, stride=2), :] = 0.25 * a + 0.75 * b
        zface[pl.ds(f * y + 1, s.sy, stride=2), :] = 0.75 * b + 0.25 * d
        a = zface[f * y : f * y + y, :]
        b = pltpu.roll(a, z - 2, 1)
        d = pltpu.roll(a, z - 4, 1)
        zface[f * y : f * y + y, :] = 0.25 * a + 0.75 * b
        zface[(q + f) * y : (q + f + 1) * y, :] = 0.75 * b + 0.25 * d
    lane = lanes_of((y, z))
    is_first, is_last = lane == 0, lane == z - 1
    row_in = lax.broadcasted_iota(jnp.int32, (y, z), 0)
    is_low, is_high = row_in == 0, row_in == y - 1
    flat_f0 = f0.reshape(q * fx * y, z)

    def pair_of_layers(k, t, inner):
        src = states[k]
        for odd in range(2):
            b = 2 * t + odd
            at = b - 2

            def field(f, at):
                return f0[f, at] if inner else layer_of(s, f0, flo, fhi, f, at, 3, 0)

            if inner:
                winds = [fw[d, at] for d in range(3)]
            else:
                winds = [layer_of(s, fw, flo, fhi, d, at, 2, 3 * q) for d in range(3)]
            w = scaled(winds)
            for f in range(q):
                if k == 0:
                    center, x_low, x_high = field(f, at), field(f, at - 1), field(f, at + 1)
                    if inner:
                        row = (f * fx + at) * y
                        y_low, y_high = flat_f0[pl.ds(row - 1, y), :], flat_f0[pl.ds(row + 1, y), :]
                    else:
                        y_low, y_high = pltpu.roll(center, 1, 0), pltpu.roll(center, y - 1, 0)
                    y_low = jnp.where(is_low, ghost_rows[pl.ds(2 * f * fe + b, 1), :], y_low)
                    y_high = jnp.where(is_high, ghost_rows[pl.ds((2 * f + 1) * fe + b, 1), :], y_high)
                    base = None
                else:
                    flat = src.reshape(q * layers * PAD, z)
                    row = (f * layers + b + 1) * PAD + TOP
                    center, x_low, x_high = src[f, b + 1, rows, :], src[f, b, rows, :], src[f, b + 2, rows, :]
                    y_low, y_high = flat[pl.ds(row - 1, y), :], flat[pl.ds(row + 1, y), :]
                    base = field(f, at)
                ghost = zface[(odd * q + f) * y : (odd * q + f + 1) * y, :]
                ghost = pltpu.roll(ghost, (2 * z - 2 * s.ex * k - 2 * t) if inner else -(2 * s.ex * k + 2 * t) % z, 1)
                value = advanced(
                    base,
                    section_weights[k],
                    w,
                    center,
                    x_low,
                    x_high,
                    y_low,
                    y_high,
                    pltpu.roll(jnp.where(is_last, ghost, center), 1, 1),
                    pltpu.roll(jnp.where(is_first, ghost, center), z - 1, 1),
                )
                states[k + 1][f, b + 1, rows, :] = value

    for move in arrivals:
        move.wait()
    moves = []
    for k in range(3):
        if k < 2:
            outer = 2 - k
            for t in list(range(outer)) + list(range(half - outer, half)):
                pair_of_layers(k, t, False)
            unrolled(outer, half - outer, 7 + k, lambda t, g, k=k: pair_of_layers(k, t, True))
            continue
        part = (half - 2) // 4
        for i in range(4):
            unrolled(1 + i * part, 1 + (i + 1) * part, 4, lambda t, g, k=k: pair_of_layers(k, t, True))
            begin, end = 2 * part * i, 2 * part * (i + 1)
            moves.append(pltpu.make_async_copy(s1.at[:, 3 + begin : 3 + end, rows], out.at[:, begin:end], sems.at[i]))
            moves[-1].start()
    rz = lax.broadcasted_iota(jnp.int32, (z, z), 0)
    cz = lax.broadcasted_iota(jnp.int32, (z, z), 1)
    flat = s1.reshape(q * layers * PAD, z)
    pairs_z = [jnp.where(cz == rz // 2 + odd * s.sz, 0.125, 0.0).astype(BF16) for odd in range(2)]
    for f in range(q):
        sums = []
        for odd in range(2):
            parts = []
            for p in range(s.x // 2):
                base = (f * layers + 3 + 4 * p + 2 * odd) * PAD + TOP
                part = None
                for more in (0, 1, PAD, PAD + 1):
                    piece = flat[pl.ds(base + more, y // 2, stride=2), :]
                    part = piece if part is None else part + piece
                parts.append(part)
            sums.append(times(jnp.concatenate(parts, axis=0), pairs_z[odd]))
        avg[f] = (sums[0] + sums[1]).reshape(s.x // 2, y // 2, z)
    for move in moves:
        move.wait()


def merge_kernel(s, c3, avg, out, made, sems):
    lane = lanes_of((s.sy, s.z))
    inside = (lane >= s.lz) & (lane < s.lz + s.sz)
    moves = []
    for f in range(s.q):
        for p in range(s.x // 2):
            both = avg[f, p]
            for odd in range(2):
                at = 2 * p + odd
                moved = pltpu.roll(both, s.lz if odd == 0 else s.z - s.lz, 1)
                made[f, at] = c3[f, at]
                made[f, at, s.ly : s.ly + s.sy, :] = jnp.where(inside, moved, c3[f, at, s.ly : s.ly + s.sy, :])
        moves.append(pltpu.make_async_copy(made.at[f], out.at[f], sems.at[f]))
        moves[-1].start()
    for move in moves:
        move.wait()


SHORT = pl.CostEstimate(flops=1, bytes_accessed=1, transcendentals=0)


def run(kernel, name, ins, outs, scratch, megabytes, spaces=None, cost=SHORT):
    spaces = spaces or [pltpu.VMEM] * len(ins)
    outs = [out if isinstance(out[0], tuple) else (out, pltpu.VMEM) for out in outs]
    ins = [i if space is pltpu.SMEM else pltpu.with_memory_space_constraint(i, space) for i, space in zip(ins, spaces)]
    return pl.pallas_call(
        kernel,
        out_shape=tuple(space(dims, F32) for dims, space in outs),
        in_specs=[pl.BlockSpec(memory_space=space) for space in spaces],
        out_specs=tuple(pl.BlockSpec(memory_space=space) for _, space in outs),
        scratch_shapes=scratch,
        compiler_params=pltpu.CompilerParams(vmem_limit_bytes=megabytes << 20),
        cost_estimate=cost,
        name=name,
    )(*ins)


def ring(array, axis, by):
    size = lax.axis_size(axis)
    return lax.ppermute(array, axis, [(i, (i + by) % size) for i in range(size)])


def move_by(array, amount, beside=None):
    size = lax.axis_size("gx")
    work, operands = beside or (lambda: (), ())
    if size <= 8:

        def branch(by, array, *operands):
            return array if by == 0 else ring(array, "gx", by), work(*operands)

        return lax.switch(amount, [functools.partial(branch, by) for by in range(size)], array, *operands)
    for bit in range((size - 1).bit_length()):
        array = jnp.where((amount >> bit) % 2 == 1, ring(array, "gx", 1 << bit), array)
    return array, work(*operands)


def z_columns(zown):
    size = lax.axis_size("gz")
    if size == 1:
        return zown
    if size == 2:
        return lax.ppermute(zown, "gz", [(0, 1), (1, 0)])
    below = lax.broadcasted_iota(jnp.int32, zown.shape, 2) % 6 < 3
    return jnp.where(below, ring(zown, "gz", 1), ring(zown, "gz", -1))


def pack(s, fields, wind, spare, name):
    return run(
        functools.partial(pack_kernel, s),
        name,
        [fields, wind],
        [(s.halo + spare, s.y, s.z)] * 2,
        [pltpu.SemaphoreType.DMA((4,))],
        1,
        [pltpu.HBM] * 2,
    )


def shards(coarse_fields, coarse_wind, fine_fields, fine_wind, fine_owner):
    s = Sizes(coarse_fields.shape, fine_fields.shape)
    q, x, y, z, fx = s.q, s.x, s.y, s.z, s.fx
    size = lax.axis_size("gx")
    offset = (fine_owner[0, 0, 0] - lax.axis_index("gx")) % size
    level = lax.axis_index("gz")
    neighbours = jnp.stack([level > 0, level < lax.axis_size("gz") - 1]).astype(jnp.int32).reshape(1, 2)
    cup, cdown = pack(s, coarse_fields, coarse_wind, 0, "pack_coarse")
    lo, hi = ring(cup, "gx", 1), ring(cdown, "gx", -1)
    part, near = run(
        functools.partial(inner_kernel, s),
        "inner",
        [coarse_fields, coarse_wind],
        [(s.slab, z), (q, 2, y, z)],
        [pltpu.VMEM((q, x, y, z), F32)] * 2,
        3,
    )
    fup, fdown = pack(s, fine_fields, fine_wind, 2, "pack_fine")
    fup, fdown, offset = lax.optimization_barrier((fup, fdown, offset))
    flo, fhi = ring(fup, "gx", 1), ring(fdown, "gx", -1)
    padded = [pltpu.VMEM((q, s.ep, WPAD, z), F32)]
    wind_rows = [pltpu.VMEM((3, s.ex, 24, z), F32)]

    coarse_fields, part, near = lax.optimization_barrier((coarse_fields, part, near))
    coarse_level = [coarse_fields, coarse_wind, lo, hi]
    yup, ydn = run(functools.partial(ypack_kernel, s), "ypack", coarse_level, [(s.rows_f + s.rows_w, z)] * 2, [], 1)
    yrows = [ring(yup, "gy", 1), ring(ydn, "gy", -1)]
    ends = [pltpu.VMEM((q, 2 * EDGE, y, z), F32)] * 3
    (slab,) = run(functools.partial(slab_kernel, s), "slab", coarse_level + [part, near], [(s.slab, z)], ends, 3)
    slab, _ = move_by(slab, (size - offset) % size)
    yrows, slab, flo, fhi = lax.optimization_barrier((yrows, slab, flo, fhi))
    kernel = functools.partial(zpack_kernel, s)
    (zown,) = run(kernel, "zpack", coarse_level + yrows, [(q + 3, 24, z)], padded + wind_rows, 4)
    zin = z_columns(zown)
    layers = fx + 6
    fine_next, averaged = run(
        functools.partial(fine_kernel, s),
        "fine",
        [fine_fields, fine_wind, flo, fhi, slab],
        [((q, fx, y, z), pltpu.HBM), (q, x // 2, y // 2, z)],
        [
            pltpu.VMEM((q, layers, PAD, z), F32),
            pltpu.VMEM((q, layers, PAD, z), F32),
            pltpu.VMEM((6 * q, s.ep, z), F32),
            pltpu.VMEM((2 * q * s.fe, z), F32),
            pltpu.VMEM((2 * q * y, z), F32),
            pltpu.VMEM(flo.shape, F32),
            pltpu.VMEM(fhi.shape, F32),
            pltpu.SemaphoreType.DMA((6,)),
        ],
        9,
        [pltpu.VMEM, pltpu.VMEM, pltpu.HBM, pltpu.HBM, pltpu.VMEM],
    )

    def coarse(*ins):
        cost = pl.CostEstimate(flops=40_000_000, bytes_accessed=4_000_000, transcendentals=0)
        columns = [pltpu.VMEM((3, q, 24, z), F32), pltpu.VMEM((2, q, 24, z), F32)]
        spaces = [pltpu.SMEM] + [pltpu.VMEM] * (len(ins) - 1)
        kernel = functools.partial(coarse_kernel, s)
        return run(kernel, "coarse", ins, [(q, x, y, z)], padded * 3 + wind_rows + columns, 9, spaces, cost)[0]

    averaged, state = move_by(averaged, offset, (coarse, (neighbours, *coarse_level, *yrows, zown, zin)))
    (coarse_next,) = run(
        functools.partial(merge_kernel, s),
        "merge",
        [state, averaged],
        [((q, x, y, z), pltpu.HBM)],
        [pltpu.VMEM((q, x, y, z), F32), pltpu.SemaphoreType.DMA((q,))],
        2,
    )
    return coarse_next, fine_next


def solution(mesh):
    spec = P(None, "gx", "gy", "gz")
    return jax.shard_map(
        shards,
        mesh=mesh,
        in_specs=(spec, spec, spec, spec, P("gx", "gy", "gz")),
        out_specs=(spec, spec),
        check_vma=False,
    )
```

```python
import functools

import jax
import jax.numpy as jnp
from jax import lax
from jax.experimental import pallas as pl
from jax.experimental.pallas import tpu as pltpu
from jax.sharding import PartitionSpec as P

diffusion = 0.05
section_weights = (1.0 / 3.0, 0.5, 1.0)
F32 = jnp.float32
BF16 = jnp.bfloat16
PAD = 32
TOP = 8


class Sizes:
    def __init__(self, coarse_shape, fine_shape):
        self.q, self.x, self.y, self.z = coarse_shape
        self.fx = fine_shape[1]
        self.ly, self.sy = self.y // 4, self.y // 2
        self.lz, self.sz = self.z // 4, self.z // 2
        self.ex = self.x + 4
        self.ep = -(-self.ex // 8) * 8
        self.fe = self.fx + 4
        self.halo = 3 * self.q + 6
        self.rows_f, self.rows_w = self.q * (3 * self.x + 6), 3 * (2 * self.x + 2)
        self.rows_y = 3 * self.q * self.ex
        self.rows_e = self.rows_y + self.ep
        self.rows_z = self.sy + 2
        self.slab = self.rows_e + self.q * self.rows_z
        assert self.q == 4 and self.y == 16 and self.z == 128 and self.ex <= 20 and self.fx == 2 * self.x


def lanes_of(shape):
    return lax.broadcasted_iota(jnp.int32, shape, len(shape) - 1)


def halves(value):
    high = value.astype(BF16)
    return high, (value - high.astype(F32)).astype(BF16)


def times(value, matrix):
    high, low = halves(value)
    return jnp.dot(high, matrix, preferred_element_type=F32) + jnp.dot(low, matrix, preferred_element_type=F32)


def scaled(wind):
    return [w * (-0.5 / diffusion) for w in wind]


def along(wind, low, high):
    return (high + low) + wind * (high - low)


def advanced(base, fraction, wind, center, x_low, x_high, y_low, y_high, vertical):
    total = (vertical + along(wind[0], x_low, x_high)) + along(wind[1], y_low, y_high)
    if base is None:
        return center * (1.0 - 6.0 * diffusion * fraction) + total * (diffusion * fraction)
    return (base - center * (6.0 * diffusion * fraction)) + total * (diffusion * fraction)


def layer_of(s, own, low, high, member, at, width, first):
    size = own.shape[1]
    if at < 0:
        return low[first + width * member + at + width]
    if at >= size:
        return high[first + width * member + at - size]
    return own[member, at]


def unrolled(begin, end, at_once, body, carry=None):
    while (end - begin) % at_once:
        at_once -= 1

    def several(i, carry):
        for more in range(at_once):
            carry = body(begin + i * at_once + more, carry)
        return carry

    return lax.fori_loop(0, (end - begin) // at_once, several, carry)


def pack_kernel(s, fields, wind, up, down, sems):
    size = fields.shape[1]
    moves = []
    for own, members, width, first in ((fields, s.q, 3, 0), (wind, 3, 2, 3 * s.q)):
        for dst, at in ((up, size - width), (down, 0)):
            place = dst.at[first : first + members * width].reshape(members, width, s.y, s.z)
            moves.append((own.at[:, at : at + width], place))
    moves = [pltpu.make_async_copy(src, dst, sems.at[i]) for i, (src, dst) in enumerate(moves)]
    for move in moves:
        move.start()
    for move in moves:
        move.wait()


def y_rows(s, members, width):
    below, above = [], []
    for out, extra in ((below, lambda r: r), (above, lambda r: width - 1 - r)):
        at = 0
        for m in range(members):
            for r in range(width):
                out.append((m, r, extra(r), at))
                at += s.x + 2 * extra(r)
    return below, above


def ypack_kernel(s, c0, cw, lo, hi, up, dn):
    x, y, z = s.x, s.y, s.z
    flat_lo = lo.reshape(s.halo * y, z)
    flat_hi = hi.reshape(s.halo * y, z)
    for own, members, width, first, place in ((c0, s.q, 3, 0, 0), (cw, 3, 2, 3 * s.q, s.rows_f)):
        flat = own.reshape(members * x * y, z)
        for dst, rows, start in zip((up, dn), y_rows(s, members, width), (y - width, 0)):
            for m, r, e, at in rows:
                row, at = start + r, at + place
                if e:
                    dst[at : at + e, :] = flat_lo[pl.ds((first + width * (m + 1) - e) * y + row, e, stride=y), :]
                    dst[at + e + x : at + x + 2 * e, :] = flat_hi[pl.ds((first + width * m) * y + row, e, stride=y), :]
                dst[at + e : at + e + x, :] = flat[pl.ds(m * x * y + row, x, stride=y), :]


EDGE = 4


def turned(base, fraction, wind, center, x_low, x_high):
    y, z = center.shape
    return advanced(
        base,
        fraction,
        wind,
        center,
        x_low,
        x_high,
        pltpu.roll(center, 1, 0),
        pltpu.roll(center, y - 1, 0),
        along(wind[2], pltpu.roll(center, 1, 1), pltpu.roll(center, z - 1, 1)),
    )


def slab_parts(s, rows_of, tile_of, layers_of, put):
    q, y, z = s.q, s.y, s.z
    lane_y = lanes_of((y, z))
    columns = (lane_y == s.lz - 1) | (lane_y == s.lz) | (lane_y == s.lz + s.sz - 1) | (lane_y == s.lz + s.sz)
    low_at = (lane_y % 2 == 0) & (lane_y < z // 2)
    high_at = (lane_y % 2 == 0) & (lane_y >= z // 2)
    ends = None
    for f in range(q):
        zfaces = None
        for k in range(3):
            rows = [rows_of(k, f, row) for row in (s.ly - 1, s.ly, s.ly + s.sy - 1, s.ly + s.sy)]
            sides = (0.75 * rows[0] + 0.25 * rows[1], 0.25 * rows[2] + 0.75 * rows[3])
            lane_x = lanes_of(sides[0].shape)
            put(
                "y",
                (k * q + f) * s.ex,
                jnp.where(lane_x < s.sz, pltpu.roll(sides[0], z - s.lz, 1), pltpu.roll(sides[1], s.lz, 1)),
            )
            for side in range(2):
                e = 4 * (q * k + f) + 2 * side + 1
                before = jnp.where(lane_x == s.lz - 1, sides[side], 0.0)
                after = jnp.where(lane_x == s.lz + s.sz, sides[side], 0.0)
                part = pltpu.roll(before, (e - s.lz + 1) % z, 1) + pltpu.roll(after, (e - 1 - s.lz - s.sz) % z, 1)
                ends = part if ends is None else ends + part
            raw = None
            for a in layers_of(k):
                part = jnp.where(columns, tile_of(k, f, a), 0.0)
                part = pltpu.roll(part, (2 * a - s.lz + 1) % z, 1)
                raw = part if raw is None else raw + part
            beside = pltpu.roll(raw, z - 1, 1)
            low = jnp.where(low_at, 0.75 * raw + 0.25 * beside, 0.0)
            high = jnp.where(high_at, 0.25 * raw + 0.75 * beside, 0.0)
            part = pltpu.roll(low, (2 * s.ex * k - 1) % z, 1) + pltpu.roll(high, (2 * s.ex * k - z // 2) % z, 1)
            zfaces = part if zfaces is None else zfaces + part
        put("z", s.rows_e + f * s.rows_z, zfaces[s.ly - 1 : s.ly + s.sy + 1])
    put("e", s.rows_y, ends)


def inner_kernel(s, c0, cw, part, near, state1, state2):
    q, x, y, z = s.q, s.x, s.y, s.z
    states = (c0, state1, state2)
    for step in range(2):
        src, dst = states[step], states[step + 1]

        def layer(j, carry, step=step, src=src, dst=dst):
            w = scaled([cw[d, j] for d in range(3)])
            for f in range(q):
                base = None if step == 0 else c0[f, j]
                dst[f, j] = turned(base, section_weights[step], w, src[f, j], src[f, j - 1], src[f, j + 1])
            return carry

        unrolled(step + 1, x - 1 - step, 7 if step == 0 else 6, layer)
    for f in range(q):
        near[f, 0] = state1[f, EDGE - 2]
        near[f, 1] = state1[f, x + 1 - EDGE]
    count = s.ex - 2 * EDGE
    part[...] = jnp.zeros_like(part)

    def rows_of(k, f, row):
        flat = states[k].reshape(q * x * y, z)
        return flat[pl.ds((f * x + EDGE - 2) * y + row, count, stride=y), :]

    def put(kind, at, rows):
        if kind == "z":
            part[at : at + s.rows_z, :] = rows
        else:
            part[at + EDGE : at + EDGE + count, :] = rows

    slab_parts(s, rows_of, lambda k, f, a: states[k][f, a - 2], lambda k: range(EDGE, s.ex - EDGE), put)


def slab_kernel(s, c0, cw, lo, hi, part, near, slab, ends0, ends1, ends2):
    q, x, y, z = s.q, s.x, s.y, s.z
    states = (ends0, ends1, ends2)
    places = list(range(-2, EDGE - 2)) + list(range(x + 2 - EDGE, x + 2))
    slab[...] = part[...]
    for j, at in enumerate(places):
        for f in range(q):
            ends0[f, j] = layer_of(s, c0, lo, hi, f, at, 3, 0)
    for step in range(2):
        for j, at in enumerate(places):
            if step == 1 and at in (-2, x + 1):
                for f in range(q):
                    ends2[f, j] = jnp.zeros((y, z), F32)
                continue
            w = scaled([layer_of(s, cw, lo, hi, d, at, 2, 3 * q) for d in range(3)])
            for f in range(q):

                def beside(at, f=f):
                    if step == 0:
                        return layer_of(s, c0, lo, hi, f, at, 3, 0)
                    if at in places:
                        return ends1[f, places.index(at)]
                    return near[f, 0 if at < x // 2 else 1]

                base = None if step == 0 else ends0[f, j]
                states[step + 1][f, j] = turned(
                    base, section_weights[step], w, beside(at), beside(at - 1), beside(at + 1)
                )

    def rows_of(k, f, row):
        flat = states[k].reshape(q * 2 * EDGE * y, z)
        return flat[pl.ds(f * 2 * EDGE * y + row, 2 * EDGE, stride=y), :]

    def put(kind, at, rows):
        if kind == "z":
            slab[at : at + s.rows_z, :] = part[at : at + s.rows_z, :] + rows
        else:
            slab[at : at + EDGE, :] = rows[:EDGE]
            slab[at + s.ex - EDGE : at + s.ex, :] = rows[EDGE:]

    def layers_of(k):
        some = range(0 if k == 0 else 1, EDGE)
        return list(some) + [s.ex - 1 - a for a in some]

    def tile_of(k, f, a):
        return states[k][f, a if a < EDGE else a - s.ex + 2 * EDGE]

    slab_parts(s, rows_of, tile_of, layers_of, put)


WTOP, WPAD = 12, 40
BLOCK = slice(8, 32)


def assemble(s, c0, cw, lo, hi, below, above, pad, wind):
    q, x, y, z = s.q, s.x, s.y, s.z
    flat = pad.reshape(q * s.ep * WPAD, z)
    flat_wind = wind.reshape(3 * s.ex * 24, z)
    for f in range(q):
        for at in range(-3, x + 3):
            pad[f, at + 3, WTOP : WTOP + y, :] = layer_of(s, c0, lo, hi, f, at, 3, 0)
    for d in range(3):
        for at in range(-2, x + 2):
            wind[d, at + 2, 4 : 4 + y, :] = layer_of(s, cw, lo, hi, d, at, 2, 3 * q)
    for src, rows, start in zip((below, above), y_rows(s, q, 3), (WTOP - 3, WTOP + y)):
        for m, r, e, at in rows:
            count = x + 2 * e
            flat[pl.ds((m * s.ep + 3 - e) * WPAD + start + r, count, stride=WPAD), :] = src[at : at + count, :]
    for src, rows, start in zip((below, above), y_rows(s, 3, 2), (2, 4 + y)):
        for m, r, e, at in rows:
            count, at = x + 2 * e, at + s.rows_f
            flat_wind[pl.ds((m * s.ex + 2 - e) * 24 + start + r, count, stride=24), :] = src[at : at + count, :]


def edge_lanes(s, lane, width):
    return (lane < width) | (lane >= s.z - width)


def zpack_kernel(s, c0, cw, lo, hi, below, above, out, pad, wind):
    assemble(s, c0, cw, lo, hi, below, above, pad, wind)
    lane = lanes_of((24, s.z))
    keep = edge_lanes(s, lane, 3)
    for m in range(s.q + 3):
        total = None
        for a in range(s.ex):
            tile = pad[m, a + 1, BLOCK, :] if m < s.q else wind[m - s.q, a]
            part = pltpu.roll(jnp.where(keep, tile, 0.0), (6 * a + 3) % s.z, 1)
            total = part if total is None else total + part
        out[m] = total


def coarse_kernel(
    s, sides, c0, cw, lo, hi, below, above, zown, zin, out, pad0, pad1, pad2, wind, beyond, nearest, vertical
):
    q, x, y, z = s.q, s.x, s.y, s.z
    assemble(s, c0, cw, lo, hi, below, above, pad0, wind)
    pads = (pad0, pad1, pad2)
    lane = lanes_of((24, z))
    group = lane % 6
    from_low = group == 2
    from_high = group == 3
    exists = jnp.where(group < 3, sides[0, 0], sides[0, 1]).astype(F32)
    wind_z = scaled([zin[q + d] for d in range(3)])
    for f in range(q):
        beyond[0, f] = zin[f] * exists
        nearest[0, f] = zown[f]
    for step in range(3):
        src, fraction = pads[step], section_weights[step]
        flat = src.reshape(q * s.ep * WPAD, z)
        flat_wind = wind.reshape(3 * s.ex * 24, z)
        flat_beyond = beyond.reshape(3 * q * 24, z)
        skip, height = (0, 24) if step < 2 else (4, y)
        here = lanes_of((height, z))
        is_first, is_last = here == 0, here == z - 1

        def at_layer(of, f, layer, by, step=step, skip=skip, height=height):
            if step < 2 and not by:
                return of[f, layer, BLOCK, :]
            row = (f * s.ep + layer) * WPAD + 8 + skip + by
            return of.reshape(q * s.ep * WPAD, z)[pl.ds(row, height), :]

        def wind_at(d, a, step=step, skip=skip, height=height):
            if step < 2:
                return wind[d, a]
            return flat_wind[pl.ds((d * s.ex + a) * 24 + skip, height), :]

        def vertical_of(a, packed, step=step, src=src, skip=skip, height=height):
            (w,) = scaled([wind_at(2, a)])
            made = []
            for f in range(q):
                center = at_layer(src, f, a + 1, 0)
                ghost = pltpu.roll(flat_beyond[pl.ds((step * q + f) * 24 + skip, height), :], 2 * z - 6 * a - 3, 1)
                vertical[f, a, :height, :] = along(
                    w,
                    pltpu.roll(jnp.where(is_last, ghost, center), 1, 1),
                    pltpu.roll(jnp.where(is_first, ghost, center), z - 1, 1),
                )
                if step == 1:
                    made.append(packed[f] + pltpu.roll(jnp.where(is_first | is_last, center, 0.0), 6 * a + 3, 1))
            return tuple(made)

        def layer(a, carry, step=step, src=src, fraction=fraction, height=height):
            w = scaled([wind_at(d, a) for d in range(2)])
            for f in range(q):
                value = advanced(
                    None if step == 0 else at_layer(pad0, f, a + 1, 0),
                    fraction,
                    w,
                    at_layer(src, f, a + 1, 0),
                    at_layer(src, f, a, 0),
                    at_layer(src, f, a + 2, 0),
                    at_layer(src, f, a + 1, -1),
                    at_layer(src, f, a + 1, 1),
                    vertical[f, a, :height, :],
                )
                if step == 2:
                    out[f, a - 2] = value
                else:
                    pads[step + 1][f, a + 1, BLOCK, :] = value
            return carry

        begin, end = step, s.ex - step
        start = tuple(jnp.zeros((24, z), F32) for _ in range(q)) if step == 1 else ()
        packed = unrolled(begin, end, 4, vertical_of, start)
        unrolled(begin, end, 4, layer)
        if step == 2:
            break
        for f in range(q):
            if step == 1:
                nearest[1, f] = packed[f]
            ghost, near = beyond[step, f], nearest[step, f]
            value = advanced(
                None if step == 0 else beyond[0, f],
                fraction,
                wind_z,
                ghost,
                pltpu.roll(ghost, 6, 1),
                pltpu.roll(ghost, z - 6, 1),
                pltpu.roll(ghost, 1, 0),
                pltpu.roll(ghost, 23, 0),
                along(
                    wind_z[2],
                    pltpu.roll(jnp.where(from_low, near, ghost), 1, 1),
                    pltpu.roll(jnp.where(from_high, near, ghost), z - 1, 1),
                ),
            )
            beyond[step + 1, f] = value * exists


def fine_kernel(s, f0, fw, flo_there, fhi_there, slab, out, avg, *scratch):
    s1, s2, faces, ghost_rows, zface, flo, fhi, vertical, sems = scratch
    arrivals = [
        pltpu.make_async_copy(flo_there, flo, sems.at[4]),
        pltpu.make_async_copy(fhi_there, fhi, sems.at[5]),
    ]
    for move in arrivals:
        move.start()
    states = (None, s1, s2, s1)
    q, y, z, fx, fe = s.q, s.y, s.z, s.fx, s.fe
    layers = fx + 6
    rows = slice(TOP, TOP + y)
    r = lax.broadcasted_iota(jnp.int32, (z, 2 * z), 0)
    c = lax.broadcasted_iota(jnp.int32, (z, 2 * z), 1)
    near = c // 2
    far = near + 2 * (c % 2) - 1
    same = (far // s.sz == near // s.sz) & (far >= 0)
    to_fine = jnp.where(r == near, 0.75, jnp.where((r == far) & same, 0.25, 0.0)).astype(BF16)
    wide = times(slab[: s.rows_y, :], to_fine)
    ends = slab[s.rows_y : s.rows_y + s.ex, :]
    lane_x = lanes_of((s.ex, z))
    edge = (lane_x == 0) | (lane_x == z - 1)
    half = fe // 2
    for k in range(3):
        for f in range(q):
            for side in range(2):
                e = 4 * (q * k + f) + 2 * side + 1
                corner = jnp.where(edge, 0.25 * pltpu.roll(ends, z - e, 1), 0.0)
                first = (k * q + f) * s.ex
                here = faces.at[(k * q + f) * 2 + side]
                here[: s.ex, :] = wide[first : first + s.ex, side * z : side * z + z] + corner
                a = here[0:half, :]
                b = here[1 : half + 1, :]
                d = here[2 : half + 2, :]
                if k == 0:
                    flat, base, stride = ghost_rows, (2 * f + side) * fe, 1
                else:
                    flat, stride = states[k].reshape(q * layers * PAD, z), PAD
                    base = (f * layers + 1) * PAD + (TOP - 1 if side == 0 else TOP + y)
                flat[pl.ds(base, half, stride=2 * stride), :] = 0.25 * a + 0.75 * b
                flat[pl.ds(base + stride, half, stride=2 * stride), :] = 0.75 * b + 0.25 * d
    for f in range(q):
        at = s.rows_e + f * s.rows_z
        a = slab[at : at + s.sy, :]
        b = slab[at + 1 : at + 1 + s.sy, :]
        d = slab[at + 2 : at + 2 + s.sy, :]
        zface[pl.ds(f * y, s.sy, stride=2), :] = 0.25 * a + 0.75 * b
        zface[pl.ds(f * y + 1, s.sy, stride=2), :] = 0.75 * b + 0.25 * d
        a = zface[f * y : f * y + y, :]
        b = pltpu.roll(a, z - 2, 1)
        d = pltpu.roll(a, z - 4, 1)
        zface[f * y : f * y + y, :] = 0.25 * a + 0.75 * b
        zface[(q + f) * y : (q + f + 1) * y, :] = 0.75 * b + 0.25 * d
    lane = lanes_of((y, z))
    is_first, is_last = lane == 0, lane == z - 1
    row_in = lax.broadcasted_iota(jnp.int32, (y, z), 0)
    is_low, is_high = row_in == 0, row_in == y - 1
    flat_f0 = f0.reshape(q * fx * y, z)

    def field(f, at, inner):
        return f0[f, at] if inner else layer_of(s, f0, flo, fhi, f, at, 3, 0)

    def wind_of(d, at, inner):
        return fw[d, at] if inner else layer_of(s, fw, flo, fhi, d, at, 2, 3 * q)

    def vertical_of(k, t, inner):
        for odd in range(2):
            b = 2 * t + odd
            (w,) = scaled([wind_of(2, b - 2, inner)])
            for f in range(q):
                center = field(f, b - 2, inner) if k == 0 else states[k][f, b + 1, rows, :]
                ghost = zface[(odd * q + f) * y : (odd * q + f + 1) * y, :]
                ghost = pltpu.roll(ghost, (2 * z - 2 * s.ex * k - 2 * t) if inner else -(2 * s.ex * k + 2 * t) % z, 1)
                vertical[f, b] = along(
                    w,
                    pltpu.roll(jnp.where(is_last, ghost, center), 1, 1),
                    pltpu.roll(jnp.where(is_first, ghost, center), z - 1, 1),
                )

    def pair_of_layers(k, t, inner):
        src = states[k]
        for odd in range(2):
            b = 2 * t + odd
            at = b - 2
            w = scaled([wind_of(d, at, inner) for d in range(2)])
            for f in range(q):
                if k == 0:
                    center, x_low, x_high = field(f, at, inner), field(f, at - 1, inner), field(f, at + 1, inner)
                    if inner:
                        row = (f * fx + at) * y
                        y_low, y_high = flat_f0[pl.ds(row - 1, y), :], flat_f0[pl.ds(row + 1, y), :]
                    else:
                        y_low, y_high = pltpu.roll(center, 1, 0), pltpu.roll(center, y - 1, 0)
                    y_low = jnp.where(is_low, ghost_rows[pl.ds(2 * f * fe + b, 1), :], y_low)
                    y_high = jnp.where(is_high, ghost_rows[pl.ds((2 * f + 1) * fe + b, 1), :], y_high)
                    base = None
                else:
                    flat = src.reshape(q * layers * PAD, z)
                    row = (f * layers + b + 1) * PAD + TOP
                    center, x_low, x_high = src[f, b + 1, rows, :], src[f, b, rows, :], src[f, b + 2, rows, :]
                    y_low, y_high = flat[pl.ds(row - 1, y), :], flat[pl.ds(row + 1, y), :]
                    base = field(f, at, inner)
                value = advanced(
                    base, section_weights[k], w, center, x_low, x_high, y_low, y_high, vertical[f, b]
                )
                states[k + 1][f, b + 1, rows, :] = value

    for move in arrivals:
        move.wait()
    moves = []
    for k in range(3):
        outer = (2, 1, 1)[k]
        for part in (vertical_of, pair_of_layers):
            if k < 2:
                for t in list(range(outer)) + list(range(half - outer, half)):
                    part(k, t, False)
            if k == 2 and part is pair_of_layers:
                break
            unrolled(outer, half - outer, 2, lambda t, g, k=k, part=part: part(k, t, True))
    quarter = (half - 2) // 4
    for i in range(4):
        unrolled(1 + i * quarter, 1 + (i + 1) * quarter, 2, lambda t, g: pair_of_layers(2, t, True))
        begin, end = 2 * quarter * i, 2 * quarter * (i + 1)
        moves.append(pltpu.make_async_copy(s1.at[:, 3 + begin : 3 + end, rows], out.at[:, begin:end], sems.at[i]))
        moves[-1].start()
    rz = lax.broadcasted_iota(jnp.int32, (z, z), 0)
    cz = lax.broadcasted_iota(jnp.int32, (z, z), 1)
    flat = s1.reshape(q * layers * PAD, z)
    pairs_z = [jnp.where(cz == rz // 2 + odd * s.sz, 0.125, 0.0).astype(BF16) for odd in range(2)]
    for f in range(q):
        sums = []
        for odd in range(2):
            parts = []
            for p in range(s.x // 2):
                base = (f * layers + 3 + 4 * p + 2 * odd) * PAD + TOP
                part = None
                for more in (0, 1, PAD, PAD + 1):
                    piece = flat[pl.ds(base + more, y // 2, stride=2), :]
                    part = piece if part is None else part + piece
                parts.append(part)
            sums.append(times(jnp.concatenate(parts, axis=0), pairs_z[odd]))
        avg[f] = (sums[0] + sums[1]).reshape(s.x // 2, y // 2, z)
    for move in moves:
        move.wait()


def merge_kernel(s, c3, avg, out, made, sems):
    lane = lanes_of((s.sy, s.z))
    inside = (lane >= s.lz) & (lane < s.lz + s.sz)
    moves = []
    for f in range(s.q):
        for p in range(s.x // 2):
            both = avg[f, p]
            for odd in range(2):
                at = 2 * p + odd
                moved = pltpu.roll(both, s.lz if odd == 0 else s.z - s.lz, 1)
                made[f, at] = c3[f, at]
                made[f, at, s.ly : s.ly + s.sy, :] = jnp.where(inside, moved, c3[f, at, s.ly : s.ly + s.sy, :])
        moves.append(pltpu.make_async_copy(made.at[f], out.at[f], sems.at[f]))
        moves[-1].start()
    for move in moves:
        move.wait()


SHORT = pl.CostEstimate(flops=1, bytes_accessed=1, transcendentals=0)


def run(kernel, name, ins, outs, scratch, megabytes, spaces=None, cost=SHORT):
    spaces = spaces or [pltpu.VMEM] * len(ins)
    outs = [out if isinstance(out[0], tuple) else (out, pltpu.VMEM) for out in outs]
    ins = [i if space is pltpu.SMEM else pltpu.with_memory_space_constraint(i, space) for i, space in zip(ins, spaces)]
    return pl.pallas_call(
        kernel,
        out_shape=tuple(space(dims, F32) for dims, space in outs),
        in_specs=[pl.BlockSpec(memory_space=space) for space in spaces],
        out_specs=tuple(pl.BlockSpec(memory_space=space) for _, space in outs),
        scratch_shapes=scratch,
        compiler_params=pltpu.CompilerParams(vmem_limit_bytes=megabytes << 20),
        cost_estimate=cost,
        name=name,
    )(*ins)


def ring(array, axis, by):
    size = lax.axis_size(axis)
    return lax.ppermute(array, axis, [(i, (i + by) % size) for i in range(size)])


def move_by(array, amount, beside=None):
    size = lax.axis_size("gx")
    work, operands = beside or (lambda: (), ())
    if size <= 8:

        def branch(by, array, *operands):
            return array if by == 0 else ring(array, "gx", by), work(*operands)

        return lax.switch(amount, [functools.partial(branch, by) for by in range(size)], array, *operands)
    for bit in range((size - 1).bit_length()):
        array = jnp.where((amount >> bit) % 2 == 1, ring(array, "gx", 1 << bit), array)
    return array, work(*operands)


def z_columns(zown):
    size = lax.axis_size("gz")
    if size == 1:
        return zown
    if size == 2:
        return lax.ppermute(zown, "gz", [(0, 1), (1, 0)])
    below = lax.broadcasted_iota(jnp.int32, zown.shape, 2) % 6 < 3
    return jnp.where(below, ring(zown, "gz", 1), ring(zown, "gz", -1))


def pack(s, fields, wind, spare, name):
    return run(
        functools.partial(pack_kernel, s),
        name,
        [fields, wind],
        [(s.halo + spare, s.y, s.z)] * 2,
        [pltpu.SemaphoreType.DMA((4,))],
        1,
        [pltpu.HBM] * 2,
    )


def shards(coarse_fields, coarse_wind, fine_fields, fine_wind, fine_owner):
    s = Sizes(coarse_fields.shape, fine_fields.shape)
    q, x, y, z, fx = s.q, s.x, s.y, s.z, s.fx
    size = lax.axis_size("gx")
    offset = (fine_owner[0, 0, 0] - lax.axis_index("gx")) % size
    level = lax.axis_index("gz")
    neighbours = jnp.stack([level > 0, level < lax.axis_size("gz") - 1]).astype(jnp.int32).reshape(1, 2)
    cup, cdown = pack(s, coarse_fields, coarse_wind, 0, "pack_coarse")
    lo, hi = ring(cup, "gx", 1), ring(cdown, "gx", -1)
    part, near = run(
        functools.partial(inner_kernel, s),
        "inner",
        [coarse_fields, coarse_wind],
        [(s.slab, z), (q, 2, y, z)],
        [pltpu.VMEM((q, x, y, z), F32)] * 2,
        3,
    )
    fup, fdown = pack(s, fine_fields, fine_wind, 2, "pack_fine")
    fup, fdown, offset = lax.optimization_barrier((fup, fdown, offset))
    flo, fhi = ring(fup, "gx", 1), ring(fdown, "gx", -1)
    padded = [pltpu.VMEM((q, s.ep, WPAD, z), F32)]
    wind_rows = [pltpu.VMEM((3, s.ex, 24, z), F32)]

    coarse_fields, part, near = lax.optimization_barrier((coarse_fields, part, near))
    coarse_level = [coarse_fields, coarse_wind, lo, hi]
    yup, ydn = run(functools.partial(ypack_kernel, s), "ypack", coarse_level, [(s.rows_f + s.rows_w, z)] * 2, [], 1)
    yrows = [ring(yup, "gy", 1), ring(ydn, "gy", -1)]
    ends = [pltpu.VMEM((q, 2 * EDGE, y, z), F32)] * 3
    (slab,) = run(functools.partial(slab_kernel, s), "slab", coarse_level + [part, near], [(s.slab, z)], ends, 3)
    slab, _ = move_by(slab, (size - offset) % size)
    yrows, slab, flo, fhi = lax.optimization_barrier((yrows, slab, flo, fhi))
    kernel = functools.partial(zpack_kernel, s)
    (zown,) = run(kernel, "zpack", coarse_level + yrows, [(q + 3, 24, z)], padded + wind_rows, 4)
    zin = z_columns(zown)
    layers = fx + 6
    fine_next, averaged = run(
        functools.partial(fine_kernel, s),
        "fine",
        [fine_fields, fine_wind, flo, fhi, slab],
        [((q, fx, y, z), pltpu.HBM), (q, x // 2, y // 2, z)],
        [
            pltpu.VMEM((q, layers, PAD, z), F32),
            pltpu.VMEM((q, layers, PAD, z), F32),
            pltpu.VMEM((6 * q, s.ep, z), F32),
            pltpu.VMEM((2 * q * s.fe, z), F32),
            pltpu.VMEM((2 * q * y, z), F32),
            pltpu.VMEM(flo.shape, F32),
            pltpu.VMEM(fhi.shape, F32),
            pltpu.VMEM((q, s.fe, y, z), F32),
            pltpu.SemaphoreType.DMA((6,)),
        ],
        10,
        [pltpu.VMEM, pltpu.VMEM, pltpu.HBM, pltpu.HBM, pltpu.VMEM],
    )

    def coarse(*ins):
        cost = pl.CostEstimate(flops=40_000_000, bytes_accessed=4_000_000, transcendentals=0)
        columns = [pltpu.VMEM((3, q, 24, z), F32), pltpu.VMEM((2, q, 24, z), F32), pltpu.VMEM((q, s.ex, 24, z), F32)]
        spaces = [pltpu.SMEM] + [pltpu.VMEM] * (len(ins) - 1)
        kernel = functools.partial(coarse_kernel, s)
        return run(kernel, "coarse", ins, [(q, x, y, z)], padded * 3 + wind_rows + columns, 11, spaces, cost)[0]

    averaged, state = move_by(averaged, offset, (coarse, (neighbours, *coarse_level, *yrows, zown, zin)))
    (coarse_next,) = run(
        functools.partial(merge_kernel, s),
        "merge",
        [state, averaged],
        [((q, x, y, z), pltpu.HBM)],
        [pltpu.VMEM((q, x, y, z), F32), pltpu.SemaphoreType.DMA((q,))],
        2,
    )
    return coarse_next, fine_next


def solution(mesh):
    spec = P(None, "gx", "gy", "gz")
    return jax.shard_map(
        shards,
        mesh=mesh,
        in_specs=(spec, spec, spec, spec, P("gx", "gy", "gz")),
        out_specs=(spec, spec),
        check_vma=False,
    )
```

```python
import functools

import jax
import jax.numpy as jnp
from jax import lax
from jax.experimental import pallas as pl
from jax.experimental.pallas import tpu as pltpu
from jax.sharding import PartitionSpec as P

diffusion = 0.05
section_weights = (1.0 / 3.0, 0.5, 1.0)
F32 = jnp.float32
BF16 = jnp.bfloat16
PAD = 32
TOP = 8


class Sizes:
    def __init__(self, coarse_shape, fine_shape):
        self.q, self.x, self.y, self.z = coarse_shape
        self.fx = fine_shape[1]
        self.ly, self.sy = self.y // 4, self.y // 2
        self.lz, self.sz = self.z // 4, self.z // 2
        self.ex = self.x + 4
        self.ep = -(-self.ex // 8) * 8
        self.fe = self.fx + 4
        self.halo = 3 * self.q + 6
        self.rows_f, self.rows_w = self.q * (3 * self.x + 6), 3 * (2 * self.x + 2)
        self.rows_y = 3 * self.q * self.ex
        self.rows_e = self.rows_y + self.ep
        self.rows_z = self.sy + 2
        self.slab = self.rows_e + self.q * self.rows_z
        assert self.q == 4 and self.y == 16 and self.z == 128 and self.ex <= 20 and self.fx == 2 * self.x


def lanes_of(shape):
    return lax.broadcasted_iota(jnp.int32, shape, len(shape) - 1)


def halves(value):
    high = value.astype(BF16)
    return high, (value - high.astype(F32)).astype(BF16)


def times(value, matrix):
    high, low = halves(value)
    return jnp.dot(high, matrix, preferred_element_type=F32) + jnp.dot(low, matrix, preferred_element_type=F32)


def coefficients(fraction, wind):
    out = []
    for w in wind:
        turned_by = w * (-0.5 * fraction)
        out += [diffusion * fraction + turned_by, diffusion * fraction - turned_by]
    return out


def advanced(base, fraction, co, center, x_low, x_high, y_low, y_high, z_low, z_high):
    along = (co[0] * x_high + co[1] * x_low) + (co[2] * y_high + co[3] * y_low) + (co[4] * z_high + co[5] * z_low)
    if base is None:
        return center * (1.0 - 6.0 * diffusion * fraction) + along
    return (base - center * (6.0 * diffusion * fraction)) + along


def layer_of(s, own, low, high, member, at, width, first):
    size = own.shape[1]
    if at < 0:
        return low[first + width * member + at + width]
    if at >= size:
        return high[first + width * member + at - size]
    return own[member, at]


def unrolled(begin, end, at_once, body, carry=None):
    while (end - begin) % at_once:
        at_once -= 1

    def several(i, carry):
        for more in range(at_once):
            carry = body(begin + i * at_once + more, carry)
        return carry

    return lax.fori_loop(0, (end - begin) // at_once, several, carry)


def pack_kernel(s, fields, wind, up, down, sems):
    size = fields.shape[1]
    moves = []
    for own, members, width, first in ((fields, s.q, 3, 0), (wind, 3, 2, 3 * s.q)):
        for dst, at in ((up, size - width), (down, 0)):
            place = dst.at[first : first + members * width].reshape(members, width, s.y, s.z)
            moves.append((own.at[:, at : at + width], place))
    moves = [pltpu.make_async_copy(src, dst, sems.at[i]) for i, (src, dst) in enumerate(moves)]
    for move in moves:
        move.start()
    for move in moves:
        move.wait()


def y_rows(s, members, width):
    below, above = [], []
    for out, extra in ((below, lambda r: r), (above, lambda r: width - 1 - r)):
        at = 0
        for m in range(members):
            for r in range(width):
                out.append((m, r, extra(r), at))
                at += s.x + 2 * extra(r)
    return below, above


def ypack_kernel(s, c0, cw, lo, hi, up, dn):
    x, y, z = s.x, s.y, s.z
    flat_lo = lo.reshape(s.halo * y, z)
    flat_hi = hi.reshape(s.halo * y, z)
    for own, members, width, first, place in ((c0, s.q, 3, 0, 0), (cw, 3, 2, 3 * s.q, s.rows_f)):
        flat = own.reshape(members * x * y, z)
        for dst, rows, start in zip((up, dn), y_rows(s, members, width), (y - width, 0)):
            for m, r, e, at in rows:
                row, at = start + r, at + place
                if e:
                    dst[at : at + e, :] = flat_lo[pl.ds((first + width * (m + 1) - e) * y + row, e, stride=y), :]
                    dst[at + e + x : at + x + 2 * e, :] = flat_hi[pl.ds((first + width * m) * y + row, e, stride=y), :]
                dst[at + e : at + e + x, :] = flat[pl.ds(m * x * y + row, x, stride=y), :]


EDGE = 4


def turned(base, fraction, wind, center, x_low, x_high):
    y, z = center.shape
    return advanced(
        base,
        fraction,
        wind,
        center,
        x_low,
        x_high,
        pltpu.roll(center, 1, 0),
        pltpu.roll(center, y - 1, 0),
        pltpu.roll(center, 1, 1),
        pltpu.roll(center, z - 1, 1),
    )


def slab_parts(s, rows_of, tile_of, layers_of, put):
    q, y, z = s.q, s.y, s.z
    lane_y = lanes_of((y, z))
    columns = (lane_y == s.lz - 1) | (lane_y == s.lz) | (lane_y == s.lz + s.sz - 1) | (lane_y == s.lz + s.sz)
    low_at = (lane_y % 2 == 0) & (lane_y < z // 2)
    high_at = (lane_y % 2 == 0) & (lane_y >= z // 2)
    ends = None
    for f in range(q):
        zfaces = None
        for k in range(3):
            rows = [rows_of(k, f, row) for row in (s.ly - 1, s.ly, s.ly + s.sy - 1, s.ly + s.sy)]
            sides = (0.75 * rows[0] + 0.25 * rows[1], 0.25 * rows[2] + 0.75 * rows[3])
            lane_x = lanes_of(sides[0].shape)
            put(
                "y",
                (k * q + f) * s.ex,
                jnp.where(lane_x < s.sz, pltpu.roll(sides[0], z - s.lz, 1), pltpu.roll(sides[1], s.lz, 1)),
            )
            for side in range(2):
                e = 4 * (q * k + f) + 2 * side + 1
                before = jnp.where(lane_x == s.lz - 1, sides[side], 0.0)
                after = jnp.where(lane_x == s.lz + s.sz, sides[side], 0.0)
                part = pltpu.roll(before, (e - s.lz + 1) % z, 1) + pltpu.roll(after, (e - 1 - s.lz - s.sz) % z, 1)
                ends = part if ends is None else ends + part
            raw = None
            for a in layers_of(k):
                part = jnp.where(columns, tile_of(k, f, a), 0.0)
                part = pltpu.roll(part, (2 * a - s.lz + 1) % z, 1)
                raw = part if raw is None else raw + part
            beside = pltpu.roll(raw, z - 1, 1)
            low = jnp.where(low_at, 0.75 * raw + 0.25 * beside, 0.0)
            high = jnp.where(high_at, 0.25 * raw + 0.75 * beside, 0.0)
            part = pltpu.roll(low, (2 * s.ex * k - 1) % z, 1) + pltpu.roll(high, (2 * s.ex * k - z // 2) % z, 1)
            zfaces = part if zfaces is None else zfaces + part
        put("z", s.rows_e + f * s.rows_z, zfaces[s.ly - 1 : s.ly + s.sy + 1])
    put("e", s.rows_y, ends)


def inner_kernel(s, c0, cw, part, near, state1, state2):
    q, x, y, z = s.q, s.x, s.y, s.z
    states = (c0, state1, state2)
    for step in range(2):
        src, dst = states[step], states[step + 1]

        def layer(j, carry, step=step, src=src, dst=dst):
            w = coefficients(section_weights[step], [cw[d, j] for d in range(3)])
            for f in range(q):
                base = None if step == 0 else c0[f, j]
                dst[f, j] = turned(base, section_weights[step], w, src[f, j], src[f, j - 1], src[f, j + 1])
            return carry

        unrolled(step + 1, x - 1 - step, 2, layer)
    for f in range(q):
        near[f, 0] = state1[f, EDGE - 2]
        near[f, 1] = state1[f, x + 1 - EDGE]
    count = s.ex - 2 * EDGE
    part[...] = jnp.zeros_like(part)

    def rows_of(k, f, row):
        flat = states[k].reshape(q * x * y, z)
        return flat[pl.ds((f * x + EDGE - 2) * y + row, count, stride=y), :]

    def put(kind, at, rows):
        if kind == "z":
            part[at : at + s.rows_z, :] = rows
        else:
            part[at + EDGE : at + EDGE + count, :] = rows

    slab_parts(s, rows_of, lambda k, f, a: states[k][f, a - 2], lambda k: range(EDGE, s.ex - EDGE), put)


def slab_kernel(s, c0, cw, lo, hi, part, near, slab, ends0, ends1, ends2):
    q, x, y, z = s.q, s.x, s.y, s.z
    states = (ends0, ends1, ends2)
    places = list(range(-2, EDGE - 2)) + list(range(x + 2 - EDGE, x + 2))
    slab[...] = part[...]
    for j, at in enumerate(places):
        for f in range(q):
            ends0[f, j] = layer_of(s, c0, lo, hi, f, at, 3, 0)
    for step in range(2):
        for j, at in enumerate(places):
            if step == 1 and at in (-2, x + 1):
                for f in range(q):
                    ends2[f, j] = jnp.zeros((y, z), F32)
                continue
            w = coefficients(section_weights[step], [layer_of(s, cw, lo, hi, d, at, 2, 3 * q) for d in range(3)])
            for f in range(q):

                def beside(at, f=f):
                    if step == 0:
                        return layer_of(s, c0, lo, hi, f, at, 3, 0)
                    if at in places:
                        return ends1[f, places.index(at)]
                    return near[f, 0 if at < x // 2 else 1]

                base = None if step == 0 else ends0[f, j]
                states[step + 1][f, j] = turned(
                    base, section_weights[step], w, beside(at), beside(at - 1), beside(at + 1)
                )

    def rows_of(k, f, row):
        flat = states[k].reshape(q * 2 * EDGE * y, z)
        return flat[pl.ds(f * 2 * EDGE * y + row, 2 * EDGE, stride=y), :]

    def put(kind, at, rows):
        if kind == "z":
            slab[at : at + s.rows_z, :] = part[at : at + s.rows_z, :] + rows
        else:
            slab[at : at + EDGE, :] = rows[:EDGE]
            slab[at + s.ex - EDGE : at + s.ex, :] = rows[EDGE:]

    def layers_of(k):
        some = range(0 if k == 0 else 1, EDGE)
        return list(some) + [s.ex - 1 - a for a in some]

    def tile_of(k, f, a):
        return states[k][f, a if a < EDGE else a - s.ex + 2 * EDGE]

    slab_parts(s, rows_of, tile_of, layers_of, put)


WTOP, WPAD = 12, 40
BLOCK = slice(8, 32)


def assemble(s, c0, cw, lo, hi, below, above, pad, wind):
    q, x, y, z = s.q, s.x, s.y, s.z
    flat = pad.reshape(q * s.ep * WPAD, z)
    flat_wind = wind.reshape(3 * s.ex * 24, z)
    for f in range(q):
        for at in range(-3, x + 3):
            pad[f, at + 3, WTOP : WTOP + y, :] = layer_of(s, c0, lo, hi, f, at, 3, 0)
    for d in range(3):
        for at in range(-2, x + 2):
            wind[d, at + 2, 4 : 4 + y, :] = layer_of(s, cw, lo, hi, d, at, 2, 3 * q)
    for src, rows, start in zip((below, above), y_rows(s, q, 3), (WTOP - 3, WTOP + y)):
        for m, r, e, at in rows:
            count = x + 2 * e
            flat[pl.ds((m * s.ep + 3 - e) * WPAD + start + r, count, stride=WPAD), :] = src[at : at + count, :]
    for src, rows, start in zip((below, above), y_rows(s, 3, 2), (2, 4 + y)):
        for m, r, e, at in rows:
            count, at = x + 2 * e, at + s.rows_f
            flat_wind[pl.ds((m * s.ex + 2 - e) * 24 + start + r, count, stride=24), :] = src[at : at + count, :]


def edge_lanes(s, lane, width):
    return (lane < width) | (lane >= s.z - width)


def zpack_kernel(s, c0, cw, lo, hi, below, above, out, pad, wind):
    assemble(s, c0, cw, lo, hi, below, above, pad, wind)
    lane = lanes_of((24, s.z))
    keep = edge_lanes(s, lane, 3)
    for m in range(s.q + 3):
        total = None
        for a in range(s.ex):
            tile = pad[m, a + 1, BLOCK, :] if m < s.q else wind[m - s.q, a]
            part = pltpu.roll(jnp.where(keep, tile, 0.0), (6 * a + 3) % s.z, 1)
            total = part if total is None else total + part
        out[m] = total


def coarse_kernel(
    s, sides, c0, cw, lo, hi, below, above, zown, zin, out, pad0, pad1, pad2, wind, beyond, nearest
):
    q, x, y, z = s.q, s.x, s.y, s.z
    assemble(s, c0, cw, lo, hi, below, above, pad0, wind)
    pads = (pad0, pad1, pad2)
    lane = lanes_of((24, z))
    group = lane % 6
    from_low = group == 2
    from_high = group == 3
    exists = jnp.where(group < 3, sides[0, 0], sides[0, 1]).astype(F32)
    wind_z = [zin[q + d] for d in range(3)]
    for f in range(q):
        beyond[0, f] = zin[f] * exists
        nearest[0, f] = zown[f]
    for step in range(3):
        src, fraction = pads[step], section_weights[step]
        flat = src.reshape(q * s.ep * WPAD, z)
        flat_wind = wind.reshape(3 * s.ex * 24, z)
        flat_beyond = beyond.reshape(3 * q * 24, z)
        skip, height = (0, 24) if step < 2 else (4, y)
        here = lanes_of((height, z))
        is_first, is_last = here == 0, here == z - 1

        def two_layers(t, packed, step=step, src=src, flat=flat, fraction=fraction, skip=skip, height=height):
            first = step + 2 * t
            packed = list(packed)
            co = []
            for a in (first, first + 1):
                if step < 2:
                    winds = [wind[d, a] for d in range(3)]
                else:
                    winds = [flat_wind[pl.ds((d * s.ex + a) * 24 + skip, height), :] for d in range(3)]
                co.append(coefficients(fraction, winds))
            for f in range(q):

                def at_layer(of, layer, by=0, f=f):
                    if step < 2 and not by:
                        return of[f, layer, BLOCK, :]
                    row = (f * s.ep + layer) * WPAD + 8 + skip + by
                    return of.reshape(flat.shape)[pl.ds(row, height), :]

                beside = flat_beyond[pl.ds((step * q + f) * 24 + skip, height), :]
                row_of = [at_layer(src, first + i) for i in range(4)]
                for i in range(2):
                    a = first + i
                    center = row_of[i + 1]
                    ghost = pltpu.roll(beside, 2 * z - 6 * a - 3, 1)
                    value = advanced(
                        None if step == 0 else at_layer(pad0, a + 1),
                        fraction,
                        co[i],
                        center,
                        row_of[i],
                        row_of[i + 2],
                        at_layer(src, a + 1, -1),
                        at_layer(src, a + 1, 1),
                        pltpu.roll(jnp.where(is_last, ghost, center), 1, 1),
                        pltpu.roll(jnp.where(is_first, ghost, center), z - 1, 1),
                    )
                    if step == 2:
                        out[f, a - 2] = value
                    else:
                        pads[step + 1][f, a + 1, BLOCK, :] = value
                    if step == 0:
                        ends = jnp.where(is_first | is_last, value, 0.0)
                        packed[f] = packed[f] + pltpu.roll(ends, 6 * a + 3, 1)
            return tuple(packed)

        start = tuple(jnp.zeros((24, z), F32) for _ in range(q)) if step == 0 else ()
        packed = unrolled(0, s.ex // 2 - step, 2 + (step == 1), two_layers, start)
        if step == 2:
            break
        for f in range(q):
            if step == 0:
                nearest[1, f] = packed[f]
            ghost, near = beyond[step, f], nearest[step, f]
            value = advanced(
                None if step == 0 else beyond[0, f],
                fraction,
                coefficients(fraction, wind_z),
                ghost,
                pltpu.roll(ghost, 6, 1),
                pltpu.roll(ghost, z - 6, 1),
                pltpu.roll(ghost, 1, 0),
                pltpu.roll(ghost, 23, 0),
                pltpu.roll(jnp.where(from_low, near, ghost), 1, 1),
                pltpu.roll(jnp.where(from_high, near, ghost), z - 1, 1),
            )
            beyond[step + 1, f] = value * exists


def fine_kernel(s, f0, fw, flo_there, fhi_there, slab, out, avg, *scratch):
    s1, s2, faces, ghost_rows, zface, flo, fhi, sems = scratch
    arrivals = [
        pltpu.make_async_copy(flo_there, flo, sems.at[4]),
        pltpu.make_async_copy(fhi_there, fhi, sems.at[5]),
    ]
    for move in arrivals:
        move.start()
    states = (None, s1, s2, s1)
    q, y, z, fx, fe = s.q, s.y, s.z, s.fx, s.fe
    layers = fx + 6
    rows = slice(TOP, TOP + y)
    r = lax.broadcasted_iota(jnp.int32, (z, 2 * z), 0)
    c = lax.broadcasted_iota(jnp.int32, (z, 2 * z), 1)
    near = c // 2
    far = near + 2 * (c % 2) - 1
    same = (far // s.sz == near // s.sz) & (far >= 0)
    to_fine = jnp.where(r == near, 0.75, jnp.where((r == far) & same, 0.25, 0.0)).astype(BF16)
    wide = times(slab[: s.rows_y, :], to_fine)
    ends = slab[s.rows_y : s.rows_y + s.ex, :]
    lane_x = lanes_of((s.ex, z))
    edge = (lane_x == 0) | (lane_x == z - 1)
    half = fe // 2
    for k in range(3):
        for f in range(q):
            for side in range(2):
                e = 4 * (q * k + f) + 2 * side + 1
                corner = jnp.where(edge, 0.25 * pltpu.roll(ends, z - e, 1), 0.0)
                first = (k * q + f) * s.ex
                here = faces.at[(k * q + f) * 2 + side]
                here[: s.ex, :] = wide[first : first + s.ex, side * z : side * z + z] + corner
                a = here[0:half, :]
                b = here[1 : half + 1, :]
                d = here[2 : half + 2, :]
                if k == 0:
                    flat, base, stride = ghost_rows, (2 * f + side) * fe, 1
                else:
                    flat, stride = states[k].reshape(q * layers * PAD, z), PAD
                    base = (f * layers + 1) * PAD + (TOP - 1 if side == 0 else TOP + y)
                flat[pl.ds(base, half, stride=2 * stride), :] = 0.25 * a + 0.75 * b
                flat[pl.ds(base + stride, half, stride=2 * stride), :] = 0.75 * b + 0.25 * d
    for f in range(q):
        at = s.rows_e + f * s.rows_z
        a = slab[at : at + s.sy, :]
        b = slab[at + 1 : at + 1 + s.sy, :]
        d = slab[at + 2 : at + 2 + s.sy, :]
        zface[pl.ds(f * y, s.sy, stride=2), :] = 0.25 * a + 0.75 * b
        zface[pl.ds(f * y + 1, s.sy, stride=2), :] = 0.75 * b + 0.25 * d
        a = zface[f * y : f * y + y, :]
        b = pltpu.roll(a, z - 2, 1)
        d = pltpu.roll(a, z - 4, 1)
        zface[f * y : f * y + y, :] = 0.25 * a + 0.75 * b
        zface[(q + f) * y : (q + f + 1) * y, :] = 0.75 * b + 0.25 * d
    lane = lanes_of((y, z))
    is_first, is_last = lane == 0, lane == z - 1
    row_in = lax.broadcasted_iota(jnp.int32, (y, z), 0)
    is_low, is_high = row_in == 0, row_in == y - 1
    flat_f0 = f0.reshape(q * fx * y, z)

    def pair_of_layers(k, t, inner):
        src, fraction = states[k], section_weights[k]

        def field(f, at):
            return f0[f, at] if inner else layer_of(s, f0, flo, fhi, f, at, 3, 0)

        co = []
        for at in (2 * t - 2, 2 * t - 1):
            if inner:
                winds = [fw[d, at] for d in range(3)]
            else:
                winds = [layer_of(s, fw, flo, fhi, d, at, 2, 3 * q) for d in range(3)]
            co.append(coefficients(fraction, winds))
        for f in range(q):
            if k == 0:
                row_of = [field(f, 2 * t - 3 + i) for i in range(4)]
            else:
                row_of = [src[f, 2 * t + i, rows, :] for i in range(4)]
            for odd in range(2):
                b = 2 * t + odd
                center = row_of[odd + 1]
                if k == 0:
                    if inner:
                        row = (f * fx + b - 2) * y
                        y_low, y_high = flat_f0[pl.ds(row - 1, y), :], flat_f0[pl.ds(row + 1, y), :]
                    else:
                        y_low, y_high = pltpu.roll(center, 1, 0), pltpu.roll(center, y - 1, 0)
                    y_low = jnp.where(is_low, ghost_rows[pl.ds(2 * f * fe + b, 1), :], y_low)
                    y_high = jnp.where(is_high, ghost_rows[pl.ds((2 * f + 1) * fe + b, 1), :], y_high)
                else:
                    flat = src.reshape(q * layers * PAD, z)
                    row = (f * layers + b + 1) * PAD + TOP
                    y_low, y_high = flat[pl.ds(row - 1, y), :], flat[pl.ds(row + 1, y), :]
                ghost = zface[(odd * q + f) * y : (odd * q + f + 1) * y, :]
                ghost = pltpu.roll(ghost, (2 * z - 2 * s.ex * k - 2 * t) if inner else -(2 * s.ex * k + 2 * t) % z, 1)
                states[k + 1][f, b + 1, rows, :] = advanced(
                    None if k == 0 else field(f, b - 2),
                    fraction,
                    co[odd],
                    center,
                    row_of[odd],
                    row_of[odd + 2],
                    y_low,
                    y_high,
                    pltpu.roll(jnp.where(is_last, ghost, center), 1, 1),
                    pltpu.roll(jnp.where(is_first, ghost, center), z - 1, 1),
                )

    for move in arrivals:
        move.wait()
    moves = []
    for k in range(3):
        if k < 2:
            outer = 2 - k
            for t in list(range(outer)) + list(range(half - outer, half)):
                pair_of_layers(k, t, False)
            unrolled(outer, half - outer, 2, lambda t, g, k=k: pair_of_layers(k, t, True))
            continue
        part = (half - 2) // 4
        for i in range(4):
            unrolled(1 + i * part, 1 + (i + 1) * part, 2, lambda t, g, k=k: pair_of_layers(k, t, True))
            begin, end = 2 * part * i, 2 * part * (i + 1)
            moves.append(pltpu.make_async_copy(s1.at[:, 3 + begin : 3 + end, rows], out.at[:, begin:end], sems.at[i]))
            moves[-1].start()
    rz = lax.broadcasted_iota(jnp.int32, (z, z), 0)
    cz = lax.broadcasted_iota(jnp.int32, (z, z), 1)
    flat = s1.reshape(q * layers * PAD, z)
    pairs_z = [jnp.where(cz == rz // 2 + odd * s.sz, 0.125, 0.0).astype(BF16) for odd in range(2)]
    for f in range(q):
        sums = []
        for odd in range(2):
            parts = []
            for p in range(s.x // 2):
                base = (f * layers + 3 + 4 * p + 2 * odd) * PAD + TOP
                part = None
                for more in (0, 1, PAD, PAD + 1):
                    piece = flat[pl.ds(base + more, y // 2, stride=2), :]
                    part = piece if part is None else part + piece
                parts.append(part)
            sums.append(times(jnp.concatenate(parts, axis=0), pairs_z[odd]))
        avg[f] = (sums[0] + sums[1]).reshape(s.x // 2, y // 2, z)
    for move in moves:
        move.wait()


def merge_kernel(s, c3, avg, out, made, sems):
    lane = lanes_of((s.sy, s.z))
    inside = (lane >= s.lz) & (lane < s.lz + s.sz)
    moves = []
    for f in range(s.q):
        for p in range(s.x // 2):
            both = avg[f, p]
            for odd in range(2):
                at = 2 * p + odd
                moved = pltpu.roll(both, s.lz if odd == 0 else s.z - s.lz, 1)
                made[f, at] = c3[f, at]
                made[f, at, s.ly : s.ly + s.sy, :] = jnp.where(inside, moved, c3[f, at, s.ly : s.ly + s.sy, :])
        moves.append(pltpu.make_async_copy(made.at[f], out.at[f], sems.at[f]))
        moves[-1].start()
    for move in moves:
        move.wait()


SHORT = pl.CostEstimate(flops=1, bytes_accessed=1, transcendentals=0)


def run(kernel, name, ins, outs, scratch, megabytes, spaces=None, cost=SHORT):
    spaces = spaces or [pltpu.VMEM] * len(ins)
    outs = [out if isinstance(out[0], tuple) else (out, pltpu.VMEM) for out in outs]
    ins = [i if space is pltpu.SMEM else pltpu.with_memory_space_constraint(i, space) for i, space in zip(ins, spaces)]
    return pl.pallas_call(
        kernel,
        out_shape=tuple(space(dims, F32) for dims, space in outs),
        in_specs=[pl.BlockSpec(memory_space=space) for space in spaces],
        out_specs=tuple(pl.BlockSpec(memory_space=space) for _, space in outs),
        scratch_shapes=scratch,
        compiler_params=pltpu.CompilerParams(vmem_limit_bytes=megabytes << 20),
        cost_estimate=cost,
        name=name,
    )(*ins)


def ring(array, axis, by):
    size = lax.axis_size(axis)
    return lax.ppermute(array, axis, [(i, (i + by) % size) for i in range(size)])


def move_by(array, amount, beside=None):
    size = lax.axis_size("gx")
    work, operands = beside or (lambda: (), ())
    if size <= 8:

        def branch(by, array, *operands):
            return array if by == 0 else ring(array, "gx", by), work(*operands)

        return lax.switch(amount, [functools.partial(branch, by) for by in range(size)], array, *operands)
    for bit in range((size - 1).bit_length()):
        array = jnp.where((amount >> bit) % 2 == 1, ring(array, "gx", 1 << bit), array)
    return array, work(*operands)


def z_columns(zown):
    size = lax.axis_size("gz")
    if size == 1:
        return zown
    if size == 2:
        return lax.ppermute(zown, "gz", [(0, 1), (1, 0)])
    below = lax.broadcasted_iota(jnp.int32, zown.shape, 2) % 6 < 3
    return jnp.where(below, ring(zown, "gz", 1), ring(zown, "gz", -1))


def pack(s, fields, wind, spare, name):
    return run(
        functools.partial(pack_kernel, s),
        name,
        [fields, wind],
        [(s.halo + spare, s.y, s.z)] * 2,
        [pltpu.SemaphoreType.DMA((4,))],
        1,
        [pltpu.HBM] * 2,
    )


def shards(coarse_fields, coarse_wind, fine_fields, fine_wind, fine_owner):
    s = Sizes(coarse_fields.shape, fine_fields.shape)
    q, x, y, z, fx = s.q, s.x, s.y, s.z, s.fx
    size = lax.axis_size("gx")
    offset = (fine_owner[0, 0, 0] - lax.axis_index("gx")) % size
    level = lax.axis_index("gz")
    neighbours = jnp.stack([level > 0, level < lax.axis_size("gz") - 1]).astype(jnp.int32).reshape(1, 2)
    cup, cdown = pack(s, coarse_fields, coarse_wind, 0, "pack_coarse")
    lo, hi = ring(cup, "gx", 1), ring(cdown, "gx", -1)
    part, near = run(
        functools.partial(inner_kernel, s),
        "inner",
        [coarse_fields, coarse_wind],
        [(s.slab, z), (q, 2, y, z)],
        [pltpu.VMEM((q, x, y, z), F32)] * 2,
        3,
    )
    fup, fdown = pack(s, fine_fields, fine_wind, 2, "pack_fine")
    fup, fdown, offset = lax.optimization_barrier((fup, fdown, offset))
    flo, fhi = ring(fup, "gx", 1), ring(fdown, "gx", -1)
    padded = [pltpu.VMEM((q, s.ep, WPAD, z), F32)]
    wind_rows = [pltpu.VMEM((3, s.ex, 24, z), F32)]

    coarse_fields, part, near = lax.optimization_barrier((coarse_fields, part, near))
    coarse_level = [coarse_fields, coarse_wind, lo, hi]
    yup, ydn = run(functools.partial(ypack_kernel, s), "ypack", coarse_level, [(s.rows_f + s.rows_w, z)] * 2, [], 1)
    yrows = [ring(yup, "gy", 1), ring(ydn, "gy", -1)]
    ends = [pltpu.VMEM((q, 2 * EDGE, y, z), F32)] * 3
    (slab,) = run(functools.partial(slab_kernel, s), "slab", coarse_level + [part, near], [(s.slab, z)], ends, 3)
    slab, _ = move_by(slab, (size - offset) % size)
    yrows, slab, flo, fhi = lax.optimization_barrier((yrows, slab, flo, fhi))
    kernel = functools.partial(zpack_kernel, s)
    (zown,) = run(kernel, "zpack", coarse_level + yrows, [(q + 3, 24, z)], padded + wind_rows, 4)
    zin = z_columns(zown)
    layers = fx + 6
    fine_next, averaged = run(
        functools.partial(fine_kernel, s),
        "fine",
        [fine_fields, fine_wind, flo, fhi, slab],
        [((q, fx, y, z), pltpu.HBM), (q, x // 2, y // 2, z)],
        [
            pltpu.VMEM((q, layers, PAD, z), F32),
            pltpu.VMEM((q, layers, PAD, z), F32),
            pltpu.VMEM((6 * q, s.ep, z), F32),
            pltpu.VMEM((2 * q * s.fe, z), F32),
            pltpu.VMEM((2 * q * y, z), F32),
            pltpu.VMEM(flo.shape, F32),
            pltpu.VMEM(fhi.shape, F32),
            pltpu.SemaphoreType.DMA((6,)),
        ],
        9,
        [pltpu.VMEM, pltpu.VMEM, pltpu.HBM, pltpu.HBM, pltpu.VMEM],
    )

    def coarse(*ins):
        cost = pl.CostEstimate(flops=40_000_000, bytes_accessed=4_000_000, transcendentals=0)
        columns = [pltpu.VMEM((3, q, 24, z), F32), pltpu.VMEM((2, q, 24, z), F32)]
        spaces = [pltpu.SMEM] + [pltpu.VMEM] * (len(ins) - 1)
        kernel = functools.partial(coarse_kernel, s)
        return run(kernel, "coarse", ins, [(q, x, y, z)], padded * 3 + wind_rows + columns, 9, spaces, cost)[0]

    averaged, state = move_by(averaged, offset, (coarse, (neighbours, *coarse_level, *yrows, zown, zin)))
    (coarse_next,) = run(
        functools.partial(merge_kernel, s),
        "merge",
        [state, averaged],
        [((q, x, y, z), pltpu.HBM)],
        [pltpu.VMEM((q, x, y, z), F32), pltpu.SemaphoreType.DMA((q,))],
        2,
    )
    return coarse_next, fine_next


def solution(mesh):
    spec = P(None, "gx", "gy", "gz")
    return jax.shard_map(
        shards,
        mesh=mesh,
        in_specs=(spec, spec, spec, spec, P("gx", "gy", "gz")),
        out_specs=(spec, spec),
        check_vma=False,
    )
```

```python
import functools

import jax
import jax.numpy as jnp
from jax import lax
from jax.experimental import pallas as pl
from jax.experimental.pallas import tpu as pltpu
from jax.sharding import PartitionSpec as P

diffusion = 0.05
section_weights = (1.0 / 3.0, 0.5, 1.0)
F32 = jnp.float32
BF16 = jnp.bfloat16
PAD = 32
TOP = 8


class Sizes:
    def __init__(self, coarse_shape, fine_shape):
        self.q, self.x, self.y, self.z = coarse_shape
        self.fx = fine_shape[1]
        self.ly, self.sy = self.y // 4, self.y // 2
        self.lz, self.sz = self.z // 4, self.z // 2
        self.ex = self.x + 4
        self.ep = -(-self.ex // 8) * 8
        self.fe = self.fx + 4
        self.halo = 3 * self.q + 6
        self.rows_f, self.rows_w = self.q * (3 * self.x + 6), 3 * (2 * self.x + 2)
        self.rows_y = 3 * self.q * self.ex
        self.rows_e = self.rows_y + self.ep
        self.rows_z = self.sy + 2
        self.slab = self.rows_e + self.q * self.rows_z
        assert self.q == 4 and self.y == 16 and self.z == 128 and self.ex <= 20 and self.fx == 2 * self.x


def lanes_of(shape):
    return lax.broadcasted_iota(jnp.int32, shape, len(shape) - 1)


def halves(value):
    high = value.astype(BF16)
    return high, (value - high.astype(F32)).astype(BF16)


def times(value, matrix):
    high, low = halves(value)
    return jnp.dot(high, matrix, preferred_element_type=F32) + jnp.dot(low, matrix, preferred_element_type=F32)


def coefficients(fraction, wind):
    out = []
    for w in wind:
        turned_by = w * (-0.5 * fraction)
        out += [diffusion * fraction + turned_by, diffusion * fraction - turned_by]
    return out


def advanced(base, fraction, co, center, x_low, x_high, y_low, y_high, z_low, z_high):
    along = (co[0] * x_high + co[1] * x_low) + (co[2] * y_high + co[3] * y_low) + (co[4] * z_high + co[5] * z_low)
    if base is None:
        return center * (1.0 - 6.0 * diffusion * fraction) + along
    return (base - center * (6.0 * diffusion * fraction)) + along


def layer_of(s, own, low, high, member, at, width, first):
    size = own.shape[1]
    if at < 0:
        return low[first + width * member + at + width]
    if at >= size:
        return high[first + width * member + at - size]
    return own[member, at]


def unrolled(begin, end, at_once, body, carry=None):
    while (end - begin) % at_once:
        at_once -= 1

    def several(i, carry):
        for more in range(at_once):
            carry = body(begin + i * at_once + more, carry)
        return carry

    return lax.fori_loop(0, (end - begin) // at_once, several, carry)


def pack_kernel(s, fields, wind, up, down, sems):
    size = fields.shape[1]
    moves = []
    for own, members, width, first in ((fields, s.q, 3, 0), (wind, 3, 2, 3 * s.q)):
        for dst, at in ((up, size - width), (down, 0)):
            place = dst.at[first : first + members * width].reshape(members, width, s.y, s.z)
            moves.append((own.at[:, at : at + width], place))
    moves = [pltpu.make_async_copy(src, dst, sems.at[i]) for i, (src, dst) in enumerate(moves)]
    for move in moves:
        move.start()
    for move in moves:
        move.wait()


def y_rows(s, members, width):
    below, above = [], []
    for out, extra in ((below, lambda r: r), (above, lambda r: width - 1 - r)):
        at = 0
        for m in range(members):
            for r in range(width):
                out.append((m, r, extra(r), at))
                at += s.x + 2 * extra(r)
    return below, above


def ypack_kernel(s, c0, cw, lo, hi, up, dn):
    x, y, z = s.x, s.y, s.z
    flat_lo = lo.reshape(s.halo * y, z)
    flat_hi = hi.reshape(s.halo * y, z)
    for own, members, width, first, place in ((c0, s.q, 3, 0, 0), (cw, 3, 2, 3 * s.q, s.rows_f)):
        flat = own.reshape(members * x * y, z)
        for dst, rows, start in zip((up, dn), y_rows(s, members, width), (y - width, 0)):
            for m, r, e, at in rows:
                row, at = start + r, at + place
                if e:
                    dst[at : at + e, :] = flat_lo[pl.ds((first + width * (m + 1) - e) * y + row, e, stride=y), :]
                    dst[at + e + x : at + x + 2 * e, :] = flat_hi[pl.ds((first + width * m) * y + row, e, stride=y), :]
                dst[at + e : at + e + x, :] = flat[pl.ds(m * x * y + row, x, stride=y), :]


EDGE = 4


def turned(base, fraction, wind, center, x_low, x_high):
    y, z = center.shape
    return advanced(
        base,
        fraction,
        wind,
        center,
        x_low,
        x_high,
        pltpu.roll(center, 1, 0),
        pltpu.roll(center, y - 1, 0),
        pltpu.roll(center, 1, 1),
        pltpu.roll(center, z - 1, 1),
    )


def slab_parts(s, rows_of, tile_of, layers_of, put):
    q, y, z = s.q, s.y, s.z
    lane_y = lanes_of((y, z))
    columns = (lane_y == s.lz - 1) | (lane_y == s.lz) | (lane_y == s.lz + s.sz - 1) | (lane_y == s.lz + s.sz)
    low_at = (lane_y % 2 == 0) & (lane_y < z // 2)
    high_at = (lane_y % 2 == 0) & (lane_y >= z // 2)
    ends = None
    for f in range(q):
        zfaces = None
        for k in range(3):
            rows = [rows_of(k, f, row) for row in (s.ly - 1, s.ly, s.ly + s.sy - 1, s.ly + s.sy)]
            sides = (0.75 * rows[0] + 0.25 * rows[1], 0.25 * rows[2] + 0.75 * rows[3])
            lane_x = lanes_of(sides[0].shape)
            put(
                "y",
                (k * q + f) * s.ex,
                jnp.where(lane_x < s.sz, pltpu.roll(sides[0], z - s.lz, 1), pltpu.roll(sides[1], s.lz, 1)),
            )
            for side in range(2):
                e = 4 * (q * k + f) + 2 * side + 1
                before = jnp.where(lane_x == s.lz - 1, sides[side], 0.0)
                after = jnp.where(lane_x == s.lz + s.sz, sides[side], 0.0)
                part = pltpu.roll(before, (e - s.lz + 1) % z, 1) + pltpu.roll(after, (e - 1 - s.lz - s.sz) % z, 1)
                ends = part if ends is None else ends + part
            raw = None
            for a in layers_of(k):
                part = jnp.where(columns, tile_of(k, f, a), 0.0)
                part = pltpu.roll(part, (2 * a - s.lz + 1) % z, 1)
                raw = part if raw is None else raw + part
            beside = pltpu.roll(raw, z - 1, 1)
            low = jnp.where(low_at, 0.75 * raw + 0.25 * beside, 0.0)
            high = jnp.where(high_at, 0.25 * raw + 0.75 * beside, 0.0)
            part = pltpu.roll(low, (2 * s.ex * k - 1) % z, 1) + pltpu.roll(high, (2 * s.ex * k - z // 2) % z, 1)
            zfaces = part if zfaces is None else zfaces + part
        put("z", s.rows_e + f * s.rows_z, zfaces[s.ly - 1 : s.ly + s.sy + 1])
    put("e", s.rows_y, ends)


def inner_kernel(s, c0, cw, part, near, state1, state2):
    q, x, y, z = s.q, s.x, s.y, s.z
    states = (c0, state1, state2)
    for step in range(2):
        src, dst = states[step], states[step + 1]

        def layer(j, carry, step=step, src=src, dst=dst):
            w = coefficients(section_weights[step], [cw[d, j] for d in range(3)])
            made = []
            for f in range(q):
                base = None if step == 0 else c0[f, j]
                made.append(turned(base, section_weights[step], w, src[f, j], src[f, j - 1], src[f, j + 1]))
            for f in range(q):
                dst[f, j] = made[f]
            return carry

        unrolled(step + 1, x - 1 - step, 7 if step == 0 else 6, layer)
    for f in range(q):
        near[f, 0] = state1[f, EDGE - 2]
        near[f, 1] = state1[f, x + 1 - EDGE]
    count = s.ex - 2 * EDGE
    part[...] = jnp.zeros_like(part)

    def rows_of(k, f, row):
        flat = states[k].reshape(q * x * y, z)
        return flat[pl.ds((f * x + EDGE - 2) * y + row, count, stride=y), :]

    def put(kind, at, rows):
        if kind == "z":
            part[at : at + s.rows_z, :] = rows
        else:
            part[at + EDGE : at + EDGE + count, :] = rows

    slab_parts(s, rows_of, lambda k, f, a: states[k][f, a - 2], lambda k: range(EDGE, s.ex - EDGE), put)


def slab_kernel(s, c0, cw, lo, hi, part, near, slab, ends0, ends1, ends2):
    q, x, y, z = s.q, s.x, s.y, s.z
    states = (ends0, ends1, ends2)
    places = list(range(-2, EDGE - 2)) + list(range(x + 2 - EDGE, x + 2))
    slab[...] = part[...]
    for j, at in enumerate(places):
        for f in range(q):
            ends0[f, j] = layer_of(s, c0, lo, hi, f, at, 3, 0)
    for step in range(2):
        for j, at in enumerate(places):
            if step == 1 and at in (-2, x + 1):
                for f in range(q):
                    ends2[f, j] = jnp.zeros((y, z), F32)
                continue
            w = coefficients(section_weights[step], [layer_of(s, cw, lo, hi, d, at, 2, 3 * q) for d in range(3)])
            for f in range(q):

                def beside(at, f=f):
                    if step == 0:
                        return layer_of(s, c0, lo, hi, f, at, 3, 0)
                    if at in places:
                        return ends1[f, places.index(at)]
                    return near[f, 0 if at < x // 2 else 1]

                base = None if step == 0 else ends0[f, j]
                states[step + 1][f, j] = turned(
                    base, section_weights[step], w, beside(at), beside(at - 1), beside(at + 1)
                )

    def rows_of(k, f, row):
        flat = states[k].reshape(q * 2 * EDGE * y, z)
        return flat[pl.ds(f * 2 * EDGE * y + row, 2 * EDGE, stride=y), :]

    def put(kind, at, rows):
        if kind == "z":
            slab[at : at + s.rows_z, :] = part[at : at + s.rows_z, :] + rows
        else:
            slab[at : at + EDGE, :] = rows[:EDGE]
            slab[at + s.ex - EDGE : at + s.ex, :] = rows[EDGE:]

    def layers_of(k):
        some = range(0 if k == 0 else 1, EDGE)
        return list(some) + [s.ex - 1 - a for a in some]

    def tile_of(k, f, a):
        return states[k][f, a if a < EDGE else a - s.ex + 2 * EDGE]

    slab_parts(s, rows_of, tile_of, layers_of, put)


WTOP, WPAD = 12, 40
BLOCK = slice(8, 32)


def assemble(s, c0, cw, lo, hi, below, above, pad, wind):
    q, x, y, z = s.q, s.x, s.y, s.z
    flat = pad.reshape(q * s.ep * WPAD, z)
    flat_wind = wind.reshape(3 * s.ex * 24, z)
    for f in range(q):
        for at in range(-3, x + 3):
            pad[f, at + 3, WTOP : WTOP + y, :] = layer_of(s, c0, lo, hi, f, at, 3, 0)
    for d in range(3):
        for at in range(-2, x + 2):
            wind[d, at + 2, 4 : 4 + y, :] = layer_of(s, cw, lo, hi, d, at, 2, 3 * q)
    for src, rows, start in zip((below, above), y_rows(s, q, 3), (WTOP - 3, WTOP + y)):
        for m, r, e, at in rows:
            count = x + 2 * e
            flat[pl.ds((m * s.ep + 3 - e) * WPAD + start + r, count, stride=WPAD), :] = src[at : at + count, :]
    for src, rows, start in zip((below, above), y_rows(s, 3, 2), (2, 4 + y)):
        for m, r, e, at in rows:
            count, at = x + 2 * e, at + s.rows_f
            flat_wind[pl.ds((m * s.ex + 2 - e) * 24 + start + r, count, stride=24), :] = src[at : at + count, :]


def edge_lanes(s, lane, width):
    return (lane < width) | (lane >= s.z - width)


def zpack_kernel(s, c0, cw, lo, hi, below, above, out, pad, wind):
    assemble(s, c0, cw, lo, hi, below, above, pad, wind)
    lane = lanes_of((24, s.z))
    keep = edge_lanes(s, lane, 3)
    for m in range(s.q + 3):
        total = None
        for a in range(s.ex):
            tile = pad[m, a + 1, BLOCK, :] if m < s.q else wind[m - s.q, a]
            part = pltpu.roll(jnp.where(keep, tile, 0.0), (6 * a + 3) % s.z, 1)
            total = part if total is None else total + part
        out[m] = total


def coarse_kernel(
    s, sides, c0, cw, lo, hi, below, above, zown, zin, out, pad0, pad1, pad2, wind, beyond, nearest
):
    q, x, y, z = s.q, s.x, s.y, s.z
    assemble(s, c0, cw, lo, hi, below, above, pad0, wind)
    pads = (pad0, pad1, pad2)
    lane = lanes_of((24, z))
    group = lane % 6
    from_low = group == 2
    from_high = group == 3
    exists = jnp.where(group < 3, sides[0, 0], sides[0, 1]).astype(F32)
    wind_z = [zin[q + d] for d in range(3)]
    for f in range(q):
        beyond[0, f] = zin[f] * exists
        nearest[0, f] = zown[f]
    for step in range(3):
        src, fraction = pads[step], section_weights[step]
        flat = src.reshape(q * s.ep * WPAD, z)
        flat_wind = wind.reshape(3 * s.ex * 24, z)
        flat_beyond = beyond.reshape(3 * q * 24, z)
        skip, height = (0, 24) if step < 2 else (4, y)
        here = lanes_of((height, z))
        is_first, is_last = here == 0, here == z - 1

        def two_layers(t, packed, step=step, src=src, flat=flat, fraction=fraction, skip=skip, height=height):
            first = step + 2 * t
            packed = list(packed)
            made = []
            co = []
            for a in (first, first + 1):
                if step < 2:
                    winds = [wind[d, a] for d in range(3)]
                else:
                    winds = [flat_wind[pl.ds((d * s.ex + a) * 24 + skip, height), :] for d in range(3)]
                co.append(coefficients(fraction, winds))
            for f in range(q):

                def at_layer(of, layer, by=0, f=f):
                    if step < 2 and not by:
                        return of[f, layer, BLOCK, :]
                    row = (f * s.ep + layer) * WPAD + 8 + skip + by
                    return of.reshape(flat.shape)[pl.ds(row, height), :]

                beside = flat_beyond[pl.ds((step * q + f) * 24 + skip, height), :]
                row_of = [at_layer(src, first + i) for i in range(4)]
                for i in range(2):
                    a = first + i
                    center = row_of[i + 1]
                    ghost = pltpu.roll(beside, 2 * z - 6 * a - 3, 1)
                    value = advanced(
                        None if step == 0 else at_layer(pad0, a + 1),
                        fraction,
                        co[i],
                        center,
                        row_of[i],
                        row_of[i + 2],
                        at_layer(src, a + 1, -1),
                        at_layer(src, a + 1, 1),
                        pltpu.roll(jnp.where(is_last, ghost, center), 1, 1),
                        pltpu.roll(jnp.where(is_first, ghost, center), z - 1, 1),
                    )
                    made.append((f, a, value))
                    if step == 0:
                        ends = jnp.where(is_first | is_last, value, 0.0)
                        packed[f] = packed[f] + pltpu.roll(ends, 6 * a + 3, 1)
            for f, a, value in made:
                if step == 2:
                    out[f, a - 2] = value
                else:
                    pads[step + 1][f, a + 1, BLOCK, :] = value
            return tuple(packed)

        start = tuple(jnp.zeros((24, z), F32) for _ in range(q)) if step == 0 else ()
        packed = unrolled(0, s.ex // 2 - step, 2 + (step == 1), two_layers, start)
        if step == 2:
            break
        for f in range(q):
            if step == 0:
                nearest[1, f] = packed[f]
            ghost, near = beyond[step, f], nearest[step, f]
            value = advanced(
                None if step == 0 else beyond[0, f],
                fraction,
                coefficients(fraction, wind_z),
                ghost,
                pltpu.roll(ghost, 6, 1),
                pltpu.roll(ghost, z - 6, 1),
                pltpu.roll(ghost, 1, 0),
                pltpu.roll(ghost, 23, 0),
                pltpu.roll(jnp.where(from_low, near, ghost), 1, 1),
                pltpu.roll(jnp.where(from_high, near, ghost), z - 1, 1),
            )
            beyond[step + 1, f] = value * exists


def fine_kernel(s, f0, fw, flo_there, fhi_there, slab, out, avg, *scratch):
    s1, s2, faces, ghost_rows, zface, flo, fhi, sems = scratch
    arrivals = [
        pltpu.make_async_copy(flo_there, flo, sems.at[4]),
        pltpu.make_async_copy(fhi_there, fhi, sems.at[5]),
    ]
    for move in arrivals:
        move.start()
    states = (None, s1, s2, s1)
    q, y, z, fx, fe = s.q, s.y, s.z, s.fx, s.fe
    layers = fx + 6
    rows = slice(TOP, TOP + y)
    r = lax.broadcasted_iota(jnp.int32, (z, 2 * z), 0)
    c = lax.broadcasted_iota(jnp.int32, (z, 2 * z), 1)
    near = c // 2
    far = near + 2 * (c % 2) - 1
    same = (far // s.sz == near // s.sz) & (far >= 0)
    to_fine = jnp.where(r == near, 0.75, jnp.where((r == far) & same, 0.25, 0.0)).astype(BF16)
    wide = times(slab[: s.rows_y, :], to_fine)
    ends = slab[s.rows_y : s.rows_y + s.ex, :]
    lane_x = lanes_of((s.ex, z))
    edge = (lane_x == 0) | (lane_x == z - 1)
    half = fe // 2
    for k in range(3):
        for f in range(q):
            for side in range(2):
                e = 4 * (q * k + f) + 2 * side + 1
                corner = jnp.where(edge, 0.25 * pltpu.roll(ends, z - e, 1), 0.0)
                first = (k * q + f) * s.ex
                here = faces.at[(k * q + f) * 2 + side]
                here[: s.ex, :] = wide[first : first + s.ex, side * z : side * z + z] + corner
                a = here[0:half, :]
                b = here[1 : half + 1, :]
                d = here[2 : half + 2, :]
                if k == 0:
                    flat, base, stride = ghost_rows, (2 * f + side) * fe, 1
                else:
                    flat, stride = states[k].reshape(q * layers * PAD, z), PAD
                    base = (f * layers + 1) * PAD + (TOP - 1 if side == 0 else TOP + y)
                flat[pl.ds(base, half, stride=2 * stride), :] = 0.25 * a + 0.75 * b
                flat[pl.ds(base + stride, half, stride=2 * stride), :] = 0.75 * b + 0.25 * d
    for f in range(q):
        at = s.rows_e + f * s.rows_z
        a = slab[at : at + s.sy, :]
        b = slab[at + 1 : at + 1 + s.sy, :]
        d = slab[at + 2 : at + 2 + s.sy, :]
        zface[pl.ds(f * y, s.sy, stride=2), :] = 0.25 * a + 0.75 * b
        zface[pl.ds(f * y + 1, s.sy, stride=2), :] = 0.75 * b + 0.25 * d
        a = zface[f * y : f * y + y, :]
        b = pltpu.roll(a, z - 2, 1)
        d = pltpu.roll(a, z - 4, 1)
        zface[f * y : f * y + y, :] = 0.25 * a + 0.75 * b
        zface[(q + f) * y : (q + f + 1) * y, :] = 0.75 * b + 0.25 * d
    lane = lanes_of((y, z))
    is_first, is_last = lane == 0, lane == z - 1
    row_in = lax.broadcasted_iota(jnp.int32, (y, z), 0)
    is_low, is_high = row_in == 0, row_in == y - 1
    flat_f0 = f0.reshape(q * fx * y, z)

    def pair_of_layers(k, t, inner):
        src, fraction = states[k], section_weights[k]

        def field(f, at):
            return f0[f, at] if inner else layer_of(s, f0, flo, fhi, f, at, 3, 0)

        co = []
        for at in (2 * t - 2, 2 * t - 1):
            if inner:
                winds = [fw[d, at] for d in range(3)]
            else:
                winds = [layer_of(s, fw, flo, fhi, d, at, 2, 3 * q) for d in range(3)]
            co.append(coefficients(fraction, winds))
        made = []
        for f in range(q):
            if k == 0:
                row_of = [field(f, 2 * t - 3 + i) for i in range(4)]
            else:
                row_of = [src[f, 2 * t + i, rows, :] for i in range(4)]
            for odd in range(2):
                b = 2 * t + odd
                center = row_of[odd + 1]
                if k == 0:
                    if inner:
                        row = (f * fx + b - 2) * y
                        y_low, y_high = flat_f0[pl.ds(row - 1, y), :], flat_f0[pl.ds(row + 1, y), :]
                    else:
                        y_low, y_high = pltpu.roll(center, 1, 0), pltpu.roll(center, y - 1, 0)
                    y_low = jnp.where(is_low, ghost_rows[pl.ds(2 * f * fe + b, 1), :], y_low)
                    y_high = jnp.where(is_high, ghost_rows[pl.ds((2 * f + 1) * fe + b, 1), :], y_high)
                else:
                    flat = src.reshape(q * layers * PAD, z)
                    row = (f * layers + b + 1) * PAD + TOP
                    y_low, y_high = flat[pl.ds(row - 1, y), :], flat[pl.ds(row + 1, y), :]
                ghost = zface[(odd * q + f) * y : (odd * q + f + 1) * y, :]
                ghost = pltpu.roll(ghost, (2 * z - 2 * s.ex * k - 2 * t) if inner else -(2 * s.ex * k + 2 * t) % z, 1)
                value = advanced(
                    None if k == 0 else field(f, b - 2),
                    fraction,
                    co[odd],
                    center,
                    row_of[odd],
                    row_of[odd + 2],
                    y_low,
                    y_high,
                    pltpu.roll(jnp.where(is_last, ghost, center), 1, 1),
                    pltpu.roll(jnp.where(is_first, ghost, center), z - 1, 1),
                )
                made.append((f, b, value))
        for f, b, value in made:
            states[k + 1][f, b + 1, rows, :] = value

    for move in arrivals:
        move.wait()
    moves = []
    for k in range(3):
        if k < 2:
            outer = 2 - k
            for t in list(range(outer)) + list(range(half - outer, half)):
                pair_of_layers(k, t, False)
            unrolled(outer, half - outer, 2, lambda t, g, k=k: pair_of_layers(k, t, True))
            continue
        part = (half - 2) // 4
        for i in range(4):
            unrolled(1 + i * part, 1 + (i + 1) * part, 2, lambda t, g, k=k: pair_of_layers(k, t, True))
            begin, end = 2 * part * i, 2 * part * (i + 1)
            moves.append(pltpu.make_async_copy(s1.at[:, 3 + begin : 3 + end, rows], out.at[:, begin:end], sems.at[i]))
            moves[-1].start()
    rz = lax.broadcasted_iota(jnp.int32, (z, z), 0)
    cz = lax.broadcasted_iota(jnp.int32, (z, z), 1)
    flat = s1.reshape(q * layers * PAD, z)
    pairs_z = [jnp.where(cz == rz // 2 + odd * s.sz, 0.125, 0.0).astype(BF16) for odd in range(2)]
    for f in range(q):
        sums = []
        for odd in range(2):
            parts = []
            for p in range(s.x // 2):
                base = (f * layers + 3 + 4 * p + 2 * odd) * PAD + TOP
                part = None
                for more in (0, 1, PAD, PAD + 1):
                    piece = flat[pl.ds(base + more, y // 2, stride=2), :]
                    part = piece if part is None else part + piece
                parts.append(part)
            sums.append(times(jnp.concatenate(parts, axis=0), pairs_z[odd]))
        avg[f] = (sums[0] + sums[1]).reshape(s.x // 2, y // 2, z)
    for move in moves:
        move.wait()


def merge_kernel(s, c3, avg, out, made, sems):
    lane = lanes_of((s.sy, s.z))
    inside = (lane >= s.lz) & (lane < s.lz + s.sz)
    moves = []
    for f in range(s.q):
        for p in range(s.x // 2):
            both = avg[f, p]
            for odd in range(2):
                at = 2 * p + odd
                moved = pltpu.roll(both, s.lz if odd == 0 else s.z - s.lz, 1)
                made[f, at] = c3[f, at]
                made[f, at, s.ly : s.ly + s.sy, :] = jnp.where(inside, moved, c3[f, at, s.ly : s.ly + s.sy, :])
        moves.append(pltpu.make_async_copy(made.at[f], out.at[f], sems.at[f]))
        moves[-1].start()
    for move in moves:
        move.wait()


SHORT = pl.CostEstimate(flops=1, bytes_accessed=1, transcendentals=0)


def run(kernel, name, ins, outs, scratch, megabytes, spaces=None, cost=SHORT):
    spaces = spaces or [pltpu.VMEM] * len(ins)
    outs = [out if isinstance(out[0], tuple) else (out, pltpu.VMEM) for out in outs]
    ins = [i if space is pltpu.SMEM else pltpu.with_memory_space_constraint(i, space) for i, space in zip(ins, spaces)]
    return pl.pallas_call(
        kernel,
        out_shape=tuple(space(dims, F32) for dims, space in outs),
        in_specs=[pl.BlockSpec(memory_space=space) for space in spaces],
        out_specs=tuple(pl.BlockSpec(memory_space=space) for _, space in outs),
        scratch_shapes=scratch,
        compiler_params=pltpu.CompilerParams(vmem_limit_bytes=megabytes << 20),
        cost_estimate=cost,
        name=name,
    )(*ins)


def ring(array, axis, by):
    size = lax.axis_size(axis)
    return lax.ppermute(array, axis, [(i, (i + by) % size) for i in range(size)])


def move_by(array, amount, beside=None):
    size = lax.axis_size("gx")
    work, operands = beside or (lambda: (), ())
    if size <= 8:

        def branch(by, array, *operands):
            return array if by == 0 else ring(array, "gx", by), work(*operands)

        return lax.switch(amount, [functools.partial(branch, by) for by in range(size)], array, *operands)
    for bit in range((size - 1).bit_length()):
        array = jnp.where((amount >> bit) % 2 == 1, ring(array, "gx", 1 << bit), array)
    return array, work(*operands)


def z_columns(zown):
    size = lax.axis_size("gz")
    if size == 1:
        return zown
    if size == 2:
        return lax.ppermute(zown, "gz", [(0, 1), (1, 0)])
    below = lax.broadcasted_iota(jnp.int32, zown.shape, 2) % 6 < 3
    return jnp.where(below, ring(zown, "gz", 1), ring(zown, "gz", -1))


def pack(s, fields, wind, spare, name):
    return run(
        functools.partial(pack_kernel, s),
        name,
        [fields, wind],
        [(s.halo + spare, s.y, s.z)] * 2,
        [pltpu.SemaphoreType.DMA((4,))],
        1,
        [pltpu.HBM] * 2,
    )


def shards(coarse_fields, coarse_wind, fine_fields, fine_wind, fine_owner):
    s = Sizes(coarse_fields.shape, fine_fields.shape)
    q, x, y, z, fx = s.q, s.x, s.y, s.z, s.fx
    size = lax.axis_size("gx")
    offset = (fine_owner[0, 0, 0] - lax.axis_index("gx")) % size
    level = lax.axis_index("gz")
    neighbours = jnp.stack([level > 0, level < lax.axis_size("gz") - 1]).astype(jnp.int32).reshape(1, 2)
    cup, cdown = pack(s, coarse_fields, coarse_wind, 0, "pack_coarse")
    lo, hi = ring(cup, "gx", 1), ring(cdown, "gx", -1)
    part, near = run(
        functools.partial(inner_kernel, s),
        "inner",
        [coarse_fields, coarse_wind],
        [(s.slab, z), (q, 2, y, z)],
        [pltpu.VMEM((q, x, y, z), F32)] * 2,
        3,
    )
    fup, fdown = pack(s, fine_fields, fine_wind, 2, "pack_fine")
    fup, fdown, offset = lax.optimization_barrier((fup, fdown, offset))
    flo, fhi = ring(fup, "gx", 1), ring(fdown, "gx", -1)
    padded = [pltpu.VMEM((q, s.ep, WPAD, z), F32)]
    wind_rows = [pltpu.VMEM((3, s.ex, 24, z), F32)]

    coarse_fields, part, near = lax.optimization_barrier((coarse_fields, part, near))
    coarse_level = [coarse_fields, coarse_wind, lo, hi]
    yup, ydn = run(functools.partial(ypack_kernel, s), "ypack", coarse_level, [(s.rows_f + s.rows_w, z)] * 2, [], 1)
    yrows = [ring(yup, "gy", 1), ring(ydn, "gy", -1)]
    ends = [pltpu.VMEM((q, 2 * EDGE, y, z), F32)] * 3
    (slab,) = run(functools.partial(slab_kernel, s), "slab", coarse_level + [part, near], [(s.slab, z)], ends, 3)
    slab, _ = move_by(slab, (size - offset) % size)
    yrows, slab, flo, fhi = lax.optimization_barrier((yrows, slab, flo, fhi))
    kernel = functools.partial(zpack_kernel, s)
    (zown,) = run(kernel, "zpack", coarse_level + yrows, [(q + 3, 24, z)], padded + wind_rows, 4)
    zin = z_columns(zown)
    layers = fx + 6
    fine_next, averaged = run(
        functools.partial(fine_kernel, s),
        "fine",
        [fine_fields, fine_wind, flo, fhi, slab],
        [((q, fx, y, z), pltpu.HBM), (q, x // 2, y // 2, z)],
        [
            pltpu.VMEM((q, layers, PAD, z), F32),
            pltpu.VMEM((q, layers, PAD, z), F32),
            pltpu.VMEM((6 * q, s.ep, z), F32),
            pltpu.VMEM((2 * q * s.fe, z), F32),
            pltpu.VMEM((2 * q * y, z), F32),
            pltpu.VMEM(flo.shape, F32),
            pltpu.VMEM(fhi.shape, F32),
            pltpu.SemaphoreType.DMA((6,)),
        ],
        9,
        [pltpu.VMEM, pltpu.VMEM, pltpu.HBM, pltpu.HBM, pltpu.VMEM],
    )

    def coarse(*ins):
        cost = pl.CostEstimate(flops=40_000_000, bytes_accessed=4_000_000, transcendentals=0)
        columns = [pltpu.VMEM((3, q, 24, z), F32), pltpu.VMEM((2, q, 24, z), F32)]
        spaces = [pltpu.SMEM] + [pltpu.VMEM] * (len(ins) - 1)
        kernel = functools.partial(coarse_kernel, s)
        return run(kernel, "coarse", ins, [(q, x, y, z)], padded * 3 + wind_rows + columns, 9, spaces, cost)[0]

    averaged, state = move_by(averaged, offset, (coarse, (neighbours, *coarse_level, *yrows, zown, zin)))
    (coarse_next,) = run(
        functools.partial(merge_kernel, s),
        "merge",
        [state, averaged],
        [((q, x, y, z), pltpu.HBM)],
        [pltpu.VMEM((q, x, y, z), F32), pltpu.SemaphoreType.DMA((q,))],
        2,
    )
    return coarse_next, fine_next


def solution(mesh):
    spec = P(None, "gx", "gy", "gz")
    return jax.shard_map(
        shards,
        mesh=mesh,
        in_specs=(spec, spec, spec, spec, P("gx", "gy", "gz")),
        out_specs=(spec, spec),
        check_vma=False,
    )
```

```python
import functools

import jax
import jax.numpy as jnp
from jax import lax
from jax.experimental import pallas as pl
from jax.experimental.pallas import tpu as pltpu
from jax.sharding import PartitionSpec as P

diffusion = 0.05
section_weights = (1.0 / 3.0, 0.5, 1.0)
F32 = jnp.float32
BF16 = jnp.bfloat16
PAD = 32
TOP = 8


class Sizes:
    def __init__(self, coarse_shape, fine_shape):
        self.q, self.x, self.y, self.z = coarse_shape
        self.fx = fine_shape[1]
        self.ly, self.sy = self.y // 4, self.y // 2
        self.lz, self.sz = self.z // 4, self.z // 2
        self.ex = self.x + 4
        self.ep = -(-self.ex // 8) * 8
        self.fe = self.fx + 4
        self.halo = 3 * self.q + 6
        self.rows_f, self.rows_w = self.q * (3 * self.x + 6), 3 * (2 * self.x + 2)
        self.rows_y = 3 * self.q * self.ex
        self.rows_e = self.rows_y + self.ep
        self.rows_z = self.sy + 2
        self.slab = self.rows_e + self.q * self.rows_z
        assert self.q == 4 and self.y == 16 and self.z == 128 and self.ex <= 20 and self.fx == 2 * self.x


def lanes_of(shape):
    return lax.broadcasted_iota(jnp.int32, shape, len(shape) - 1)


def halves(value):
    high = value.astype(BF16)
    return high, (value - high.astype(F32)).astype(BF16)


def times(value, matrix):
    high, low = halves(value)
    return jnp.dot(high, matrix, preferred_element_type=F32) + jnp.dot(low, matrix, preferred_element_type=F32)


def coefficients(fraction, wind):
    out = []
    for w in wind:
        turned_by = w * (-0.5 * fraction)
        out += [diffusion * fraction + turned_by, diffusion * fraction - turned_by]
    return out


def advanced(base, fraction, co, center, x_low, x_high, y_low, y_high, z_low, z_high):
    along = (co[0] * x_high + co[1] * x_low) + (co[2] * y_high + co[3] * y_low) + (co[4] * z_high + co[5] * z_low)
    if base is None:
        return center * (1.0 - 6.0 * diffusion * fraction) + along
    return (base - center * (6.0 * diffusion * fraction)) + along


def layer_of(s, own, low, high, member, at, width, first):
    size = own.shape[1]
    if at < 0:
        return low[first + width * member + at + width]
    if at >= size:
        return high[first + width * member + at - size]
    return own[member, at]


def unrolled(begin, end, at_once, body, carry=None):
    while (end - begin) % at_once:
        at_once -= 1

    def several(i, carry):
        for more in range(at_once):
            carry = body(begin + i * at_once + more, carry)
        return carry

    return lax.fori_loop(0, (end - begin) // at_once, several, carry)


def pack_kernel(s, fields, wind, up, down, sems):
    size = fields.shape[1]
    moves = []
    for own, members, width, first in ((fields, s.q, 3, 0), (wind, 3, 2, 3 * s.q)):
        for dst, at in ((up, size - width), (down, 0)):
            place = dst.at[first : first + members * width].reshape(members, width, s.y, s.z)
            moves.append((own.at[:, at : at + width], place))
    moves = [pltpu.make_async_copy(src, dst, sems.at[i]) for i, (src, dst) in enumerate(moves)]
    for move in moves:
        move.start()
    for move in moves:
        move.wait()


def y_rows(s, members, width):
    below, above = [], []
    for out, extra in ((below, lambda r: r), (above, lambda r: width - 1 - r)):
        at = 0
        for m in range(members):
            for r in range(width):
                out.append((m, r, extra(r), at))
                at += s.x + 2 * extra(r)
    return below, above


def ypack_kernel(s, c0, cw, lo, hi, up, dn):
    x, y, z = s.x, s.y, s.z
    flat_lo = lo.reshape(s.halo * y, z)
    flat_hi = hi.reshape(s.halo * y, z)
    for own, members, width, first, place in ((c0, s.q, 3, 0, 0), (cw, 3, 2, 3 * s.q, s.rows_f)):
        flat = own.reshape(members * x * y, z)
        for dst, rows, start in zip((up, dn), y_rows(s, members, width), (y - width, 0)):
            for m, r, e, at in rows:
                row, at = start + r, at + place
                if e:
                    dst[at : at + e, :] = flat_lo[pl.ds((first + width * (m + 1) - e) * y + row, e, stride=y), :]
                    dst[at + e + x : at + x + 2 * e, :] = flat_hi[pl.ds((first + width * m) * y + row, e, stride=y), :]
                dst[at + e : at + e + x, :] = flat[pl.ds(m * x * y + row, x, stride=y), :]


EDGE = 4


def turned(base, fraction, wind, center, x_low, x_high):
    y, z = center.shape
    return advanced(
        base,
        fraction,
        wind,
        center,
        x_low,
        x_high,
        pltpu.roll(center, 1, 0),
        pltpu.roll(center, y - 1, 0),
        pltpu.roll(center, 1, 1),
        pltpu.roll(center, z - 1, 1),
    )


def slab_parts(s, rows_of, tile_of, layers_of, put):
    q, y, z = s.q, s.y, s.z
    lane_y = lanes_of((y, z))
    columns = (lane_y == s.lz - 1) | (lane_y == s.lz) | (lane_y == s.lz + s.sz - 1) | (lane_y == s.lz + s.sz)
    low_at = (lane_y % 2 == 0) & (lane_y < z // 2)
    high_at = (lane_y % 2 == 0) & (lane_y >= z // 2)
    ends = None
    for f in range(q):
        zfaces = None
        for k in range(3):
            rows = [rows_of(k, f, row) for row in (s.ly - 1, s.ly, s.ly + s.sy - 1, s.ly + s.sy)]
            sides = (0.75 * rows[0] + 0.25 * rows[1], 0.25 * rows[2] + 0.75 * rows[3])
            lane_x = lanes_of(sides[0].shape)
            put(
                "y",
                (k * q + f) * s.ex,
                jnp.where(lane_x < s.sz, pltpu.roll(sides[0], z - s.lz, 1), pltpu.roll(sides[1], s.lz, 1)),
            )
            for side in range(2):
                e = 4 * (q * k + f) + 2 * side + 1
                before = jnp.where(lane_x == s.lz - 1, sides[side], 0.0)
                after = jnp.where(lane_x == s.lz + s.sz, sides[side], 0.0)
                part = pltpu.roll(before, (e - s.lz + 1) % z, 1) + pltpu.roll(after, (e - 1 - s.lz - s.sz) % z, 1)
                ends = part if ends is None else ends + part
            raw = None
            for a in layers_of(k):
                part = jnp.where(columns, tile_of(k, f, a), 0.0)
                part = pltpu.roll(part, (2 * a - s.lz + 1) % z, 1)
                raw = part if raw is None else raw + part
            beside = pltpu.roll(raw, z - 1, 1)
            low = jnp.where(low_at, 0.75 * raw + 0.25 * beside, 0.0)
            high = jnp.where(high_at, 0.25 * raw + 0.75 * beside, 0.0)
            part = pltpu.roll(low, (2 * s.ex * k - 1) % z, 1) + pltpu.roll(high, (2 * s.ex * k - z // 2) % z, 1)
            zfaces = part if zfaces is None else zfaces + part
        put("z", s.rows_e + f * s.rows_z, zfaces[s.ly - 1 : s.ly + s.sy + 1])
    put("e", s.rows_y, ends)


def inner_kernel(s, c0, cw, part, near, state1, state2):
    q, x, y, z = s.q, s.x, s.y, s.z
    states = (c0, state1, state2)
    for step in range(2):
        src, dst = states[step], states[step + 1]

        def layer(j, carry, step=step, src=src, dst=dst):
            w = coefficients(section_weights[step], [cw[d, j] for d in range(3)])
            made = []
            for f in range(q):
                base = None if step == 0 else c0[f, j]
                made.append(turned(base, section_weights[step], w, src[f, j], src[f, j - 1], src[f, j + 1]))
            for f in range(q):
                dst[f, j] = made[f]
            return carry

        unrolled(step + 1, x - 1 - step, 7 if step == 0 else 6, layer)
    for f in range(q):
        near[f, 0] = state1[f, EDGE - 2]
        near[f, 1] = state1[f, x + 1 - EDGE]
    count = s.ex - 2 * EDGE
    part[...] = jnp.zeros_like(part)

    def rows_of(k, f, row):
        flat = states[k].reshape(q * x * y, z)
        return flat[pl.ds((f * x + EDGE - 2) * y + row, count, stride=y), :]

    def put(kind, at, rows):
        if kind == "z":
            part[at : at + s.rows_z, :] = rows
        else:
            part[at + EDGE : at + EDGE + count, :] = rows

    slab_parts(s, rows_of, lambda k, f, a: states[k][f, a - 2], lambda k: range(EDGE, s.ex - EDGE), put)


def slab_kernel(s, c0, cw, lo, hi, part, near, slab, ends0, ends1, ends2):
    q, x, y, z = s.q, s.x, s.y, s.z
    states = (ends0, ends1, ends2)
    places = list(range(-2, EDGE - 2)) + list(range(x + 2 - EDGE, x + 2))
    slab[...] = part[...]
    for j, at in enumerate(places):
        for f in range(q):
            ends0[f, j] = layer_of(s, c0, lo, hi, f, at, 3, 0)
    for step in range(2):
        for j, at in enumerate(places):
            if step == 1 and at in (-2, x + 1):
                for f in range(q):
                    ends2[f, j] = jnp.zeros((y, z), F32)
                continue
            w = coefficients(section_weights[step], [layer_of(s, cw, lo, hi, d, at, 2, 3 * q) for d in range(3)])
            for f in range(q):

                def beside(at, f=f):
                    if step == 0:
                        return layer_of(s, c0, lo, hi, f, at, 3, 0)
                    if at in places:
                        return ends1[f, places.index(at)]
                    return near[f, 0 if at < x // 2 else 1]

                base = None if step == 0 else ends0[f, j]
                states[step + 1][f, j] = turned(
                    base, section_weights[step], w, beside(at), beside(at - 1), beside(at + 1)
                )

    def rows_of(k, f, row):
        flat = states[k].reshape(q * 2 * EDGE * y, z)
        return flat[pl.ds(f * 2 * EDGE * y + row, 2 * EDGE, stride=y), :]

    def put(kind, at, rows):
        if kind == "z":
            slab[at : at + s.rows_z, :] = part[at : at + s.rows_z, :] + rows
        else:
            slab[at : at + EDGE, :] = rows[:EDGE]
            slab[at + s.ex - EDGE : at + s.ex, :] = rows[EDGE:]

    def layers_of(k):
        some = range(0 if k == 0 else 1, EDGE)
        return list(some) + [s.ex - 1 - a for a in some]

    def tile_of(k, f, a):
        return states[k][f, a if a < EDGE else a - s.ex + 2 * EDGE]

    slab_parts(s, rows_of, tile_of, layers_of, put)


WTOP, WPAD = 12, 40
BLOCK = slice(8, 32)


def assemble(s, c0, cw, lo, hi, below, above, pad, wind):
    q, x, y, z = s.q, s.x, s.y, s.z
    flat = pad.reshape(q * s.ep * WPAD, z)
    flat_wind = wind.reshape(3 * s.ex * 24, z)
    for f in range(q):
        for at in range(-3, x + 3):
            pad[f, at + 3, WTOP : WTOP + y, :] = layer_of(s, c0, lo, hi, f, at, 3, 0)
    for d in range(3):
        for at in range(-2, x + 2):
            wind[d, at + 2, 4 : 4 + y, :] = layer_of(s, cw, lo, hi, d, at, 2, 3 * q)
    for src, rows, start in zip((below, above), y_rows(s, q, 3), (WTOP - 3, WTOP + y)):
        for m, r, e, at in rows:
            count = x + 2 * e
            flat[pl.ds((m * s.ep + 3 - e) * WPAD + start + r, count, stride=WPAD), :] = src[at : at + count, :]
    for src, rows, start in zip((below, above), y_rows(s, 3, 2), (2, 4 + y)):
        for m, r, e, at in rows:
            count, at = x + 2 * e, at + s.rows_f
            flat_wind[pl.ds((m * s.ex + 2 - e) * 24 + start + r, count, stride=24), :] = src[at : at + count, :]


def edge_lanes(s, lane, width):
    return (lane < width) | (lane >= s.z - width)


def zpack_kernel(s, c0, cw, lo, hi, below, above, out, pad, wind):
    assemble(s, c0, cw, lo, hi, below, above, pad, wind)
    lane = lanes_of((24, s.z))
    keep = edge_lanes(s, lane, 3)
    for m in range(s.q + 3):
        total = None
        for a in range(s.ex):
            tile = pad[m, a + 1, BLOCK, :] if m < s.q else wind[m - s.q, a]
            part = pltpu.roll(jnp.where(keep, tile, 0.0), (6 * a + 3) % s.z, 1)
            total = part if total is None else total + part
        out[m] = total


def coarse_kernel(
    s, sides, c0, cw, lo, hi, below, above, zown, zin, out, pad0, pad1, pad2, wind, beyond, nearest
):
    q, x, y, z = s.q, s.x, s.y, s.z
    assemble(s, c0, cw, lo, hi, below, above, pad0, wind)
    pads = (pad0, pad1, pad2)
    lane = lanes_of((24, z))
    group = lane % 6
    from_low = group == 2
    from_high = group == 3
    exists = jnp.where(group < 3, sides[0, 0], sides[0, 1]).astype(F32)
    wind_z = [zin[q + d] for d in range(3)]
    for f in range(q):
        beyond[0, f] = zin[f] * exists
        nearest[0, f] = zown[f]
    for step in range(3):
        src, fraction = pads[step], section_weights[step]
        flat = src.reshape(q * s.ep * WPAD, z)
        flat_wind = wind.reshape(3 * s.ex * 24, z)
        flat_beyond = beyond.reshape(3 * q * 24, z)
        skip, height = (0, 24) if step < 2 else (4, y)
        here = lanes_of((height, z))
        is_first, is_last = here == 0, here == z - 1

        def two_layers(t, packed, step=step, src=src, flat=flat, fraction=fraction, skip=skip, height=height):
            first = step + 2 * t
            ghosts, packed = (list(some) for some in packed)
            made = []
            co = []
            for a in (first, first + 1):
                if step < 2:
                    winds = [wind[d, a] for d in range(3)]
                else:
                    winds = [flat_wind[pl.ds((d * s.ex + a) * 24 + skip, height), :] for d in range(3)]
                co.append(coefficients(fraction, winds))
            for f in range(q):

                def at_layer(of, layer, by=0, f=f):
                    if step < 2 and not by:
                        return of[f, layer, BLOCK, :]
                    row = (f * s.ep + layer) * WPAD + 8 + skip + by
                    return of.reshape(flat.shape)[pl.ds(row, height), :]

                row_of = [at_layer(src, first + i) for i in range(4)]
                for i in range(2):
                    a = first + i
                    center = row_of[i + 1]
                    ghost = ghosts[f]
                    ghosts[f] = pltpu.roll(ghost, z - 6, 1)
                    value = advanced(
                        None if step == 0 else at_layer(pad0, a + 1),
                        fraction,
                        co[i],
                        center,
                        row_of[i],
                        row_of[i + 2],
                        at_layer(src, a + 1, -1),
                        at_layer(src, a + 1, 1),
                        pltpu.roll(jnp.where(is_last, ghost, center), 1, 1),
                        pltpu.roll(jnp.where(is_first, ghost, center), z - 1, 1),
                    )
                    made.append((f, a, value))
                    if step == 0:
                        packed[f] = pltpu.roll(packed[f] + jnp.where(is_first | is_last, value, 0.0), z - 6, 1)
            for f, a, value in made:
                if step == 2:
                    out[f, a - 2] = value
                else:
                    pads[step + 1][f, a + 1, BLOCK, :] = value
            return tuple(ghosts), tuple(packed)

        zeros = tuple(jnp.zeros((24, z), F32) for _ in range(q)) if step == 0 else ()
        ghosts = tuple(
            pltpu.roll(flat_beyond[(step * q + f) * 24 + skip : (step * q + f) * 24 + skip + height, :], z - 6 * step - 3, 1)
            for f in range(q)
        )
        _, packed = unrolled(0, s.ex // 2 - step, 2 + (step == 1), two_layers, (ghosts, zeros))
        if step == 2:
            break
        for f in range(q):
            if step == 0:
                nearest[1, f] = pltpu.roll(packed[f], (6 * s.ex + 3) % z, 1)
            ghost, near = beyond[step, f], nearest[step, f]
            value = advanced(
                None if step == 0 else beyond[0, f],
                fraction,
                coefficients(fraction, wind_z),
                ghost,
                pltpu.roll(ghost, 6, 1),
                pltpu.roll(ghost, z - 6, 1),
                pltpu.roll(ghost, 1, 0),
                pltpu.roll(ghost, 23, 0),
                pltpu.roll(jnp.where(from_low, near, ghost), 1, 1),
                pltpu.roll(jnp.where(from_high, near, ghost), z - 1, 1),
            )
            beyond[step + 1, f] = value * exists


def fine_kernel(s, f0, fw, flo_there, fhi_there, slab, out, avg, *scratch):
    s1, s2, faces, ghost_rows, zface, flo, fhi, summed, sems = scratch
    arrivals = [
        pltpu.make_async_copy(flo_there, flo, sems.at[4]),
        pltpu.make_async_copy(fhi_there, fhi, sems.at[5]),
    ]
    for move in arrivals:
        move.start()
    states = (None, s1, s2, s1)
    q, y, z, fx, fe = s.q, s.y, s.z, s.fx, s.fe
    layers = fx + 6
    rows = slice(TOP, TOP + y)
    r = lax.broadcasted_iota(jnp.int32, (z, 2 * z), 0)
    c = lax.broadcasted_iota(jnp.int32, (z, 2 * z), 1)
    near = c // 2
    far = near + 2 * (c % 2) - 1
    same = (far // s.sz == near // s.sz) & (far >= 0)
    to_fine = jnp.where(r == near, 0.75, jnp.where((r == far) & same, 0.25, 0.0)).astype(BF16)
    wide = times(slab[: s.rows_y, :], to_fine)
    ends = slab[s.rows_y : s.rows_y + s.ex, :]
    lane_x = lanes_of((s.ex, z))
    edge = (lane_x == 0) | (lane_x == z - 1)
    half = fe // 2
    for k in range(3):
        for f in range(q):
            for side in range(2):
                e = 4 * (q * k + f) + 2 * side + 1
                corner = jnp.where(edge, 0.25 * pltpu.roll(ends, z - e, 1), 0.0)
                first = (k * q + f) * s.ex
                here = faces.at[(k * q + f) * 2 + side]
                here[: s.ex, :] = wide[first : first + s.ex, side * z : side * z + z] + corner
                a = here[0:half, :]
                b = here[1 : half + 1, :]
                d = here[2 : half + 2, :]
                if k == 0:
                    flat, base, stride = ghost_rows, (2 * f + side) * fe, 1
                else:
                    flat, stride = states[k].reshape(q * layers * PAD, z), PAD
                    base = (f * layers + 1) * PAD + (TOP - 1 if side == 0 else TOP + y)
                flat[pl.ds(base, half, stride=2 * stride), :] = 0.25 * a + 0.75 * b
                flat[pl.ds(base + stride, half, stride=2 * stride), :] = 0.75 * b + 0.25 * d
    for f in range(q):
        at = s.rows_e + f * s.rows_z
        a = slab[at : at + s.sy, :]
        b = slab[at + 1 : at + 1 + s.sy, :]
        d = slab[at + 2 : at + 2 + s.sy, :]
        zface[pl.ds(f * y, s.sy, stride=2), :] = 0.25 * a + 0.75 * b
        zface[pl.ds(f * y + 1, s.sy, stride=2), :] = 0.75 * b + 0.25 * d
        a = zface[f * y : f * y + y, :]
        b = pltpu.roll(a, z - 2, 1)
        d = pltpu.roll(a, z - 4, 1)
        zface[f * y : f * y + y, :] = 0.25 * a + 0.75 * b
        zface[(q + f) * y : (q + f + 1) * y, :] = 0.75 * b + 0.25 * d
    lane = lanes_of((y, z))
    is_first, is_last = lane == 0, lane == z - 1
    row_in = lax.broadcasted_iota(jnp.int32, (y, z), 0)
    is_low, is_high = row_in == 0, row_in == y - 1
    flat_f0 = f0.reshape(q * fx * y, z)

    def ghosts_at(k, t):
        shift = -(2 * s.ex * k + 2 * t) % z
        return tuple(pltpu.roll(zface[i * y : (i + 1) * y, :], shift, 1) if shift else zface[i * y : (i + 1) * y, :] for i in range(2 * q))

    def pair_of_layers(k, t, ghosts, inner):
        src, fraction = states[k], section_weights[k]

        def field(f, at):
            return f0[f, at] if inner else layer_of(s, f0, flo, fhi, f, at, 3, 0)

        co = []
        for at in (2 * t - 2, 2 * t - 1):
            if inner:
                winds = [fw[d, at] for d in range(3)]
            else:
                winds = [layer_of(s, fw, flo, fhi, d, at, 2, 3 * q) for d in range(3)]
            co.append(coefficients(fraction, winds))
        made = []
        for f in range(q):
            if k == 0:
                row_of = [field(f, 2 * t - 3 + i) for i in range(4)]
            else:
                row_of = [src[f, 2 * t + i, rows, :] for i in range(4)]
            for odd in range(2):
                b = 2 * t + odd
                center = row_of[odd + 1]
                if k == 0:
                    if inner:
                        row = (f * fx + b - 2) * y
                        y_low, y_high = flat_f0[pl.ds(row - 1, y), :], flat_f0[pl.ds(row + 1, y), :]
                    else:
                        y_low, y_high = pltpu.roll(center, 1, 0), pltpu.roll(center, y - 1, 0)
                    y_low = jnp.where(is_low, ghost_rows[pl.ds(2 * f * fe + b, 1), :], y_low)
                    y_high = jnp.where(is_high, ghost_rows[pl.ds((2 * f + 1) * fe + b, 1), :], y_high)
                else:
                    flat = src.reshape(q * layers * PAD, z)
                    row = (f * layers + b + 1) * PAD + TOP
                    y_low, y_high = flat[pl.ds(row - 1, y), :], flat[pl.ds(row + 1, y), :]
                ghost = ghosts[odd * q + f]
                value = advanced(
                    None if k == 0 else field(f, b - 2),
                    fraction,
                    co[odd],
                    center,
                    row_of[odd],
                    row_of[odd + 2],
                    y_low,
                    y_high,
                    pltpu.roll(jnp.where(is_last, ghost, center), 1, 1),
                    pltpu.roll(jnp.where(is_first, ghost, center), z - 1, 1),
                )
                made.append((f, b, value))
        for f, b, value in made:
            states[k + 1][f, b + 1, rows, :] = value
        return tuple(pltpu.roll(g, z - 2, 1) for g in ghosts)

    for move in arrivals:
        move.wait()
    moves = []
    for k in range(3):
        if k < 2:
            outer = 2 - k
            for t in list(range(outer)) + list(range(half - outer, half)):
                pair_of_layers(k, t, ghosts_at(k, t), False)
            unrolled(outer, half - outer, 2, lambda t, g, k=k: pair_of_layers(k, t, g, True), ghosts_at(k, outer))
            continue
        carried, part = ghosts_at(k, 1), (half - 2) // 4
        for i in range(4):
            begin = 1 + i * part
            carried = unrolled(begin, begin + part, 2, lambda t, g, k=k: pair_of_layers(k, t, g, True), carried)
            begin, end = 2 * part * i, 2 * part * (i + 1)
            moves.append(pltpu.make_async_copy(s1.at[:, 3 + begin : 3 + end, rows], out.at[:, begin:end], sems.at[i]))
            moves[-1].start()
    rz = lax.broadcasted_iota(jnp.int32, (z, z), 0)
    cz = lax.broadcasted_iota(jnp.int32, (z, z), 1)
    flat = summed.reshape(q * s.x * y, z)
    pairs_z = [jnp.where(cz == rz // 2 + odd * s.sz, 0.125, 0.0).astype(BF16) for odd in range(2)]
    for f in range(q):
        for p in range(s.x):
            both = s1[f, 3 + 2 * p, rows, :] + s1[f, 4 + 2 * p, rows, :]
            summed[f, p] = both + pltpu.roll(both, y - 1, 0)
    for f in range(q):
        sums = []
        for odd in range(2):
            parts = [flat[pl.ds((f * s.x + 2 * p + odd) * y, y // 2, stride=2), :] for p in range(s.x // 2)]
            sums.append(times(jnp.concatenate(parts, axis=0), pairs_z[odd]))
        avg[f] = (sums[0] + sums[1]).reshape(s.x // 2, y // 2, z)
    for move in moves:
        move.wait()


def merge_kernel(s, c3, avg, out, made, sems):
    lane = lanes_of((s.sy, s.z))
    inside = (lane >= s.lz) & (lane < s.lz + s.sz)
    moves = []
    for f in range(s.q):
        for p in range(s.x // 2):
            both = avg[f, p]
            for odd in range(2):
                at = 2 * p + odd
                moved = pltpu.roll(both, s.lz if odd == 0 else s.z - s.lz, 1)
                made[f, at] = c3[f, at]
                made[f, at, s.ly : s.ly + s.sy, :] = jnp.where(inside, moved, c3[f, at, s.ly : s.ly + s.sy, :])
        moves.append(pltpu.make_async_copy(made.at[f], out.at[f], sems.at[f]))
        moves[-1].start()
    for move in moves:
        move.wait()


SHORT = pl.CostEstimate(flops=1, bytes_accessed=1, transcendentals=0)


def run(kernel, name, ins, outs, scratch, megabytes, spaces=None, cost=SHORT):
    spaces = spaces or [pltpu.VMEM] * len(ins)
    outs = [out if isinstance(out[0], tuple) else (out, pltpu.VMEM) for out in outs]
    ins = [i if space is pltpu.SMEM else pltpu.with_memory_space_constraint(i, space) for i, space in zip(ins, spaces)]
    return pl.pallas_call(
        kernel,
        out_shape=tuple(space(dims, F32) for dims, space in outs),
        in_specs=[pl.BlockSpec(memory_space=space) for space in spaces],
        out_specs=tuple(pl.BlockSpec(memory_space=space) for _, space in outs),
        scratch_shapes=scratch,
        compiler_params=pltpu.CompilerParams(vmem_limit_bytes=megabytes << 20),
        cost_estimate=cost,
        name=name,
    )(*ins)


def ring(array, axis, by):
    size = lax.axis_size(axis)
    return lax.ppermute(array, axis, [(i, (i + by) % size) for i in range(size)])


def move_by(array, amount, beside=None):
    size = lax.axis_size("gx")
    work, operands = beside or (lambda: (), ())
    if size <= 8:

        def branch(by, array, *operands):
            return array if by == 0 else ring(array, "gx", by), work(*operands)

        return lax.switch(amount, [functools.partial(branch, by) for by in range(size)], array, *operands)
    for bit in range((size - 1).bit_length()):
        array = jnp.where((amount >> bit) % 2 == 1, ring(array, "gx", 1 << bit), array)
    return array, work(*operands)


def z_columns(zown):
    size = lax.axis_size("gz")
    if size == 1:
        return zown
    if size == 2:
        return lax.ppermute(zown, "gz", [(0, 1), (1, 0)])
    below = lax.broadcasted_iota(jnp.int32, zown.shape, 2) % 6 < 3
    return jnp.where(below, ring(zown, "gz", 1), ring(zown, "gz", -1))


def pack(s, fields, wind, spare, name):
    return run(
        functools.partial(pack_kernel, s),
        name,
        [fields, wind],
        [(s.halo + spare, s.y, s.z)] * 2,
        [pltpu.SemaphoreType.DMA((4,))],
        1,
        [pltpu.HBM] * 2,
    )


def shards(coarse_fields, coarse_wind, fine_fields, fine_wind, fine_owner):
    s = Sizes(coarse_fields.shape, fine_fields.shape)
    q, x, y, z, fx = s.q, s.x, s.y, s.z, s.fx
    size = lax.axis_size("gx")
    offset = (fine_owner[0, 0, 0] - lax.axis_index("gx")) % size
    level = lax.axis_index("gz")
    neighbours = jnp.stack([level > 0, level < lax.axis_size("gz") - 1]).astype(jnp.int32).reshape(1, 2)
    cup, cdown = pack(s, coarse_fields, coarse_wind, 0, "pack_coarse")
    lo, hi = ring(cup, "gx", 1), ring(cdown, "gx", -1)
    part, near = run(
        functools.partial(inner_kernel, s),
        "inner",
        [coarse_fields, coarse_wind],
        [(s.slab, z), (q, 2, y, z)],
        [pltpu.VMEM((q, x, y, z), F32)] * 2,
        3,
    )
    fup, fdown = pack(s, fine_fields, fine_wind, 2, "pack_fine")
    fup, fdown, offset = lax.optimization_barrier((fup, fdown, offset))
    flo, fhi = ring(fup, "gx", 1), ring(fdown, "gx", -1)
    padded = [pltpu.VMEM((q, s.ep, WPAD, z), F32)]
    wind_rows = [pltpu.VMEM((3, s.ex, 24, z), F32)]

    coarse_fields, part, near = lax.optimization_barrier((coarse_fields, part, near))
    coarse_level = [coarse_fields, coarse_wind, lo, hi]
    yup, ydn = run(functools.partial(ypack_kernel, s), "ypack", coarse_level, [(s.rows_f + s.rows_w, z)] * 2, [], 1)
    yrows = [ring(yup, "gy", 1), ring(ydn, "gy", -1)]
    ends = [pltpu.VMEM((q, 2 * EDGE, y, z), F32)] * 3
    (slab,) = run(functools.partial(slab_kernel, s), "slab", coarse_level + [part, near], [(s.slab, z)], ends, 3)
    slab, _ = move_by(slab, (size - offset) % size)
    yrows, slab, flo, fhi = lax.optimization_barrier((yrows, slab, flo, fhi))
    kernel = functools.partial(zpack_kernel, s)
    (zown,) = run(kernel, "zpack", coarse_level + yrows, [(q + 3, 24, z)], padded + wind_rows, 4)
    zin = z_columns(zown)
    layers = fx + 6
    fine_next, averaged = run(
        functools.partial(fine_kernel, s),
        "fine",
        [fine_fields, fine_wind, flo, fhi, slab],
        [((q, fx, y, z), pltpu.HBM), (q, x // 2, y // 2, z)],
        [
            pltpu.VMEM((q, layers, PAD, z), F32),
            pltpu.VMEM((q, layers, PAD, z), F32),
            pltpu.VMEM((6 * q, s.ep, z), F32),
            pltpu.VMEM((2 * q * s.fe, z), F32),
            pltpu.VMEM((2 * q * y, z), F32),
            pltpu.VMEM(flo.shape, F32),
            pltpu.VMEM(fhi.shape, F32),
            pltpu.VMEM((q, s.x, y, z), F32),
            pltpu.SemaphoreType.DMA((6,)),
        ],
        9,
        [pltpu.VMEM, pltpu.VMEM, pltpu.HBM, pltpu.HBM, pltpu.VMEM],
    )

    def coarse(*ins):
        cost = pl.CostEstimate(flops=40_000_000, bytes_accessed=4_000_000, transcendentals=0)
        columns = [pltpu.VMEM((3, q, 24, z), F32), pltpu.VMEM((2, q, 24, z), F32)]
        spaces = [pltpu.SMEM] + [pltpu.VMEM] * (len(ins) - 1)
        kernel = functools.partial(coarse_kernel, s)
        return run(kernel, "coarse", ins, [(q, x, y, z)], padded * 3 + wind_rows + columns, 9, spaces, cost)[0]

    averaged, state = move_by(averaged, offset, (coarse, (neighbours, *coarse_level, *yrows, zown, zin)))
    (coarse_next,) = run(
        functools.partial(merge_kernel, s),
        "merge",
        [state, averaged],
        [((q, x, y, z), pltpu.HBM)],
        [pltpu.VMEM((q, x, y, z), F32), pltpu.SemaphoreType.DMA((q,))],
        2,
    )
    return coarse_next, fine_next


def solution(mesh):
    spec = P(None, "gx", "gy", "gz")
    return jax.shard_map(
        shards,
        mesh=mesh,
        in_specs=(spec, spec, spec, spec, P("gx", "gy", "gz")),
        out_specs=(spec, spec),
        check_vma=False,
    )
```

```python
import functools

import jax
import jax.numpy as jnp
from jax import lax
from jax.experimental import pallas as pl
from jax.experimental.pallas import tpu as pltpu
from jax.sharding import PartitionSpec as P

diffusion = 0.05
section_weights = (1.0 / 3.0, 0.5, 1.0)
F32 = jnp.float32
BF16 = jnp.bfloat16
PAD = 32
TOP = 8


class Sizes:
    def __init__(self, coarse_shape, fine_shape):
        self.q, self.x, self.y, self.z = coarse_shape
        self.fx = fine_shape[1]
        self.ly, self.sy = self.y // 4, self.y // 2
        self.lz, self.sz = self.z // 4, self.z // 2
        self.ex = self.x + 4
        self.ep = -(-self.ex // 8) * 8
        self.fe = self.fx + 4
        self.halo = 3 * self.q + 6
        self.rows_f, self.rows_w = self.q * (3 * self.x + 6), 3 * (2 * self.x + 2)
        self.rows_y = 3 * self.q * self.ex
        self.rows_e = self.rows_y + self.ep
        self.rows_z = self.sy + 2
        self.slab = self.rows_e + self.q * self.rows_z
        assert self.q == 4 and self.y == 16 and self.z == 128 and self.ex <= 20 and self.fx == 2 * self.x


def lanes_of(shape):
    return lax.broadcasted_iota(jnp.int32, shape, len(shape) - 1)


def halves(value):
    high = value.astype(BF16)
    return high, (value - high.astype(F32)).astype(BF16)


def times(value, matrix):
    high, low = halves(value)
    return jnp.dot(high, matrix, preferred_element_type=F32) + jnp.dot(low, matrix, preferred_element_type=F32)


def coefficients(fraction, wind):
    out = []
    for w in wind:
        turned_by = w * (-0.5 * fraction)
        out += [diffusion * fraction + turned_by, diffusion * fraction - turned_by]
    return out


def advanced(base, fraction, co, center, x_low, x_high, y_low, y_high, z_low, z_high):
    along = (co[0] * x_high + co[1] * x_low) + (co[2] * y_high + co[3] * y_low) + (co[4] * z_high + co[5] * z_low)
    if base is None:
        return center * (1.0 - 6.0 * diffusion * fraction) + along
    return (base - center * (6.0 * diffusion * fraction)) + along


def layer_of(s, own, low, high, member, at, width, first):
    size = own.shape[1]
    if at < 0:
        return low[first + width * member + at + width]
    if at >= size:
        return high[first + width * member + at - size]
    return own[member, at]


def unrolled(begin, end, at_once, body, carry=None):
    while (end - begin) % at_once:
        at_once -= 1

    def several(i, carry):
        for more in range(at_once):
            carry = body(begin + i * at_once + more, carry)
        return carry

    return lax.fori_loop(0, (end - begin) // at_once, several, carry)


def pack_kernel(s, fields, wind, up, down, sems):
    size = fields.shape[1]
    moves = []
    for own, members, width, first in ((fields, s.q, 3, 0), (wind, 3, 2, 3 * s.q)):
        for dst, at in ((up, size - width), (down, 0)):
            place = dst.at[first : first + members * width].reshape(members, width, s.y, s.z)
            moves.append((own.at[:, at : at + width], place))
    moves = [pltpu.make_async_copy(src, dst, sems.at[i]) for i, (src, dst) in enumerate(moves)]
    for move in moves:
        move.start()
    for move in moves:
        move.wait()


def y_rows(s, members, width):
    below, above = [], []
    for out, extra in ((below, lambda r: r), (above, lambda r: width - 1 - r)):
        at = 0
        for m in range(members):
            for r in range(width):
                out.append((m, r, extra(r), at))
                at += s.x + 2 * extra(r)
    return below, above


def ypack_kernel(s, c0, cw, lo, hi, up, dn):
    x, y, z = s.x, s.y, s.z
    flat_lo = lo.reshape(s.halo * y, z)
    flat_hi = hi.reshape(s.halo * y, z)
    for own, members, width, first, place in ((c0, s.q, 3, 0, 0), (cw, 3, 2, 3 * s.q, s.rows_f)):
        flat = own.reshape(members * x * y, z)
        for dst, rows, start in zip((up, dn), y_rows(s, members, width), (y - width, 0)):
            for m, r, e, at in rows:
                row, at = start + r, at + place
                if e:
                    dst[at : at + e, :] = flat_lo[pl.ds((first + width * (m + 1) - e) * y + row, e, stride=y), :]
                    dst[at + e + x : at + x + 2 * e, :] = flat_hi[pl.ds((first + width * m) * y + row, e, stride=y), :]
                dst[at + e : at + e + x, :] = flat[pl.ds(m * x * y + row, x, stride=y), :]


EDGE = 4


def turned(base, fraction, wind, center, x_low, x_high):
    y, z = center.shape
    return advanced(
        base,
        fraction,
        wind,
        center,
        x_low,
        x_high,
        pltpu.roll(center, 1, 0),
        pltpu.roll(center, y - 1, 0),
        pltpu.roll(center, 1, 1),
        pltpu.roll(center, z - 1, 1),
    )


def slab_parts(s, rows_of, tile_of, layers_of, put):
    q, y, z = s.q, s.y, s.z
    lane_y = lanes_of((y, z))
    columns = (lane_y == s.lz - 1) | (lane_y == s.lz) | (lane_y == s.lz + s.sz - 1) | (lane_y == s.lz + s.sz)
    low_at = (lane_y % 2 == 0) & (lane_y < z // 2)
    high_at = (lane_y % 2 == 0) & (lane_y >= z // 2)
    ends = None
    for f in range(q):
        zfaces = None
        for k in range(3):
            rows = [rows_of(k, f, row) for row in (s.ly - 1, s.ly, s.ly + s.sy - 1, s.ly + s.sy)]
            sides = (0.75 * rows[0] + 0.25 * rows[1], 0.25 * rows[2] + 0.75 * rows[3])
            lane_x = lanes_of(sides[0].shape)
            put(
                "y",
                (k * q + f) * s.ex,
                jnp.where(lane_x < s.sz, pltpu.roll(sides[0], z - s.lz, 1), pltpu.roll(sides[1], s.lz, 1)),
            )
            for side in range(2):
                e = 4 * (q * k + f) + 2 * side + 1
                before = jnp.where(lane_x == s.lz - 1, sides[side], 0.0)
                after = jnp.where(lane_x == s.lz + s.sz, sides[side], 0.0)
                part = pltpu.roll(before, (e - s.lz + 1) % z, 1) + pltpu.roll(after, (e - 1 - s.lz - s.sz) % z, 1)
                ends = part if ends is None else ends + part
            raw = None
            for a in layers_of(k):
                part = jnp.where(columns, tile_of(k, f, a), 0.0)
                part = pltpu.roll(part, (2 * a - s.lz + 1) % z, 1)
                raw = part if raw is None else raw + part
            beside = pltpu.roll(raw, z - 1, 1)
            low = jnp.where(low_at, 0.75 * raw + 0.25 * beside, 0.0)
            high = jnp.where(high_at, 0.25 * raw + 0.75 * beside, 0.0)
            part = pltpu.roll(low, (2 * s.ex * k - 1) % z, 1) + pltpu.roll(high, (2 * s.ex * k - z // 2) % z, 1)
            zfaces = part if zfaces is None else zfaces + part
        put("z", s.rows_e + f * s.rows_z, zfaces[s.ly - 1 : s.ly + s.sy + 1])
    put("e", s.rows_y, ends)


def inner_kernel(s, c0, cw, part, near, state1, state2):
    q, x, y, z = s.q, s.x, s.y, s.z
    states = (c0, state1, state2)
    for step in range(2):
        src, dst = states[step], states[step + 1]

        def layer(j, carry, step=step, src=src, dst=dst):
            w = coefficients(section_weights[step], [cw[d, j] for d in range(3)])
            made = []
            for f in range(q):
                base = None if step == 0 else c0[f, j]
                made.append(turned(base, section_weights[step], w, src[f, j], src[f, j - 1], src[f, j + 1]))
            for f in range(q):
                dst[f, j] = made[f]
            return carry

        unrolled(step + 1, x - 1 - step, 7 if step == 0 else 6, layer)
    for f in range(q):
        near[f, 0] = state1[f, EDGE - 2]
        near[f, 1] = state1[f, x + 1 - EDGE]
    count = s.ex - 2 * EDGE
    part[...] = jnp.zeros_like(part)

    def rows_of(k, f, row):
        flat = states[k].reshape(q * x * y, z)
        return flat[pl.ds((f * x + EDGE - 2) * y + row, count, stride=y), :]

    def put(kind, at, rows):
        if kind == "z":
            part[at : at + s.rows_z, :] = rows
        else:
            part[at + EDGE : at + EDGE + count, :] = rows

    slab_parts(s, rows_of, lambda k, f, a: states[k][f, a - 2], lambda k: range(EDGE, s.ex - EDGE), put)


def slab_kernel(s, c0, cw, lo, hi, part, near, slab, ends0, ends1, ends2):
    q, x, y, z = s.q, s.x, s.y, s.z
    states = (ends0, ends1, ends2)
    places = list(range(-2, EDGE - 2)) + list(range(x + 2 - EDGE, x + 2))
    slab[...] = part[...]
    for j, at in enumerate(places):
        for f in range(q):
            ends0[f, j] = layer_of(s, c0, lo, hi, f, at, 3, 0)
    for step in range(2):
        for j, at in enumerate(places):
            if step == 1 and at in (-2, x + 1):
                for f in range(q):
                    ends2[f, j] = jnp.zeros((y, z), F32)
                continue
            w = coefficients(section_weights[step], [layer_of(s, cw, lo, hi, d, at, 2, 3 * q) for d in range(3)])
            for f in range(q):

                def beside(at, f=f):
                    if step == 0:
                        return layer_of(s, c0, lo, hi, f, at, 3, 0)
                    if at in places:
                        return ends1[f, places.index(at)]
                    return near[f, 0 if at < x // 2 else 1]

                base = None if step == 0 else ends0[f, j]
                states[step + 1][f, j] = turned(
                    base, section_weights[step], w, beside(at), beside(at - 1), beside(at + 1)
                )

    def rows_of(k, f, row):
        flat = states[k].reshape(q * 2 * EDGE * y, z)
        return flat[pl.ds(f * 2 * EDGE * y + row, 2 * EDGE, stride=y), :]

    def put(kind, at, rows):
        if kind == "z":
            slab[at : at + s.rows_z, :] = part[at : at + s.rows_z, :] + rows
        else:
            slab[at : at + EDGE, :] = rows[:EDGE]
            slab[at + s.ex - EDGE : at + s.ex, :] = rows[EDGE:]

    def layers_of(k):
        some = range(0 if k == 0 else 1, EDGE)
        return list(some) + [s.ex - 1 - a for a in some]

    def tile_of(k, f, a):
        return states[k][f, a if a < EDGE else a - s.ex + 2 * EDGE]

    slab_parts(s, rows_of, tile_of, layers_of, put)


WTOP, WPAD = 12, 40
BLOCK = slice(8, 32)


def assemble(s, c0, cw, lo, hi, below, above, pad, wind):
    q, x, y, z = s.q, s.x, s.y, s.z
    flat = pad.reshape(q * s.ep * WPAD, z)
    flat_wind = wind.reshape(3 * s.ex * 24, z)
    for f in range(q):
        for at in range(-3, x + 3):
            pad[f, at + 3, WTOP : WTOP + y, :] = layer_of(s, c0, lo, hi, f, at, 3, 0)
    for d in range(3):
        for at in range(-2, x + 2):
            wind[d, at + 2, 4 : 4 + y, :] = layer_of(s, cw, lo, hi, d, at, 2, 3 * q)
    for src, rows, start in zip((below, above), y_rows(s, q, 3), (WTOP - 3, WTOP + y)):
        for m, r, e, at in rows:
            count = x + 2 * e
            flat[pl.ds((m * s.ep + 3 - e) * WPAD + start + r, count, stride=WPAD), :] = src[at : at + count, :]
    for src, rows, start in zip((below, above), y_rows(s, 3, 2), (2, 4 + y)):
        for m, r, e, at in rows:
            count, at = x + 2 * e, at + s.rows_f
            flat_wind[pl.ds((m * s.ex + 2 - e) * 24 + start + r, count, stride=24), :] = src[at : at + count, :]


def edge_lanes(s, lane, width):
    return (lane < width) | (lane >= s.z - width)


def zpack_kernel(s, c0, cw, lo, hi, below, above, out, rows):
    q, x, y, z = s.q, s.x, s.y, s.z
    flat = rows.reshape((q + 3) * s.ex * 8, z)
    rows[...] = jnp.zeros_like(rows)
    for src, place in ((below, 0), (above, 3)):
        for member, width, first in ((0, 3, 0), (q, 2, s.rows_f)):
            skip = 3 - width if place == 0 else 0
            for m, r, e, at in y_rows(s, q if width == 3 else 3, width)[place // 3]:
                e = min(e, 2)
                count = x + 2 * e
                start = ((member + m) * s.ex + 2 - e) * 8 + place + skip + r
                flat[pl.ds(start, count, stride=8), :] = src[first + at : first + at + count, :]
    lane = lanes_of((y, z))
    keep = edge_lanes(s, lane, 3)
    for m in range(q + 3):
        inside, outside = None, None
        for a in range(s.ex):
            if m < q:
                tile = layer_of(s, c0, lo, hi, m, a - 2, 3, 0)
            else:
                tile = layer_of(s, cw, lo, hi, m - q, a - 2, 2, 3 * q)
            shift = (6 * a + 3) % z
            part = pltpu.roll(jnp.where(keep, tile, 0.0), shift, 1)
            inside = part if inside is None else inside + part
            part = pltpu.roll(jnp.where(keep[:8], rows[m, a], 0.0), shift, 1)
            outside = part if outside is None else outside + part
        out[m, 0:1, :] = jnp.zeros((1, z), F32)
        out[m, 1:4, :] = outside[0:3]
        out[m, 4 : 4 + y, :] = inside
        out[m, 4 + y : 7 + y, :] = outside[3:6]
        out[m, 7 + y : 8 + y, :] = jnp.zeros((1, z), F32)


def coarse_kernel(
    s, sides, c0, cw, lo, hi, below, above, zown, zin, out, pad0, pad1, pad2, wind, beyond, nearest
):
    q, x, y, z = s.q, s.x, s.y, s.z
    assemble(s, c0, cw, lo, hi, below, above, pad0, wind)
    pads = (pad0, pad1, pad2)
    lane = lanes_of((24, z))
    group = lane % 6
    from_low = group == 2
    from_high = group == 3
    exists = jnp.where(group < 3, sides[0, 0], sides[0, 1]).astype(F32)
    wind_z = [zin[q + d] for d in range(3)]
    for f in range(q):
        beyond[0, f] = zin[f] * exists
        nearest[0, f] = zown[f]
    for step in range(3):
        src, fraction = pads[step], section_weights[step]
        flat = src.reshape(q * s.ep * WPAD, z)
        flat_wind = wind.reshape(3 * s.ex * 24, z)
        flat_beyond = beyond.reshape(3 * q * 24, z)
        skip, height = (0, 24) if step < 2 else (4, y)
        here = lanes_of((height, z))
        is_first, is_last = here == 0, here == z - 1

        def two_layers(t, packed, step=step, src=src, flat=flat, fraction=fraction, skip=skip, height=height):
            first = step + 2 * t
            ghosts, packed = (list(some) for some in packed)
            made = []
            co = []
            for a in (first, first + 1):
                if step < 2:
                    winds = [wind[d, a] for d in range(3)]
                else:
                    winds = [flat_wind[pl.ds((d * s.ex + a) * 24 + skip, height), :] for d in range(3)]
                co.append(coefficients(fraction, winds))
            for f in range(q):

                def at_layer(of, layer, by=0, f=f):
                    if step < 2 and not by:
                        return of[f, layer, BLOCK, :]
                    row = (f * s.ep + layer) * WPAD + 8 + skip + by
                    return of.reshape(flat.shape)[pl.ds(row, height), :]

                row_of = [at_layer(src, first + i) for i in range(4)]
                for i in range(2):
                    a = first + i
                    center = row_of[i + 1]
                    ghost = ghosts[f]
                    ghosts[f] = pltpu.roll(ghost, z - 6, 1)
                    value = advanced(
                        None if step == 0 else at_layer(pad0, a + 1),
                        fraction,
                        co[i],
                        center,
                        row_of[i],
                        row_of[i + 2],
                        at_layer(src, a + 1, -1),
                        at_layer(src, a + 1, 1),
                        pltpu.roll(jnp.where(is_last, ghost, center), 1, 1),
                        pltpu.roll(jnp.where(is_first, ghost, center), z - 1, 1),
                    )
                    made.append((f, a, value))
                    if step == 0:
                        packed[f] = pltpu.roll(packed[f] + jnp.where(is_first | is_last, value, 0.0), z - 6, 1)
            for f, a, value in made:
                if step == 2:
                    out[f, a - 2] = value
                else:
                    pads[step + 1][f, a + 1, BLOCK, :] = value
            return tuple(ghosts), tuple(packed)

        zeros = tuple(jnp.zeros((24, z), F32) for _ in range(q)) if step == 0 else ()
        ghosts = tuple(
            pltpu.roll(flat_beyond[(step * q + f) * 24 + skip : (step * q + f) * 24 + skip + height, :], z - 6 * step - 3, 1)
            for f in range(q)
        )
        _, packed = unrolled(0, s.ex // 2 - step, 2 + (step == 1), two_layers, (ghosts, zeros))
        if step == 2:
            break
        for f in range(q):
            if step == 0:
                nearest[1, f] = pltpu.roll(packed[f], (6 * s.ex + 3) % z, 1)
            ghost, near = beyond[step, f], nearest[step, f]
            value = advanced(
                None if step == 0 else beyond[0, f],
                fraction,
                coefficients(fraction, wind_z),
                ghost,
                pltpu.roll(ghost, 6, 1),
                pltpu.roll(ghost, z - 6, 1),
                pltpu.roll(ghost, 1, 0),
                pltpu.roll(ghost, 23, 0),
                pltpu.roll(jnp.where(from_low, near, ghost), 1, 1),
                pltpu.roll(jnp.where(from_high, near, ghost), z - 1, 1),
            )
            beyond[step + 1, f] = value * exists


def fine_kernel(s, f0, fw, flo_there, fhi_there, slab, out, avg, *scratch):
    s1, s2, faces, ghost_rows, zface, flo, fhi, summed, sems = scratch
    arrivals = [
        pltpu.make_async_copy(flo_there, flo, sems.at[4]),
        pltpu.make_async_copy(fhi_there, fhi, sems.at[5]),
    ]
    for move in arrivals:
        move.start()
    states = (None, s1, s2, s1)
    q, y, z, fx, fe = s.q, s.y, s.z, s.fx, s.fe
    layers = fx + 6
    rows = slice(TOP, TOP + y)
    shift_z, shift_sz = z.bit_length() - 1, s.sz.bit_length() - 1
    r = lax.broadcasted_iota(jnp.int32, (2 * z, 2 * z), 0)
    c = lax.broadcasted_iota(jnp.int32, (2 * z, 2 * z), 1)
    near = c >> 1
    far = near + 2 * (c & 1) - 1
    same = (far >> shift_sz) == (near >> shift_sz)
    to_fine = jnp.where(r == near, 0.75, jnp.where((r == far) & same, 0.25, 0.0))
    ends_at = ((r & 2) << (shift_z - 1)) + jnp.where((r & 1) == 1, 0, z - 1)
    to_fine = jnp.where(r < z, to_fine, jnp.where(c == ends_at, 0.25, 0.0)).astype(BF16)
    ends = slab[s.rows_y : s.rows_y + s.ex, :]
    lane_x = lanes_of((s.ex, z))
    own_ends = [jnp.where((lane_x >> 2) == i, ends, 0.0) for i in range(3 * q)]
    wide = times(jnp.concatenate([slab[: s.rows_y, :], jnp.concatenate(own_ends, axis=0)], axis=1), to_fine)
    half = fe // 2
    for k in range(3):
        for f in range(q):
            for side in range(2):
                first = (k * q + f) * s.ex
                here = faces.at[(k * q + f) * 2 + side]
                here[: s.ex, :] = wide[first : first + s.ex, side * z : side * z + z]
                a = here[0:half, :]
                b = here[1 : half + 1, :]
                d = here[2 : half + 2, :]
                if k == 0:
                    flat, base, stride = ghost_rows, (2 * f + side) * fe, 1
                else:
                    flat, stride = states[k].reshape(q * layers * PAD, z), PAD
                    base = (f * layers + 1) * PAD + (TOP - 1 if side == 0 else TOP + y)
                flat[pl.ds(base, half, stride=2 * stride), :] = 0.25 * a + 0.75 * b
                flat[pl.ds(base + stride, half, stride=2 * stride), :] = 0.75 * b + 0.25 * d
    for f in range(q):
        at = s.rows_e + f * s.rows_z
        a = slab[at : at + s.sy, :]
        b = slab[at + 1 : at + 1 + s.sy, :]
        d = slab[at + 2 : at + 2 + s.sy, :]
        zface[pl.ds(f * y, s.sy, stride=2), :] = 0.25 * a + 0.75 * b
        zface[pl.ds(f * y + 1, s.sy, stride=2), :] = 0.75 * b + 0.25 * d
        a = zface[f * y : f * y + y, :]
        b = pltpu.roll(a, z - 2, 1)
        d = pltpu.roll(a, z - 4, 1)
        zface[f * y : f * y + y, :] = 0.25 * a + 0.75 * b
        zface[(q + f) * y : (q + f + 1) * y, :] = 0.75 * b + 0.25 * d
    lane = lanes_of((y, z))
    is_first, is_last = lane == 0, lane == z - 1
    row_in = lax.broadcasted_iota(jnp.int32, (y, z), 0)
    is_low, is_high = row_in == 0, row_in == y - 1
    flat_f0 = f0.reshape(q * fx * y, z)

    def ghosts_at(k, t):
        shift = -(2 * s.ex * k + 2 * t) % z
        return tuple(pltpu.roll(zface[i * y : (i + 1) * y, :], shift, 1) if shift else zface[i * y : (i + 1) * y, :] for i in range(2 * q))

    def pair_of_layers(k, t, ghosts, inner):
        src, fraction = states[k], section_weights[k]

        def field(f, at):
            return f0[f, at] if inner else layer_of(s, f0, flo, fhi, f, at, 3, 0)

        co = []
        for at in (2 * t - 2, 2 * t - 1):
            if inner:
                winds = [fw[d, at] for d in range(3)]
            else:
                winds = [layer_of(s, fw, flo, fhi, d, at, 2, 3 * q) for d in range(3)]
            co.append(coefficients(fraction, winds))
        made = []
        for f in range(q):
            if k == 0:
                row_of = [field(f, 2 * t - 3 + i) for i in range(4)]
            else:
                row_of = [src[f, 2 * t + i, rows, :] for i in range(4)]
            for odd in range(2):
                b = 2 * t + odd
                center = row_of[odd + 1]
                if k == 0:
                    if inner:
                        row = (f * fx + b - 2) * y
                        y_low, y_high = flat_f0[pl.ds(row - 1, y), :], flat_f0[pl.ds(row + 1, y), :]
                    else:
                        y_low, y_high = pltpu.roll(center, 1, 0), pltpu.roll(center, y - 1, 0)
                    y_low = jnp.where(is_low, ghost_rows[pl.ds(2 * f * fe + b, 1), :], y_low)
                    y_high = jnp.where(is_high, ghost_rows[pl.ds((2 * f + 1) * fe + b, 1), :], y_high)
                else:
                    flat = src.reshape(q * layers * PAD, z)
                    row = (f * layers + b + 1) * PAD + TOP
                    y_low, y_high = flat[pl.ds(row - 1, y), :], flat[pl.ds(row + 1, y), :]
                ghost = ghosts[odd * q + f]
                value = advanced(
                    None if k == 0 else field(f, b - 2),
                    fraction,
                    co[odd],
                    center,
                    row_of[odd],
                    row_of[odd + 2],
                    y_low,
                    y_high,
                    pltpu.roll(jnp.where(is_last, ghost, center), 1, 1),
                    pltpu.roll(jnp.where(is_first, ghost, center), z - 1, 1),
                )
                made.append((f, b, value))
        for f, b, value in made:
            states[k + 1][f, b + 1, rows, :] = value
        return tuple(pltpu.roll(g, z - 2, 1) for g in ghosts)

    for move in arrivals:
        move.wait()
    moves = []
    for k in range(3):
        if k < 2:
            outer = 2 - k
            for t in list(range(outer)) + list(range(half - outer, half)):
                pair_of_layers(k, t, ghosts_at(k, t), False)
            unrolled(outer, half - outer, 2, lambda t, g, k=k: pair_of_layers(k, t, g, True), ghosts_at(k, outer))
            continue
        carried, part = ghosts_at(k, 1), (half - 2) // 4
        for i in range(4):
            begin = 1 + i * part
            carried = unrolled(begin, begin + part, 2, lambda t, g, k=k: pair_of_layers(k, t, g, True), carried)
            begin, end = 2 * part * i, 2 * part * (i + 1)
            moves.append(pltpu.make_async_copy(s1.at[:, 3 + begin : 3 + end, rows], out.at[:, begin:end], sems.at[i]))
            moves[-1].start()
    rz = lax.broadcasted_iota(jnp.int32, (z, z), 0)
    cz = lax.broadcasted_iota(jnp.int32, (z, z), 1)
    flat = summed.reshape(q * s.x * y, z)
    pairs_z = [jnp.where(cz == (rz >> 1) + odd * s.sz, 0.125, 0.0).astype(BF16) for odd in range(2)]
    for f in range(q):
        for p in range(s.x):
            both = s1[f, 3 + 2 * p, rows, :] + s1[f, 4 + 2 * p, rows, :]
            summed[f, p] = both + pltpu.roll(both, y - 1, 0)
    for f in range(q):
        sums = []
        for odd in range(2):
            parts = [flat[pl.ds((f * s.x + 2 * p + odd) * y, y // 2, stride=2), :] for p in range(s.x // 2)]
            sums.append(times(jnp.concatenate(parts, axis=0), pairs_z[odd]))
        avg[f] = (sums[0] + sums[1]).reshape(s.x // 2, y // 2, z)
    for move in moves:
        move.wait()


def merge_kernel(s, c3, avg, out, made, sems):
    lane = lanes_of((s.sy, s.z))
    inside = (lane >= s.lz) & (lane < s.lz + s.sz)
    moves = []
    for f in range(s.q):
        for p in range(s.x // 2):
            both = avg[f, p]
            for odd in range(2):
                at = 2 * p + odd
                moved = pltpu.roll(both, s.lz if odd == 0 else s.z - s.lz, 1)
                made[f, at] = c3[f, at]
                made[f, at, s.ly : s.ly + s.sy, :] = jnp.where(inside, moved, c3[f, at, s.ly : s.ly + s.sy, :])
        moves.append(pltpu.make_async_copy(made.at[f], out.at[f], sems.at[f]))
        moves[-1].start()
    for move in moves:
        move.wait()


SHORT = pl.CostEstimate(flops=1, bytes_accessed=1, transcendentals=0)


def run(kernel, name, ins, outs, scratch, megabytes, spaces=None, cost=SHORT):
    spaces = spaces or [pltpu.VMEM] * len(ins)
    outs = [out if isinstance(out[0], tuple) else (out, pltpu.VMEM) for out in outs]
    ins = [i if space is pltpu.SMEM else pltpu.with_memory_space_constraint(i, space) for i, space in zip(ins, spaces)]
    return pl.pallas_call(
        kernel,
        out_shape=tuple(space(dims, F32) for dims, space in outs),
        in_specs=[pl.BlockSpec(memory_space=space) for space in spaces],
        out_specs=tuple(pl.BlockSpec(memory_space=space) for _, space in outs),
        scratch_shapes=scratch,
        compiler_params=pltpu.CompilerParams(vmem_limit_bytes=megabytes << 20),
        cost_estimate=cost,
        name=name,
    )(*ins)


def ring(array, axis, by):
    size = lax.axis_size(axis)
    return lax.ppermute(array, axis, [(i, (i + by) % size) for i in range(size)])


def move_by(array, amount, beside=None):
    size = lax.axis_size("gx")
    work, operands = beside or (lambda: (), ())
    if size <= 8:

        def branch(by, array, *operands):
            return array if by == 0 else ring(array, "gx", by), work(*operands)

        return lax.switch(amount, [functools.partial(branch, by) for by in range(size)], array, *operands)
    for bit in range((size - 1).bit_length()):
        array = jnp.where((amount >> bit) % 2 == 1, ring(array, "gx", 1 << bit), array)
    return array, work(*operands)


def z_columns(zown):
    size = lax.axis_size("gz")
    if size == 1:
        return zown
    if size == 2:
        return lax.ppermute(zown, "gz", [(0, 1), (1, 0)])
    below = lax.broadcasted_iota(jnp.int32, zown.shape, 2) % 6 < 3
    return jnp.where(below, ring(zown, "gz", 1), ring(zown, "gz", -1))


def pack(s, fields, wind, spare, name):
    return run(
        functools.partial(pack_kernel, s),
        name,
        [fields, wind],
        [(s.halo + spare, s.y, s.z)] * 2,
        [pltpu.SemaphoreType.DMA((4,))],
        1,
        [pltpu.HBM] * 2,
    )


def shards(coarse_fields, coarse_wind, fine_fields, fine_wind, fine_owner):
    s = Sizes(coarse_fields.shape, fine_fields.shape)
    q, x, y, z, fx = s.q, s.x, s.y, s.z, s.fx
    size = lax.axis_size("gx")
    offset = (fine_owner[0, 0, 0] - lax.axis_index("gx")) % size
    level = lax.axis_index("gz")
    neighbours = jnp.stack([level > 0, level < lax.axis_size("gz") - 1]).astype(jnp.int32).reshape(1, 2)
    cup, cdown = pack(s, coarse_fields, coarse_wind, 0, "pack_coarse")
    lo, hi = ring(cup, "gx", 1), ring(cdown, "gx", -1)
    part, near = run(
        functools.partial(inner_kernel, s),
        "inner",
        [coarse_fields, coarse_wind],
        [(s.slab, z), (q, 2, y, z)],
        [pltpu.VMEM((q, x, y, z), F32)] * 2,
        3,
    )
    fup, fdown = pack(s, fine_fields, fine_wind, 2, "pack_fine")
    fup, fdown, offset = lax.optimization_barrier((fup, fdown, offset))
    flo, fhi = ring(fup, "gx", 1), ring(fdown, "gx", -1)
    padded = [pltpu.VMEM((q, s.ep, WPAD, z), F32)]
    wind_rows = [pltpu.VMEM((3, s.ex, 24, z), F32)]
    coarse_fields, part, near = lax.optimization_barrier((coarse_fields, part, near))
    coarse_level = [coarse_fields, coarse_wind, lo, hi]
    yup, ydn = run(functools.partial(ypack_kernel, s), "ypack", coarse_level, [(s.rows_f + s.rows_w, z)] * 2, [], 1)
    yrows = [ring(yup, "gy", 1), ring(ydn, "gy", -1)]
    ends = [pltpu.VMEM((q, 2 * EDGE, y, z), F32)] * 3
    (slab,) = run(functools.partial(slab_kernel, s), "slab", coarse_level + [part, near], [(s.slab, z)], ends, 3)
    slab, _ = move_by(slab, (size - offset) % size)
    yrows, slab, flo, fhi = lax.optimization_barrier((yrows, slab, flo, fhi))
    kernel = functools.partial(zpack_kernel, s)
    beyond_rows = [pltpu.VMEM((q + 3, s.ex, 8, z), F32)]
    (zown,) = run(kernel, "zpack", coarse_level + yrows, [(q + 3, 24, z)], beyond_rows, 2)
    zin = z_columns(zown)
    layers = fx + 6
    fine_next, averaged = run(
        functools.partial(fine_kernel, s),
        "fine",
        [fine_fields, fine_wind, flo, fhi, slab],
        [((q, fx, y, z), pltpu.HBM), (q, x // 2, y // 2, z)],
        [
            pltpu.VMEM((q, layers, PAD, z), F32),
            pltpu.VMEM((q, layers, PAD, z), F32),
            pltpu.VMEM((6 * q, s.ep, z), F32),
            pltpu.VMEM((2 * q * s.fe, z), F32),
            pltpu.VMEM((2 * q * y, z), F32),
            pltpu.VMEM(flo.shape, F32),
            pltpu.VMEM(fhi.shape, F32),
            pltpu.VMEM((q, s.x, y, z), F32),
            pltpu.SemaphoreType.DMA((6,)),
        ],
        9,
        [pltpu.VMEM, pltpu.VMEM, pltpu.HBM, pltpu.HBM, pltpu.VMEM],
    )

    def coarse(*ins):
        cost = pl.CostEstimate(flops=40_000_000, bytes_accessed=4_000_000, transcendentals=0)
        columns = [pltpu.VMEM((3, q, 24, z), F32), pltpu.VMEM((2, q, 24, z), F32)]
        spaces = [pltpu.SMEM] + [pltpu.VMEM] * (len(ins) - 1)
        kernel = functools.partial(coarse_kernel, s)
        return run(kernel, "coarse", ins, [(q, x, y, z)], padded * 3 + wind_rows + columns, 9, spaces, cost)[0]

    averaged, state = move_by(averaged, offset, (coarse, (neighbours, *coarse_level, *yrows, zown, zin)))
    (coarse_next,) = run(
        functools.partial(merge_kernel, s),
        "merge",
        [state, averaged],
        [((q, x, y, z), pltpu.HBM)],
        [pltpu.VMEM((q, x, y, z), F32), pltpu.SemaphoreType.DMA((q,))],
        2,
    )
    return coarse_next, fine_next


def solution(mesh):
    spec = P(None, "gx", "gy", "gz")
    return jax.shard_map(
        shards,
        mesh=mesh,
        in_specs=(spec, spec, spec, spec, P("gx", "gy", "gz")),
        out_specs=(spec, spec),
        check_vma=False,
    )
```

```python
import functools

import jax
import jax.numpy as jnp
from jax import lax
from jax.experimental import pallas as pl
from jax.experimental.pallas import tpu as pltpu
from jax.sharding import PartitionSpec as P

diffusion = 0.05
section_weights = (1.0 / 3.0, 0.5, 1.0)
F32 = jnp.float32
BF16 = jnp.bfloat16
PAD = 32
TOP = 8


class Sizes:
    def __init__(self, coarse_shape, fine_shape):
        self.q, self.x, self.y, self.z = coarse_shape
        self.fx = fine_shape[1]
        self.ly, self.sy = self.y // 4, self.y // 2
        self.lz, self.sz = self.z // 4, self.z // 2
        self.ex = self.x + 4
        self.ep = -(-self.ex // 8) * 8
        self.fe = self.fx + 4
        self.halo = 3 * self.q + 6
        self.rows_f, self.rows_w = self.q * (3 * self.x + 6), 3 * (2 * self.x + 2)
        self.rows_y = 3 * self.q * self.ex
        self.rows_e = self.rows_y + self.ep
        self.rows_z = self.sy + 2
        self.slab = self.rows_e + self.q * self.rows_z
        assert self.q == 4 and self.y == 16 and self.z == 128 and self.ex <= 20 and self.fx == 2 * self.x


def lanes_of(shape):
    return lax.broadcasted_iota(jnp.int32, shape, len(shape) - 1)


def halves(value):
    high = value.astype(BF16)
    return high, (value - high.astype(F32)).astype(BF16)


def times(value, matrix):
    high, low = halves(value)
    return jnp.dot(high, matrix, preferred_element_type=F32) + jnp.dot(low, matrix, preferred_element_type=F32)


def coefficients(fraction, wind):
    out = []
    for w in wind:
        turned_by = w * (-0.5 * fraction)
        out += [diffusion * fraction + turned_by, diffusion * fraction - turned_by]
    return out


def advanced(base, fraction, co, center, x_low, x_high, y_low, y_high, z_low, z_high):
    along = (co[0] * x_high + co[1] * x_low) + (co[2] * y_high + co[3] * y_low) + (co[4] * z_high + co[5] * z_low)
    if base is None:
        return center * (1.0 - 6.0 * diffusion * fraction) + along
    return (base - center * (6.0 * diffusion * fraction)) + along


def layer_of(s, own, low, high, member, at, width, first):
    size = own.shape[1]
    if at < 0:
        return low[first + width * member + at + width]
    if at >= size:
        return high[first + width * member + at - size]
    return own[member, at]


def unrolled(begin, end, at_once, body, carry=None):
    while (end - begin) % at_once:
        at_once -= 1

    def several(i, carry):
        for more in range(at_once):
            carry = body(begin + i * at_once + more, carry)
        return carry

    return lax.fori_loop(0, (end - begin) // at_once, several, carry)


def pack_kernel(s, fields, wind, up, down, sems):
    size = fields.shape[1]
    moves = []
    for own, members, width, first in ((fields, s.q, 3, 0), (wind, 3, 2, 3 * s.q)):
        for dst, at in ((up, size - width), (down, 0)):
            place = dst.at[first : first + members * width].reshape(members, width, s.y, s.z)
            moves.append((own.at[:, at : at + width], place))
    moves = [pltpu.make_async_copy(src, dst, sems.at[i]) for i, (src, dst) in enumerate(moves)]
    for move in moves:
        move.start()
    for move in moves:
        move.wait()


def y_rows(s, members, width):
    below, above = [], []
    for out, extra in ((below, lambda r: r), (above, lambda r: width - 1 - r)):
        at = 0
        for m in range(members):
            for r in range(width):
                out.append((m, r, extra(r), at))
                at += s.x + 2 * extra(r)
    return below, above


def ypack_kernel(s, c0, cw, lo, hi, up, dn):
    x, y, z = s.x, s.y, s.z
    flat_lo = lo.reshape(s.halo * y, z)
    flat_hi = hi.reshape(s.halo * y, z)
    for own, members, width, first, place in ((c0, s.q, 3, 0, 0), (cw, 3, 2, 3 * s.q, s.rows_f)):
        flat = own.reshape(members * x * y, z)
        for dst, rows, start in zip((up, dn), y_rows(s, members, width), (y - width, 0)):
            for m, r, e, at in rows:
                row, at = start + r, at + place
                if e:
                    dst[at : at + e, :] = flat_lo[pl.ds((first + width * (m + 1) - e) * y + row, e, stride=y), :]
                    dst[at + e + x : at + x + 2 * e, :] = flat_hi[pl.ds((first + width * m) * y + row, e, stride=y), :]
                dst[at + e : at + e + x, :] = flat[pl.ds(m * x * y + row, x, stride=y), :]


EDGE = 4


def turned(base, fraction, wind, center, x_low, x_high):
    y, z = center.shape
    return advanced(
        base,
        fraction,
        wind,
        center,
        x_low,
        x_high,
        pltpu.roll(center, 1, 0),
        pltpu.roll(center, y - 1, 0),
        pltpu.roll(center, 1, 1),
        pltpu.roll(center, z - 1, 1),
    )


def slab_parts(s, rows_of, tile_of, layers_of, put):
    q, y, z = s.q, s.y, s.z
    lane_y = lanes_of((y, z))
    columns = (lane_y == s.lz - 1) | (lane_y == s.lz) | (lane_y == s.lz + s.sz - 1) | (lane_y == s.lz + s.sz)
    low_at = (lane_y % 2 == 0) & (lane_y < z // 2)
    high_at = (lane_y % 2 == 0) & (lane_y >= z // 2)
    ends = None
    for f in range(q):
        zfaces = None
        for k in range(3):
            rows = [rows_of(k, f, row) for row in (s.ly - 1, s.ly, s.ly + s.sy - 1, s.ly + s.sy)]
            sides = (0.75 * rows[0] + 0.25 * rows[1], 0.25 * rows[2] + 0.75 * rows[3])
            lane_x = lanes_of(sides[0].shape)
            put(
                "y",
                (k * q + f) * s.ex,
                jnp.where(lane_x < s.sz, pltpu.roll(sides[0], z - s.lz, 1), pltpu.roll(sides[1], s.lz, 1)),
            )
            for side in range(2):
                e = 4 * (q * k + f) + 2 * side + 1
                before = jnp.where(lane_x == s.lz - 1, sides[side], 0.0)
                after = jnp.where(lane_x == s.lz + s.sz, sides[side], 0.0)
                part = pltpu.roll(before, (e - s.lz + 1) % z, 1) + pltpu.roll(after, (e - 1 - s.lz - s.sz) % z, 1)
                ends = part if ends is None else ends + part
            raw = None
            for a in layers_of(k):
                part = jnp.where(columns, tile_of(k, f, a), 0.0)
                part = pltpu.roll(part, (2 * a - s.lz + 1) % z, 1)
                raw = part if raw is None else raw + part
            beside = pltpu.roll(raw, z - 1, 1)
            low = jnp.where(low_at, 0.75 * raw + 0.25 * beside, 0.0)
            high = jnp.where(high_at, 0.25 * raw + 0.75 * beside, 0.0)
            part = pltpu.roll(low, (2 * s.ex * k - 1) % z, 1) + pltpu.roll(high, (2 * s.ex * k - z // 2) % z, 1)
            zfaces = part if zfaces is None else zfaces + part
        put("z", s.rows_e + f * s.rows_z, zfaces[s.ly - 1 : s.ly + s.sy + 1])
    put("e", s.rows_y, ends)


def inner_kernel(s, c0, cw, part, near, state1, state2):
    q, x, y, z = s.q, s.x, s.y, s.z
    states = (c0, state1, state2)
    for step in range(2):
        src, dst = states[step], states[step + 1]

        def layer(j, carry, step=step, src=src, dst=dst):
            w = coefficients(section_weights[step], [cw[d, j] for d in range(3)])
            made = []
            for f in range(q):
                base = None if step == 0 else c0[f, j]
                made.append(turned(base, section_weights[step], w, src[f, j], src[f, j - 1], src[f, j + 1]))
            for f in range(q):
                dst[f, j] = made[f]
            return carry

        unrolled(step + 1, x - 1 - step, 7 if step == 0 else 6, layer)
    for f in range(q):
        near[f, 0] = state1[f, EDGE - 2]
        near[f, 1] = state1[f, x + 1 - EDGE]
    count = s.ex - 2 * EDGE
    part[...] = jnp.zeros_like(part)

    def rows_of(k, f, row):
        flat = states[k].reshape(q * x * y, z)
        return flat[pl.ds((f * x + EDGE - 2) * y + row, count, stride=y), :]

    def put(kind, at, rows):
        if kind == "z":
            part[at : at + s.rows_z, :] = rows
        else:
            part[at + EDGE : at + EDGE + count, :] = rows

    slab_parts(s, rows_of, lambda k, f, a: states[k][f, a - 2], lambda k: range(EDGE, s.ex - EDGE), put)


def slab_kernel(s, c0, cw, lo, hi, part, near, slab, ends0, ends1, ends2):
    q, x, y, z = s.q, s.x, s.y, s.z
    states = (ends0, ends1, ends2)
    places = list(range(-2, EDGE - 2)) + list(range(x + 2 - EDGE, x + 2))
    slab[...] = part[...]
    for j, at in enumerate(places):
        for f in range(q):
            ends0[f, j] = layer_of(s, c0, lo, hi, f, at, 3, 0)
    for step in range(2):
        for j, at in enumerate(places):
            if step == 1 and at in (-2, x + 1):
                for f in range(q):
                    ends2[f, j] = jnp.zeros((y, z), F32)
                continue
            w = coefficients(section_weights[step], [layer_of(s, cw, lo, hi, d, at, 2, 3 * q) for d in range(3)])
            for f in range(q):

                def beside(at, f=f):
                    if step == 0:
                        return layer_of(s, c0, lo, hi, f, at, 3, 0)
                    if at in places:
                        return ends1[f, places.index(at)]
                    return near[f, 0 if at < x // 2 else 1]

                base = None if step == 0 else ends0[f, j]
                states[step + 1][f, j] = turned(
                    base, section_weights[step], w, beside(at), beside(at - 1), beside(at + 1)
                )

    def rows_of(k, f, row):
        flat = states[k].reshape(q * 2 * EDGE * y, z)
        return flat[pl.ds(f * 2 * EDGE * y + row, 2 * EDGE, stride=y), :]

    def put(kind, at, rows):
        if kind == "z":
            slab[at : at + s.rows_z, :] = part[at : at + s.rows_z, :] + rows
        else:
            slab[at : at + EDGE, :] = rows[:EDGE]
            slab[at + s.ex - EDGE : at + s.ex, :] = rows[EDGE:]

    def layers_of(k):
        some = range(0 if k == 0 else 1, EDGE)
        return list(some) + [s.ex - 1 - a for a in some]

    def tile_of(k, f, a):
        return states[k][f, a if a < EDGE else a - s.ex + 2 * EDGE]

    slab_parts(s, rows_of, tile_of, layers_of, put)


WTOP, WPAD = 12, 40
BLOCK = slice(8, 32)


def assemble(s, c0, cw, lo, hi, below, above, pad, wind):
    q, x, y, z = s.q, s.x, s.y, s.z
    flat = pad.reshape(q * s.ep * WPAD, z)
    flat_wind = wind.reshape(3 * s.ex * 24, z)
    for f in range(q):
        for at in range(-3, x + 3):
            pad[f, at + 3, WTOP : WTOP + y, :] = layer_of(s, c0, lo, hi, f, at, 3, 0)
    for d in range(3):
        for at in range(-2, x + 2):
            wind[d, at + 2, 4 : 4 + y, :] = layer_of(s, cw, lo, hi, d, at, 2, 3 * q)
    for src, rows, start in zip((below, above), y_rows(s, q, 3), (WTOP - 3, WTOP + y)):
        for m, r, e, at in rows:
            count = x + 2 * e
            flat[pl.ds((m * s.ep + 3 - e) * WPAD + start + r, count, stride=WPAD), :] = src[at : at + count, :]
    for src, rows, start in zip((below, above), y_rows(s, 3, 2), (2, 4 + y)):
        for m, r, e, at in rows:
            count, at = x + 2 * e, at + s.rows_f
            flat_wind[pl.ds((m * s.ex + 2 - e) * 24 + start + r, count, stride=24), :] = src[at : at + count, :]


def edge_lanes(s, lane, width):
    return (lane < width) | (lane >= s.z - width)


def zpack_kernel(s, c0, cw, lo, hi, below, above, out, rows):
    q, x, y, z = s.q, s.x, s.y, s.z
    flat = rows.reshape((q + 3) * s.ex * 8, z)
    rows[...] = jnp.zeros_like(rows)
    for src, place in ((below, 0), (above, 3)):
        for member, width, first in ((0, 3, 0), (q, 2, s.rows_f)):
            skip = 3 - width if place == 0 else 0
            for m, r, e, at in y_rows(s, q if width == 3 else 3, width)[place // 3]:
                e = min(e, 2)
                count = x + 2 * e
                start = ((member + m) * s.ex + 2 - e) * 8 + place + skip + r
                flat[pl.ds(start, count, stride=8), :] = src[first + at : first + at + count, :]
    lane = lanes_of((y, z))
    keep = edge_lanes(s, lane, 3)
    for m in range(q + 3):
        inside, outside = None, None
        for a in range(s.ex):
            if m < q:
                tile = layer_of(s, c0, lo, hi, m, a - 2, 3, 0)
            else:
                tile = layer_of(s, cw, lo, hi, m - q, a - 2, 2, 3 * q)
            shift = (6 * a + 3) % z
            part = pltpu.roll(jnp.where(keep, tile, 0.0), shift, 1)
            inside = part if inside is None else inside + part
            part = pltpu.roll(jnp.where(keep[:8], rows[m, a], 0.0), shift, 1)
            outside = part if outside is None else outside + part
        out[m, 0:1, :] = jnp.zeros((1, z), F32)
        out[m, 1:4, :] = outside[0:3]
        out[m, 4 : 4 + y, :] = inside
        out[m, 4 + y : 7 + y, :] = outside[3:6]
        out[m, 7 + y : 8 + y, :] = jnp.zeros((1, z), F32)


def coarse_kernel(
    s, sides, c0, cw, lo, hi, below, above, zown, zin, out, pad0, pad1, pad2, wind, beyond, nearest, turning
):
    q, x, y, z = s.q, s.x, s.y, s.z
    assemble(s, c0, cw, lo, hi, below, above, pad0, wind)
    pads = (pad0, pad1, pad2)
    lane = lanes_of((24, z))
    group = lane % 6
    from_low = group == 2
    from_high = group == 3
    exists = jnp.where(group < 3, sides[0, 0], sides[0, 1]).astype(F32)
    wind_z = [zin[q + d] for d in range(3)]
    for f in range(q):
        beyond[0, f] = zin[f] * exists
        nearest[0, f] = zown[f]
    for step in range(3):
        src, fraction = pads[step], section_weights[step]
        flat = src.reshape(q * s.ep * WPAD, z)
        flat_wind = wind.reshape(3 * s.ex * 24, z)
        flat_beyond = beyond.reshape(3 * q * 24, z)
        skip, height = (0, 24) if step < 2 else (4, y)
        here = lanes_of((height, z))
        is_first, is_last = here == 0, here == z - 1

        def layer(a, carry, step=step, src=src, flat=flat, fraction=fraction, skip=skip, height=height):
            if step < 2:
                winds = [wind[d, a] for d in range(3)]
            else:
                winds = [flat_wind[pl.ds((d * s.ex + a) * 24 + skip, height), :] for d in range(3)]
            co = coefficients(fraction, winds)
            for f in range(q):

                def at_layer(of, layer, by=0, f=f):
                    if step < 2 and not by:
                        return of[f, layer, BLOCK, :]
                    row = (f * s.ep + layer) * WPAD + 8 + skip + by
                    return of.reshape(flat.shape)[pl.ds(row, height), :]

                center = at_layer(src, a + 1)
                ghost = turning[f, :height, :]
                turning[f, :height, :] = pltpu.roll(ghost, z - 6, 1)
                value = advanced(
                    None if step == 0 else at_layer(pad0, a + 1),
                    fraction,
                    co,
                    center,
                    at_layer(src, a),
                    at_layer(src, a + 2),
                    at_layer(src, a + 1, -1),
                    at_layer(src, a + 1, 1),
                    pltpu.roll(jnp.where(is_last, ghost, center), 1, 1),
                    pltpu.roll(jnp.where(is_first, ghost, center), z - 1, 1),
                )
                if step == 2:
                    out[f, a - 2] = value
                else:
                    pads[step + 1][f, a + 1, BLOCK, :] = value
                if step == 0:
                    nearest[1, f] = pltpu.roll(nearest[1, f] + jnp.where(is_first | is_last, value, 0.0), z - 6, 1)
            return carry

        for f in range(q):
            start = (step * q + f) * 24 + skip
            turning[f, :height, :] = pltpu.roll(flat_beyond[start : start + height, :], z - 6 * step - 3, 1)
            if step == 0:
                nearest[1, f] = jnp.zeros((24, z), F32)
        unrolled(step, s.ex - step, 4 + 2 * (step == 1), layer)
        if step == 2:
            break
        for f in range(q):
            if step == 0:
                nearest[1, f] = pltpu.roll(nearest[1, f], (6 * s.ex + 3) % z, 1)
            ghost, near = beyond[step, f], nearest[step, f]
            value = advanced(
                None if step == 0 else beyond[0, f],
                fraction,
                coefficients(fraction, wind_z),
                ghost,
                pltpu.roll(ghost, 6, 1),
                pltpu.roll(ghost, z - 6, 1),
                pltpu.roll(ghost, 1, 0),
                pltpu.roll(ghost, 23, 0),
                pltpu.roll(jnp.where(from_low, near, ghost), 1, 1),
                pltpu.roll(jnp.where(from_high, near, ghost), z - 1, 1),
            )
            beyond[step + 1, f] = value * exists


def fine_kernel(s, f0, fw, flo_there, fhi_there, slab, out, avg, *scratch):
    s1, s2, faces, ghost_rows, zface, turning, flo, fhi, summed, sems = scratch
    arrivals = [
        pltpu.make_async_copy(flo_there, flo, sems.at[4]),
        pltpu.make_async_copy(fhi_there, fhi, sems.at[5]),
    ]
    for move in arrivals:
        move.start()
    states = (None, s1, s2, s1)
    q, y, z, fx, fe = s.q, s.y, s.z, s.fx, s.fe
    layers = fx + 6
    rows = slice(TOP, TOP + y)
    shift_z, shift_sz = z.bit_length() - 1, s.sz.bit_length() - 1
    r = lax.broadcasted_iota(jnp.int32, (2 * z, 2 * z), 0)
    c = lax.broadcasted_iota(jnp.int32, (2 * z, 2 * z), 1)
    near = c >> 1
    far = near + 2 * (c & 1) - 1
    same = (far >> shift_sz) == (near >> shift_sz)
    to_fine = jnp.where(r == near, 0.75, jnp.where((r == far) & same, 0.25, 0.0))
    ends_at = ((r & 2) << (shift_z - 1)) + jnp.where((r & 1) == 1, 0, z - 1)
    to_fine = jnp.where(r < z, to_fine, jnp.where(c == ends_at, 0.25, 0.0)).astype(BF16)
    ends = slab[s.rows_y : s.rows_y + s.ex, :]
    lane_x = lanes_of((s.ex, z))
    own_ends = [jnp.where((lane_x >> 2) == i, ends, 0.0) for i in range(3 * q)]
    wide = times(jnp.concatenate([slab[: s.rows_y, :], jnp.concatenate(own_ends, axis=0)], axis=1), to_fine)
    half = fe // 2
    for k in range(3):
        for f in range(q):
            for side in range(2):
                first = (k * q + f) * s.ex
                here = faces.at[(k * q + f) * 2 + side]
                here[: s.ex, :] = wide[first : first + s.ex, side * z : side * z + z]
                a = here[0:half, :]
                b = here[1 : half + 1, :]
                d = here[2 : half + 2, :]
                if k == 0:
                    flat, base, stride = ghost_rows, (2 * f + side) * fe, 1
                else:
                    flat, stride = states[k].reshape(q * layers * PAD, z), PAD
                    base = (f * layers + 1) * PAD + (TOP - 1 if side == 0 else TOP + y)
                flat[pl.ds(base, half, stride=2 * stride), :] = 0.25 * a + 0.75 * b
                flat[pl.ds(base + stride, half, stride=2 * stride), :] = 0.75 * b + 0.25 * d
    for f in range(q):
        at = s.rows_e + f * s.rows_z
        a = slab[at : at + s.sy, :]
        b = slab[at + 1 : at + 1 + s.sy, :]
        d = slab[at + 2 : at + 2 + s.sy, :]
        zface[pl.ds(f * y, s.sy, stride=2), :] = 0.25 * a + 0.75 * b
        zface[pl.ds(f * y + 1, s.sy, stride=2), :] = 0.75 * b + 0.25 * d
        a = zface[f * y : f * y + y, :]
        b = pltpu.roll(a, z - 2, 1)
        d = pltpu.roll(a, z - 4, 1)
        zface[f * y : f * y + y, :] = 0.25 * a + 0.75 * b
        zface[(q + f) * y : (q + f + 1) * y, :] = 0.75 * b + 0.25 * d
    lane = lanes_of((y, z))
    is_first, is_last = lane == 0, lane == z - 1
    row_in = lax.broadcasted_iota(jnp.int32, (y, z), 0)
    is_low, is_high = row_in == 0, row_in == y - 1
    flat_f0 = f0.reshape(q * fx * y, z)

    def turn_to(k, t):
        shift = -(2 * s.ex * k + 2 * t) % z
        for i in range(2 * q):
            packed = zface[i * y : (i + 1) * y, :]
            turning[i * y : (i + 1) * y, :] = pltpu.roll(packed, shift, 1) if shift else packed

    def pair_of_layers(k, t, inner):
        src, fraction = states[k], section_weights[k]

        def field(f, at):
            return f0[f, at] if inner else layer_of(s, f0, flo, fhi, f, at, 3, 0)

        for odd in range(2):
            b = 2 * t + odd
            at = b - 2
            if inner:
                winds = [fw[d, at] for d in range(3)]
            else:
                winds = [layer_of(s, fw, flo, fhi, d, at, 2, 3 * q) for d in range(3)]
            co = coefficients(fraction, winds)
            for f in range(q):
                if k == 0:
                    center, x_low, x_high = field(f, at), field(f, at - 1), field(f, at + 1)
                    if inner:
                        row = (f * fx + at) * y
                        y_low, y_high = flat_f0[pl.ds(row - 1, y), :], flat_f0[pl.ds(row + 1, y), :]
                    else:
                        y_low, y_high = pltpu.roll(center, 1, 0), pltpu.roll(center, y - 1, 0)
                    y_low = jnp.where(is_low, ghost_rows[pl.ds(2 * f * fe + b, 1), :], y_low)
                    y_high = jnp.where(is_high, ghost_rows[pl.ds((2 * f + 1) * fe + b, 1), :], y_high)
                else:
                    flat = src.reshape(q * layers * PAD, z)
                    row = (f * layers + b + 1) * PAD + TOP
                    center, x_low, x_high = src[f, b + 1, rows, :], src[f, b, rows, :], src[f, b + 2, rows, :]
                    y_low, y_high = flat[pl.ds(row - 1, y), :], flat[pl.ds(row + 1, y), :]
                i = odd * q + f
                ghost = turning[i * y : (i + 1) * y, :]
                turning[i * y : (i + 1) * y, :] = pltpu.roll(ghost, z - 2, 1)
                states[k + 1][f, b + 1, rows, :] = advanced(
                    None if k == 0 else field(f, at),
                    fraction,
                    co,
                    center,
                    x_low,
                    x_high,
                    y_low,
                    y_high,
                    pltpu.roll(jnp.where(is_last, ghost, center), 1, 1),
                    pltpu.roll(jnp.where(is_first, ghost, center), z - 1, 1),
                )

    for move in arrivals:
        move.wait()
    moves = []
    for k in range(3):
        if k < 2:
            outer = 2 - k
            for t in range(outer):
                turn_to(k, t)
                pair_of_layers(k, t, False)
            unrolled(outer, half - outer, 2, lambda t, g, k=k: pair_of_layers(k, t, True))
            for t in range(half - outer, half):
                pair_of_layers(k, t, False)
            continue
        turn_to(k, 1)
        quarter = (half - 2) // 4
        for i in range(4):
            unrolled(1 + i * quarter, 1 + (i + 1) * quarter, 2, lambda t, g, k=k: pair_of_layers(k, t, True))
            begin, end = 2 * quarter * i, 2 * quarter * (i + 1)
            moves.append(pltpu.make_async_copy(s1.at[:, 3 + begin : 3 + end, rows], out.at[:, begin:end], sems.at[i]))
            moves[-1].start()
    rz = lax.broadcasted_iota(jnp.int32, (z, z), 0)
    cz = lax.broadcasted_iota(jnp.int32, (z, z), 1)
    flat = summed.reshape(q * s.x * y, z)
    pairs_z = [jnp.where(cz == (rz >> 1) + odd * s.sz, 0.125, 0.0).astype(BF16) for odd in range(2)]
    for f in range(q):
        for p in range(s.x):
            both = s1[f, 3 + 2 * p, rows, :] + s1[f, 4 + 2 * p, rows, :]
            summed[f, p] = both + pltpu.roll(both, y - 1, 0)
    for f in range(q):
        sums = []
        for odd in range(2):
            parts = [flat[pl.ds((f * s.x + 2 * p + odd) * y, y // 2, stride=2), :] for p in range(s.x // 2)]
            sums.append(times(jnp.concatenate(parts, axis=0), pairs_z[odd]))
        avg[f] = (sums[0] + sums[1]).reshape(s.x // 2, y // 2, z)
    for move in moves:
        move.wait()


def merge_kernel(s, c3, avg, out, made, sems):
    lane = lanes_of((s.sy, s.z))
    inside = (lane >= s.lz) & (lane < s.lz + s.sz)
    moves = []
    for f in range(s.q):
        for p in range(s.x // 2):
            both = avg[f, p]
            for odd in range(2):
                at = 2 * p + odd
                moved = pltpu.roll(both, s.lz if odd == 0 else s.z - s.lz, 1)
                made[f, at] = c3[f, at]
                made[f, at, s.ly : s.ly + s.sy, :] = jnp.where(inside, moved, c3[f, at, s.ly : s.ly + s.sy, :])
        moves.append(pltpu.make_async_copy(made.at[f], out.at[f], sems.at[f]))
        moves[-1].start()
    for move in moves:
        move.wait()


SHORT = pl.CostEstimate(flops=1, bytes_accessed=1, transcendentals=0)


def run(kernel, name, ins, outs, scratch, megabytes, spaces=None, cost=SHORT):
    spaces = spaces or [pltpu.VMEM] * len(ins)
    outs = [out if isinstance(out[0], tuple) else (out, pltpu.VMEM) for out in outs]
    ins = [i if space is pltpu.SMEM else pltpu.with_memory_space_constraint(i, space) for i, space in zip(ins, spaces)]
    return pl.pallas_call(
        kernel,
        out_shape=tuple(space(dims, F32) for dims, space in outs),
        in_specs=[pl.BlockSpec(memory_space=space) for space in spaces],
        out_specs=tuple(pl.BlockSpec(memory_space=space) for _, space in outs),
        scratch_shapes=scratch,
        compiler_params=pltpu.CompilerParams(vmem_limit_bytes=megabytes << 20),
        cost_estimate=cost,
        name=name,
    )(*ins)


def ring(array, axis, by):
    size = lax.axis_size(axis)
    return lax.ppermute(array, axis, [(i, (i + by) % size) for i in range(size)])


def move_by(array, amount, beside=None):
    size = lax.axis_size("gx")
    work, operands = beside or (lambda: (), ())
    if size <= 8:

        def branch(by, array, *operands):
            return array if by == 0 else ring(array, "gx", by), work(*operands)

        return lax.switch(amount, [functools.partial(branch, by) for by in range(size)], array, *operands)
    for bit in range((size - 1).bit_length()):
        array = jnp.where((amount >> bit) % 2 == 1, ring(array, "gx", 1 << bit), array)
    return array, work(*operands)


def z_columns(zown):
    size = lax.axis_size("gz")
    if size == 1:
        return zown
    if size == 2:
        return lax.ppermute(zown, "gz", [(0, 1), (1, 0)])
    below = lax.broadcasted_iota(jnp.int32, zown.shape, 2) % 6 < 3
    return jnp.where(below, ring(zown, "gz", 1), ring(zown, "gz", -1))


def pack(s, fields, wind, spare, name):
    return run(
        functools.partial(pack_kernel, s),
        name,
        [fields, wind],
        [(s.halo + spare, s.y, s.z)] * 2,
        [pltpu.SemaphoreType.DMA((4,))],
        1,
        [pltpu.HBM] * 2,
    )


def shards(coarse_fields, coarse_wind, fine_fields, fine_wind, fine_owner):
    s = Sizes(coarse_fields.shape, fine_fields.shape)
    q, x, y, z, fx = s.q, s.x, s.y, s.z, s.fx
    size = lax.axis_size("gx")
    offset = (fine_owner[0, 0, 0] - lax.axis_index("gx")) % size
    level = lax.axis_index("gz")
    neighbours = jnp.stack([level > 0, level < lax.axis_size("gz") - 1]).astype(jnp.int32).reshape(1, 2)
    cup, cdown = pack(s, coarse_fields, coarse_wind, 0, "pack_coarse")
    lo, hi = ring(cup, "gx", 1), ring(cdown, "gx", -1)
    part, near = run(
        functools.partial(inner_kernel, s),
        "inner",
        [coarse_fields, coarse_wind],
        [(s.slab, z), (q, 2, y, z)],
        [pltpu.VMEM((q, x, y, z), F32)] * 2,
        3,
    )
    fup, fdown = pack(s, fine_fields, fine_wind, 2, "pack_fine")
    fup, fdown, offset = lax.optimization_barrier((fup, fdown, offset))
    flo, fhi = ring(fup, "gx", 1), ring(fdown, "gx", -1)
    padded = [pltpu.VMEM((q, s.ep, WPAD, z), F32)]
    wind_rows = [pltpu.VMEM((3, s.ex, 24, z), F32)]
    coarse_fields, part, near = lax.optimization_barrier((coarse_fields, part, near))
    coarse_level = [coarse_fields, coarse_wind, lo, hi]
    yup, ydn = run(functools.partial(ypack_kernel, s), "ypack", coarse_level, [(s.rows_f + s.rows_w, z)] * 2, [], 1)
    yrows = [ring(yup, "gy", 1), ring(ydn, "gy", -1)]
    ends = [pltpu.VMEM((q, 2 * EDGE, y, z), F32)] * 3
    (slab,) = run(functools.partial(slab_kernel, s), "slab", coarse_level + [part, near], [(s.slab, z)], ends, 3)
    slab, _ = move_by(slab, (size - offset) % size)
    yrows, slab, flo, fhi = lax.optimization_barrier((yrows, slab, flo, fhi))
    kernel = functools.partial(zpack_kernel, s)
    beyond_rows = [pltpu.VMEM((q + 3, s.ex, 8, z), F32)]
    (zown,) = run(kernel, "zpack", coarse_level + yrows, [(q + 3, 24, z)], beyond_rows, 2)
    zin = z_columns(zown)
    layers = fx + 6
    fine_next, averaged = run(
        functools.partial(fine_kernel, s),
        "fine",
        [fine_fields, fine_wind, flo, fhi, slab],
        [((q, fx, y, z), pltpu.HBM), (q, x // 2, y // 2, z)],
        [
            pltpu.VMEM((q, layers, PAD, z), F32),
            pltpu.VMEM((q, layers, PAD, z), F32),
            pltpu.VMEM((6 * q, s.ep, z), F32),
            pltpu.VMEM((2 * q * s.fe, z), F32),
            pltpu.VMEM((2 * q * y, z), F32),
            pltpu.VMEM((2 * q * y, z), F32),
            pltpu.VMEM(flo.shape, F32),
            pltpu.VMEM(fhi.shape, F32),
            pltpu.VMEM((q, s.x, y, z), F32),
            pltpu.SemaphoreType.DMA((6,)),
        ],
        9,
        [pltpu.VMEM, pltpu.VMEM, pltpu.HBM, pltpu.HBM, pltpu.VMEM],
    )

    def coarse(*ins):
        cost = pl.CostEstimate(flops=40_000_000, bytes_accessed=4_000_000, transcendentals=0)
        columns = [pltpu.VMEM((n, q, 24, z), F32) for n in (3, 2)] + [pltpu.VMEM((q, 24, z), F32)]
        spaces = [pltpu.SMEM] + [pltpu.VMEM] * (len(ins) - 1)
        kernel = functools.partial(coarse_kernel, s)
        return run(kernel, "coarse", ins, [(q, x, y, z)], padded * 3 + wind_rows + columns, 9, spaces, cost)[0]

    averaged, state = move_by(averaged, offset, (coarse, (neighbours, *coarse_level, *yrows, zown, zin)))
    (coarse_next,) = run(
        functools.partial(merge_kernel, s),
        "merge",
        [state, averaged],
        [((q, x, y, z), pltpu.HBM)],
        [pltpu.VMEM((q, x, y, z), F32), pltpu.SemaphoreType.DMA((q,))],
        2,
    )
    return coarse_next, fine_next


def solution(mesh):
    spec = P(None, "gx", "gy", "gz")
    return jax.shard_map(
        shards,
        mesh=mesh,
        in_specs=(spec, spec, spec, spec, P("gx", "gy", "gz")),
        out_specs=(spec, spec),
        check_vma=False,
    )
```

```python
import functools

import jax
import jax.numpy as jnp
from jax import lax
from jax.experimental import pallas as pl
from jax.experimental.pallas import tpu as pltpu
from jax.sharding import PartitionSpec as P

diffusion = 0.05
section_weights = (1.0 / 3.0, 0.5, 1.0)
F32 = jnp.float32
BF16 = jnp.bfloat16
PAD = 32
TOP = 8


class Sizes:
    def __init__(self, coarse_shape, fine_shape):
        self.q, self.x, self.y, self.z = coarse_shape
        self.fx = fine_shape[1]
        self.ly, self.sy = self.y // 4, self.y // 2
        self.lz, self.sz = self.z // 4, self.z // 2
        self.ex = self.x + 4
        self.ep = -(-self.ex // 8) * 8
        self.fe = self.fx + 4
        self.halo = 3 * self.q + 6
        self.rows_f, self.rows_w = self.q * (3 * self.x + 6), 3 * (2 * self.x + 2)
        self.rows_y = 3 * self.q * self.ex
        self.rows_e = self.rows_y + self.ep
        self.rows_z = self.sy + 2
        self.slab = self.rows_e + self.q * self.rows_z
        assert self.q == 4 and self.y == 16 and self.z == 128 and self.ex <= 20 and self.fx == 2 * self.x


def lanes_of(shape):
    return lax.broadcasted_iota(jnp.int32, shape, len(shape) - 1)


def halves(value):
    high = value.astype(BF16)
    return high, (value - high.astype(F32)).astype(BF16)


def times(value, matrix):
    high, low = halves(value)
    return jnp.dot(high, matrix, preferred_element_type=F32) + jnp.dot(low, matrix, preferred_element_type=F32)


def coefficients(fraction, wind):
    out = []
    for w in wind:
        turned_by = w * (-0.5 * fraction)
        out += [diffusion * fraction + turned_by, diffusion * fraction - turned_by]
    return out


def advanced(base, fraction, co, center, x_low, x_high, y_low, y_high, z_low, z_high):
    along = (co[0] * x_high + co[1] * x_low) + (co[2] * y_high + co[3] * y_low) + (co[4] * z_high + co[5] * z_low)
    if base is None:
        return center * (1.0 - 6.0 * diffusion * fraction) + along
    return (base - center * (6.0 * diffusion * fraction)) + along


def layer_of(s, own, low, high, member, at, width, first):
    size = own.shape[1]
    if at < 0:
        return low[first + width * member + at + width]
    if at >= size:
        return high[first + width * member + at - size]
    return own[member, at]


def unrolled(begin, end, at_once, body, carry=None):
    while (end - begin) % at_once:
        at_once -= 1

    def several(i, carry):
        for more in range(at_once):
            carry = body(begin + i * at_once + more, carry)
        return carry

    return lax.fori_loop(0, (end - begin) // at_once, several, carry)


def pack_kernel(s, fields, wind, up, down, sems):
    size = fields.shape[1]
    moves = []
    for own, members, width, first in ((fields, s.q, 3, 0), (wind, 3, 2, 3 * s.q)):
        for dst, at in ((up, size - width), (down, 0)):
            place = dst.at[first : first + members * width].reshape(members, width, s.y, s.z)
            moves.append((own.at[:, at : at + width], place))
    moves = [pltpu.make_async_copy(src, dst, sems.at[i]) for i, (src, dst) in enumerate(moves)]
    for move in moves:
        move.start()
    for move in moves:
        move.wait()


def y_rows(s, members, width):
    below, above = [], []
    for out, extra in ((below, lambda r: r), (above, lambda r: width - 1 - r)):
        at = 0
        for m in range(members):
            for r in range(width):
                out.append((m, r, extra(r), at))
                at += s.x + 2 * extra(r)
    return below, above


def ypack_kernel(s, c0, cw, lo, hi, up, dn):
    x, y, z = s.x, s.y, s.z
    flat_lo = lo.reshape(s.halo * y, z)
    flat_hi = hi.reshape(s.halo * y, z)
    for own, members, width, first, place in ((c0, s.q, 3, 0, 0), (cw, 3, 2, 3 * s.q, s.rows_f)):
        flat = own.reshape(members * x * y, z)
        for dst, rows, start in zip((up, dn), y_rows(s, members, width), (y - width, 0)):
            for m, r, e, at in rows:
                row, at = start + r, at + place
                if e:
                    dst[at : at + e, :] = flat_lo[pl.ds((first + width * (m + 1) - e) * y + row, e, stride=y), :]
                    dst[at + e + x : at + x + 2 * e, :] = flat_hi[pl.ds((first + width * m) * y + row, e, stride=y), :]
                dst[at + e : at + e + x, :] = flat[pl.ds(m * x * y + row, x, stride=y), :]


EDGE = 4


def turned(base, fraction, wind, center, x_low, x_high):
    y, z = center.shape
    return advanced(
        base,
        fraction,
        wind,
        center,
        x_low,
        x_high,
        pltpu.roll(center, 1, 0),
        pltpu.roll(center, y - 1, 0),
        pltpu.roll(center, 1, 1),
        pltpu.roll(center, z - 1, 1),
    )


def slab_parts(s, rows_of, tile_of, layers_of, put):
    q, y, z = s.q, s.y, s.z
    lane_y = lanes_of((y, z))
    columns = (lane_y == s.lz - 1) | (lane_y == s.lz) | (lane_y == s.lz + s.sz - 1) | (lane_y == s.lz + s.sz)
    low_at = (lane_y % 2 == 0) & (lane_y < z // 2)
    high_at = (lane_y % 2 == 0) & (lane_y >= z // 2)
    ends = None
    for f in range(q):
        zfaces = None
        for k in range(3):
            rows = [rows_of(k, f, row) for row in (s.ly - 1, s.ly, s.ly + s.sy - 1, s.ly + s.sy)]
            sides = (0.75 * rows[0] + 0.25 * rows[1], 0.25 * rows[2] + 0.75 * rows[3])
            lane_x = lanes_of(sides[0].shape)
            put(
                "y",
                (k * q + f) * s.ex,
                jnp.where(lane_x < s.sz, pltpu.roll(sides[0], z - s.lz, 1), pltpu.roll(sides[1], s.lz, 1)),
            )
            for side in range(2):
                e = 4 * (q * k + f) + 2 * side + 1
                before = jnp.where(lane_x == s.lz - 1, sides[side], 0.0)
                after = jnp.where(lane_x == s.lz + s.sz, sides[side], 0.0)
                part = pltpu.roll(before, (e - s.lz + 1) % z, 1) + pltpu.roll(after, (e - 1 - s.lz - s.sz) % z, 1)
                ends = part if ends is None else ends + part
            raw = None
            for a in layers_of(k):
                part = jnp.where(columns, tile_of(k, f, a), 0.0)
                part = pltpu.roll(part, (2 * a - s.lz + 1) % z, 1)
                raw = part if raw is None else raw + part
            beside = pltpu.roll(raw, z - 1, 1)
            low = jnp.where(low_at, 0.75 * raw + 0.25 * beside, 0.0)
            high = jnp.where(high_at, 0.25 * raw + 0.75 * beside, 0.0)
            part = pltpu.roll(low, (2 * s.ex * k - 1) % z, 1) + pltpu.roll(high, (2 * s.ex * k - z // 2) % z, 1)
            zfaces = part if zfaces is None else zfaces + part
        put("z", s.rows_e + f * s.rows_z, zfaces[s.ly - 1 : s.ly + s.sy + 1])
    put("e", s.rows_y, ends)


def inner_kernel(s, c0, cw, part, near, state1, state2):
    q, x, y, z = s.q, s.x, s.y, s.z
    states = (c0, state1, state2)
    for step in range(2):
        src, dst = states[step], states[step + 1]

        def layer(j, carry, step=step, src=src, dst=dst):
            w = coefficients(section_weights[step], [cw[d, j] for d in range(3)])
            made = []
            for f in range(q):
                base = None if step == 0 else c0[f, j]
                made.append(turned(base, section_weights[step], w, src[f, j], src[f, j - 1], src[f, j + 1]))
            for f in range(q):
                dst[f, j] = made[f]
            return carry

        unrolled(step + 1, x - 1 - step, 7 if step == 0 else 6, layer)
    for f in range(q):
        near[f, 0] = state1[f, EDGE - 2]
        near[f, 1] = state1[f, x + 1 - EDGE]
    count = s.ex - 2 * EDGE
    part[...] = jnp.zeros_like(part)

    def rows_of(k, f, row):
        flat = states[k].reshape(q * x * y, z)
        return flat[pl.ds((f * x + EDGE - 2) * y + row, count, stride=y), :]

    def put(kind, at, rows):
        if kind == "z":
            part[at : at + s.rows_z, :] = rows
        else:
            part[at + EDGE : at + EDGE + count, :] = rows

    slab_parts(s, rows_of, lambda k, f, a: states[k][f, a - 2], lambda k: range(EDGE, s.ex - EDGE), put)


def slab_kernel(s, c0, cw, lo, hi, part, near, slab, ends0, ends1, ends2):
    q, x, y, z = s.q, s.x, s.y, s.z
    states = (ends0, ends1, ends2)
    places = list(range(-2, EDGE - 2)) + list(range(x + 2 - EDGE, x + 2))
    slab[...] = part[...]
    for j, at in enumerate(places):
        for f in range(q):
            ends0[f, j] = layer_of(s, c0, lo, hi, f, at, 3, 0)
    for step in range(2):
        for j, at in enumerate(places):
            if step == 1 and at in (-2, x + 1):
                for f in range(q):
                    ends2[f, j] = jnp.zeros((y, z), F32)
                continue
            w = coefficients(section_weights[step], [layer_of(s, cw, lo, hi, d, at, 2, 3 * q) for d in range(3)])
            for f in range(q):

                def beside(at, f=f):
                    if step == 0:
                        return layer_of(s, c0, lo, hi, f, at, 3, 0)
                    if at in places:
                        return ends1[f, places.index(at)]
                    return near[f, 0 if at < x // 2 else 1]

                base = None if step == 0 else ends0[f, j]
                states[step + 1][f, j] = turned(
                    base, section_weights[step], w, beside(at), beside(at - 1), beside(at + 1)
                )

    def rows_of(k, f, row):
        flat = states[k].reshape(q * 2 * EDGE * y, z)
        return flat[pl.ds(f * 2 * EDGE * y + row, 2 * EDGE, stride=y), :]

    def put(kind, at, rows):
        if kind == "z":
            slab[at : at + s.rows_z, :] = part[at : at + s.rows_z, :] + rows
        else:
            slab[at : at + EDGE, :] = rows[:EDGE]
            slab[at + s.ex - EDGE : at + s.ex, :] = rows[EDGE:]

    def layers_of(k):
        some = range(0 if k == 0 else 1, EDGE)
        return list(some) + [s.ex - 1 - a for a in some]

    def tile_of(k, f, a):
        return states[k][f, a if a < EDGE else a - s.ex + 2 * EDGE]

    slab_parts(s, rows_of, tile_of, layers_of, put)


WTOP, WPAD = 12, 40
BLOCK = slice(8, 32)


def assemble(s, c0, cw, lo, hi, below, above, pad, wind):
    q, x, y, z = s.q, s.x, s.y, s.z
    flat = pad.reshape(q * s.ep * WPAD, z)
    flat_wind = wind.reshape(3 * s.ex * 24, z)
    for f in range(q):
        for at in range(-3, x + 3):
            pad[f, at + 3, WTOP : WTOP + y, :] = layer_of(s, c0, lo, hi, f, at, 3, 0)
    for d in range(3):
        for at in range(-2, x + 2):
            wind[d, at + 2, 4 : 4 + y, :] = layer_of(s, cw, lo, hi, d, at, 2, 3 * q)
    for src, rows, start in zip((below, above), y_rows(s, q, 3), (WTOP - 3, WTOP + y)):
        for m, r, e, at in rows:
            count = x + 2 * e
            flat[pl.ds((m * s.ep + 3 - e) * WPAD + start + r, count, stride=WPAD), :] = src[at : at + count, :]
    for src, rows, start in zip((below, above), y_rows(s, 3, 2), (2, 4 + y)):
        for m, r, e, at in rows:
            count, at = x + 2 * e, at + s.rows_f
            flat_wind[pl.ds((m * s.ex + 2 - e) * 24 + start + r, count, stride=24), :] = src[at : at + count, :]


def edge_lanes(s, lane, width):
    return (lane < width) | (lane >= s.z - width)


def zpack_kernel(s, c0, cw, lo, hi, below, above, out, rows):
    q, x, y, z = s.q, s.x, s.y, s.z
    flat = rows.reshape((q + 3) * s.ex * 8, z)
    rows[...] = jnp.zeros_like(rows)
    for src, place in ((below, 0), (above, 3)):
        for member, width, first in ((0, 3, 0), (q, 2, s.rows_f)):
            skip = 3 - width if place == 0 else 0
            for m, r, e, at in y_rows(s, q if width == 3 else 3, width)[place // 3]:
                e = min(e, 2)
                count = x + 2 * e
                start = ((member + m) * s.ex + 2 - e) * 8 + place + skip + r
                flat[pl.ds(start, count, stride=8), :] = src[first + at : first + at + count, :]
    lane = lanes_of((y, z))
    keep = edge_lanes(s, lane, 3)
    for m in range(q + 3):
        inside, outside = None, None
        for a in range(s.ex):
            if m < q:
                tile = layer_of(s, c0, lo, hi, m, a - 2, 3, 0)
            else:
                tile = layer_of(s, cw, lo, hi, m - q, a - 2, 2, 3 * q)
            shift = (6 * a + 3) % z
            part = pltpu.roll(jnp.where(keep, tile, 0.0), shift, 1)
            inside = part if inside is None else inside + part
            part = pltpu.roll(jnp.where(keep[:8], rows[m, a], 0.0), shift, 1)
            outside = part if outside is None else outside + part
        out[m, 0:1, :] = jnp.zeros((1, z), F32)
        out[m, 1:4, :] = outside[0:3]
        out[m, 4 : 4 + y, :] = inside
        out[m, 4 + y : 7 + y, :] = outside[3:6]
        out[m, 7 + y : 8 + y, :] = jnp.zeros((1, z), F32)


def coarse_kernel(
    s, sides, c0, cw, lo, hi, below, above, zown, zin, out, pad0, pad1, pad2, wind, beyond, nearest, turning
):
    q, x, y, z = s.q, s.x, s.y, s.z
    assemble(s, c0, cw, lo, hi, below, above, pad0, wind)
    pads = (pad0, pad1, pad2)
    lane = lanes_of((24, z))
    group = lane % 6
    from_low = group == 2
    from_high = group == 3
    exists = jnp.where(group < 3, sides[0, 0], sides[0, 1]).astype(F32)
    wind_z = [zin[q + d] for d in range(3)]
    for f in range(q):
        beyond[0, f] = zin[f] * exists
        nearest[0, f] = zown[f]
    for step in range(3):
        src, fraction = pads[step], section_weights[step]
        flat = src.reshape(q * s.ep * WPAD, z)
        flat_wind = wind.reshape(3 * s.ex * 24, z)
        flat_beyond = beyond.reshape(3 * q * 24, z)
        skip, height = (0, 24) if step < 2 else (4, y)
        here = lanes_of((8, z))
        is_first, is_last = here == 0, here == z - 1

        def layer(a, carry, step=step, flat=flat, fraction=fraction, skip=skip, height=height):
            for r in range(0, height, 8):
                if step < 2:
                    winds = [wind[d, a, r : r + 8, :] for d in range(3)]
                else:
                    winds = [flat_wind[pl.ds((d * s.ex + a) * 24 + skip + r, 8), :] for d in range(3)]
                co = coefficients(fraction, winds)
                for f in range(q):

                    def at_layer(of, layer, by=0, f=f, r=r):
                        if step < 2 and not by:
                            return of[f, layer, 8 + r : 16 + r, :]
                        row = (f * s.ep + layer) * WPAD + 8 + skip + r + by
                        return of.reshape(flat.shape)[pl.ds(row, 8), :]

                    src = pads[step]
                    center = at_layer(src, a + 1)
                    ghost = turning[f, r : r + 8, :]
                    turning[f, r : r + 8, :] = pltpu.roll(ghost, z - 6, 1)
                    value = advanced(
                        None if step == 0 else at_layer(pad0, a + 1),
                        fraction,
                        co,
                        center,
                        at_layer(src, a),
                        at_layer(src, a + 2),
                        at_layer(src, a + 1, -1),
                        at_layer(src, a + 1, 1),
                        pltpu.roll(jnp.where(is_last, ghost, center), 1, 1),
                        pltpu.roll(jnp.where(is_first, ghost, center), z - 1, 1),
                    )
                    if step == 2:
                        out[f, a - 2, r : r + 8, :] = value
                    else:
                        pads[step + 1][f, a + 1, 8 + r : 16 + r, :] = value
                    if step == 0:
                        total = nearest[1, f, r : r + 8, :] + jnp.where(is_first | is_last, value, 0.0)
                        nearest[1, f, r : r + 8, :] = pltpu.roll(total, z - 6, 1)
            return carry

        for f in range(q):
            start = (step * q + f) * 24 + skip
            turning[f, :height, :] = pltpu.roll(flat_beyond[start : start + height, :], z - 6 * step - 3, 1)
            if step == 0:
                nearest[1, f] = jnp.zeros((24, z), F32)
        unrolled(step, s.ex - step, 4 + 2 * (step == 1), layer)
        if step == 2:
            break
        for f in range(q):
            if step == 0:
                nearest[1, f] = pltpu.roll(nearest[1, f], (6 * s.ex + 3) % z, 1)
            ghost, near = beyond[step, f], nearest[step, f]
            value = advanced(
                None if step == 0 else beyond[0, f],
                fraction,
                coefficients(fraction, wind_z),
                ghost,
                pltpu.roll(ghost, 6, 1),
                pltpu.roll(ghost, z - 6, 1),
                pltpu.roll(ghost, 1, 0),
                pltpu.roll(ghost, 23, 0),
                pltpu.roll(jnp.where(from_low, near, ghost), 1, 1),
                pltpu.roll(jnp.where(from_high, near, ghost), z - 1, 1),
            )
            beyond[step + 1, f] = value * exists


def fine_kernel(s, f0, fw, flo_there, fhi_there, slab, out, avg, *scratch):
    s1, s2, faces, ghost_rows, zface, turning, flo, fhi, summed, sems = scratch
    arrivals = [
        pltpu.make_async_copy(flo_there, flo, sems.at[4]),
        pltpu.make_async_copy(fhi_there, fhi, sems.at[5]),
    ]
    for move in arrivals:
        move.start()
    states = (None, s1, s2, s1)
    q, y, z, fx, fe = s.q, s.y, s.z, s.fx, s.fe
    layers = fx + 6
    rows = slice(TOP, TOP + y)
    shift_z, shift_sz = z.bit_length() - 1, s.sz.bit_length() - 1
    r = lax.broadcasted_iota(jnp.int32, (2 * z, 2 * z), 0)
    c = lax.broadcasted_iota(jnp.int32, (2 * z, 2 * z), 1)
    near = c >> 1
    far = near + 2 * (c & 1) - 1
    same = (far >> shift_sz) == (near >> shift_sz)
    to_fine = jnp.where(r == near, 0.75, jnp.where((r == far) & same, 0.25, 0.0))
    ends_at = ((r & 2) << (shift_z - 1)) + jnp.where((r & 1) == 1, 0, z - 1)
    to_fine = jnp.where(r < z, to_fine, jnp.where(c == ends_at, 0.25, 0.0)).astype(BF16)
    ends = slab[s.rows_y : s.rows_y + s.ex, :]
    lane_x = lanes_of((s.ex, z))
    own_ends = [jnp.where((lane_x >> 2) == i, ends, 0.0) for i in range(3 * q)]
    wide = times(jnp.concatenate([slab[: s.rows_y, :], jnp.concatenate(own_ends, axis=0)], axis=1), to_fine)
    half = fe // 2
    for k in range(3):
        for f in range(q):
            for side in range(2):
                first = (k * q + f) * s.ex
                here = faces.at[(k * q + f) * 2 + side]
                here[: s.ex, :] = wide[first : first + s.ex, side * z : side * z + z]
                a = here[0:half, :]
                b = here[1 : half + 1, :]
                d = here[2 : half + 2, :]
                if k == 0:
                    flat, base, stride = ghost_rows, (2 * f + side) * fe, 1
                else:
                    flat, stride = states[k].reshape(q * layers * PAD, z), PAD
                    base = (f * layers + 1) * PAD + (TOP - 1 if side == 0 else TOP + y)
                flat[pl.ds(base, half, stride=2 * stride), :] = 0.25 * a + 0.75 * b
                flat[pl.ds(base + stride, half, stride=2 * stride), :] = 0.75 * b + 0.25 * d
    for f in range(q):
        at = s.rows_e + f * s.rows_z
        a = slab[at : at + s.sy, :]
        b = slab[at + 1 : at + 1 + s.sy, :]
        d = slab[at + 2 : at + 2 + s.sy, :]
        zface[pl.ds(f * y, s.sy, stride=2), :] = 0.25 * a + 0.75 * b
        zface[pl.ds(f * y + 1, s.sy, stride=2), :] = 0.75 * b + 0.25 * d
        a = zface[f * y : f * y + y, :]
        b = pltpu.roll(a, z - 2, 1)
        d = pltpu.roll(a, z - 4, 1)
        zface[f * y : f * y + y, :] = 0.25 * a + 0.75 * b
        zface[(q + f) * y : (q + f + 1) * y, :] = 0.75 * b + 0.25 * d
    lane = lanes_of((8, z))
    is_first, is_last = lane == 0, lane == z - 1
    row_in = lax.broadcasted_iota(jnp.int32, (8, z), 0)
    is_low, is_high = row_in == 0, row_in == 7
    flat_f0 = f0.reshape(q * fx * y, z)

    def turn_to(k, t):
        shift = -(2 * s.ex * k + 2 * t) % z
        for i in range(2 * q):
            packed = zface[i * y : (i + 1) * y, :]
            turning[i * y : (i + 1) * y, :] = pltpu.roll(packed, shift, 1) if shift else packed

    def pair_of_layers(k, t, inner):
        src, fraction = states[k], section_weights[k]

        def field(f, at):
            return layer_of(s, f0, flo, fhi, f, at, 3, 0)

        for odd, r in ((odd, r) for odd in range(2) for r in range(0, y, 8)):
            b = 2 * t + odd
            at = b - 2
            half_tile = slice(r, r + 8)
            if inner:
                winds = [fw[d, at, half_tile, :] for d in range(3)]
            else:
                winds = [layer_of(s, fw, flo, fhi, d, at, 2, 3 * q)[half_tile] for d in range(3)]
            co = coefficients(fraction, winds)
            for f in range(q):
                if k == 0:
                    if inner:
                        center, x_low, x_high = (f0[f, at + by, half_tile, :] for by in (0, -1, 1))
                        row = (f * fx + at) * y + r
                        y_low, y_high = flat_f0[pl.ds(row - 1, 8), :], flat_f0[pl.ds(row + 1, 8), :]
                    else:
                        whole = field(f, at)
                        y_low, y_high = pltpu.roll(whole, 1, 0)[half_tile], pltpu.roll(whole, y - 1, 0)[half_tile]
                        center, x_low, x_high = (field(f, at + by)[half_tile] for by in (0, -1, 1))
                    if r == 0:
                        y_low = jnp.where(is_low, ghost_rows[pl.ds(2 * f * fe + b, 1), :], y_low)
                    if r == y - 8:
                        y_high = jnp.where(is_high, ghost_rows[pl.ds((2 * f + 1) * fe + b, 1), :], y_high)
                    base = None
                else:
                    flat = src.reshape(q * layers * PAD, z)
                    row = (f * layers + b + 1) * PAD + TOP + r
                    center, x_low, x_high = (src[f, b + by, TOP + r : TOP + r + 8, :] for by in (1, 0, 2))
                    y_low, y_high = flat[pl.ds(row - 1, 8), :], flat[pl.ds(row + 1, 8), :]
                    base = f0[f, at, half_tile, :] if inner else field(f, at)[half_tile]
                i = (odd * q + f) * y + r
                ghost = turning[i : i + 8, :]
                turning[i : i + 8, :] = pltpu.roll(ghost, z - 2, 1)
                states[k + 1][f, b + 1, TOP + r : TOP + r + 8, :] = advanced(
                    base,
                    fraction,
                    co,
                    center,
                    x_low,
                    x_high,
                    y_low,
                    y_high,
                    pltpu.roll(jnp.where(is_last, ghost, center), 1, 1),
                    pltpu.roll(jnp.where(is_first, ghost, center), z - 1, 1),
                )

    for move in arrivals:
        move.wait()
    moves = []
    for k in range(3):
        if k < 2:
            outer = 2 - k
            for t in range(outer):
                turn_to(k, t)
                pair_of_layers(k, t, False)
            unrolled(outer, half - outer, 2, lambda t, g, k=k: pair_of_layers(k, t, True))
            for t in range(half - outer, half):
                pair_of_layers(k, t, False)
            continue
        turn_to(k, 1)
        quarter = (half - 2) // 4
        for i in range(4):
            unrolled(1 + i * quarter, 1 + (i + 1) * quarter, 2, lambda t, g, k=k: pair_of_layers(k, t, True))
            begin, end = 2 * quarter * i, 2 * quarter * (i + 1)
            moves.append(pltpu.make_async_copy(s1.at[:, 3 + begin : 3 + end, rows], out.at[:, begin:end], sems.at[i]))
            moves[-1].start()
    rz = lax.broadcasted_iota(jnp.int32, (z, z), 0)
    cz = lax.broadcasted_iota(jnp.int32, (z, z), 1)
    flat = summed.reshape(q * s.x * y, z)
    pairs_z = [jnp.where(cz == (rz >> 1) + odd * s.sz, 0.125, 0.0).astype(BF16) for odd in range(2)]
    for f in range(q):
        for p in range(s.x):
            both = s1[f, 3 + 2 * p, rows, :] + s1[f, 4 + 2 * p, rows, :]
            summed[f, p] = both + pltpu.roll(both, y - 1, 0)
    for f in range(q):
        sums = []
        for odd in range(2):
            parts = [flat[pl.ds((f * s.x + 2 * p + odd) * y, y // 2, stride=2), :] for p in range(s.x // 2)]
            sums.append(times(jnp.concatenate(parts, axis=0), pairs_z[odd]))
        avg[f] = (sums[0] + sums[1]).reshape(s.x // 2, y // 2, z)
    for move in moves:
        move.wait()


def merge_kernel(s, c3, avg, out, made, sems):
    lane = lanes_of((s.sy, s.z))
    inside = (lane >= s.lz) & (lane < s.lz + s.sz)
    moves = []
    for f in range(s.q):
        for p in range(s.x // 2):
            both = avg[f, p]
            for odd in range(2):
                at = 2 * p + odd
                moved = pltpu.roll(both, s.lz if odd == 0 else s.z - s.lz, 1)
                made[f, at] = c3[f, at]
                made[f, at, s.ly : s.ly + s.sy, :] = jnp.where(inside, moved, c3[f, at, s.ly : s.ly + s.sy, :])
        moves.append(pltpu.make_async_copy(made.at[f], out.at[f], sems.at[f]))
        moves[-1].start()
    for move in moves:
        move.wait()


SHORT = pl.CostEstimate(flops=1, bytes_accessed=1, transcendentals=0)


def run(kernel, name, ins, outs, scratch, megabytes, spaces=None, cost=SHORT):
    spaces = spaces or [pltpu.VMEM] * len(ins)
    outs = [out if isinstance(out[0], tuple) else (out, pltpu.VMEM) for out in outs]
    ins = [i if space is pltpu.SMEM else pltpu.with_memory_space_constraint(i, space) for i, space in zip(ins, spaces)]
    return pl.pallas_call(
        kernel,
        out_shape=tuple(space(dims, F32) for dims, space in outs),
        in_specs=[pl.BlockSpec(memory_space=space) for space in spaces],
        out_specs=tuple(pl.BlockSpec(memory_space=space) for _, space in outs),
        scratch_shapes=scratch,
        compiler_params=pltpu.CompilerParams(vmem_limit_bytes=megabytes << 20),
        cost_estimate=cost,
        name=name,
    )(*ins)


def ring(array, axis, by):
    size = lax.axis_size(axis)
    return lax.ppermute(array, axis, [(i, (i + by) % size) for i in range(size)])


def move_by(array, amount, beside=None):
    size = lax.axis_size("gx")
    work, operands = beside or (lambda: (), ())
    if size <= 8:

        def branch(by, array, *operands):
            return array if by == 0 else ring(array, "gx", by), work(*operands)

        return lax.switch(amount, [functools.partial(branch, by) for by in range(size)], array, *operands)
    for bit in range((size - 1).bit_length()):
        array = jnp.where((amount >> bit) % 2 == 1, ring(array, "gx", 1 << bit), array)
    return array, work(*operands)


def z_columns(zown):
    size = lax.axis_size("gz")
    if size == 1:
        return zown
    if size == 2:
        return lax.ppermute(zown, "gz", [(0, 1), (1, 0)])
    below = lax.broadcasted_iota(jnp.int32, zown.shape, 2) % 6 < 3
    return jnp.where(below, ring(zown, "gz", 1), ring(zown, "gz", -1))


def pack(s, fields, wind, spare, name):
    return run(
        functools.partial(pack_kernel, s),
        name,
        [fields, wind],
        [(s.halo + spare, s.y, s.z)] * 2,
        [pltpu.SemaphoreType.DMA((4,))],
        1,
        [pltpu.HBM] * 2,
    )


def shards(coarse_fields, coarse_wind, fine_fields, fine_wind, fine_owner):
    s = Sizes(coarse_fields.shape, fine_fields.shape)
    q, x, y, z, fx = s.q, s.x, s.y, s.z, s.fx
    size = lax.axis_size("gx")
    offset = (fine_owner[0, 0, 0] - lax.axis_index("gx")) % size
    level = lax.axis_index("gz")
    neighbours = jnp.stack([level > 0, level < lax.axis_size("gz") - 1]).astype(jnp.int32).reshape(1, 2)
    cup, cdown = pack(s, coarse_fields, coarse_wind, 0, "pack_coarse")
    lo, hi = ring(cup, "gx", 1), ring(cdown, "gx", -1)
    part, near = run(
        functools.partial(inner_kernel, s),
        "inner",
        [coarse_fields, coarse_wind],
        [(s.slab, z), (q, 2, y, z)],
        [pltpu.VMEM((q, x, y, z), F32)] * 2,
        3,
    )
    fup, fdown = pack(s, fine_fields, fine_wind, 2, "pack_fine")
    fup, fdown, offset = lax.optimization_barrier((fup, fdown, offset))
    flo, fhi = ring(fup, "gx", 1), ring(fdown, "gx", -1)
    padded = [pltpu.VMEM((q, s.ep, WPAD, z), F32)]
    wind_rows = [pltpu.VMEM((3, s.ex, 24, z), F32)]
    coarse_fields, part, near = lax.optimization_barrier((coarse_fields, part, near))
    coarse_level = [coarse_fields, coarse_wind, lo, hi]
    yup, ydn = run(functools.partial(ypack_kernel, s), "ypack", coarse_level, [(s.rows_f + s.rows_w, z)] * 2, [], 1)
    yrows = [ring(yup, "gy", 1), ring(ydn, "gy", -1)]
    ends = [pltpu.VMEM((q, 2 * EDGE, y, z), F32)] * 3
    (slab,) = run(functools.partial(slab_kernel, s), "slab", coarse_level + [part, near], [(s.slab, z)], ends, 3)
    slab, _ = move_by(slab, (size - offset) % size)
    yrows, slab, flo, fhi = lax.optimization_barrier((yrows, slab, flo, fhi))
    kernel = functools.partial(zpack_kernel, s)
    beyond_rows = [pltpu.VMEM((q + 3, s.ex, 8, z), F32)]
    (zown,) = run(kernel, "zpack", coarse_level + yrows, [(q + 3, 24, z)], beyond_rows, 2)
    zin = z_columns(zown)
    layers = fx + 6
    fine_next, averaged = run(
        functools.partial(fine_kernel, s),
        "fine",
        [fine_fields, fine_wind, flo, fhi, slab],
        [((q, fx, y, z), pltpu.HBM), (q, x // 2, y // 2, z)],
        [
            pltpu.VMEM((q, layers, PAD, z), F32),
            pltpu.VMEM((q, layers, PAD, z), F32),
            pltpu.VMEM((6 * q, s.ep, z), F32),
            pltpu.VMEM((2 * q * s.fe, z), F32),
            pltpu.VMEM((2 * q * y, z), F32),
            pltpu.VMEM((2 * q * y, z), F32),
            pltpu.VMEM(flo.shape, F32),
            pltpu.VMEM(fhi.shape, F32),
            pltpu.VMEM((q, s.x, y, z), F32),
            pltpu.SemaphoreType.DMA((6,)),
        ],
        9,
        [pltpu.VMEM, pltpu.VMEM, pltpu.HBM, pltpu.HBM, pltpu.VMEM],
    )

    def coarse(*ins):
        cost = pl.CostEstimate(flops=40_000_000, bytes_accessed=4_000_000, transcendentals=0)
        columns = [pltpu.VMEM((n, q, 24, z), F32) for n in (3, 2)] + [pltpu.VMEM((q, 24, z), F32)]
        spaces = [pltpu.SMEM] + [pltpu.VMEM] * (len(ins) - 1)
        kernel = functools.partial(coarse_kernel, s)
        return run(kernel, "coarse", ins, [(q, x, y, z)], padded * 3 + wind_rows + columns, 9, spaces, cost)[0]

    averaged, state = move_by(averaged, offset, (coarse, (neighbours, *coarse_level, *yrows, zown, zin)))
    (coarse_next,) = run(
        functools.partial(merge_kernel, s),
        "merge",
        [state, averaged],
        [((q, x, y, z), pltpu.HBM)],
        [pltpu.VMEM((q, x, y, z), F32), pltpu.SemaphoreType.DMA((q,))],
        2,
    )
    return coarse_next, fine_next


def solution(mesh):
    spec = P(None, "gx", "gy", "gz")
    return jax.shard_map(
        shards,
        mesh=mesh,
        in_specs=(spec, spec, spec, spec, P("gx", "gy", "gz")),
        out_specs=(spec, spec),
        check_vma=False,
    )
```

```python
import functools

import jax
import jax.numpy as jnp
from jax import lax
from jax.experimental import pallas as pl
from jax.experimental.pallas import tpu as pltpu
from jax.sharding import PartitionSpec as P

diffusion = 0.05
section_weights = (1.0 / 3.0, 0.5, 1.0)
F32 = jnp.float32
BF16 = jnp.bfloat16
PAD = 32
TOP = 8


class Sizes:
    def __init__(self, coarse_shape, fine_shape):
        self.q, self.x, self.y, self.z = coarse_shape
        self.fx = fine_shape[1]
        self.ly, self.sy = self.y // 4, self.y // 2
        self.lz, self.sz = self.z // 4, self.z // 2
        self.ex = self.x + 4
        self.ep = -(-self.ex // 8) * 8
        self.fe = self.fx + 4
        self.halo = 3 * self.q + 6
        self.rows_f, self.rows_w = self.q * (3 * self.x + 6), 3 * (2 * self.x + 2)
        self.rows_y = 3 * self.q * self.ex
        self.rows_e = self.rows_y + self.ep
        self.rows_z = self.sy + 2
        self.slab = self.rows_e + self.q * self.rows_z
        assert self.q == 4 and self.y == 16 and self.z == 128 and self.ex <= 20 and self.fx == 2 * self.x


def lanes_of(shape):
    return lax.broadcasted_iota(jnp.int32, shape, len(shape) - 1)


def halves(value):
    high = value.astype(BF16)
    return high, (value - high.astype(F32)).astype(BF16)


def times(value, matrix):
    high, low = halves(value)
    return jnp.dot(high, matrix, preferred_element_type=F32) + jnp.dot(low, matrix, preferred_element_type=F32)


def coefficients(fraction, wind):
    out = []
    for w in wind:
        turned_by = w * (-0.5 * fraction)
        out += [diffusion * fraction + turned_by, diffusion * fraction - turned_by]
    return out


def advanced(base, fraction, co, center, x_low, x_high, y_low, y_high, z_low, z_high):
    along = (co[0] * x_high + co[1] * x_low) + (co[2] * y_high + co[3] * y_low) + (co[4] * z_high + co[5] * z_low)
    if base is None:
        return center * (1.0 - 6.0 * diffusion * fraction) + along
    return (base - center * (6.0 * diffusion * fraction)) + along


def layer_of(s, own, low, high, member, at, width, first):
    size = own.shape[1]
    if at < 0:
        return low[first + width * member + at + width]
    if at >= size:
        return high[first + width * member + at - size]
    return own[member, at]


def unrolled(begin, end, at_once, body, carry=None):
    while (end - begin) % at_once:
        at_once -= 1

    def several(i, carry):
        for more in range(at_once):
            carry = body(begin + i * at_once + more, carry)
        return carry

    return lax.fori_loop(0, (end - begin) // at_once, several, carry)


def pack_kernel(s, fields, wind, up, down, sems):
    size = fields.shape[1]
    moves = []
    for own, members, width, first in ((fields, s.q, 3, 0), (wind, 3, 2, 3 * s.q)):
        for dst, at in ((up, size - width), (down, 0)):
            place = dst.at[first : first + members * width].reshape(members, width, s.y, s.z)
            moves.append((own.at[:, at : at + width], place))
    moves = [pltpu.make_async_copy(src, dst, sems.at[i]) for i, (src, dst) in enumerate(moves)]
    for move in moves:
        move.start()
    for move in moves:
        move.wait()


def y_rows(s, members, width):
    below, above = [], []
    for out, extra in ((below, lambda r: r), (above, lambda r: width - 1 - r)):
        at = 0
        for m in range(members):
            for r in range(width):
                out.append((m, r, extra(r), at))
                at += s.x + 2 * extra(r)
    return below, above


def ypack_kernel(s, c0, cw, lo, hi, up, dn):
    x, y, z = s.x, s.y, s.z
    flat_lo = lo.reshape(s.halo * y, z)
    flat_hi = hi.reshape(s.halo * y, z)
    for own, members, width, first, place in ((c0, s.q, 3, 0, 0), (cw, 3, 2, 3 * s.q, s.rows_f)):
        flat = own.reshape(members * x * y, z)
        for dst, rows, start in zip((up, dn), y_rows(s, members, width), (y - width, 0)):
            for m, r, e, at in rows:
                row, at = start + r, at + place
                if e:
                    dst[at : at + e, :] = flat_lo[pl.ds((first + width * (m + 1) - e) * y + row, e, stride=y), :]
                    dst[at + e + x : at + x + 2 * e, :] = flat_hi[pl.ds((first + width * m) * y + row, e, stride=y), :]
                dst[at + e : at + e + x, :] = flat[pl.ds(m * x * y + row, x, stride=y), :]


EDGE = 4


def turned(base, fraction, wind, center, x_low, x_high):
    y, z = center.shape
    return advanced(
        base,
        fraction,
        wind,
        center,
        x_low,
        x_high,
        pltpu.roll(center, 1, 0),
        pltpu.roll(center, y - 1, 0),
        pltpu.roll(center, 1, 1),
        pltpu.roll(center, z - 1, 1),
    )


def slab_parts(s, rows_of, tile_of, layers_of, put):
    q, y, z = s.q, s.y, s.z
    lane_y = lanes_of((y, z))
    columns = (lane_y == s.lz - 1) | (lane_y == s.lz) | (lane_y == s.lz + s.sz - 1) | (lane_y == s.lz + s.sz)
    low_at = (lane_y % 2 == 0) & (lane_y < z // 2)
    high_at = (lane_y % 2 == 0) & (lane_y >= z // 2)
    ends = None
    for f in range(q):
        zfaces = None
        for k in range(3):
            rows = [rows_of(k, f, row) for row in (s.ly - 1, s.ly, s.ly + s.sy - 1, s.ly + s.sy)]
            sides = (0.75 * rows[0] + 0.25 * rows[1], 0.25 * rows[2] + 0.75 * rows[3])
            lane_x = lanes_of(sides[0].shape)
            put(
                "y",
                (k * q + f) * s.ex,
                jnp.where(lane_x < s.sz, pltpu.roll(sides[0], z - s.lz, 1), pltpu.roll(sides[1], s.lz, 1)),
            )
            for side in range(2):
                e = 4 * (q * k + f) + 2 * side + 1
                before = jnp.where(lane_x == s.lz - 1, sides[side], 0.0)
                after = jnp.where(lane_x == s.lz + s.sz, sides[side], 0.0)
                part = pltpu.roll(before, (e - s.lz + 1) % z, 1) + pltpu.roll(after, (e - 1 - s.lz - s.sz) % z, 1)
                ends = part if ends is None else ends + part
            raw = None
            for a in layers_of(k):
                part = jnp.where(columns, tile_of(k, f, a), 0.0)
                part = pltpu.roll(part, (2 * a - s.lz + 1) % z, 1)
                raw = part if raw is None else raw + part
            beside = pltpu.roll(raw, z - 1, 1)
            low = jnp.where(low_at, 0.75 * raw + 0.25 * beside, 0.0)
            high = jnp.where(high_at, 0.25 * raw + 0.75 * beside, 0.0)
            part = pltpu.roll(low, (2 * s.ex * k - 1) % z, 1) + pltpu.roll(high, (2 * s.ex * k - z // 2) % z, 1)
            zfaces = part if zfaces is None else zfaces + part
        put("z", s.rows_e + f * s.rows_z, zfaces[s.ly - 1 : s.ly + s.sy + 1])
    put("e", s.rows_y, ends)


def inner_kernel(s, c0, cw, part, near, state1, state2):
    q, x, y, z = s.q, s.x, s.y, s.z
    states = (c0, state1, state2)
    for step in range(2):
        src, dst = states[step], states[step + 1]

        def layer(j, carry, step=step, src=src, dst=dst):
            w = coefficients(section_weights[step], [cw[d, j] for d in range(3)])
            made = []
            for f in range(q):
                base = None if step == 0 else c0[f, j]
                made.append(turned(base, section_weights[step], w, src[f, j], src[f, j - 1], src[f, j + 1]))
            for f in range(q):
                dst[f, j] = made[f]
            return carry

        unrolled(step + 1, x - 1 - step, 7 if step == 0 else 6, layer)
    for f in range(q):
        near[f, 0] = state1[f, EDGE - 2]
        near[f, 1] = state1[f, x + 1 - EDGE]
    count = s.ex - 2 * EDGE
    part[...] = jnp.zeros_like(part)

    def rows_of(k, f, row):
        flat = states[k].reshape(q * x * y, z)
        return flat[pl.ds((f * x + EDGE - 2) * y + row, count, stride=y), :]

    def put(kind, at, rows):
        if kind == "z":
            part[at : at + s.rows_z, :] = rows
        else:
            part[at + EDGE : at + EDGE + count, :] = rows

    slab_parts(s, rows_of, lambda k, f, a: states[k][f, a - 2], lambda k: range(EDGE, s.ex - EDGE), put)


def slab_kernel(s, c0, cw, lo, hi, part, near, slab, ends0, ends1, ends2):
    q, x, y, z = s.q, s.x, s.y, s.z
    states = (ends0, ends1, ends2)
    places = list(range(-2, EDGE - 2)) + list(range(x + 2 - EDGE, x + 2))
    slab[...] = part[...]
    for j, at in enumerate(places):
        for f in range(q):
            ends0[f, j] = layer_of(s, c0, lo, hi, f, at, 3, 0)
    for step in range(2):
        for j, at in enumerate(places):
            if step == 1 and at in (-2, x + 1):
                for f in range(q):
                    ends2[f, j] = jnp.zeros((y, z), F32)
                continue
            w = coefficients(section_weights[step], [layer_of(s, cw, lo, hi, d, at, 2, 3 * q) for d in range(3)])
            for f in range(q):

                def beside(at, f=f):
                    if step == 0:
                        return layer_of(s, c0, lo, hi, f, at, 3, 0)
                    if at in places:
                        return ends1[f, places.index(at)]
                    return near[f, 0 if at < x // 2 else 1]

                base = None if step == 0 else ends0[f, j]
                states[step + 1][f, j] = turned(
                    base, section_weights[step], w, beside(at), beside(at - 1), beside(at + 1)
                )

    def rows_of(k, f, row):
        flat = states[k].reshape(q * 2 * EDGE * y, z)
        return flat[pl.ds(f * 2 * EDGE * y + row, 2 * EDGE, stride=y), :]

    def put(kind, at, rows):
        if kind == "z":
            slab[at : at + s.rows_z, :] = part[at : at + s.rows_z, :] + rows
        else:
            slab[at : at + EDGE, :] = rows[:EDGE]
            slab[at + s.ex - EDGE : at + s.ex, :] = rows[EDGE:]

    def layers_of(k):
        some = range(0 if k == 0 else 1, EDGE)
        return list(some) + [s.ex - 1 - a for a in some]

    def tile_of(k, f, a):
        return states[k][f, a if a < EDGE else a - s.ex + 2 * EDGE]

    slab_parts(s, rows_of, tile_of, layers_of, put)


WTOP, WPAD = 12, 40
BLOCK = slice(8, 32)


def assemble(s, c0, cw, lo, hi, below, above, pad, wind):
    q, x, y, z = s.q, s.x, s.y, s.z
    flat = pad.reshape(q * s.ep * WPAD, z)
    flat_wind = wind.reshape(3 * s.ex * 24, z)
    for f in range(q):
        for at in range(-3, x + 3):
            pad[f, at + 3, WTOP : WTOP + y, :] = layer_of(s, c0, lo, hi, f, at, 3, 0)
    for d in range(3):
        for at in range(-2, x + 2):
            wind[d, at + 2, 4 : 4 + y, :] = layer_of(s, cw, lo, hi, d, at, 2, 3 * q)
    for src, rows, start in zip((below, above), y_rows(s, q, 3), (WTOP - 3, WTOP + y)):
        for m, r, e, at in rows:
            count = x + 2 * e
            flat[pl.ds((m * s.ep + 3 - e) * WPAD + start + r, count, stride=WPAD), :] = src[at : at + count, :]
    for src, rows, start in zip((below, above), y_rows(s, 3, 2), (2, 4 + y)):
        for m, r, e, at in rows:
            count, at = x + 2 * e, at + s.rows_f
            flat_wind[pl.ds((m * s.ex + 2 - e) * 24 + start + r, count, stride=24), :] = src[at : at + count, :]


def edge_lanes(s, lane, width):
    return (lane < width) | (lane >= s.z - width)


def zpack_kernel(s, c0, cw, lo, hi, below, above, out, rows):
    q, x, y, z = s.q, s.x, s.y, s.z
    flat = rows.reshape((q + 3) * s.ex * 8, z)
    rows[...] = jnp.zeros_like(rows)
    for src, place in ((below, 0), (above, 3)):
        for member, width, first in ((0, 3, 0), (q, 2, s.rows_f)):
            skip = 3 - width if place == 0 else 0
            for m, r, e, at in y_rows(s, q if width == 3 else 3, width)[place // 3]:
                e = min(e, 2)
                count = x + 2 * e
                start = ((member + m) * s.ex + 2 - e) * 8 + place + skip + r
                flat[pl.ds(start, count, stride=8), :] = src[first + at : first + at + count, :]
    lane = lanes_of((y, z))
    keep = edge_lanes(s, lane, 3)
    for m in range(q + 3):
        inside, outside = None, None
        for a in range(s.ex):
            if m < q:
                tile = layer_of(s, c0, lo, hi, m, a - 2, 3, 0)
            else:
                tile = layer_of(s, cw, lo, hi, m - q, a - 2, 2, 3 * q)
            shift = (6 * a + 3) % z
            part = pltpu.roll(jnp.where(keep, tile, 0.0), shift, 1)
            inside = part if inside is None else inside + part
            part = pltpu.roll(jnp.where(keep[:8], rows[m, a], 0.0), shift, 1)
            outside = part if outside is None else outside + part
        out[m, 0:1, :] = jnp.zeros((1, z), F32)
        out[m, 1:4, :] = outside[0:3]
        out[m, 4 : 4 + y, :] = inside
        out[m, 4 + y : 7 + y, :] = outside[3:6]
        out[m, 7 + y : 8 + y, :] = jnp.zeros((1, z), F32)


def coarse_kernel(
    s, sides, c0, cw, lo, hi, below, above, zown, zin, out, pad0, pad1, pad2, wind, beyond, nearest, turning
):
    q, x, y, z = s.q, s.x, s.y, s.z
    assemble(s, c0, cw, lo, hi, below, above, pad0, wind)
    pads = (pad0, pad1, pad2)
    lane = lanes_of((24, z))
    group = lane % 6
    from_low = group == 2
    from_high = group == 3
    exists = jnp.where(group < 3, sides[0, 0], sides[0, 1]).astype(F32)
    wind_z = [zin[q + d] for d in range(3)]
    for f in range(q):
        beyond[0, f] = zin[f] * exists
        nearest[0, f] = zown[f]
    for step in range(3):
        src, fraction = pads[step], section_weights[step]
        flat = src.reshape(q * s.ep * WPAD, z)
        flat_wind = wind.reshape(3 * s.ex * 24, z)
        flat_beyond = beyond.reshape(3 * q * 24, z)
        skip, height = (0, 24) if step < 2 else (4, y)
        here = lanes_of((height, z))
        is_first, is_last = here == 0, here == z - 1

        def layer(a, carry, step=step, src=src, flat=flat, fraction=fraction, skip=skip, height=height):
            if step < 2:
                winds = [wind[d, a] for d in range(3)]
            else:
                winds = [flat_wind[pl.ds((d * s.ex + a) * 24 + skip, height), :] for d in range(3)]
            co = coefficients(fraction, winds)
            for f in range(q):

                def at_layer(of, layer, by=0, f=f):
                    if step < 2 and not by:
                        return of[f, layer, BLOCK, :]
                    row = (f * s.ep + layer) * WPAD + 8 + skip + by
                    return of.reshape(flat.shape)[pl.ds(row, height), :]

                center = at_layer(src, a + 1)
                ghost = turning[f, :height, :]
                turning[f, :height, :] = pltpu.roll(ghost, z - 6, 1)
                value = advanced(
                    None if step == 0 else at_layer(pad0, a + 1),
                    fraction,
                    co,
                    center,
                    at_layer(src, a),
                    at_layer(src, a + 2),
                    at_layer(src, a + 1, -1),
                    at_layer(src, a + 1, 1),
                    pltpu.roll(jnp.where(is_last, ghost, center), 1, 1),
                    pltpu.roll(jnp.where(is_first, ghost, center), z - 1, 1),
                )
                if step == 2:
                    out[f, a - 2] = value
                else:
                    pads[step + 1][f, a + 1, BLOCK, :] = value
                if step == 0:
                    nearest[1, f] = pltpu.roll(nearest[1, f] + jnp.where(is_first | is_last, value, 0.0), z - 6, 1)
            return carry

        for f in range(q):
            start = (step * q + f) * 24 + skip
            turning[f, :height, :] = pltpu.roll(flat_beyond[start : start + height, :], z - 6 * step - 3, 1)
            if step == 0:
                nearest[1, f] = jnp.zeros((24, z), F32)
        unrolled(step, s.ex - step, 2, layer)
        if step == 2:
            break
        for f in range(q):
            if step == 0:
                nearest[1, f] = pltpu.roll(nearest[1, f], (6 * s.ex + 3) % z, 1)
            ghost, near = beyond[step, f], nearest[step, f]
            value = advanced(
                None if step == 0 else beyond[0, f],
                fraction,
                coefficients(fraction, wind_z),
                ghost,
                pltpu.roll(ghost, 6, 1),
                pltpu.roll(ghost, z - 6, 1),
                pltpu.roll(ghost, 1, 0),
                pltpu.roll(ghost, 23, 0),
                pltpu.roll(jnp.where(from_low, near, ghost), 1, 1),
                pltpu.roll(jnp.where(from_high, near, ghost), z - 1, 1),
            )
            beyond[step + 1, f] = value * exists


def fine_kernel(s, f0, fw, flo_there, fhi_there, slab, out, avg, *scratch):
    s1, s2, faces, ghost_rows, zface, turning, flo, fhi, summed, sems = scratch
    arrivals = [
        pltpu.make_async_copy(flo_there, flo, sems.at[4]),
        pltpu.make_async_copy(fhi_there, fhi, sems.at[5]),
    ]
    for move in arrivals:
        move.start()
    states = (None, s1, s2, s1)
    q, y, z, fx, fe = s.q, s.y, s.z, s.fx, s.fe
    layers = fx + 6
    rows = slice(TOP, TOP + y)
    shift_z, shift_sz = z.bit_length() - 1, s.sz.bit_length() - 1
    r = lax.broadcasted_iota(jnp.int32, (2 * z, 2 * z), 0)
    c = lax.broadcasted_iota(jnp.int32, (2 * z, 2 * z), 1)
    near = c >> 1
    far = near + 2 * (c & 1) - 1
    same = (far >> shift_sz) == (near >> shift_sz)
    to_fine = jnp.where(r == near, 0.75, jnp.where((r == far) & same, 0.25, 0.0))
    ends_at = ((r & 2) << (shift_z - 1)) + jnp.where((r & 1) == 1, 0, z - 1)
    to_fine = jnp.where(r < z, to_fine, jnp.where(c == ends_at, 0.25, 0.0)).astype(BF16)
    ends = slab[s.rows_y : s.rows_y + s.ex, :]
    lane_x = lanes_of((s.ex, z))
    own_ends = [jnp.where((lane_x >> 2) == i, ends, 0.0) for i in range(3 * q)]
    wide = times(jnp.concatenate([slab[: s.rows_y, :], jnp.concatenate(own_ends, axis=0)], axis=1), to_fine)
    half = fe // 2
    for k in range(3):
        for f in range(q):
            for side in range(2):
                first = (k * q + f) * s.ex
                here = faces.at[(k * q + f) * 2 + side]
                here[: s.ex, :] = wide[first : first + s.ex, side * z : side * z + z]
                a = here[0:half, :]
                b = here[1 : half + 1, :]
                d = here[2 : half + 2, :]
                if k == 0:
                    flat, base, stride = ghost_rows, (2 * f + side) * fe, 1
                else:
                    flat, stride = states[k].reshape(q * layers * PAD, z), PAD
                    base = (f * layers + 1) * PAD + (TOP - 1 if side == 0 else TOP + y)
                flat[pl.ds(base, half, stride=2 * stride), :] = 0.25 * a + 0.75 * b
                flat[pl.ds(base + stride, half, stride=2 * stride), :] = 0.75 * b + 0.25 * d
    for f in range(q):
        at = s.rows_e + f * s.rows_z
        a = slab[at : at + s.sy, :]
        b = slab[at + 1 : at + 1 + s.sy, :]
        d = slab[at + 2 : at + 2 + s.sy, :]
        zface[pl.ds(f * y, s.sy, stride=2), :] = 0.25 * a + 0.75 * b
        zface[pl.ds(f * y + 1, s.sy, stride=2), :] = 0.75 * b + 0.25 * d
        a = zface[f * y : f * y + y, :]
        b = pltpu.roll(a, z - 2, 1)
        d = pltpu.roll(a, z - 4, 1)
        zface[f * y : f * y + y, :] = 0.25 * a + 0.75 * b
        zface[(q + f) * y : (q + f + 1) * y, :] = 0.75 * b + 0.25 * d
    lane = lanes_of((y, z))
    is_first, is_last = lane == 0, lane == z - 1
    row_in = lax.broadcasted_iota(jnp.int32, (y, z), 0)
    is_low, is_high = row_in == 0, row_in == y - 1
    flat_f0 = f0.reshape(q * fx * y, z)

    def turn_to(k, t):
        shift = -(2 * s.ex * k + 2 * t) % z
        for i in range(2 * q):
            packed = zface[i * y : (i + 1) * y, :]
            turning[i * y : (i + 1) * y, :] = pltpu.roll(packed, shift, 1) if shift else packed

    def pair_of_layers(k, t, inner):
        src, fraction = states[k], section_weights[k]

        def field(f, at):
            return f0[f, at] if inner else layer_of(s, f0, flo, fhi, f, at, 3, 0)

        for odd in range(2):
            b = 2 * t + odd
            at = b - 2
            if inner:
                winds = [fw[d, at] for d in range(3)]
            else:
                winds = [layer_of(s, fw, flo, fhi, d, at, 2, 3 * q) for d in range(3)]
            co = coefficients(fraction, winds)
            for f in range(q):
                if k == 0:
                    center, x_low, x_high = field(f, at), field(f, at - 1), field(f, at + 1)
                    if inner:
                        row = (f * fx + at) * y
                        y_low, y_high = flat_f0[pl.ds(row - 1, y), :], flat_f0[pl.ds(row + 1, y), :]
                    else:
                        y_low, y_high = pltpu.roll(center, 1, 0), pltpu.roll(center, y - 1, 0)
                    y_low = jnp.where(is_low, ghost_rows[pl.ds(2 * f * fe + b, 1), :], y_low)
                    y_high = jnp.where(is_high, ghost_rows[pl.ds((2 * f + 1) * fe + b, 1), :], y_high)
                else:
                    flat = src.reshape(q * layers * PAD, z)
                    row = (f * layers + b + 1) * PAD + TOP
                    center, x_low, x_high = src[f, b + 1, rows, :], src[f, b, rows, :], src[f, b + 2, rows, :]
                    y_low, y_high = flat[pl.ds(row - 1, y), :], flat[pl.ds(row + 1, y), :]
                i = odd * q + f
                ghost = turning[i * y : (i + 1) * y, :]
                turning[i * y : (i + 1) * y, :] = pltpu.roll(ghost, z - 2, 1)
                states[k + 1][f, b + 1, rows, :] = advanced(
                    None if k == 0 else field(f, at),
                    fraction,
                    co,
                    center,
                    x_low,
                    x_high,
                    y_low,
                    y_high,
                    pltpu.roll(jnp.where(is_last, ghost, center), 1, 1),
                    pltpu.roll(jnp.where(is_first, ghost, center), z - 1, 1),
                )

    for move in arrivals:
        move.wait()
    moves = []
    for k in range(3):
        if k < 2:
            outer = 2 - k
            for t in range(outer):
                turn_to(k, t)
                pair_of_layers(k, t, False)
            unrolled(outer, half - outer, 1, lambda t, g, k=k: pair_of_layers(k, t, True))
            for t in range(half - outer, half):
                pair_of_layers(k, t, False)
            continue
        turn_to(k, 1)
        quarter = (half - 2) // 4
        for i in range(4):
            unrolled(1 + i * quarter, 1 + (i + 1) * quarter, 1, lambda t, g, k=k: pair_of_layers(k, t, True))
            begin, end = 2 * quarter * i, 2 * quarter * (i + 1)
            moves.append(pltpu.make_async_copy(s1.at[:, 3 + begin : 3 + end, rows], out.at[:, begin:end], sems.at[i]))
            moves[-1].start()
    rz = lax.broadcasted_iota(jnp.int32, (z, z), 0)
    cz = lax.broadcasted_iota(jnp.int32, (z, z), 1)
    flat = summed.reshape(q * s.x * y, z)
    pairs_z = [jnp.where(cz == (rz >> 1) + odd * s.sz, 0.125, 0.0).astype(BF16) for odd in range(2)]
    for f in range(q):
        for p in range(s.x):
            both = s1[f, 3 + 2 * p, rows, :] + s1[f, 4 + 2 * p, rows, :]
            summed[f, p] = both + pltpu.roll(both, y - 1, 0)
    for f in range(q):
        sums = []
        for odd in range(2):
            parts = [flat[pl.ds((f * s.x + 2 * p + odd) * y, y // 2, stride=2), :] for p in range(s.x // 2)]
            sums.append(times(jnp.concatenate(parts, axis=0), pairs_z[odd]))
        avg[f] = (sums[0] + sums[1]).reshape(s.x // 2, y // 2, z)
    for move in moves:
        move.wait()


def merge_kernel(s, c3, avg, out, made, sems):
    lane = lanes_of((s.sy, s.z))
    inside = (lane >= s.lz) & (lane < s.lz + s.sz)
    moves = []
    for f in range(s.q):
        for p in range(s.x // 2):
            both = avg[f, p]
            for odd in range(2):
                at = 2 * p + odd
                moved = pltpu.roll(both, s.lz if odd == 0 else s.z - s.lz, 1)
                made[f, at] = c3[f, at]
                made[f, at, s.ly : s.ly + s.sy, :] = jnp.where(inside, moved, c3[f, at, s.ly : s.ly + s.sy, :])
        moves.append(pltpu.make_async_copy(made.at[f], out.at[f], sems.at[f]))
        moves[-1].start()
    for move in moves:
        move.wait()


SHORT = pl.CostEstimate(flops=1, bytes_accessed=1, transcendentals=0)


def run(kernel, name, ins, outs, scratch, megabytes, spaces=None, cost=SHORT):
    spaces = spaces or [pltpu.VMEM] * len(ins)
    outs = [out if isinstance(out[0], tuple) else (out, pltpu.VMEM) for out in outs]
    ins = [i if space is pltpu.SMEM else pltpu.with_memory_space_constraint(i, space) for i, space in zip(ins, spaces)]
    return pl.pallas_call(
        kernel,
        out_shape=tuple(space(dims, F32) for dims, space in outs),
        in_specs=[pl.BlockSpec(memory_space=space) for space in spaces],
        out_specs=tuple(pl.BlockSpec(memory_space=space) for _, space in outs),
        scratch_shapes=scratch,
        compiler_params=pltpu.CompilerParams(vmem_limit_bytes=megabytes << 20),
        cost_estimate=cost,
        name=name,
    )(*ins)


def ring(array, axis, by):
    size = lax.axis_size(axis)
    return lax.ppermute(array, axis, [(i, (i + by) % size) for i in range(size)])


def move_by(array, amount, beside=None):
    size = lax.axis_size("gx")
    work, operands = beside or (lambda: (), ())
    if size <= 8:

        def branch(by, array, *operands):
            return array if by == 0 else ring(array, "gx", by), work(*operands)

        return lax.switch(amount, [functools.partial(branch, by) for by in range(size)], array, *operands)
    for bit in range((size - 1).bit_length()):
        array = jnp.where((amount >> bit) % 2 == 1, ring(array, "gx", 1 << bit), array)
    return array, work(*operands)


def z_columns(zown):
    size = lax.axis_size("gz")
    if size == 1:
        return zown
    if size == 2:
        return lax.ppermute(zown, "gz", [(0, 1), (1, 0)])
    below = lax.broadcasted_iota(jnp.int32, zown.shape, 2) % 6 < 3
    return jnp.where(below, ring(zown, "gz", 1), ring(zown, "gz", -1))


def pack(s, fields, wind, spare, name):
    return run(
        functools.partial(pack_kernel, s),
        name,
        [fields, wind],
        [(s.halo + spare, s.y, s.z)] * 2,
        [pltpu.SemaphoreType.DMA((4,))],
        1,
        [pltpu.HBM] * 2,
    )


def shards(coarse_fields, coarse_wind, fine_fields, fine_wind, fine_owner):
    s = Sizes(coarse_fields.shape, fine_fields.shape)
    q, x, y, z, fx = s.q, s.x, s.y, s.z, s.fx
    size = lax.axis_size("gx")
    offset = (fine_owner[0, 0, 0] - lax.axis_index("gx")) % size
    level = lax.axis_index("gz")
    neighbours = jnp.stack([level > 0, level < lax.axis_size("gz") - 1]).astype(jnp.int32).reshape(1, 2)
    cup, cdown = pack(s, coarse_fields, coarse_wind, 0, "pack_coarse")
    lo, hi = ring(cup, "gx", 1), ring(cdown, "gx", -1)
    part, near = run(
        functools.partial(inner_kernel, s),
        "inner",
        [coarse_fields, coarse_wind],
        [(s.slab, z), (q, 2, y, z)],
        [pltpu.VMEM((q, x, y, z), F32)] * 2,
        3,
    )
    fup, fdown = pack(s, fine_fields, fine_wind, 2, "pack_fine")
    fup, fdown, offset = lax.optimization_barrier((fup, fdown, offset))
    flo, fhi = ring(fup, "gx", 1), ring(fdown, "gx", -1)
    padded = [pltpu.VMEM((q, s.ep, WPAD, z), F32)]
    wind_rows = [pltpu.VMEM((3, s.ex, 24, z), F32)]
    coarse_fields, part, near = lax.optimization_barrier((coarse_fields, part, near))
    coarse_level = [coarse_fields, coarse_wind, lo, hi]
    yup, ydn = run(functools.partial(ypack_kernel, s), "ypack", coarse_level, [(s.rows_f + s.rows_w, z)] * 2, [], 1)
    yrows = [ring(yup, "gy", 1), ring(ydn, "gy", -1)]
    ends = [pltpu.VMEM((q, 2 * EDGE, y, z), F32)] * 3
    (slab,) = run(functools.partial(slab_kernel, s), "slab", coarse_level + [part, near], [(s.slab, z)], ends, 3)
    slab, _ = move_by(slab, (size - offset) % size)
    yrows, slab, flo, fhi = lax.optimization_barrier((yrows, slab, flo, fhi))
    kernel = functools.partial(zpack_kernel, s)
    beyond_rows = [pltpu.VMEM((q + 3, s.ex, 8, z), F32)]
    (zown,) = run(kernel, "zpack", coarse_level + yrows, [(q + 3, 24, z)], beyond_rows, 2)
    zin = z_columns(zown)
    layers = fx + 6
    fine_next, averaged = run(
        functools.partial(fine_kernel, s),
        "fine",
        [fine_fields, fine_wind, flo, fhi, slab],
        [((q, fx, y, z), pltpu.HBM), (q, x // 2, y // 2, z)],
        [
            pltpu.VMEM((q, layers, PAD, z), F32),
            pltpu.VMEM((q, layers, PAD, z), F32),
            pltpu.VMEM((6 * q, s.ep, z), F32),
            pltpu.VMEM((2 * q * s.fe, z), F32),
            pltpu.VMEM((2 * q * y, z), F32),
            pltpu.VMEM((2 * q * y, z), F32),
            pltpu.VMEM(flo.shape, F32),
            pltpu.VMEM(fhi.shape, F32),
            pltpu.VMEM((q, s.x, y, z), F32),
            pltpu.SemaphoreType.DMA((6,)),
        ],
        9,
        [pltpu.VMEM, pltpu.VMEM, pltpu.HBM, pltpu.HBM, pltpu.VMEM],
    )

    def coarse(*ins):
        cost = pl.CostEstimate(flops=40_000_000, bytes_accessed=4_000_000, transcendentals=0)
        columns = [pltpu.VMEM((n, q, 24, z), F32) for n in (3, 2)] + [pltpu.VMEM((q, 24, z), F32)]
        spaces = [pltpu.SMEM] + [pltpu.VMEM] * (len(ins) - 1)
        kernel = functools.partial(coarse_kernel, s)
        return run(kernel, "coarse", ins, [(q, x, y, z)], padded * 3 + wind_rows + columns, 9, spaces, cost)[0]

    averaged, state = move_by(averaged, offset, (coarse, (neighbours, *coarse_level, *yrows, zown, zin)))
    (coarse_next,) = run(
        functools.partial(merge_kernel, s),
        "merge",
        [state, averaged],
        [((q, x, y, z), pltpu.HBM)],
        [pltpu.VMEM((q, x, y, z), F32), pltpu.SemaphoreType.DMA((q,))],
        2,
    )
    return coarse_next, fine_next


def solution(mesh):
    spec = P(None, "gx", "gy", "gz")
    return jax.shard_map(
        shards,
        mesh=mesh,
        in_specs=(spec, spec, spec, spec, P("gx", "gy", "gz")),
        out_specs=(spec, spec),
        check_vma=False,
    )
```

```python
import functools

import jax
import jax.numpy as jnp
from jax import lax
from jax.experimental import pallas as pl
from jax.experimental.pallas import tpu as pltpu
from jax.sharding import PartitionSpec as P

diffusion = 0.05
section_weights = (1.0 / 3.0, 0.5, 1.0)
F32 = jnp.float32
BF16 = jnp.bfloat16
PAD = 32
TOP = 8


class Sizes:
    def __init__(self, coarse_shape, fine_shape):
        self.q, self.x, self.y, self.z = coarse_shape
        self.fx = fine_shape[1]
        self.ly, self.sy = self.y // 4, self.y // 2
        self.lz, self.sz = self.z // 4, self.z // 2
        self.ex = self.x + 4
        self.ep = -(-self.ex // 8) * 8
        self.fe = self.fx + 4
        self.halo = 3 * self.q + 6
        self.rows_f, self.rows_w = self.q * (3 * self.x + 6), 3 * (2 * self.x + 2)
        self.rows_y = 3 * self.q * self.ex
        self.rows_e = self.rows_y + self.ep
        self.rows_z = self.sy + 2
        self.slab = self.rows_e + self.q * self.rows_z
        assert self.q == 4 and self.y == 16 and self.z == 128 and self.ex <= 20 and self.fx == 2 * self.x


def lanes_of(shape):
    return lax.broadcasted_iota(jnp.int32, shape, len(shape) - 1)


def halves(value):
    high = value.astype(BF16)
    return high, (value - high.astype(F32)).astype(BF16)


def times(value, matrix):
    high, low = halves(value)
    return jnp.dot(high, matrix, preferred_element_type=F32) + jnp.dot(low, matrix, preferred_element_type=F32)


def coefficients(fraction, wind):
    out = []
    for w in wind:
        turned_by = w * (-0.5 * fraction)
        out += [diffusion * fraction + turned_by, diffusion * fraction - turned_by]
    return out


def advanced(base, fraction, co, center, x_low, x_high, y_low, y_high, z_low, z_high):
    along = (co[0] * x_high + co[1] * x_low) + (co[2] * y_high + co[3] * y_low) + (co[4] * z_high + co[5] * z_low)
    if base is None:
        return center * (1.0 - 6.0 * diffusion * fraction) + along
    return (base - center * (6.0 * diffusion * fraction)) + along


def layer_of(s, own, low, high, member, at, width, first):
    size = own.shape[1]
    if at < 0:
        return low[first + width * member + at + width]
    if at >= size:
        return high[first + width * member + at - size]
    return own[member, at]


def unrolled(begin, end, at_once, body, carry=None):
    while (end - begin) % at_once:
        at_once -= 1

    def several(i, carry):
        for more in range(at_once):
            carry = body(begin + i * at_once + more, carry)
        return carry

    return lax.fori_loop(0, (end - begin) // at_once, several, carry)


def pack_kernel(s, fields, wind, up, down, sems):
    size = fields.shape[1]
    moves = []
    for own, members, width, first in ((fields, s.q, 3, 0), (wind, 3, 2, 3 * s.q)):
        for dst, at in ((up, size - width), (down, 0)):
            place = dst.at[first : first + members * width].reshape(members, width, s.y, s.z)
            moves.append((own.at[:, at : at + width], place))
    moves = [pltpu.make_async_copy(src, dst, sems.at[i]) for i, (src, dst) in enumerate(moves)]
    for move in moves:
        move.start()
    for move in moves:
        move.wait()


def y_rows(s, members, width):
    below, above = [], []
    for out, extra in ((below, lambda r: r), (above, lambda r: width - 1 - r)):
        at = 0
        for m in range(members):
            for r in range(width):
                out.append((m, r, extra(r), at))
                at += s.x + 2 * extra(r)
    return below, above


def ypack_kernel(s, c0, cw, lo, hi, up, dn):
    x, y, z = s.x, s.y, s.z
    flat_lo = lo.reshape(s.halo * y, z)
    flat_hi = hi.reshape(s.halo * y, z)
    for own, members, width, first, place in ((c0, s.q, 3, 0, 0), (cw, 3, 2, 3 * s.q, s.rows_f)):
        flat = own.reshape(members * x * y, z)
        for dst, rows, start in zip((up, dn), y_rows(s, members, width), (y - width, 0)):
            for m, r, e, at in rows:
                row, at = start + r, at + place
                if e:
                    dst[at : at + e, :] = flat_lo[pl.ds((first + width * (m + 1) - e) * y + row, e, stride=y), :]
                    dst[at + e + x : at + x + 2 * e, :] = flat_hi[pl.ds((first + width * m) * y + row, e, stride=y), :]
                dst[at + e : at + e + x, :] = flat[pl.ds(m * x * y + row, x, stride=y), :]


EDGE = 4


def turned(base, fraction, wind, center, x_low, x_high):
    y, z = center.shape
    return advanced(
        base,
        fraction,
        wind,
        center,
        x_low,
        x_high,
        pltpu.roll(center, 1, 0),
        pltpu.roll(center, y - 1, 0),
        pltpu.roll(center, 1, 1),
        pltpu.roll(center, z - 1, 1),
    )


def slab_parts(s, rows_of, tile_of, layers_of, put):
    q, y, z = s.q, s.y, s.z
    lane_y = lanes_of((y, z))
    columns = (lane_y == s.lz - 1) | (lane_y == s.lz) | (lane_y == s.lz + s.sz - 1) | (lane_y == s.lz + s.sz)
    low_at = (lane_y % 2 == 0) & (lane_y < z // 2)
    high_at = (lane_y % 2 == 0) & (lane_y >= z // 2)
    ends = None
    for f in range(q):
        zfaces = None
        for k in range(3):
            rows = [rows_of(k, f, row) for row in (s.ly - 1, s.ly, s.ly + s.sy - 1, s.ly + s.sy)]
            sides = (0.75 * rows[0] + 0.25 * rows[1], 0.25 * rows[2] + 0.75 * rows[3])
            lane_x = lanes_of(sides[0].shape)
            put(
                "y",
                (k * q + f) * s.ex,
                jnp.where(lane_x < s.sz, pltpu.roll(sides[0], z - s.lz, 1), pltpu.roll(sides[1], s.lz, 1)),
            )
            for side in range(2):
                e = 4 * (q * k + f) + 2 * side + 1
                before = jnp.where(lane_x == s.lz - 1, sides[side], 0.0)
                after = jnp.where(lane_x == s.lz + s.sz, sides[side], 0.0)
                part = pltpu.roll(before, (e - s.lz + 1) % z, 1) + pltpu.roll(after, (e - 1 - s.lz - s.sz) % z, 1)
                ends = part if ends is None else ends + part
            raw = None
            for a in layers_of(k):
                part = jnp.where(columns, tile_of(k, f, a), 0.0)
                part = pltpu.roll(part, (2 * a - s.lz + 1) % z, 1)
                raw = part if raw is None else raw + part
            beside = pltpu.roll(raw, z - 1, 1)
            low = jnp.where(low_at, 0.75 * raw + 0.25 * beside, 0.0)
            high = jnp.where(high_at, 0.25 * raw + 0.75 * beside, 0.0)
            part = pltpu.roll(low, (2 * s.ex * k - 1) % z, 1) + pltpu.roll(high, (2 * s.ex * k - z // 2) % z, 1)
            zfaces = part if zfaces is None else zfaces + part
        put("z", s.rows_e + f * s.rows_z, zfaces[s.ly - 1 : s.ly + s.sy + 1])
    put("e", s.rows_y, ends)


def inner_kernel(s, c0, cw, part, near, state1, state2):
    q, x, y, z = s.q, s.x, s.y, s.z
    states = (c0, state1, state2)
    for step in range(2):
        src, dst = states[step], states[step + 1]

        def layer(j, carry, step=step, src=src, dst=dst):
            w = coefficients(section_weights[step], [cw[d, j] for d in range(3)])
            made = []
            for f in range(q):
                base = None if step == 0 else c0[f, j]
                made.append(turned(base, section_weights[step], w, src[f, j], src[f, j - 1], src[f, j + 1]))
            for f in range(q):
                dst[f, j] = made[f]
            return carry

        unrolled(step + 1, x - 1 - step, 7 if step == 0 else 6, layer)
    for f in range(q):
        near[f, 0] = state1[f, EDGE - 2]
        near[f, 1] = state1[f, x + 1 - EDGE]
    count = s.ex - 2 * EDGE
    part[...] = jnp.zeros_like(part)

    def rows_of(k, f, row):
        flat = states[k].reshape(q * x * y, z)
        return flat[pl.ds((f * x + EDGE - 2) * y + row, count, stride=y), :]

    def put(kind, at, rows):
        if kind == "z":
            part[at : at + s.rows_z, :] = rows
        else:
            part[at + EDGE : at + EDGE + count, :] = rows

    slab_parts(s, rows_of, lambda k, f, a: states[k][f, a - 2], lambda k: range(EDGE, s.ex - EDGE), put)


def slab_kernel(s, c0, cw, lo, hi, part, near, slab, ends0, ends1, ends2):
    q, x, y, z = s.q, s.x, s.y, s.z
    states = (ends0, ends1, ends2)
    places = list(range(-2, EDGE - 2)) + list(range(x + 2 - EDGE, x + 2))
    slab[...] = part[...]
    for j, at in enumerate(places):
        for f in range(q):
            ends0[f, j] = layer_of(s, c0, lo, hi, f, at, 3, 0)
    for step in range(2):
        for j, at in enumerate(places):
            if step == 1 and at in (-2, x + 1):
                for f in range(q):
                    ends2[f, j] = jnp.zeros((y, z), F32)
                continue
            w = coefficients(section_weights[step], [layer_of(s, cw, lo, hi, d, at, 2, 3 * q) for d in range(3)])
            for f in range(q):

                def beside(at, f=f):
                    if step == 0:
                        return layer_of(s, c0, lo, hi, f, at, 3, 0)
                    if at in places:
                        return ends1[f, places.index(at)]
                    return near[f, 0 if at < x // 2 else 1]

                base = None if step == 0 else ends0[f, j]
                states[step + 1][f, j] = turned(
                    base, section_weights[step], w, beside(at), beside(at - 1), beside(at + 1)
                )

    def rows_of(k, f, row):
        flat = states[k].reshape(q * 2 * EDGE * y, z)
        return flat[pl.ds(f * 2 * EDGE * y + row, 2 * EDGE, stride=y), :]

    def put(kind, at, rows):
        if kind == "z":
            slab[at : at + s.rows_z, :] = part[at : at + s.rows_z, :] + rows
        else:
            slab[at : at + EDGE, :] = rows[:EDGE]
            slab[at + s.ex - EDGE : at + s.ex, :] = rows[EDGE:]

    def layers_of(k):
        some = range(0 if k == 0 else 1, EDGE)
        return list(some) + [s.ex - 1 - a for a in some]

    def tile_of(k, f, a):
        return states[k][f, a if a < EDGE else a - s.ex + 2 * EDGE]

    slab_parts(s, rows_of, tile_of, layers_of, put)


WTOP, WPAD = 12, 40
BLOCK = slice(8, 32)


def assemble(s, c0, cw, lo, hi, below, above, pad, wind):
    q, x, y, z = s.q, s.x, s.y, s.z
    flat = pad.reshape(q * s.ep * WPAD, z)
    flat_wind = wind.reshape(3 * s.ex * 24, z)
    for f in range(q):
        for at in range(-3, x + 3):
            pad[f, at + 3, WTOP : WTOP + y, :] = layer_of(s, c0, lo, hi, f, at, 3, 0)
    for d in range(3):
        for at in range(-2, x + 2):
            wind[d, at + 2, 4 : 4 + y, :] = layer_of(s, cw, lo, hi, d, at, 2, 3 * q)
    for src, rows, start in zip((below, above), y_rows(s, q, 3), (WTOP - 3, WTOP + y)):
        for m, r, e, at in rows:
            count = x + 2 * e
            flat[pl.ds((m * s.ep + 3 - e) * WPAD + start + r, count, stride=WPAD), :] = src[at : at + count, :]
    for src, rows, start in zip((below, above), y_rows(s, 3, 2), (2, 4 + y)):
        for m, r, e, at in rows:
            count, at = x + 2 * e, at + s.rows_f
            flat_wind[pl.ds((m * s.ex + 2 - e) * 24 + start + r, count, stride=24), :] = src[at : at + count, :]


def edge_lanes(s, lane, width):
    return (lane < width) | (lane >= s.z - width)


def zpack_kernel(s, c0, cw, lo, hi, below, above, out, rows):
    q, x, y, z = s.q, s.x, s.y, s.z
    flat = rows.reshape((q + 3) * s.ex * 8, z)
    rows[...] = jnp.zeros_like(rows)
    for src, place in ((below, 0), (above, 3)):
        for member, width, first in ((0, 3, 0), (q, 2, s.rows_f)):
            skip = 3 - width if place == 0 else 0
            for m, r, e, at in y_rows(s, q if width == 3 else 3, width)[place // 3]:
                e = min(e, 2)
                count = x + 2 * e
                start = ((member + m) * s.ex + 2 - e) * 8 + place + skip + r
                flat[pl.ds(start, count, stride=8), :] = src[first + at : first + at + count, :]
    lane = lanes_of((y, z))
    keep = edge_lanes(s, lane, 3)
    for m in range(q + 3):
        inside, outside = None, None
        for a in range(s.ex):
            if m < q:
                tile = layer_of(s, c0, lo, hi, m, a - 2, 3, 0)
            else:
                tile = layer_of(s, cw, lo, hi, m - q, a - 2, 2, 3 * q)
            shift = (6 * a + 3) % z
            part = pltpu.roll(jnp.where(keep, tile, 0.0), shift, 1)
            inside = part if inside is None else inside + part
            part = pltpu.roll(jnp.where(keep[:8], rows[m, a], 0.0), shift, 1)
            outside = part if outside is None else outside + part
        out[m, 0:1, :] = jnp.zeros((1, z), F32)
        out[m, 1:4, :] = outside[0:3]
        out[m, 4 : 4 + y, :] = inside
        out[m, 4 + y : 7 + y, :] = outside[3:6]
        out[m, 7 + y : 8 + y, :] = jnp.zeros((1, z), F32)


def coarse_kernel(
    s, sides, c0, cw, lo, hi, below, above, zown, zin, out, pad0, pad1, pad2, wind, beyond, nearest, turning
):
    q, x, y, z = s.q, s.x, s.y, s.z
    assemble(s, c0, cw, lo, hi, below, above, pad0, wind)
    pads = (pad0, pad1, pad2)
    lane = lanes_of((24, z))
    group = lane % 6
    from_low = group == 2
    from_high = group == 3
    exists = jnp.where(group < 3, sides[0, 0], sides[0, 1]).astype(F32)
    wind_z = [zin[q + d] for d in range(3)]
    for f in range(q):
        beyond[0, f] = zin[f] * exists
        nearest[0, f] = zown[f]
    for step in range(3):
        src, fraction = pads[step], section_weights[step]
        flat = src.reshape(q * s.ep * WPAD, z)
        flat_wind = wind.reshape(3 * s.ex * 24, z)
        flat_beyond = beyond.reshape(3 * q * 24, z)
        skip, height = (0, 24) if step < 2 else (4, y)
        here = lanes_of((8, z))
        is_first, is_last = here == 0, here == z - 1

        def layer(a, carry, step=step, flat=flat, fraction=fraction, skip=skip, height=height):
            for r in range(0, height, 8):
                if step < 2:
                    winds = [wind[d, a, r : r + 8, :] for d in range(3)]
                else:
                    winds = [flat_wind[pl.ds((d * s.ex + a) * 24 + skip + r, 8), :] for d in range(3)]
                co = coefficients(fraction, winds)
                for f in range(q):

                    def at_layer(of, layer, by=0, f=f, r=r):
                        if step < 2 and not by:
                            return of[f, layer, 8 + r : 16 + r, :]
                        row = (f * s.ep + layer) * WPAD + 8 + skip + r + by
                        return of.reshape(flat.shape)[pl.ds(row, 8), :]

                    src = pads[step]
                    center = at_layer(src, a + 1)
                    ghost = turning[f, r : r + 8, :]
                    turning[f, r : r + 8, :] = pltpu.roll(ghost, z - 6, 1)
                    value = advanced(
                        None if step == 0 else at_layer(pad0, a + 1),
                        fraction,
                        co,
                        center,
                        at_layer(src, a),
                        at_layer(src, a + 2),
                        at_layer(src, a + 1, -1),
                        at_layer(src, a + 1, 1),
                        pltpu.roll(jnp.where(is_last, ghost, center), 1, 1),
                        pltpu.roll(jnp.where(is_first, ghost, center), z - 1, 1),
                    )
                    if step == 2:
                        out[f, a - 2, r : r + 8, :] = value
                    else:
                        pads[step + 1][f, a + 1, 8 + r : 16 + r, :] = value
                    if step == 0:
                        total = nearest[1, f, r : r + 8, :] + jnp.where(is_first | is_last, value, 0.0)
                        nearest[1, f, r : r + 8, :] = pltpu.roll(total, z - 6, 1)
            return carry

        for f in range(q):
            start = (step * q + f) * 24 + skip
            turning[f, :height, :] = pltpu.roll(flat_beyond[start : start + height, :], z - 6 * step - 3, 1)
            if step == 0:
                nearest[1, f] = jnp.zeros((24, z), F32)
        unrolled(step, s.ex - step, (5, 6, 8)[step], layer)
        if step == 2:
            break
        for f in range(q):
            if step == 0:
                nearest[1, f] = pltpu.roll(nearest[1, f], (6 * s.ex + 3) % z, 1)
            ghost, near = beyond[step, f], nearest[step, f]
            value = advanced(
                None if step == 0 else beyond[0, f],
                fraction,
                coefficients(fraction, wind_z),
                ghost,
                pltpu.roll(ghost, 6, 1),
                pltpu.roll(ghost, z - 6, 1),
                pltpu.roll(ghost, 1, 0),
                pltpu.roll(ghost, 23, 0),
                pltpu.roll(jnp.where(from_low, near, ghost), 1, 1),
                pltpu.roll(jnp.where(from_high, near, ghost), z - 1, 1),
            )
            beyond[step + 1, f] = value * exists


def fine_kernel(s, f0, fw, flo_there, fhi_there, slab, out, avg, *scratch):
    s1, s2, faces, ghost_rows, zface, turning, flo, fhi, summed, sems = scratch
    arrivals = [
        pltpu.make_async_copy(flo_there, flo, sems.at[4]),
        pltpu.make_async_copy(fhi_there, fhi, sems.at[5]),
    ]
    for move in arrivals:
        move.start()
    states = (None, s1, s2, s1)
    q, y, z, fx, fe = s.q, s.y, s.z, s.fx, s.fe
    layers = fx + 6
    rows = slice(TOP, TOP + y)
    shift_z, shift_sz = z.bit_length() - 1, s.sz.bit_length() - 1
    r = lax.broadcasted_iota(jnp.int32, (2 * z, 2 * z), 0)
    c = lax.broadcasted_iota(jnp.int32, (2 * z, 2 * z), 1)
    near = c >> 1
    far = near + 2 * (c & 1) - 1
    same = (far >> shift_sz) == (near >> shift_sz)
    to_fine = jnp.where(r == near, 0.75, jnp.where((r == far) & same, 0.25, 0.0))
    ends_at = ((r & 2) << (shift_z - 1)) + jnp.where((r & 1) == 1, 0, z - 1)
    to_fine = jnp.where(r < z, to_fine, jnp.where(c == ends_at, 0.25, 0.0)).astype(BF16)
    ends = slab[s.rows_y : s.rows_y + s.ex, :]
    lane_x = lanes_of((s.ex, z))
    own_ends = [jnp.where((lane_x >> 2) == i, ends, 0.0) for i in range(3 * q)]
    wide = times(jnp.concatenate([slab[: s.rows_y, :], jnp.concatenate(own_ends, axis=0)], axis=1), to_fine)
    half = fe // 2
    for k in range(3):
        for f in range(q):
            for side in range(2):
                first = (k * q + f) * s.ex
                here = faces.at[(k * q + f) * 2 + side]
                here[: s.ex, :] = wide[first : first + s.ex, side * z : side * z + z]
                a = here[0:half, :]
                b = here[1 : half + 1, :]
                d = here[2 : half + 2, :]
                if k == 0:
                    flat, base, stride = ghost_rows, (2 * f + side) * fe, 1
                else:
                    flat, stride = states[k].reshape(q * layers * PAD, z), PAD
                    base = (f * layers + 1) * PAD + (TOP - 1 if side == 0 else TOP + y)
                flat[pl.ds(base, half, stride=2 * stride), :] = 0.25 * a + 0.75 * b
                flat[pl.ds(base + stride, half, stride=2 * stride), :] = 0.75 * b + 0.25 * d
    for f in range(q):
        at = s.rows_e + f * s.rows_z
        a = slab[at : at + s.sy, :]
        b = slab[at + 1 : at + 1 + s.sy, :]
        d = slab[at + 2 : at + 2 + s.sy, :]
        zface[pl.ds(f * y, s.sy, stride=2), :] = 0.25 * a + 0.75 * b
        zface[pl.ds(f * y + 1, s.sy, stride=2), :] = 0.75 * b + 0.25 * d
        a = zface[f * y : f * y + y, :]
        b = pltpu.roll(a, z - 2, 1)
        d = pltpu.roll(a, z - 4, 1)
        zface[f * y : f * y + y, :] = 0.25 * a + 0.75 * b
        zface[(q + f) * y : (q + f + 1) * y, :] = 0.75 * b + 0.25 * d
    lane = lanes_of((8, z))
    is_first, is_last = lane == 0, lane == z - 1
    row_in = lax.broadcasted_iota(jnp.int32, (8, z), 0)
    is_low, is_high = row_in == 0, row_in == 7
    flat_f0 = f0.reshape(q * fx * y, z)

    def turn_to(k, t):
        shift = -(2 * s.ex * k + 2 * t) % z
        for i in range(2 * q):
            packed = zface[i * y : (i + 1) * y, :]
            turning[i * y : (i + 1) * y, :] = pltpu.roll(packed, shift, 1) if shift else packed

    def pair_of_layers(k, t, inner):
        src, fraction = states[k], section_weights[k]

        def field(f, at):
            return layer_of(s, f0, flo, fhi, f, at, 3, 0)

        for odd, r in ((odd, r) for odd in range(2) for r in range(0, y, 8)):
            b = 2 * t + odd
            at = b - 2
            half_tile = slice(r, r + 8)
            if inner:
                winds = [fw[d, at, half_tile, :] for d in range(3)]
            else:
                winds = [layer_of(s, fw, flo, fhi, d, at, 2, 3 * q)[half_tile] for d in range(3)]
            co = coefficients(fraction, winds)
            for f in range(q):
                if k == 0:
                    if inner:
                        center, x_low, x_high = (f0[f, at + by, half_tile, :] for by in (0, -1, 1))
                        row = (f * fx + at) * y + r
                        y_low, y_high = flat_f0[pl.ds(row - 1, 8), :], flat_f0[pl.ds(row + 1, 8), :]
                    else:
                        whole = field(f, at)
                        y_low, y_high = pltpu.roll(whole, 1, 0)[half_tile], pltpu.roll(whole, y - 1, 0)[half_tile]
                        center, x_low, x_high = (field(f, at + by)[half_tile] for by in (0, -1, 1))
                    if r == 0:
                        y_low = jnp.where(is_low, ghost_rows[pl.ds(2 * f * fe + b, 1), :], y_low)
                    if r == y - 8:
                        y_high = jnp.where(is_high, ghost_rows[pl.ds((2 * f + 1) * fe + b, 1), :], y_high)
                    base = None
                else:
                    flat = src.reshape(q * layers * PAD, z)
                    row = (f * layers + b + 1) * PAD + TOP + r
                    center, x_low, x_high = (src[f, b + by, TOP + r : TOP + r + 8, :] for by in (1, 0, 2))
                    y_low, y_high = flat[pl.ds(row - 1, 8), :], flat[pl.ds(row + 1, 8), :]
                    base = f0[f, at, half_tile, :] if inner else field(f, at)[half_tile]
                i = (odd * q + f) * y + r
                ghost = turning[i : i + 8, :]
                turning[i : i + 8, :] = pltpu.roll(ghost, z - 2, 1)
                states[k + 1][f, b + 1, TOP + r : TOP + r + 8, :] = advanced(
                    base,
                    fraction,
                    co,
                    center,
                    x_low,
                    x_high,
                    y_low,
                    y_high,
                    pltpu.roll(jnp.where(is_last, ghost, center), 1, 1),
                    pltpu.roll(jnp.where(is_first, ghost, center), z - 1, 1),
                )

    for move in arrivals:
        move.wait()
    moves = []
    for k in range(3):
        if k < 2:
            outer = 2 - k
            for t in range(outer):
                turn_to(k, t)
                pair_of_layers(k, t, False)
            unrolled(outer, half - outer, 2 + 2 * k, lambda t, g, k=k: pair_of_layers(k, t, True))
            for t in range(half - outer, half):
                pair_of_layers(k, t, False)
            continue
        turn_to(k, 1)
        quarter = (half - 2) // 4
        for i in range(4):
            unrolled(1 + i * quarter, 1 + (i + 1) * quarter, 4, lambda t, g, k=k: pair_of_layers(k, t, True))
            begin, end = 2 * quarter * i, 2 * quarter * (i + 1)
            moves.append(pltpu.make_async_copy(s1.at[:, 3 + begin : 3 + end, rows], out.at[:, begin:end], sems.at[i]))
            moves[-1].start()
    rz = lax.broadcasted_iota(jnp.int32, (z, z), 0)
    cz = lax.broadcasted_iota(jnp.int32, (z, z), 1)
    flat = summed.reshape(q * s.x * y, z)
    pairs_z = [jnp.where(cz == (rz >> 1) + odd * s.sz, 0.125, 0.0).astype(BF16) for odd in range(2)]
    for f in range(q):
        for p in range(s.x):
            both = s1[f, 3 + 2 * p, rows, :] + s1[f, 4 + 2 * p, rows, :]
            summed[f, p] = both + pltpu.roll(both, y - 1, 0)
    for f in range(q):
        sums = []
        for odd in range(2):
            parts = [flat[pl.ds((f * s.x + 2 * p + odd) * y, y // 2, stride=2), :] for p in range(s.x // 2)]
            sums.append(times(jnp.concatenate(parts, axis=0), pairs_z[odd]))
        avg[f] = (sums[0] + sums[1]).reshape(s.x // 2, y // 2, z)
    for move in moves:
        move.wait()


def merge_kernel(s, c3, avg, out, made, sems):
    lane = lanes_of((s.sy, s.z))
    inside = (lane >= s.lz) & (lane < s.lz + s.sz)
    moves = []
    for f in range(s.q):
        for p in range(s.x // 2):
            both = avg[f, p]
            for odd in range(2):
                at = 2 * p + odd
                moved = pltpu.roll(both, s.lz if odd == 0 else s.z - s.lz, 1)
                made[f, at] = c3[f, at]
                made[f, at, s.ly : s.ly + s.sy, :] = jnp.where(inside, moved, c3[f, at, s.ly : s.ly + s.sy, :])
        moves.append(pltpu.make_async_copy(made.at[f], out.at[f], sems.at[f]))
        moves[-1].start()
    for move in moves:
        move.wait()


SHORT = pl.CostEstimate(flops=1, bytes_accessed=1, transcendentals=0)


def run(kernel, name, ins, outs, scratch, megabytes, spaces=None, cost=SHORT):
    spaces = spaces or [pltpu.VMEM] * len(ins)
    outs = [out if isinstance(out[0], tuple) else (out, pltpu.VMEM) for out in outs]
    ins = [i if space is pltpu.SMEM else pltpu.with_memory_space_constraint(i, space) for i, space in zip(ins, spaces)]
    return pl.pallas_call(
        kernel,
        out_shape=tuple(space(dims, F32) for dims, space in outs),
        in_specs=[pl.BlockSpec(memory_space=space) for space in spaces],
        out_specs=tuple(pl.BlockSpec(memory_space=space) for _, space in outs),
        scratch_shapes=scratch,
        compiler_params=pltpu.CompilerParams(vmem_limit_bytes=megabytes << 20),
        cost_estimate=cost,
        name=name,
    )(*ins)


def ring(array, axis, by):
    size = lax.axis_size(axis)
    return lax.ppermute(array, axis, [(i, (i + by) % size) for i in range(size)])


def move_by(array, amount, beside=None):
    size = lax.axis_size("gx")
    work, operands = beside or (lambda: (), ())
    if size <= 8:

        def branch(by, array, *operands):
            return array if by == 0 else ring(array, "gx", by), work(*operands)

        return lax.switch(amount, [functools.partial(branch, by) for by in range(size)], array, *operands)
    for bit in range((size - 1).bit_length()):
        array = jnp.where((amount >> bit) % 2 == 1, ring(array, "gx", 1 << bit), array)
    return array, work(*operands)


def z_columns(zown):
    size = lax.axis_size("gz")
    if size == 1:
        return zown
    if size == 2:
        return lax.ppermute(zown, "gz", [(0, 1), (1, 0)])
    below = lax.broadcasted_iota(jnp.int32, zown.shape, 2) % 6 < 3
    return jnp.where(below, ring(zown, "gz", 1), ring(zown, "gz", -1))


def pack(s, fields, wind, spare, name):
    return run(
        functools.partial(pack_kernel, s),
        name,
        [fields, wind],
        [(s.halo + spare, s.y, s.z)] * 2,
        [pltpu.SemaphoreType.DMA((4,))],
        1,
        [pltpu.HBM] * 2,
    )


def shards(coarse_fields, coarse_wind, fine_fields, fine_wind, fine_owner):
    s = Sizes(coarse_fields.shape, fine_fields.shape)
    q, x, y, z, fx = s.q, s.x, s.y, s.z, s.fx
    size = lax.axis_size("gx")
    offset = (fine_owner[0, 0, 0] - lax.axis_index("gx")) % size
    level = lax.axis_index("gz")
    neighbours = jnp.stack([level > 0, level < lax.axis_size("gz") - 1]).astype(jnp.int32).reshape(1, 2)
    cup, cdown = pack(s, coarse_fields, coarse_wind, 0, "pack_coarse")
    lo, hi = ring(cup, "gx", 1), ring(cdown, "gx", -1)
    part, near = run(
        functools.partial(inner_kernel, s),
        "inner",
        [coarse_fields, coarse_wind],
        [(s.slab, z), (q, 2, y, z)],
        [pltpu.VMEM((q, x, y, z), F32)] * 2,
        3,
    )
    fup, fdown = pack(s, fine_fields, fine_wind, 2, "pack_fine")
    fup, fdown, offset = lax.optimization_barrier((fup, fdown, offset))
    flo, fhi = ring(fup, "gx", 1), ring(fdown, "gx", -1)
    padded = [pltpu.VMEM((q, s.ep, WPAD, z), F32)]
    wind_rows = [pltpu.VMEM((3, s.ex, 24, z), F32)]
    coarse_fields, part, near = lax.optimization_barrier((coarse_fields, part, near))
    coarse_level = [coarse_fields, coarse_wind, lo, hi]
    yup, ydn = run(functools.partial(ypack_kernel, s), "ypack", coarse_level, [(s.rows_f + s.rows_w, z)] * 2, [], 1)
    yrows = [ring(yup, "gy", 1), ring(ydn, "gy", -1)]
    ends = [pltpu.VMEM((q, 2 * EDGE, y, z), F32)] * 3
    (slab,) = run(functools.partial(slab_kernel, s), "slab", coarse_level + [part, near], [(s.slab, z)], ends, 3)
    slab, _ = move_by(slab, (size - offset) % size)
    yrows, slab, flo, fhi = lax.optimization_barrier((yrows, slab, flo, fhi))
    kernel = functools.partial(zpack_kernel, s)
    beyond_rows = [pltpu.VMEM((q + 3, s.ex, 8, z), F32)]
    (zown,) = run(kernel, "zpack", coarse_level + yrows, [(q + 3, 24, z)], beyond_rows, 2)
    zin = z_columns(zown)
    layers = fx + 6
    fine_next, averaged = run(
        functools.partial(fine_kernel, s),
        "fine",
        [fine_fields, fine_wind, flo, fhi, slab],
        [((q, fx, y, z), pltpu.HBM), (q, x // 2, y // 2, z)],
        [
            pltpu.VMEM((q, layers, PAD, z), F32),
            pltpu.VMEM((q, layers, PAD, z), F32),
            pltpu.VMEM((6 * q, s.ep, z), F32),
            pltpu.VMEM((2 * q * s.fe, z), F32),
            pltpu.VMEM((2 * q * y, z), F32),
            pltpu.VMEM((2 * q * y, z), F32),
            pltpu.VMEM(flo.shape, F32),
            pltpu.VMEM(fhi.shape, F32),
            pltpu.VMEM((q, s.x, y, z), F32),
            pltpu.SemaphoreType.DMA((6,)),
        ],
        9,
        [pltpu.VMEM, pltpu.VMEM, pltpu.HBM, pltpu.HBM, pltpu.VMEM],
    )

    def coarse(*ins):
        cost = pl.CostEstimate(flops=40_000_000, bytes_accessed=4_000_000, transcendentals=0)
        columns = [pltpu.VMEM((n, q, 24, z), F32) for n in (3, 2)] + [pltpu.VMEM((q, 24, z), F32)]
        spaces = [pltpu.SMEM] + [pltpu.VMEM] * (len(ins) - 1)
        kernel = functools.partial(coarse_kernel, s)
        return run(kernel, "coarse", ins, [(q, x, y, z)], padded * 3 + wind_rows + columns, 9, spaces, cost)[0]

    averaged, state = move_by(averaged, offset, (coarse, (neighbours, *coarse_level, *yrows, zown, zin)))
    (coarse_next,) = run(
        functools.partial(merge_kernel, s),
        "merge",
        [state, averaged],
        [((q, x, y, z), pltpu.HBM)],
        [pltpu.VMEM((q, x, y, z), F32), pltpu.SemaphoreType.DMA((q,))],
        2,
    )
    return coarse_next, fine_next


def solution(mesh):
    spec = P(None, "gx", "gy", "gz")
    return jax.shard_map(
        shards,
        mesh=mesh,
        in_specs=(spec, spec, spec, spec, P("gx", "gy", "gz")),
        out_specs=(spec, spec),
        check_vma=False,
    )
```

```python
import functools

import jax
import jax.numpy as jnp
from jax import lax
from jax.experimental import pallas as pl
from jax.experimental.pallas import tpu as pltpu
from jax.sharding import PartitionSpec as P

diffusion = 0.05
section_weights = (1.0 / 3.0, 0.5, 1.0)
F32 = jnp.float32
BF16 = jnp.bfloat16
PAD = 32
TOP = 8


class Sizes:
    def __init__(self, coarse_shape, fine_shape):
        self.q, self.x, self.y, self.z = coarse_shape
        self.fx = fine_shape[1]
        self.ly, self.sy = self.y // 4, self.y // 2
        self.lz, self.sz = self.z // 4, self.z // 2
        self.ex = self.x + 4
        self.ep = -(-self.ex // 8) * 8
        self.fe = self.fx + 4
        self.halo = 3 * self.q + 6
        self.rows_f, self.rows_w = self.q * (3 * self.x + 6), 3 * (2 * self.x + 2)
        self.rows_y = 3 * self.q * self.ex
        self.rows_e = self.rows_y + self.ep
        self.rows_z = self.sy + 2
        self.slab = self.rows_e + self.q * self.rows_z
        assert self.q == 4 and self.y == 16 and self.z == 128 and self.ex <= 20 and self.fx == 2 * self.x


def lanes_of(shape):
    return lax.broadcasted_iota(jnp.int32, shape, len(shape) - 1)


def halves(value):
    high = value.astype(BF16)
    return high, (value - high.astype(F32)).astype(BF16)


def times(value, matrix):
    high, low = halves(value)
    return jnp.dot(high, matrix, preferred_element_type=F32) + jnp.dot(low, matrix, preferred_element_type=F32)


def coefficients(fraction, wind):
    out = []
    for w in wind:
        turned_by = w * (-0.5 * fraction)
        out += [diffusion * fraction + turned_by, diffusion * fraction - turned_by]
    return out


def advanced(base, fraction, co, center, x_low, x_high, y_low, y_high, z_low, z_high):
    along = (co[0] * x_high + co[1] * x_low) + (co[2] * y_high + co[3] * y_low) + (co[4] * z_high + co[5] * z_low)
    if base is None:
        return center * (1.0 - 6.0 * diffusion * fraction) + along
    return (base - center * (6.0 * diffusion * fraction)) + along


def layer_of(s, own, low, high, member, at, width, first):
    size = own.shape[1]
    if at < 0:
        return low[first + width * member + at + width]
    if at >= size:
        return high[first + width * member + at - size]
    return own[member, at]


def unrolled(begin, end, at_once, body, carry=None):
    while (end - begin) % at_once:
        at_once -= 1

    def several(i, carry):
        for more in range(at_once):
            carry = body(begin + i * at_once + more, carry)
        return carry

    return lax.fori_loop(0, (end - begin) // at_once, several, carry)


def pack_kernel(s, fields, wind, up, down, sems):
    size = fields.shape[1]
    moves = []
    for own, members, width, first in ((fields, s.q, 3, 0), (wind, 3, 2, 3 * s.q)):
        for dst, at in ((up, size - width), (down, 0)):
            place = dst.at[first : first + members * width].reshape(members, width, s.y, s.z)
            moves.append((own.at[:, at : at + width], place))
    moves = [pltpu.make_async_copy(src, dst, sems.at[i]) for i, (src, dst) in enumerate(moves)]
    for move in moves:
        move.start()
    for move in moves:
        move.wait()


def y_rows(s, members, width):
    below, above = [], []
    for out, extra in ((below, lambda r: r), (above, lambda r: width - 1 - r)):
        at = 0
        for m in range(members):
            for r in range(width):
                out.append((m, r, extra(r), at))
                at += s.x + 2 * extra(r)
    return below, above


def ypack_kernel(s, c0, cw, lo, hi, up, dn):
    x, y, z = s.x, s.y, s.z
    flat_lo = lo.reshape(s.halo * y, z)
    flat_hi = hi.reshape(s.halo * y, z)
    for own, members, width, first, place in ((c0, s.q, 3, 0, 0), (cw, 3, 2, 3 * s.q, s.rows_f)):
        flat = own.reshape(members * x * y, z)
        for dst, rows, start in zip((up, dn), y_rows(s, members, width), (y - width, 0)):
            for m, r, e, at in rows:
                row, at = start + r, at + place
                if e:
                    dst[at : at + e, :] = flat_lo[pl.ds((first + width * (m + 1) - e) * y + row, e, stride=y), :]
                    dst[at + e + x : at + x + 2 * e, :] = flat_hi[pl.ds((first + width * m) * y + row, e, stride=y), :]
                dst[at + e : at + e + x, :] = flat[pl.ds(m * x * y + row, x, stride=y), :]


EDGE = 4


def turned(base, fraction, wind, center, x_low, x_high):
    y, z = center.shape
    return advanced(
        base,
        fraction,
        wind,
        center,
        x_low,
        x_high,
        pltpu.roll(center, 1, 0),
        pltpu.roll(center, y - 1, 0),
        pltpu.roll(center, 1, 1),
        pltpu.roll(center, z - 1, 1),
    )


def slab_parts(s, rows_of, tile_of, layers_of, put):
    q, y, z = s.q, s.y, s.z
    lane_y = lanes_of((y, z))
    columns = (lane_y == s.lz - 1) | (lane_y == s.lz) | (lane_y == s.lz + s.sz - 1) | (lane_y == s.lz + s.sz)
    low_at = (lane_y % 2 == 0) & (lane_y < z // 2)
    high_at = (lane_y % 2 == 0) & (lane_y >= z // 2)
    ends = None
    for f in range(q):
        zfaces = None
        for k in range(3):
            rows = [rows_of(k, f, row) for row in (s.ly - 1, s.ly, s.ly + s.sy - 1, s.ly + s.sy)]
            sides = (0.75 * rows[0] + 0.25 * rows[1], 0.25 * rows[2] + 0.75 * rows[3])
            lane_x = lanes_of(sides[0].shape)
            put(
                "y",
                (k * q + f) * s.ex,
                jnp.where(lane_x < s.sz, pltpu.roll(sides[0], z - s.lz, 1), pltpu.roll(sides[1], s.lz, 1)),
            )
            for side in range(2):
                e = 4 * (q * k + f) + 2 * side + 1
                before = jnp.where(lane_x == s.lz - 1, sides[side], 0.0)
                after = jnp.where(lane_x == s.lz + s.sz, sides[side], 0.0)
                part = pltpu.roll(before, (e - s.lz + 1) % z, 1) + pltpu.roll(after, (e - 1 - s.lz - s.sz) % z, 1)
                ends = part if ends is None else ends + part
            raw = None
            for a in layers_of(k):
                part = jnp.where(columns, tile_of(k, f, a), 0.0)
                part = pltpu.roll(part, (2 * a - s.lz + 1) % z, 1)
                raw = part if raw is None else raw + part
            beside = pltpu.roll(raw, z - 1, 1)
            low = jnp.where(low_at, 0.75 * raw + 0.25 * beside, 0.0)
            high = jnp.where(high_at, 0.25 * raw + 0.75 * beside, 0.0)
            part = pltpu.roll(low, (2 * s.ex * k - 1) % z, 1) + pltpu.roll(high, (2 * s.ex * k - z // 2) % z, 1)
            zfaces = part if zfaces is None else zfaces + part
        put("z", s.rows_e + f * s.rows_z, zfaces[s.ly - 1 : s.ly + s.sy + 1])
    put("e", s.rows_y, ends)


def inner_kernel(s, c0, cw, part, near, state1, state2):
    q, x, y, z = s.q, s.x, s.y, s.z
    states = (c0, state1, state2)
    for step in range(2):
        src, dst = states[step], states[step + 1]

        def layer(j, carry, step=step, src=src, dst=dst):
            w = coefficients(section_weights[step], [cw[d, j] for d in range(3)])
            made = []
            for f in range(q):
                base = None if step == 0 else c0[f, j]
                made.append(turned(base, section_weights[step], w, src[f, j], src[f, j - 1], src[f, j + 1]))
            for f in range(q):
                dst[f, j] = made[f]
            return carry

        unrolled(step + 1, x - 1 - step, 7 if step == 0 else 6, layer)
    for f in range(q):
        near[f, 0] = state1[f, EDGE - 2]
        near[f, 1] = state1[f, x + 1 - EDGE]
    count = s.ex - 2 * EDGE
    part[...] = jnp.zeros_like(part)

    def rows_of(k, f, row):
        flat = states[k].reshape(q * x * y, z)
        return flat[pl.ds((f * x + EDGE - 2) * y + row, count, stride=y), :]

    def put(kind, at, rows):
        if kind == "z":
            part[at : at + s.rows_z, :] = rows
        else:
            part[at + EDGE : at + EDGE + count, :] = rows

    slab_parts(s, rows_of, lambda k, f, a: states[k][f, a - 2], lambda k: range(EDGE, s.ex - EDGE), put)


def slab_kernel(s, c0, cw, lo, hi, part, near, slab, ends0, ends1, ends2):
    q, x, y, z = s.q, s.x, s.y, s.z
    states = (ends0, ends1, ends2)
    places = list(range(-2, EDGE - 2)) + list(range(x + 2 - EDGE, x + 2))
    slab[...] = part[...]
    for j, at in enumerate(places):
        for f in range(q):
            ends0[f, j] = layer_of(s, c0, lo, hi, f, at, 3, 0)
    for step in range(2):
        for j, at in enumerate(places):
            if step == 1 and at in (-2, x + 1):
                for f in range(q):
                    ends2[f, j] = jnp.zeros((y, z), F32)
                continue
            w = coefficients(section_weights[step], [layer_of(s, cw, lo, hi, d, at, 2, 3 * q) for d in range(3)])
            for f in range(q):

                def beside(at, f=f):
                    if step == 0:
                        return layer_of(s, c0, lo, hi, f, at, 3, 0)
                    if at in places:
                        return ends1[f, places.index(at)]
                    return near[f, 0 if at < x // 2 else 1]

                base = None if step == 0 else ends0[f, j]
                states[step + 1][f, j] = turned(
                    base, section_weights[step], w, beside(at), beside(at - 1), beside(at + 1)
                )

    def rows_of(k, f, row):
        flat = states[k].reshape(q * 2 * EDGE * y, z)
        return flat[pl.ds(f * 2 * EDGE * y + row, 2 * EDGE, stride=y), :]

    def put(kind, at, rows):
        if kind == "z":
            slab[at : at + s.rows_z, :] = part[at : at + s.rows_z, :] + rows
        else:
            slab[at : at + EDGE, :] = rows[:EDGE]
            slab[at + s.ex - EDGE : at + s.ex, :] = rows[EDGE:]

    def layers_of(k):
        some = range(0 if k == 0 else 1, EDGE)
        return list(some) + [s.ex - 1 - a for a in some]

    def tile_of(k, f, a):
        return states[k][f, a if a < EDGE else a - s.ex + 2 * EDGE]

    slab_parts(s, rows_of, tile_of, layers_of, put)


WTOP, WPAD = 12, 40
BLOCK = slice(8, 32)


def assemble(s, c0, cw, lo, hi, below, above, pad, wind):
    q, x, y, z = s.q, s.x, s.y, s.z
    flat = pad.reshape(q * s.ep * WPAD, z)
    flat_wind = wind.reshape(3 * s.ex * 24, z)
    for f in range(q):
        for at in range(-3, x + 3):
            pad[f, at + 3, WTOP : WTOP + y, :] = layer_of(s, c0, lo, hi, f, at, 3, 0)
    for d in range(3):
        for at in range(-2, x + 2):
            wind[d, at + 2, 4 : 4 + y, :] = layer_of(s, cw, lo, hi, d, at, 2, 3 * q)
    for src, rows, start in zip((below, above), y_rows(s, q, 3), (WTOP - 3, WTOP + y)):
        for m, r, e, at in rows:
            count = x + 2 * e
            flat[pl.ds((m * s.ep + 3 - e) * WPAD + start + r, count, stride=WPAD), :] = src[at : at + count, :]
    for src, rows, start in zip((below, above), y_rows(s, 3, 2), (2, 4 + y)):
        for m, r, e, at in rows:
            count, at = x + 2 * e, at + s.rows_f
            flat_wind[pl.ds((m * s.ex + 2 - e) * 24 + start + r, count, stride=24), :] = src[at : at + count, :]


def edge_lanes(s, lane, width):
    return (lane < width) | (lane >= s.z - width)


def zpack_kernel(s, c0, cw, lo, hi, below, above, out, rows):
    q, x, y, z = s.q, s.x, s.y, s.z
    flat = rows.reshape((q + 3) * s.ex * 8, z)
    rows[...] = jnp.zeros_like(rows)
    for src, place in ((below, 0), (above, 3)):
        for member, width, first in ((0, 3, 0), (q, 2, s.rows_f)):
            skip = 3 - width if place == 0 else 0
            for m, r, e, at in y_rows(s, q if width == 3 else 3, width)[place // 3]:
                e = min(e, 2)
                count = x + 2 * e
                start = ((member + m) * s.ex + 2 - e) * 8 + place + skip + r
                flat[pl.ds(start, count, stride=8), :] = src[first + at : first + at + count, :]
    lane = lanes_of((y, z))
    keep = edge_lanes(s, lane, 3)
    for m in range(q + 3):
        inside, outside = None, None
        for a in range(s.ex):
            if m < q:
                tile = layer_of(s, c0, lo, hi, m, a - 2, 3, 0)
            else:
                tile = layer_of(s, cw, lo, hi, m - q, a - 2, 2, 3 * q)
            shift = (6 * a + 3) % z
            part = pltpu.roll(jnp.where(keep, tile, 0.0), shift, 1)
            inside = part if inside is None else inside + part
            part = pltpu.roll(jnp.where(keep[:8], rows[m, a], 0.0), shift, 1)
            outside = part if outside is None else outside + part
        out[m, 0:1, :] = jnp.zeros((1, z), F32)
        out[m, 1:4, :] = outside[0:3]
        out[m, 4 : 4 + y, :] = inside
        out[m, 4 + y : 7 + y, :] = outside[3:6]
        out[m, 7 + y : 8 + y, :] = jnp.zeros((1, z), F32)


def coarse_kernel(
    s, sides, c0, cw, lo, hi, below, above, zown, zin, out, pad0, pad1, pad2, wind, beyond, nearest, turning
):
    q, x, y, z = s.q, s.x, s.y, s.z
    assemble(s, c0, cw, lo, hi, below, above, pad0, wind)
    pads = (pad0, pad1, pad2)
    lane = lanes_of((24, z))
    group = lane % 6
    from_low = group == 2
    from_high = group == 3
    exists = jnp.where(group < 3, sides[0, 0], sides[0, 1]).astype(F32)
    wind_z = [zin[q + d] for d in range(3)]
    for f in range(q):
        beyond[0, f] = zin[f] * exists
        nearest[0, f] = zown[f]
    for step in range(3):
        src, fraction = pads[step], section_weights[step]
        flat = src.reshape(q * s.ep * WPAD, z)
        flat_wind = wind.reshape(3 * s.ex * 24, z)
        flat_beyond = beyond.reshape(3 * q * 24, z)
        skip, height = (0, 24) if step < 2 else (4, y)
        here = lanes_of((8, z))
        is_first, is_last = here == 0, here == z - 1

        def layer(a, carry, step=step, flat=flat, fraction=fraction, skip=skip, height=height):
            for r in range(0, height, 8):
                if step < 2:
                    winds = [wind[d, a, r : r + 8, :] for d in range(3)]
                else:
                    winds = [flat_wind[pl.ds((d * s.ex + a) * 24 + skip + r, 8), :] for d in range(3)]
                co = coefficients(fraction, winds)
                for f in range(q):

                    def at_layer(of, layer, by=0, f=f, r=r):
                        if step < 2 and not by:
                            return of[f, layer, 8 + r : 16 + r, :]
                        row = (f * s.ep + layer) * WPAD + 8 + skip + r + by
                        return of.reshape(flat.shape)[pl.ds(row, 8), :]

                    src = pads[step]
                    center = at_layer(src, a + 1)
                    ghost = turning[f, r : r + 8, :]
                    turning[f, r : r + 8, :] = pltpu.roll(ghost, z - 6, 1)
                    value = advanced(
                        None if step == 0 else at_layer(pad0, a + 1),
                        fraction,
                        co,
                        center,
                        at_layer(src, a),
                        at_layer(src, a + 2),
                        at_layer(src, a + 1, -1),
                        at_layer(src, a + 1, 1),
                        pltpu.roll(jnp.where(is_last, ghost, center), 1, 1),
                        pltpu.roll(jnp.where(is_first, ghost, center), z - 1, 1),
                    )
                    if step == 2:
                        out[f, a - 2, r : r + 8, :] = value
                    else:
                        pads[step + 1][f, a + 1, 8 + r : 16 + r, :] = value
                    if step == 0:
                        total = nearest[1, f, r : r + 8, :] + jnp.where(is_first | is_last, value, 0.0)
                        nearest[1, f, r : r + 8, :] = pltpu.roll(total, z - 6, 1)
            return carry

        for f in range(q):
            start = (step * q + f) * 24 + skip
            turning[f, :height, :] = pltpu.roll(flat_beyond[start : start + height, :], z - 6 * step - 3, 1)
            if step == 0:
                nearest[1, f] = jnp.zeros((24, z), F32)
        unrolled(step, s.ex - step, (10, 9, 8)[step], layer)
        if step == 2:
            break
        for f in range(q):
            if step == 0:
                nearest[1, f] = pltpu.roll(nearest[1, f], (6 * s.ex + 3) % z, 1)
            ghost, near = beyond[step, f], nearest[step, f]
            value = advanced(
                None if step == 0 else beyond[0, f],
                fraction,
                coefficients(fraction, wind_z),
                ghost,
                pltpu.roll(ghost, 6, 1),
                pltpu.roll(ghost, z - 6, 1),
                pltpu.roll(ghost, 1, 0),
                pltpu.roll(ghost, 23, 0),
                pltpu.roll(jnp.where(from_low, near, ghost), 1, 1),
                pltpu.roll(jnp.where(from_high, near, ghost), z - 1, 1),
            )
            beyond[step + 1, f] = value * exists


def fine_kernel(s, f0, fw, flo_there, fhi_there, slab, out, avg, *scratch):
    s1, s2, faces, ghost_rows, zface, turning, flo, fhi, summed, sems = scratch
    arrivals = [
        pltpu.make_async_copy(flo_there, flo, sems.at[4]),
        pltpu.make_async_copy(fhi_there, fhi, sems.at[5]),
    ]
    for move in arrivals:
        move.start()
    states = (None, s1, s2, s1)
    q, y, z, fx, fe = s.q, s.y, s.z, s.fx, s.fe
    layers = fx + 6
    rows = slice(TOP, TOP + y)
    shift_z, shift_sz = z.bit_length() - 1, s.sz.bit_length() - 1
    r = lax.broadcasted_iota(jnp.int32, (2 * z, 2 * z), 0)
    c = lax.broadcasted_iota(jnp.int32, (2 * z, 2 * z), 1)
    near = c >> 1
    far = near + 2 * (c & 1) - 1
    same = (far >> shift_sz) == (near >> shift_sz)
    to_fine = jnp.where(r == near, 0.75, jnp.where((r == far) & same, 0.25, 0.0))
    ends_at = ((r & 2) << (shift_z - 1)) + jnp.where((r & 1) == 1, 0, z - 1)
    to_fine = jnp.where(r < z, to_fine, jnp.where(c == ends_at, 0.25, 0.0)).astype(BF16)
    ends = slab[s.rows_y : s.rows_y + s.ex, :]
    lane_x = lanes_of((s.ex, z))
    own_ends = [jnp.where((lane_x >> 2) == i, ends, 0.0) for i in range(3 * q)]
    wide = times(jnp.concatenate([slab[: s.rows_y, :], jnp.concatenate(own_ends, axis=0)], axis=1), to_fine)
    half = fe // 2
    for k in range(3):
        for f in range(q):
            for side in range(2):
                first = (k * q + f) * s.ex
                here = faces.at[(k * q + f) * 2 + side]
                here[: s.ex, :] = wide[first : first + s.ex, side * z : side * z + z]
                a = here[0:half, :]
                b = here[1 : half + 1, :]
                d = here[2 : half + 2, :]
                if k == 0:
                    flat, base, stride = ghost_rows, (2 * f + side) * fe, 1
                else:
                    flat, stride = states[k].reshape(q * layers * PAD, z), PAD
                    base = (f * layers + 1) * PAD + (TOP - 1 if side == 0 else TOP + y)
                flat[pl.ds(base, half, stride=2 * stride), :] = 0.25 * a + 0.75 * b
                flat[pl.ds(base + stride, half, stride=2 * stride), :] = 0.75 * b + 0.25 * d
    for f in range(q):
        at = s.rows_e + f * s.rows_z
        a = slab[at : at + s.sy, :]
        b = slab[at + 1 : at + 1 + s.sy, :]
        d = slab[at + 2 : at + 2 + s.sy, :]
        zface[pl.ds(f * y, s.sy, stride=2), :] = 0.25 * a + 0.75 * b
        zface[pl.ds(f * y + 1, s.sy, stride=2), :] = 0.75 * b + 0.25 * d
        a = zface[f * y : f * y + y, :]
        b = pltpu.roll(a, z - 2, 1)
        d = pltpu.roll(a, z - 4, 1)
        zface[f * y : f * y + y, :] = 0.25 * a + 0.75 * b
        zface[(q + f) * y : (q + f + 1) * y, :] = 0.75 * b + 0.25 * d
    lane = lanes_of((8, z))
    is_first, is_last = lane == 0, lane == z - 1
    row_in = lax.broadcasted_iota(jnp.int32, (8, z), 0)
    is_low, is_high = row_in == 0, row_in == 7
    flat_f0 = f0.reshape(q * fx * y, z)

    def turn_to(k, t):
        shift = -(2 * s.ex * k + 2 * t) % z
        for i in range(2 * q):
            packed = zface[i * y : (i + 1) * y, :]
            turning[i * y : (i + 1) * y, :] = pltpu.roll(packed, shift, 1) if shift else packed

    def pair_of_layers(k, t, inner):
        src, fraction = states[k], section_weights[k]

        def field(f, at):
            return layer_of(s, f0, flo, fhi, f, at, 3, 0)

        for odd, r in ((odd, r) for odd in range(2) for r in range(0, y, 8)):
            b = 2 * t + odd
            at = b - 2
            half_tile = slice(r, r + 8)
            if inner:
                winds = [fw[d, at, half_tile, :] for d in range(3)]
            else:
                winds = [layer_of(s, fw, flo, fhi, d, at, 2, 3 * q)[half_tile] for d in range(3)]
            co = coefficients(fraction, winds)
            for f in range(q):
                if k == 0:
                    if inner:
                        center, x_low, x_high = (f0[f, at + by, half_tile, :] for by in (0, -1, 1))
                        row = (f * fx + at) * y + r
                        y_low, y_high = flat_f0[pl.ds(row - 1, 8), :], flat_f0[pl.ds(row + 1, 8), :]
                    else:
                        whole = field(f, at)
                        y_low, y_high = pltpu.roll(whole, 1, 0)[half_tile], pltpu.roll(whole, y - 1, 0)[half_tile]
                        center, x_low, x_high = (field(f, at + by)[half_tile] for by in (0, -1, 1))
                    if r == 0:
                        y_low = jnp.where(is_low, ghost_rows[pl.ds(2 * f * fe + b, 1), :], y_low)
                    if r == y - 8:
                        y_high = jnp.where(is_high, ghost_rows[pl.ds((2 * f + 1) * fe + b, 1), :], y_high)
                    base = None
                else:
                    flat = src.reshape(q * layers * PAD, z)
                    row = (f * layers + b + 1) * PAD + TOP + r
                    center, x_low, x_high = (src[f, b + by, TOP + r : TOP + r + 8, :] for by in (1, 0, 2))
                    y_low, y_high = flat[pl.ds(row - 1, 8), :], flat[pl.ds(row + 1, 8), :]
                    base = f0[f, at, half_tile, :] if inner else field(f, at)[half_tile]
                i = (odd * q + f) * y + r
                ghost = turning[i : i + 8, :]
                turning[i : i + 8, :] = pltpu.roll(ghost, z - 2, 1)
                states[k + 1][f, b + 1, TOP + r : TOP + r + 8, :] = advanced(
                    base,
                    fraction,
                    co,
                    center,
                    x_low,
                    x_high,
                    y_low,
                    y_high,
                    pltpu.roll(jnp.where(is_last, ghost, center), 1, 1),
                    pltpu.roll(jnp.where(is_first, ghost, center), z - 1, 1),
                )

    for move in arrivals:
        move.wait()
    moves = []
    for k in range(3):
        if k < 2:
            outer = 2 - k
            for t in range(outer):
                turn_to(k, t)
                pair_of_layers(k, t, False)
            unrolled(outer, half - outer, 7 + k, lambda t, g, k=k: pair_of_layers(k, t, True))
            for t in range(half - outer, half):
                pair_of_layers(k, t, False)
            continue
        turn_to(k, 1)
        quarter = (half - 2) // 4
        for i in range(4):
            unrolled(1 + i * quarter, 1 + (i + 1) * quarter, 4, lambda t, g, k=k: pair_of_layers(k, t, True))
            begin, end = 2 * quarter * i, 2 * quarter * (i + 1)
            moves.append(pltpu.make_async_copy(s1.at[:, 3 + begin : 3 + end, rows], out.at[:, begin:end], sems.at[i]))
            moves[-1].start()
    rz = lax.broadcasted_iota(jnp.int32, (z, z), 0)
    cz = lax.broadcasted_iota(jnp.int32, (z, z), 1)
    flat = summed.reshape(q * s.x * y, z)
    pairs_z = [jnp.where(cz == (rz >> 1) + odd * s.sz, 0.125, 0.0).astype(BF16) for odd in range(2)]
    for f in range(q):
        for p in range(s.x):
            both = s1[f, 3 + 2 * p, rows, :] + s1[f, 4 + 2 * p, rows, :]
            summed[f, p] = both + pltpu.roll(both, y - 1, 0)
    for f in range(q):
        sums = []
        for odd in range(2):
            parts = [flat[pl.ds((f * s.x + 2 * p + odd) * y, y // 2, stride=2), :] for p in range(s.x // 2)]
            sums.append(times(jnp.concatenate(parts, axis=0), pairs_z[odd]))
        avg[f] = (sums[0] + sums[1]).reshape(s.x // 2, y // 2, z)
    for move in moves:
        move.wait()


def merge_kernel(s, c3, avg, out, made, sems):
    lane = lanes_of((s.sy, s.z))
    inside = (lane >= s.lz) & (lane < s.lz + s.sz)
    moves = []
    for f in range(s.q):
        for p in range(s.x // 2):
            both = avg[f, p]
            for odd in range(2):
                at = 2 * p + odd
                moved = pltpu.roll(both, s.lz if odd == 0 else s.z - s.lz, 1)
                made[f, at] = c3[f, at]
                made[f, at, s.ly : s.ly + s.sy, :] = jnp.where(inside, moved, c3[f, at, s.ly : s.ly + s.sy, :])
        moves.append(pltpu.make_async_copy(made.at[f], out.at[f], sems.at[f]))
        moves[-1].start()
    for move in moves:
        move.wait()


SHORT = pl.CostEstimate(flops=1, bytes_accessed=1, transcendentals=0)


def run(kernel, name, ins, outs, scratch, megabytes, spaces=None, cost=SHORT):
    spaces = spaces or [pltpu.VMEM] * len(ins)
    outs = [out if isinstance(out[0], tuple) else (out, pltpu.VMEM) for out in outs]
    ins = [i if space is pltpu.SMEM else pltpu.with_memory_space_constraint(i, space) for i, space in zip(ins, spaces)]
    return pl.pallas_call(
        kernel,
        out_shape=tuple(space(dims, F32) for dims, space in outs),
        in_specs=[pl.BlockSpec(memory_space=space) for space in spaces],
        out_specs=tuple(pl.BlockSpec(memory_space=space) for _, space in outs),
        scratch_shapes=scratch,
        compiler_params=pltpu.CompilerParams(vmem_limit_bytes=megabytes << 20),
        cost_estimate=cost,
        name=name,
    )(*ins)


def ring(array, axis, by):
    size = lax.axis_size(axis)
    return lax.ppermute(array, axis, [(i, (i + by) % size) for i in range(size)])


def move_by(array, amount, beside=None):
    size = lax.axis_size("gx")
    work, operands = beside or (lambda: (), ())
    if size <= 8:

        def branch(by, array, *operands):
            return array if by == 0 else ring(array, "gx", by), work(*operands)

        return lax.switch(amount, [functools.partial(branch, by) for by in range(size)], array, *operands)
    for bit in range((size - 1).bit_length()):
        array = jnp.where((amount >> bit) % 2 == 1, ring(array, "gx", 1 << bit), array)
    return array, work(*operands)


def z_columns(zown):
    size = lax.axis_size("gz")
    if size == 1:
        return zown
    if size == 2:
        return lax.ppermute(zown, "gz", [(0, 1), (1, 0)])
    below = lax.broadcasted_iota(jnp.int32, zown.shape, 2) % 6 < 3
    return jnp.where(below, ring(zown, "gz", 1), ring(zown, "gz", -1))


def pack(s, fields, wind, spare, name):
    return run(
        functools.partial(pack_kernel, s),
        name,
        [fields, wind],
        [(s.halo + spare, s.y, s.z)] * 2,
        [pltpu.SemaphoreType.DMA((4,))],
        1,
        [pltpu.HBM] * 2,
    )


def shards(coarse_fields, coarse_wind, fine_fields, fine_wind, fine_owner):
    s = Sizes(coarse_fields.shape, fine_fields.shape)
    q, x, y, z, fx = s.q, s.x, s.y, s.z, s.fx
    size = lax.axis_size("gx")
    offset = (fine_owner[0, 0, 0] - lax.axis_index("gx")) % size
    level = lax.axis_index("gz")
    neighbours = jnp.stack([level > 0, level < lax.axis_size("gz") - 1]).astype(jnp.int32).reshape(1, 2)
    cup, cdown = pack(s, coarse_fields, coarse_wind, 0, "pack_coarse")
    lo, hi = ring(cup, "gx", 1), ring(cdown, "gx", -1)
    part, near = run(
        functools.partial(inner_kernel, s),
        "inner",
        [coarse_fields, coarse_wind],
        [(s.slab, z), (q, 2, y, z)],
        [pltpu.VMEM((q, x, y, z), F32)] * 2,
        3,
    )
    fup, fdown = pack(s, fine_fields, fine_wind, 2, "pack_fine")
    fup, fdown, offset = lax.optimization_barrier((fup, fdown, offset))
    flo, fhi = ring(fup, "gx", 1), ring(fdown, "gx", -1)
    padded = [pltpu.VMEM((q, s.ep, WPAD, z), F32)]
    wind_rows = [pltpu.VMEM((3, s.ex, 24, z), F32)]
    coarse_fields, part, near = lax.optimization_barrier((coarse_fields, part, near))
    coarse_level = [coarse_fields, coarse_wind, lo, hi]
    yup, ydn = run(functools.partial(ypack_kernel, s), "ypack", coarse_level, [(s.rows_f + s.rows_w, z)] * 2, [], 1)
    yrows = [ring(yup, "gy", 1), ring(ydn, "gy", -1)]
    ends = [pltpu.VMEM((q, 2 * EDGE, y, z), F32)] * 3
    (slab,) = run(functools.partial(slab_kernel, s), "slab", coarse_level + [part, near], [(s.slab, z)], ends, 3)
    slab, _ = move_by(slab, (size - offset) % size)
    yrows, slab, flo, fhi = lax.optimization_barrier((yrows, slab, flo, fhi))
    kernel = functools.partial(zpack_kernel, s)
    beyond_rows = [pltpu.VMEM((q + 3, s.ex, 8, z), F32)]
    (zown,) = run(kernel, "zpack", coarse_level + yrows, [(q + 3, 24, z)], beyond_rows, 2)
    zin = z_columns(zown)
    layers = fx + 6
    fine_next, averaged = run(
        functools.partial(fine_kernel, s),
        "fine",
        [fine_fields, fine_wind, flo, fhi, slab],
        [((q, fx, y, z), pltpu.HBM), (q, x // 2, y // 2, z)],
        [
            pltpu.VMEM((q, layers, PAD, z), F32),
            pltpu.VMEM((q, layers, PAD, z), F32),
            pltpu.VMEM((6 * q, s.ep, z), F32),
            pltpu.VMEM((2 * q * s.fe, z), F32),
            pltpu.VMEM((2 * q * y, z), F32),
            pltpu.VMEM((2 * q * y, z), F32),
            pltpu.VMEM(flo.shape, F32),
            pltpu.VMEM(fhi.shape, F32),
            pltpu.VMEM((q, s.x, y, z), F32),
            pltpu.SemaphoreType.DMA((6,)),
        ],
        9,
        [pltpu.VMEM, pltpu.VMEM, pltpu.HBM, pltpu.HBM, pltpu.VMEM],
    )

    def coarse(*ins):
        cost = pl.CostEstimate(flops=40_000_000, bytes_accessed=4_000_000, transcendentals=0)
        columns = [pltpu.VMEM((n, q, 24, z), F32) for n in (3, 2)] + [pltpu.VMEM((q, 24, z), F32)]
        spaces = [pltpu.SMEM] + [pltpu.VMEM] * (len(ins) - 1)
        kernel = functools.partial(coarse_kernel, s)
        return run(kernel, "coarse", ins, [(q, x, y, z)], padded * 3 + wind_rows + columns, 9, spaces, cost)[0]

    averaged, state = move_by(averaged, offset, (coarse, (neighbours, *coarse_level, *yrows, zown, zin)))
    (coarse_next,) = run(
        functools.partial(merge_kernel, s),
        "merge",
        [state, averaged],
        [((q, x, y, z), pltpu.HBM)],
        [pltpu.VMEM((q, x, y, z), F32), pltpu.SemaphoreType.DMA((q,))],
        2,
    )
    return coarse_next, fine_next


def solution(mesh):
    spec = P(None, "gx", "gy", "gz")
    return jax.shard_map(
        shards,
        mesh=mesh,
        in_specs=(spec, spec, spec, spec, P("gx", "gy", "gz")),
        out_specs=(spec, spec),
        check_vma=False,
    )
```

```python
import functools

import jax
import jax.numpy as jnp
from jax import lax
from jax.experimental import pallas as pl
from jax.experimental.pallas import tpu as pltpu
from jax.sharding import PartitionSpec as P

diffusion = 0.05
section_weights = (1.0 / 3.0, 0.5, 1.0)
F32 = jnp.float32
BF16 = jnp.bfloat16
PAD = 32
TOP = 8


class Sizes:
    def __init__(self, coarse_shape, fine_shape):
        self.q, self.x, self.y, self.z = coarse_shape
        self.fx = fine_shape[1]
        self.ly, self.sy = self.y // 4, self.y // 2
        self.lz, self.sz = self.z // 4, self.z // 2
        self.ex = self.x + 4
        self.ep = -(-self.ex // 8) * 8
        self.fe = self.fx + 4
        self.halo = 3 * self.q + 6
        self.rows_f, self.rows_w = self.q * (3 * self.x + 6), 3 * (2 * self.x + 2)
        self.rows_y = 3 * self.q * self.ex
        self.rows_e = self.rows_y + self.ep
        self.rows_z = self.sy + 2
        self.slab = self.rows_e + self.q * self.rows_z
        assert self.q == 4 and self.y == 16 and self.z == 128 and self.ex <= 20 and self.fx == 2 * self.x


def lanes_of(shape):
    return lax.broadcasted_iota(jnp.int32, shape, len(shape) - 1)


def halves(value):
    high = value.astype(BF16)
    return high, (value - high.astype(F32)).astype(BF16)


def times(value, matrix):
    high, low = halves(value)
    return jnp.dot(high, matrix, preferred_element_type=F32) + jnp.dot(low, matrix, preferred_element_type=F32)


def coefficients(fraction, wind):
    out = []
    for w in wind:
        turned_by = w * (-0.5 * fraction)
        out += [diffusion * fraction + turned_by, diffusion * fraction - turned_by]
    return out


def advanced(base, fraction, co, center, x_low, x_high, y_low, y_high, z_low, z_high):
    along = (co[0] * x_high + co[1] * x_low) + (co[2] * y_high + co[3] * y_low) + (co[4] * z_high + co[5] * z_low)
    if base is None:
        return center * (1.0 - 6.0 * diffusion * fraction) + along
    return (base - center * (6.0 * diffusion * fraction)) + along


def layer_of(s, own, low, high, member, at, width, first):
    size = own.shape[1]
    if at < 0:
        return low[first + width * member + at + width]
    if at >= size:
        return high[first + width * member + at - size]
    return own[member, at]


def unrolled(begin, end, at_once, body, carry=None):
    while (end - begin) % at_once:
        at_once -= 1

    def several(i, carry):
        for more in range(at_once):
            carry = body(begin + i * at_once + more, carry)
        return carry

    return lax.fori_loop(0, (end - begin) // at_once, several, carry)


def pack_kernel(s, fields, wind, up, down, sems):
    size = fields.shape[1]
    moves = []
    for own, members, width, first in ((fields, s.q, 3, 0), (wind, 3, 2, 3 * s.q)):
        for dst, at in ((up, size - width), (down, 0)):
            place = dst.at[first : first + members * width].reshape(members, width, s.y, s.z)
            moves.append((own.at[:, at : at + width], place))
    moves = [pltpu.make_async_copy(src, dst, sems.at[i]) for i, (src, dst) in enumerate(moves)]
    for move in moves:
        move.start()
    for move in moves:
        move.wait()


def y_rows(s, members, width):
    below, above = [], []
    for out, extra in ((below, lambda r: r), (above, lambda r: width - 1 - r)):
        at = 0
        for m in range(members):
            for r in range(width):
                out.append((m, r, extra(r), at))
                at += s.x + 2 * extra(r)
    return below, above


def ypack_kernel(s, c0, cw, lo, hi, up, dn):
    x, y, z = s.x, s.y, s.z
    flat_lo = lo.reshape(s.halo * y, z)
    flat_hi = hi.reshape(s.halo * y, z)
    for own, members, width, first, place in ((c0, s.q, 3, 0, 0), (cw, 3, 2, 3 * s.q, s.rows_f)):
        flat = own.reshape(members * x * y, z)
        for dst, rows, start in zip((up, dn), y_rows(s, members, width), (y - width, 0)):
            for m, r, e, at in rows:
                row, at = start + r, at + place
                if e:
                    dst[at : at + e, :] = flat_lo[pl.ds((first + width * (m + 1) - e) * y + row, e, stride=y), :]
                    dst[at + e + x : at + x + 2 * e, :] = flat_hi[pl.ds((first + width * m) * y + row, e, stride=y), :]
                dst[at + e : at + e + x, :] = flat[pl.ds(m * x * y + row, x, stride=y), :]


EDGE = 4


def turned(base, fraction, wind, center, x_low, x_high):
    y, z = center.shape
    return advanced(
        base,
        fraction,
        wind,
        center,
        x_low,
        x_high,
        pltpu.roll(center, 1, 0),
        pltpu.roll(center, y - 1, 0),
        pltpu.roll(center, 1, 1),
        pltpu.roll(center, z - 1, 1),
    )


def slab_parts(s, rows_of, tile_of, layers_of, put):
    q, y, z = s.q, s.y, s.z
    lane_y = lanes_of((y, z))
    columns = (lane_y == s.lz - 1) | (lane_y == s.lz) | (lane_y == s.lz + s.sz - 1) | (lane_y == s.lz + s.sz)
    low_at = (lane_y % 2 == 0) & (lane_y < z // 2)
    high_at = (lane_y % 2 == 0) & (lane_y >= z // 2)
    ends = None
    for f in range(q):
        zfaces = None
        for k in range(3):
            rows = [rows_of(k, f, row) for row in (s.ly - 1, s.ly, s.ly + s.sy - 1, s.ly + s.sy)]
            sides = (0.75 * rows[0] + 0.25 * rows[1], 0.25 * rows[2] + 0.75 * rows[3])
            lane_x = lanes_of(sides[0].shape)
            put(
                "y",
                (k * q + f) * s.ex,
                jnp.where(lane_x < s.sz, pltpu.roll(sides[0], z - s.lz, 1), pltpu.roll(sides[1], s.lz, 1)),
            )
            for side in range(2):
                e = 4 * (q * k + f) + 2 * side + 1
                before = jnp.where(lane_x == s.lz - 1, sides[side], 0.0)
                after = jnp.where(lane_x == s.lz + s.sz, sides[side], 0.0)
                part = pltpu.roll(before, (e - s.lz + 1) % z, 1) + pltpu.roll(after, (e - 1 - s.lz - s.sz) % z, 1)
                ends = part if ends is None else ends + part
            raw = None
            for a in layers_of(k):
                part = jnp.where(columns, tile_of(k, f, a), 0.0)
                part = pltpu.roll(part, (2 * a - s.lz + 1) % z, 1)
                raw = part if raw is None else raw + part
            beside = pltpu.roll(raw, z - 1, 1)
            low = jnp.where(low_at, 0.75 * raw + 0.25 * beside, 0.0)
            high = jnp.where(high_at, 0.25 * raw + 0.75 * beside, 0.0)
            part = pltpu.roll(low, (2 * s.ex * k - 1) % z, 1) + pltpu.roll(high, (2 * s.ex * k - z // 2) % z, 1)
            zfaces = part if zfaces is None else zfaces + part
        put("z", s.rows_e + f * s.rows_z, zfaces[s.ly - 1 : s.ly + s.sy + 1])
    put("e", s.rows_y, ends)


def inner_kernel(s, c0, cw, part, near, state1, state2):
    q, x, y, z = s.q, s.x, s.y, s.z
    states = (c0, state1, state2)
    for step in range(2):
        src, dst = states[step], states[step + 1]

        def layer(j, carry, step=step, src=src, dst=dst):
            w = coefficients(section_weights[step], [cw[d, j] for d in range(3)])
            made = []
            for f in range(q):
                base = None if step == 0 else c0[f, j]
                made.append(turned(base, section_weights[step], w, src[f, j], src[f, j - 1], src[f, j + 1]))
            for f in range(q):
                dst[f, j] = made[f]
            return carry

        unrolled(step + 1, x - 1 - step, 7 if step == 0 else 6, layer)
    for f in range(q):
        near[f, 0] = state1[f, EDGE - 2]
        near[f, 1] = state1[f, x + 1 - EDGE]
    count = s.ex - 2 * EDGE
    part[...] = jnp.zeros_like(part)

    def rows_of(k, f, row):
        flat = states[k].reshape(q * x * y, z)
        return flat[pl.ds((f * x + EDGE - 2) * y + row, count, stride=y), :]

    def put(kind, at, rows):
        if kind == "z":
            part[at : at + s.rows_z, :] = rows
        else:
            part[at + EDGE : at + EDGE + count, :] = rows

    slab_parts(s, rows_of, lambda k, f, a: states[k][f, a - 2], lambda k: range(EDGE, s.ex - EDGE), put)


def slab_kernel(s, c0, cw, lo, hi, part, near, slab, ends0, ends1, ends2):
    q, x, y, z = s.q, s.x, s.y, s.z
    states = (ends0, ends1, ends2)
    places = list(range(-2, EDGE - 2)) + list(range(x + 2 - EDGE, x + 2))
    slab[...] = part[...]
    for j, at in enumerate(places):
        for f in range(q):
            ends0[f, j] = layer_of(s, c0, lo, hi, f, at, 3, 0)
    for step in range(2):
        for j, at in enumerate(places):
            if step == 1 and at in (-2, x + 1):
                for f in range(q):
                    ends2[f, j] = jnp.zeros((y, z), F32)
                continue
            w = coefficients(section_weights[step], [layer_of(s, cw, lo, hi, d, at, 2, 3 * q) for d in range(3)])
            for f in range(q):

                def beside(at, f=f):
                    if step == 0:
                        return layer_of(s, c0, lo, hi, f, at, 3, 0)
                    if at in places:
                        return ends1[f, places.index(at)]
                    return near[f, 0 if at < x // 2 else 1]

                base = None if step == 0 else ends0[f, j]
                states[step + 1][f, j] = turned(
                    base, section_weights[step], w, beside(at), beside(at - 1), beside(at + 1)
                )

    def rows_of(k, f, row):
        flat = states[k].reshape(q * 2 * EDGE * y, z)
        return flat[pl.ds(f * 2 * EDGE * y + row, 2 * EDGE, stride=y), :]

    def put(kind, at, rows):
        if kind == "z":
            slab[at : at + s.rows_z, :] = part[at : at + s.rows_z, :] + rows
        else:
            slab[at : at + EDGE, :] = rows[:EDGE]
            slab[at + s.ex - EDGE : at + s.ex, :] = rows[EDGE:]

    def layers_of(k):
        some = range(0 if k == 0 else 1, EDGE)
        return list(some) + [s.ex - 1 - a for a in some]

    def tile_of(k, f, a):
        return states[k][f, a if a < EDGE else a - s.ex + 2 * EDGE]

    slab_parts(s, rows_of, tile_of, layers_of, put)


WTOP, WPAD = 12, 40
BLOCK = slice(8, 32)


def assemble(s, c0, cw, lo, hi, below, above, pad, wind):
    q, x, y, z = s.q, s.x, s.y, s.z
    flat = pad.reshape(q * s.ep * WPAD, z)
    flat_wind = wind.reshape(3 * s.ex * 24, z)
    for f in range(q):
        for at in range(-3, x + 3):
            pad[f, at + 3, WTOP : WTOP + y, :] = layer_of(s, c0, lo, hi, f, at, 3, 0)
    for d in range(3):
        for at in range(-2, x + 2):
            wind[d, at + 2, 4 : 4 + y, :] = layer_of(s, cw, lo, hi, d, at, 2, 3 * q)
    for src, rows, start in zip((below, above), y_rows(s, q, 3), (WTOP - 3, WTOP + y)):
        for m, r, e, at in rows:
            count = x + 2 * e
            flat[pl.ds((m * s.ep + 3 - e) * WPAD + start + r, count, stride=WPAD), :] = src[at : at + count, :]
    for src, rows, start in zip((below, above), y_rows(s, 3, 2), (2, 4 + y)):
        for m, r, e, at in rows:
            count, at = x + 2 * e, at + s.rows_f
            flat_wind[pl.ds((m * s.ex + 2 - e) * 24 + start + r, count, stride=24), :] = src[at : at + count, :]


def edge_lanes(s, lane, width):
    return (lane < width) | (lane >= s.z - width)


def zpack_kernel(s, c0, cw, lo, hi, below, above, out, rows):
    q, x, y, z = s.q, s.x, s.y, s.z
    flat = rows.reshape((q + 3) * s.ex * 8, z)
    rows[...] = jnp.zeros_like(rows)
    for src, place in ((below, 0), (above, 3)):
        for member, width, first in ((0, 3, 0), (q, 2, s.rows_f)):
            skip = 3 - width if place == 0 else 0
            for m, r, e, at in y_rows(s, q if width == 3 else 3, width)[place // 3]:
                e = min(e, 2)
                count = x + 2 * e
                start = ((member + m) * s.ex + 2 - e) * 8 + place + skip + r
                flat[pl.ds(start, count, stride=8), :] = src[first + at : first + at + count, :]
    lane = lanes_of((y, z))
    keep = edge_lanes(s, lane, 3)
    for m in range(q + 3):
        inside, outside = None, None
        for a in range(s.ex):
            if m < q:
                tile = layer_of(s, c0, lo, hi, m, a - 2, 3, 0)
            else:
                tile = layer_of(s, cw, lo, hi, m - q, a - 2, 2, 3 * q)
            shift = (6 * a + 3) % z
            part = pltpu.roll(jnp.where(keep, tile, 0.0), shift, 1)
            inside = part if inside is None else inside + part
            part = pltpu.roll(jnp.where(keep[:8], rows[m, a], 0.0), shift, 1)
            outside = part if outside is None else outside + part
        out[m, 0:1, :] = jnp.zeros((1, z), F32)
        out[m, 1:4, :] = outside[0:3]
        out[m, 4 : 4 + y, :] = inside
        out[m, 4 + y : 7 + y, :] = outside[3:6]
        out[m, 7 + y : 8 + y, :] = jnp.zeros((1, z), F32)


def coarse_kernel(
    s, sides, c0, cw, lo, hi, below, above, zown, zin, out, pad0, pad1, pad2, wind, beyond, nearest, turning
):
    q, x, y, z = s.q, s.x, s.y, s.z
    assemble(s, c0, cw, lo, hi, below, above, pad0, wind)
    pads = (pad0, pad1, pad2)
    lane = lanes_of((24, z))
    group = lane % 6
    from_low = group == 2
    from_high = group == 3
    exists = jnp.where(group < 3, sides[0, 0], sides[0, 1]).astype(F32)
    wind_z = [zin[q + d] for d in range(3)]
    for f in range(q):
        beyond[0, f] = zin[f] * exists
        nearest[0, f] = zown[f]
    for step in range(3):
        src, fraction = pads[step], section_weights[step]
        flat = src.reshape(q * s.ep * WPAD, z)
        flat_wind = wind.reshape(3 * s.ex * 24, z)
        flat_beyond = beyond.reshape(3 * q * 24, z)
        skip, height = (0, 24) if step < 2 else (4, y)
        here = lanes_of((8, z))
        is_first, is_last = here == 0, here == z - 1

        def layer(a, carry, step=step, flat=flat, fraction=fraction, skip=skip, height=height):
            for r in range(0, height, 8):
                if step < 2:
                    winds = [wind[d, a, r : r + 8, :] for d in range(3)]
                else:
                    winds = [flat_wind[pl.ds((d * s.ex + a) * 24 + skip + r, 8), :] for d in range(3)]
                co = coefficients(fraction, winds)
                for f in range(q):

                    def at_layer(of, layer, by=0, f=f, r=r):
                        if step < 2 and not by:
                            return of[f, layer, 8 + r : 16 + r, :]
                        row = (f * s.ep + layer) * WPAD + 8 + skip + r + by
                        return of.reshape(flat.shape)[pl.ds(row, 8), :]

                    src = pads[step]
                    center = at_layer(src, a + 1)
                    ghost = turning[f, r : r + 8, :]
                    turning[f, r : r + 8, :] = pltpu.roll(ghost, z - 6, 1)
                    value = advanced(
                        None if step == 0 else at_layer(pad0, a + 1),
                        fraction,
                        co,
                        center,
                        at_layer(src, a),
                        at_layer(src, a + 2),
                        at_layer(src, a + 1, -1),
                        at_layer(src, a + 1, 1),
                        pltpu.roll(jnp.where(is_last, ghost, center), 1, 1),
                        pltpu.roll(jnp.where(is_first, ghost, center), z - 1, 1),
                    )
                    if step == 2:
                        out[f, a - 2, r : r + 8, :] = value
                    else:
                        pads[step + 1][f, a + 1, 8 + r : 16 + r, :] = value
                    if step == 0:
                        total = nearest[1, f, r : r + 8, :] + jnp.where(is_first | is_last, value, 0.0)
                        nearest[1, f, r : r + 8, :] = pltpu.roll(total, z - 6, 1)
            return carry

        for f in range(q):
            start = (step * q + f) * 24 + skip
            turning[f, :height, :] = pltpu.roll(flat_beyond[start : start + height, :], z - 6 * step - 3, 1)
            if step == 0:
                nearest[1, f] = jnp.zeros((24, z), F32)
        unrolled(step, s.ex - step, s.ex - 2 * step, layer)
        if step == 2:
            break
        for f in range(q):
            if step == 0:
                nearest[1, f] = pltpu.roll(nearest[1, f], (6 * s.ex + 3) % z, 1)
            ghost, near = beyond[step, f], nearest[step, f]
            value = advanced(
                None if step == 0 else beyond[0, f],
                fraction,
                coefficients(fraction, wind_z),
                ghost,
                pltpu.roll(ghost, 6, 1),
                pltpu.roll(ghost, z - 6, 1),
                pltpu.roll(ghost, 1, 0),
                pltpu.roll(ghost, 23, 0),
                pltpu.roll(jnp.where(from_low, near, ghost), 1, 1),
                pltpu.roll(jnp.where(from_high, near, ghost), z - 1, 1),
            )
            beyond[step + 1, f] = value * exists


def fine_kernel(s, f0, fw, flo_there, fhi_there, slab, out, avg, *scratch):
    s1, s2, faces, ghost_rows, zface, turning, flo, fhi, summed, sems = scratch
    arrivals = [
        pltpu.make_async_copy(flo_there, flo, sems.at[4]),
        pltpu.make_async_copy(fhi_there, fhi, sems.at[5]),
    ]
    for move in arrivals:
        move.start()
    states = (None, s1, s2, s1)
    q, y, z, fx, fe = s.q, s.y, s.z, s.fx, s.fe
    layers = fx + 6
    rows = slice(TOP, TOP + y)
    shift_z, shift_sz = z.bit_length() - 1, s.sz.bit_length() - 1
    r = lax.broadcasted_iota(jnp.int32, (2 * z, 2 * z), 0)
    c = lax.broadcasted_iota(jnp.int32, (2 * z, 2 * z), 1)
    near = c >> 1
    far = near + 2 * (c & 1) - 1
    same = (far >> shift_sz) == (near >> shift_sz)
    to_fine = jnp.where(r == near, 0.75, jnp.where((r == far) & same, 0.25, 0.0))
    ends_at = ((r & 2) << (shift_z - 1)) + jnp.where((r & 1) == 1, 0, z - 1)
    to_fine = jnp.where(r < z, to_fine, jnp.where(c == ends_at, 0.25, 0.0)).astype(BF16)
    ends = slab[s.rows_y : s.rows_y + s.ex, :]
    lane_x = lanes_of((s.ex, z))
    own_ends = [jnp.where((lane_x >> 2) == i, ends, 0.0) for i in range(3 * q)]
    wide = times(jnp.concatenate([slab[: s.rows_y, :], jnp.concatenate(own_ends, axis=0)], axis=1), to_fine)
    half = fe // 2
    for k in range(3):
        for f in range(q):
            for side in range(2):
                first = (k * q + f) * s.ex
                here = faces.at[(k * q + f) * 2 + side]
                here[: s.ex, :] = wide[first : first + s.ex, side * z : side * z + z]
                a = here[0:half, :]
                b = here[1 : half + 1, :]
                d = here[2 : half + 2, :]
                if k == 0:
                    flat, base, stride = ghost_rows, (2 * f + side) * fe, 1
                else:
                    flat, stride = states[k].reshape(q * layers * PAD, z), PAD
                    base = (f * layers + 1) * PAD + (TOP - 1 if side == 0 else TOP + y)
                flat[pl.ds(base, half, stride=2 * stride), :] = 0.25 * a + 0.75 * b
                flat[pl.ds(base + stride, half, stride=2 * stride), :] = 0.75 * b + 0.25 * d
    for f in range(q):
        at = s.rows_e + f * s.rows_z
        a = slab[at : at + s.sy, :]
        b = slab[at + 1 : at + 1 + s.sy, :]
        d = slab[at + 2 : at + 2 + s.sy, :]
        zface[pl.ds(f * y, s.sy, stride=2), :] = 0.25 * a + 0.75 * b
        zface[pl.ds(f * y + 1, s.sy, stride=2), :] = 0.75 * b + 0.25 * d
        a = zface[f * y : f * y + y, :]
        b = pltpu.roll(a, z - 2, 1)
        d = pltpu.roll(a, z - 4, 1)
        zface[f * y : f * y + y, :] = 0.25 * a + 0.75 * b
        zface[(q + f) * y : (q + f + 1) * y, :] = 0.75 * b + 0.25 * d
    lane = lanes_of((8, z))
    is_first, is_last = lane == 0, lane == z - 1
    row_in = lax.broadcasted_iota(jnp.int32, (8, z), 0)
    is_low, is_high = row_in == 0, row_in == 7
    flat_f0 = f0.reshape(q * fx * y, z)

    def turn_to(k, t):
        shift = -(2 * s.ex * k + 2 * t) % z
        for i in range(2 * q):
            packed = zface[i * y : (i + 1) * y, :]
            turning[i * y : (i + 1) * y, :] = pltpu.roll(packed, shift, 1) if shift else packed

    def pair_of_layers(k, t, inner):
        src, fraction = states[k], section_weights[k]

        def field(f, at):
            return layer_of(s, f0, flo, fhi, f, at, 3, 0)

        for odd, r in ((odd, r) for odd in range(2) for r in range(0, y, 8)):
            b = 2 * t + odd
            at = b - 2
            half_tile = slice(r, r + 8)
            if inner:
                winds = [fw[d, at, half_tile, :] for d in range(3)]
            else:
                winds = [layer_of(s, fw, flo, fhi, d, at, 2, 3 * q)[half_tile] for d in range(3)]
            co = coefficients(fraction, winds)
            for f in range(q):
                if k == 0:
                    if inner:
                        center, x_low, x_high = (f0[f, at + by, half_tile, :] for by in (0, -1, 1))
                        row = (f * fx + at) * y + r
                        y_low, y_high = flat_f0[pl.ds(row - 1, 8), :], flat_f0[pl.ds(row + 1, 8), :]
                    else:
                        whole = field(f, at)
                        y_low, y_high = pltpu.roll(whole, 1, 0)[half_tile], pltpu.roll(whole, y - 1, 0)[half_tile]
                        center, x_low, x_high = (field(f, at + by)[half_tile] for by in (0, -1, 1))
                    if r == 0:
                        y_low = jnp.where(is_low, ghost_rows[pl.ds(2 * f * fe + b, 1), :], y_low)
                    if r == y - 8:
                        y_high = jnp.where(is_high, ghost_rows[pl.ds((2 * f + 1) * fe + b, 1), :], y_high)
                    base = None
                else:
                    flat = src.reshape(q * layers * PAD, z)
                    row = (f * layers + b + 1) * PAD + TOP + r
                    center, x_low, x_high = (src[f, b + by, TOP + r : TOP + r + 8, :] for by in (1, 0, 2))
                    y_low, y_high = flat[pl.ds(row - 1, 8), :], flat[pl.ds(row + 1, 8), :]
                    base = f0[f, at, half_tile, :] if inner else field(f, at)[half_tile]
                i = (odd * q + f) * y + r
                ghost = turning[i : i + 8, :]
                turning[i : i + 8, :] = pltpu.roll(ghost, z - 2, 1)
                states[k + 1][f, b + 1, TOP + r : TOP + r + 8, :] = advanced(
                    base,
                    fraction,
                    co,
                    center,
                    x_low,
                    x_high,
                    y_low,
                    y_high,
                    pltpu.roll(jnp.where(is_last, ghost, center), 1, 1),
                    pltpu.roll(jnp.where(is_first, ghost, center), z - 1, 1),
                )

    for move in arrivals:
        move.wait()
    moves = []
    for k in range(3):
        if k < 2:
            outer = 2 - k
            for t in range(outer):
                turn_to(k, t)
                pair_of_layers(k, t, False)
            unrolled(outer, half - outer, half - 2 * outer, lambda t, g, k=k: pair_of_layers(k, t, True))
            for t in range(half - outer, half):
                pair_of_layers(k, t, False)
            continue
        turn_to(k, 1)
        quarter = (half - 2) // 4
        for i in range(4):
            unrolled(1 + i * quarter, 1 + (i + 1) * quarter, 4, lambda t, g, k=k: pair_of_layers(k, t, True))
            begin, end = 2 * quarter * i, 2 * quarter * (i + 1)
            moves.append(pltpu.make_async_copy(s1.at[:, 3 + begin : 3 + end, rows], out.at[:, begin:end], sems.at[i]))
            moves[-1].start()
    rz = lax.broadcasted_iota(jnp.int32, (z, z), 0)
    cz = lax.broadcasted_iota(jnp.int32, (z, z), 1)
    flat = summed.reshape(q * s.x * y, z)
    pairs_z = [jnp.where(cz == (rz >> 1) + odd * s.sz, 0.125, 0.0).astype(BF16) for odd in range(2)]
    for f in range(q):
        for p in range(s.x):
            both = s1[f, 3 + 2 * p, rows, :] + s1[f, 4 + 2 * p, rows, :]
            summed[f, p] = both + pltpu.roll(both, y - 1, 0)
    for f in range(q):
        sums = []
        for odd in range(2):
            parts = [flat[pl.ds((f * s.x + 2 * p + odd) * y, y // 2, stride=2), :] for p in range(s.x // 2)]
            sums.append(times(jnp.concatenate(parts, axis=0), pairs_z[odd]))
        avg[f] = (sums[0] + sums[1]).reshape(s.x // 2, y // 2, z)
    for move in moves:
        move.wait()


def merge_kernel(s, c3, avg, out, made, sems):
    lane = lanes_of((s.sy, s.z))
    inside = (lane >= s.lz) & (lane < s.lz + s.sz)
    moves = []
    for f in range(s.q):
        for p in range(s.x // 2):
            both = avg[f, p]
            for odd in range(2):
                at = 2 * p + odd
                moved = pltpu.roll(both, s.lz if odd == 0 else s.z - s.lz, 1)
                made[f, at] = c3[f, at]
                made[f, at, s.ly : s.ly + s.sy, :] = jnp.where(inside, moved, c3[f, at, s.ly : s.ly + s.sy, :])
        moves.append(pltpu.make_async_copy(made.at[f], out.at[f], sems.at[f]))
        moves[-1].start()
    for move in moves:
        move.wait()


SHORT = pl.CostEstimate(flops=1, bytes_accessed=1, transcendentals=0)


def run(kernel, name, ins, outs, scratch, megabytes, spaces=None, cost=SHORT):
    spaces = spaces or [pltpu.VMEM] * len(ins)
    outs = [out if isinstance(out[0], tuple) else (out, pltpu.VMEM) for out in outs]
    ins = [i if space is pltpu.SMEM else pltpu.with_memory_space_constraint(i, space) for i, space in zip(ins, spaces)]
    return pl.pallas_call(
        kernel,
        out_shape=tuple(space(dims, F32) for dims, space in outs),
        in_specs=[pl.BlockSpec(memory_space=space) for space in spaces],
        out_specs=tuple(pl.BlockSpec(memory_space=space) for _, space in outs),
        scratch_shapes=scratch,
        compiler_params=pltpu.CompilerParams(vmem_limit_bytes=megabytes << 20),
        cost_estimate=cost,
        name=name,
    )(*ins)


def ring(array, axis, by):
    size = lax.axis_size(axis)
    return lax.ppermute(array, axis, [(i, (i + by) % size) for i in range(size)])


def move_by(array, amount, beside=None):
    size = lax.axis_size("gx")
    work, operands = beside or (lambda: (), ())
    if size <= 8:

        def branch(by, array, *operands):
            return array if by == 0 else ring(array, "gx", by), work(*operands)

        return lax.switch(amount, [functools.partial(branch, by) for by in range(size)], array, *operands)
    for bit in range((size - 1).bit_length()):
        array = jnp.where((amount >> bit) % 2 == 1, ring(array, "gx", 1 << bit), array)
    return array, work(*operands)


def z_columns(zown):
    size = lax.axis_size("gz")
    if size == 1:
        return zown
    if size == 2:
        return lax.ppermute(zown, "gz", [(0, 1), (1, 0)])
    below = lax.broadcasted_iota(jnp.int32, zown.shape, 2) % 6 < 3
    return jnp.where(below, ring(zown, "gz", 1), ring(zown, "gz", -1))


def pack(s, fields, wind, spare, name):
    return run(
        functools.partial(pack_kernel, s),
        name,
        [fields, wind],
        [(s.halo + spare, s.y, s.z)] * 2,
        [pltpu.SemaphoreType.DMA((4,))],
        1,
        [pltpu.HBM] * 2,
    )


def shards(coarse_fields, coarse_wind, fine_fields, fine_wind, fine_owner):
    s = Sizes(coarse_fields.shape, fine_fields.shape)
    q, x, y, z, fx = s.q, s.x, s.y, s.z, s.fx
    size = lax.axis_size("gx")
    offset = (fine_owner[0, 0, 0] - lax.axis_index("gx")) % size
    level = lax.axis_index("gz")
    neighbours = jnp.stack([level > 0, level < lax.axis_size("gz") - 1]).astype(jnp.int32).reshape(1, 2)
    cup, cdown = pack(s, coarse_fields, coarse_wind, 0, "pack_coarse")
    lo, hi = ring(cup, "gx", 1), ring(cdown, "gx", -1)
    part, near = run(
        functools.partial(inner_kernel, s),
        "inner",
        [coarse_fields, coarse_wind],
        [(s.slab, z), (q, 2, y, z)],
        [pltpu.VMEM((q, x, y, z), F32)] * 2,
        3,
    )
    fup, fdown = pack(s, fine_fields, fine_wind, 2, "pack_fine")
    fup, fdown, offset = lax.optimization_barrier((fup, fdown, offset))
    flo, fhi = ring(fup, "gx", 1), ring(fdown, "gx", -1)
    padded = [pltpu.VMEM((q, s.ep, WPAD, z), F32)]
    wind_rows = [pltpu.VMEM((3, s.ex, 24, z), F32)]
    coarse_fields, part, near = lax.optimization_barrier((coarse_fields, part, near))
    coarse_level = [coarse_fields, coarse_wind, lo, hi]
    yup, ydn = run(functools.partial(ypack_kernel, s), "ypack", coarse_level, [(s.rows_f + s.rows_w, z)] * 2, [], 1)
    yrows = [ring(yup, "gy", 1), ring(ydn, "gy", -1)]
    ends = [pltpu.VMEM((q, 2 * EDGE, y, z), F32)] * 3
    (slab,) = run(functools.partial(slab_kernel, s), "slab", coarse_level + [part, near], [(s.slab, z)], ends, 3)
    slab, _ = move_by(slab, (size - offset) % size)
    yrows, slab, flo, fhi = lax.optimization_barrier((yrows, slab, flo, fhi))
    kernel = functools.partial(zpack_kernel, s)
    beyond_rows = [pltpu.VMEM((q + 3, s.ex, 8, z), F32)]
    (zown,) = run(kernel, "zpack", coarse_level + yrows, [(q + 3, 24, z)], beyond_rows, 2)
    zin = z_columns(zown)
    layers = fx + 6
    fine_next, averaged = run(
        functools.partial(fine_kernel, s),
        "fine",
        [fine_fields, fine_wind, flo, fhi, slab],
        [((q, fx, y, z), pltpu.HBM), (q, x // 2, y // 2, z)],
        [
            pltpu.VMEM((q, layers, PAD, z), F32),
            pltpu.VMEM((q, layers, PAD, z), F32),
            pltpu.VMEM((6 * q, s.ep, z), F32),
            pltpu.VMEM((2 * q * s.fe, z), F32),
            pltpu.VMEM((2 * q * y, z), F32),
            pltpu.VMEM((2 * q * y, z), F32),
            pltpu.VMEM(flo.shape, F32),
            pltpu.VMEM(fhi.shape, F32),
            pltpu.VMEM((q, s.x, y, z), F32),
            pltpu.SemaphoreType.DMA((6,)),
        ],
        9,
        [pltpu.VMEM, pltpu.VMEM, pltpu.HBM, pltpu.HBM, pltpu.VMEM],
    )

    def coarse(*ins):
        cost = pl.CostEstimate(flops=40_000_000, bytes_accessed=4_000_000, transcendentals=0)
        columns = [pltpu.VMEM((n, q, 24, z), F32) for n in (3, 2)] + [pltpu.VMEM((q, 24, z), F32)]
        spaces = [pltpu.SMEM] + [pltpu.VMEM] * (len(ins) - 1)
        kernel = functools.partial(coarse_kernel, s)
        return run(kernel, "coarse", ins, [(q, x, y, z)], padded * 3 + wind_rows + columns, 9, spaces, cost)[0]

    averaged, state = move_by(averaged, offset, (coarse, (neighbours, *coarse_level, *yrows, zown, zin)))
    (coarse_next,) = run(
        functools.partial(merge_kernel, s),
        "merge",
        [state, averaged],
        [((q, x, y, z), pltpu.HBM)],
        [pltpu.VMEM((q, x, y, z), F32), pltpu.SemaphoreType.DMA((q,))],
        2,
    )
    return coarse_next, fine_next


def solution(mesh):
    spec = P(None, "gx", "gy", "gz")
    return jax.shard_map(
        shards,
        mesh=mesh,
        in_specs=(spec, spec, spec, spec, P("gx", "gy", "gz")),
        out_specs=(spec, spec),
        check_vma=False,
    )
```
